128 devices in a mesh: lat: 8 (over x_lo, y), lon: 16 (over x_hi, z, core).
Axes of the slice: x: 4 (x_hi: 2, x_lo: 2; x = x_hi * 2 + x_lo), y: 4, z: 4, core: 2. Of those that a mesh axis runs over, the one named last changes fastest.
Arguments:
- field_in: bfloat16 [256, 1024, 256], P('lat', 'lon'), may hold values from -6 to 6
- cotangent: bfloat16 [256, 1024, 256], P('lat', 'lon'), may hold values from -6 to 6
- expand_weight: bfloat16 [256, 1024], replicated, may hold values from -0.375 to 0.375
- depth_kernel: float32 [3, 3, 1024], replicated, may hold values from -2 to 2
- project_weight: bfloat16 [1024, 256], replicated, may hold values from -0.1875 to 0.1875
- qkv_weight: bfloat16 [256, 768], replicated, may hold values from -0.375 to 0.375
- out_weight: bfloat16 [256, 256], replicated, may hold values from -0.375 to 0.375
- rel_bias: float32 [4, 15, 15], replicated, may hold values from -2 to 250
Outputs:
- grad_in: bfloat16 [256, 1024, 256], P('lat', 'lon')
- expand_grad: float32 [256, 1024], replicated
- depth_grad: float32 [3, 3, 1024], replicated
- project_grad: float32 [1024, 256], replicated
- qkv_grad: float32 [256, 768], replicated
- out_grad: float32 [256, 256], replicated
- bias_grad: float32 [4, 15, 15], replicated
The draws below stay inside these ranges and needn't reach their ends.
All inputs are finite; a program needn't handle non-finite values.
Results may differ from the reference program's by a relative error of at most 0.013.
Values may be sent and summed in bfloat16 or wider, within the bound.
No kernel may reach another device: no remote copies, remote signals or barrier semaphores. Data moves between devices by JAX's collectives and lax.ppermute only.
A program may use at most 192 MiB of HBM per device.

```python
import math
import jax
import jax.numpy as jnp
from jax import lax

C = 256
E = 1024
HEADS = 4
H = 256
W = 1024


def draw_rel_bias(key, part):
    key = jax.random.fold_in(key, 7)
    base = jax.random.uniform(key, (HEADS, 15, 15), jnp.float32, -2.0, 2.0)
    return base


def steps_of(stream_key, dims, shards, smallest, top_value):
    gain = 1.0
    for axis_at, shards_of in shards:
        heights = jax.random.uniform(jax.random.fold_in(jax.random.fold_in(stream_key, 6), axis_at), (shards_of,), jnp.float32, smallest / len(shards), top_value / len(shards))
        gain = gain * jnp.repeat(jnp.exp(heights), dims[axis_at] // shards_of).reshape((-1,) + (1,) * (len(dims) - 1 - axis_at))
    return gain


def noise(stream_key, extent, scale, bound, shards=(), dtype=jnp.bfloat16):
    loudness = steps_of(stream_key, extent, shards, -0.22, 0.18) if shards else 1.0
    array = jax.random.normal(stream_key, extent, jnp.float32) * scale * loudness
    return jnp.minimum(jnp.maximum(array, -bound), bound).astype(dtype)


def setup_inputs(seed: int = 0) -> dict:
    keys = jax.random.split(jax.random.key(seed), 9)
    field_in = noise(keys[0], (H, W, C), 1.0, 6.0, ((0, 8), (1, 16)))
    cotangent = noise(keys[1], (H, W, C), 1.0, 6.0, ((0, 8), (1, 16)))
    expand_weight = noise(keys[2], (C, E), C ** -0.5, 0.375)
    depth_kernel = noise(keys[3], (3, 3, E), 9 ** -0.5, 2.0, (), jnp.float32)
    project_weight = noise(keys[4], (E, C), E ** -0.5, 0.1875)
    qkv_weight = noise(keys[5], (C, 3 * C), C ** -0.5, 0.375)
    out_weight = noise(keys[6], (C, C), C ** -0.5, 0.375)
    rel_bias = draw_rel_bias(jax.random.fold_in(keys[8], 71), 0)
    return {"field_in": field_in, "cotangent": cotangent, "expand_weight": expand_weight, "depth_kernel": depth_kernel, "project_weight": project_weight, "qkv_weight": qkv_weight, "out_weight": out_weight, "rel_bias": rel_bias}


EPSILON = 1e-05
GELU_C = math.sqrt(2.0 / math.pi)

def layer_norm(values):
    average = lax.optimization_barrier(jnp.mean(values, axis=-1, keepdims=True))
    centred = values - average
    variance = lax.optimization_barrier(jnp.mean(centred * centred, axis=-1, keepdims=True))
    inv_std = lax.rsqrt(variance + EPSILON)
    return (centred * inv_std, inv_std)

def layer_norm_back(normed, inv_std, grads):
    mean_grad = lax.optimization_barrier(jnp.mean(grads, axis=-1, keepdims=True))
    mean_cross = lax.optimization_barrier(jnp.mean(grads * normed, axis=-1, keepdims=True))
    return (grads - mean_grad - normed * mean_cross) * inv_std

def gelu_slope(values):
    inner_arg = GELU_C * (values + 0.044715 * values * values * values)
    tanh_val = jnp.tanh(inner_arg)
    result = 0.5 * values * (1.0 + tanh_val)
    slopes = 0.5 * (1.0 + tanh_val) + 0.5 * values * (1.0 - tanh_val * tanh_val) * GELU_C * (1.0 + 3.0 * 0.044715 * values * values)
    return (result, slopes)

def pad_field(field):
    padded_rows = jnp.pad(field, ((1, 1), (0, 0), (0, 0)))
    return jnp.concatenate([padded_rows[:, -1:], padded_rows, padded_rows[:, :1]], axis=1)

def depthwise(padded, kernel):
    n_rows = padded.shape[0] - 2
    n_cols = padded.shape[1] - 2
    summed = jnp.zeros((n_rows, n_cols, padded.shape[2]), jnp.float32)
    for row_off in range(3):
        for col_off in range(3):
            summed = summed + padded[row_off:row_off + n_rows, col_off:col_off + n_cols].astype(jnp.float32) * kernel[row_off, col_off]
    return summed

def depthwise_back(padded_grad, kernel):
    n_rows = padded_grad.shape[0] - 2
    n_cols = padded_grad.shape[1] - 2
    summed = jnp.zeros((n_rows, n_cols, padded_grad.shape[2]), jnp.float32)
    for row_off in range(3):
        for col_off in range(3):
            summed = summed + padded_grad[2 - row_off:2 - row_off + n_rows, 2 - col_off:2 - col_off + n_cols].astype(jnp.float32) * kernel[row_off, col_off]
    return summed

def kernel_grad(padded, grads):
    n_rows, n_cols = (grads.shape[0], grads.shape[1])
    grads32 = grads.astype(jnp.float32)
    outer_list = []
    for row_off in range(3):
        inner_list = []
        for col_off in range(3):
            window = padded[row_off:row_off + n_rows, col_off:col_off + n_cols].astype(jnp.float32)
            inner_list.append(lax.optimization_barrier(jnp.sum(window * grads32, axis=(0, 1))))
        outer_list.append(jnp.stack(inner_list))
    return jnp.stack(outer_list)

def product(form, left, right):
    return jnp.einsum(form, left.astype(jnp.float32), right.astype(jnp.float32))

def contract_rows(left, right):
    return jnp.dot(left.astype(jnp.float32).T, right.astype(jnp.float32))

def rel_table():
    position = jnp.arange(64)
    pos_row = position // 8
    pos_col = position % 8
    rel_index = (pos_row[:, None] - pos_row[None, :] + 7) * 15 + (pos_col[:, None] - pos_col[None, :] + 7)
    return (rel_index[:, :, None] == jnp.arange(225)[None, None, :]).astype(jnp.float32)

def grid_attention_back(tokens, grads, qkv_weight, out_weight, rel_bias):
    n_groups = tokens.shape[0]
    n_chan = tokens.shape[2]
    n_heads = rel_bias.shape[0]
    head_dim = n_chan // n_heads
    head_scale = head_dim ** (-0.5)
    onehot = rel_table()
    bias_full = jnp.einsum('ijr,hr->hij', onehot, rel_bias.reshape(n_heads, 225), precision=lax.Precision.HIGHEST)
    normed, inv_std = layer_norm(tokens.astype(jnp.float32))
    normed_b = normed.astype(jnp.bfloat16)
    projected = product('gtc,cf->gtf', normed_b, qkv_weight).astype(jnp.bfloat16)
    queries = projected[..., :n_chan].reshape(n_groups, 64, n_heads, head_dim)
    keys_h = projected[..., n_chan:2 * n_chan].reshape(n_groups, 64, n_heads, head_dim)
    values = projected[..., 2 * n_chan:].reshape(n_groups, 64, n_heads, head_dim)
    scores = product('gthd,gshd->ghts', queries, keys_h) * head_scale + bias_full[None]
    attn_w = jax.nn.softmax(scores, axis=-1)
    attn_b = attn_w.astype(jnp.bfloat16)
    attended = product('ghts,gshd->gthd', attn_b, values).astype(jnp.bfloat16).reshape(n_groups, 64, n_chan)
    out_sum = product('gtc,gtf->cf', attended, grads)
    d_att = product('gtf,cf->gtc', grads, out_weight).astype(jnp.bfloat16).reshape(n_groups, 64, n_heads, head_dim)
    d_probs = product('gthd,gshd->ghts', d_att, values)
    d_value = product('ghts,gthd->gshd', attn_b, d_att).astype(jnp.bfloat16)
    d_scores = attn_w * (d_probs - lax.optimization_barrier(jnp.sum(attn_w * d_probs, axis=-1, keepdims=True)))
    bias_sum = jnp.einsum('ghts,tsr->hr', d_scores, onehot, precision=lax.Precision.HIGHEST).reshape(n_heads, 15, 15)
    d_scores_b = d_scores.astype(jnp.bfloat16)
    d_query = (product('ghts,gshd->gthd', d_scores_b, keys_h) * head_scale).astype(jnp.bfloat16)
    d_key = (product('ghts,gthd->gshd', d_scores_b, queries) * head_scale).astype(jnp.bfloat16)
    d_proj = jnp.concatenate([d_query.reshape(n_groups, 64, n_chan), d_key.reshape(n_groups, 64, n_chan), d_value.reshape(n_groups, 64, n_chan)], axis=-1)
    qkv_sum = product('gtc,gtf->cf', normed_b, d_proj)
    d_normed = product('gtf,cf->gtc', d_proj, qkv_weight)
    d_tokens = layer_norm_back(normed, inv_std, d_normed).astype(jnp.bfloat16)
    return (d_tokens, qkv_sum, out_sum, bias_sum)

def to_groups(field):
    n_rows, n_cols, n_chan = field.shape
    grid_view = field.reshape(8, n_rows // 8, 8, n_cols // 8, n_chan).transpose(1, 3, 0, 2, 4)
    return grid_view.reshape(-1, 64, n_chan)

def from_groups(field, n_rows, n_cols):
    n_chan = field.shape[-1]
    grid_view = field.reshape(n_rows // 8, n_cols // 8, 8, 8, n_chan).transpose(2, 0, 3, 1, 4)
    return grid_view.reshape(n_rows, n_cols, n_chan)

def reference(field_in, cotangent, expand_weight, depth_kernel, project_weight, qkv_weight, out_weight, rel_bias):
    n_rows, n_cols, n_chan = field_in.shape
    n_flat = n_rows * n_cols
    n_exp = expand_weight.shape[1]
    normed, inv_std = layer_norm(field_in.astype(jnp.float32))
    normed_b = normed.astype(jnp.bfloat16)
    pre_act = jnp.dot(normed_b.reshape(n_flat, n_chan), expand_weight, preferred_element_type=jnp.float32)
    act_val, act_slope = gelu_slope(pre_act)
    hidden = act_val.astype(jnp.bfloat16).reshape(n_rows, n_cols, n_exp)
    padded_hidden = pad_field(hidden)
    mixed_pre = depthwise(padded_hidden, depth_kernel)
    mixed_val, mixed_slope = gelu_slope(mixed_pre)
    mixed_b = mixed_val.astype(jnp.bfloat16).reshape(n_flat, n_exp)
    branch = jnp.dot(mixed_b, project_weight, preferred_element_type=jnp.float32)
    section = (field_in.astype(jnp.float32) + branch.reshape(n_rows, n_cols, n_chan)).astype(jnp.bfloat16)
    grouped = to_groups(section)
    grouped_grad = to_groups(cotangent)
    n_groups = grouped.shape[0]
    block = math.gcd(n_groups, 256)

    def step_fn(carry, pieces):
        d_tok, qkv_part, out_part, bias_part = grid_attention_back(pieces[0], pieces[1], qkv_weight, out_weight, rel_bias)
        return ((carry[0] + qkv_part, carry[1] + out_part, carry[2] + bias_part), d_tok)
    init = (jnp.zeros((n_chan, 3 * n_chan), jnp.float32), jnp.zeros((n_chan, n_chan), jnp.float32), jnp.zeros(rel_bias.shape, jnp.float32))
    carried, d_blocks = lax.scan(step_fn, init, (grouped.reshape(-1, block, 64, n_chan), grouped_grad.reshape(-1, block, 64, n_chan)))
    qkv_sum, out_sum, bias_sum = carried
    d_branch = from_groups(d_blocks.reshape(n_groups, 64, n_chan), n_rows, n_cols)
    d_section = cotangent.astype(jnp.float32) + d_branch.astype(jnp.float32)
    d_section_b = d_section.astype(jnp.bfloat16).reshape(n_flat, n_chan)
    project_sum = contract_rows(mixed_b, d_section_b)
    d_mixed_val = jnp.dot(d_section_b, project_weight.T, preferred_element_type=jnp.float32)
    d_mixed = (d_mixed_val * mixed_slope.reshape(n_flat, n_exp)).astype(jnp.bfloat16).reshape(n_rows, n_cols, n_exp)
    depth_sum = kernel_grad(padded_hidden, d_mixed)
    d_hidden = depthwise_back(pad_field(d_mixed), depth_kernel).reshape(n_flat, n_exp)
    d_pre = (d_hidden * act_slope).astype(jnp.bfloat16)
    expand_sum = contract_rows(normed_b.reshape(n_flat, n_chan), d_pre)
    d_normed = jnp.dot(d_pre, expand_weight.T, preferred_element_type=jnp.float32)
    d_input = layer_norm_back(normed, inv_std, d_normed.reshape(n_rows, n_cols, n_chan))
    grad_in = (d_section + d_input).astype(jnp.bfloat16)
    factor = float(n_flat) ** (-0.5)
    return (grad_in, expand_sum * factor, depth_sum * factor, project_sum * factor, qkv_sum * factor, out_sum * factor, bias_sum * factor)
```

```python
import math

import jax
import jax.numpy as jnp
import numpy as np
from jax import lax
from jax.experimental import pallas as pl
from jax.experimental.pallas import tpu as pltpu
from jax.sharding import PartitionSpec as P

EPSILON = 1e-05
GELU_C = math.sqrt(2.0 / math.pi)
F32 = jnp.float32
BF16 = jnp.bfloat16
MIB = 1 << 20

ROWS, COLS, CHAN, EXP = 32, 64, 256, 1024
BLK = 4
STEPS = ROWS // BLK
TOK = BLK * COLS
LANES = 128
EDGE = 40
HALO = 2 * COLS + 2 * EDGE


def layer_norm(values):
    average = jnp.mean(values, axis=-1, keepdims=True)
    centred = values - average
    variance = jnp.mean(centred * centred, axis=-1, keepdims=True)
    inv_std = lax.rsqrt(variance + EPSILON)
    return (centred * inv_std, inv_std)


def layer_norm_back(normed, inv_std, grads):
    mean_grad = jnp.mean(grads, axis=-1, keepdims=True)
    mean_cross = jnp.mean(grads * normed, axis=-1, keepdims=True)
    return (grads - mean_grad - normed * mean_cross) * inv_std


def gelu_slope(values):
    squared = values * values
    tanh_val = jnp.tanh(values * (GELU_C + (GELU_C * 0.044715) * squared))
    gate = 0.5 + 0.5 * tanh_val
    result = values * gate
    slopes = gate + result * (1.0 - gate) * (2.0 * GELU_C + (6.0 * GELU_C * 0.044715) * squared)
    return (result, slopes)


def dot(left, right):
    return lax.dot_general(left, right, (((1,), (0,)), ((), ())), preferred_element_type=F32)


def dot_nt(left, right):
    return lax.dot_general(left, right, (((1,), (1,)), ((), ())), preferred_element_type=F32)


def dot_tn(left, right):
    return lax.dot_general(left, right, (((0,), (0,)), ((), ())), preferred_element_type=F32)


def params(mib):
    return pltpu.CompilerParams(vmem_limit_bytes=mib * MIB)


def whole(shape):
    return pl.BlockSpec(shape, lambda i: (0,) * len(shape))


def band(shape):
    return pl.BlockSpec(shape, lambda i: (i,) + (0,) * (len(shape) - 1))


ROW_BEFORE = pl.BlockSpec((1, COLS, EXP), lambda i: (jnp.maximum(BLK * i - 1, 0), 0, 0))
ROW_AFTER = pl.BlockSpec((1, COLS, EXP), lambda i: (jnp.minimum(BLK * i + BLK, ROWS - 1), 0, 0))


def expand_body(x_ref, we_ref, hid_ref, slope_ref):
    normed, _ = layer_norm(x_ref[...].reshape(TOK, CHAN).astype(F32))
    normed_b = normed.astype(BF16)
    for at in range(0, EXP, 256):
        val, slope = gelu_slope(dot(normed_b, we_ref[:, at : at + 256]))
        hid_ref[:, :, at : at + 256] = val.astype(BF16).reshape(BLK, COLS, 256)
        slope_ref[:, :, at : at + 256] = slope.astype(BF16).reshape(BLK, COLS, 256)


def expand(x, we):
    wide = jax.ShapeDtypeStruct((ROWS, COLS, EXP), BF16)
    return pl.pallas_call(
        expand_body,
        grid=(STEPS,),
        in_specs=[band((BLK, COLS, CHAN)), whole((CHAN, EXP))],
        out_specs=[band((BLK, COLS, EXP))] * 2,
        out_shape=[wide, wide],
        compiler_params=params(32),
        cost_estimate=pl.CostEstimate(
            flops=2 * ROWS * COLS * CHAN * EXP, bytes_accessed=10 * MIB, transcendentals=ROWS * COLS * EXP
        ),
        name="expand",
    )(x, we)


def mix_body(
    cur_ref, before_ref, after_ref, halo_ref, we_ref, dk_ref, wp_ref, x_ref,
    section_ref, mixed_ref, slope_ref, top_ref, bottom_ref, left_ref, right_ref,
):
    step = pl.program_id(0)

    @pl.when(step == 0)
    def _():
        normed, _ = layer_norm(halo_ref[...].astype(F32))
        normed_b = normed.astype(BF16)
        for at in range(0, EXP, 256):
            span = slice(at, at + 256)
            val, _ = gelu_slope(dot(normed_b, we_ref[:, span]))
            val = val.astype(BF16).astype(F32)
            top_ref[:, span] = val[:COLS]
            bottom_ref[:, span] = val[COLS : 2 * COLS]
            for ref, base, col in ((left_ref, 2 * COLS, 0), (right_ref, 2 * COLS + EDGE, 2)):
                total = 0.0
                for a in range(3):
                    total = total + dk_ref[3 * a + col, span][None] * val[base + a : base + a + ROWS]
                for s in range(STEPS):
                    ref[s, :BLK, span] = total[BLK * s : BLK * s + BLK]

    first, last = step == 0, step == STEPS - 1
    for at in range(0, EXP, LANES):
        span = slice(at, at + LANES)
        rows = [jnp.where(first, top_ref[:, span], before_ref[0, :, span].astype(F32))]
        rows += [cur_ref[r, :, span].astype(F32) for r in range(BLK)]
        rows += [jnp.where(last, bottom_ref[:, span], after_ref[0, :, span].astype(F32))]
        kern = [dk_ref[n, span][None] for n in range(9)]
        for r in range(BLK):
            parts = [
                kern[b] * rows[r] + kern[3 + b] * rows[r + 1] + kern[6 + b] * rows[r + 2]
                for b in range(3)
            ]
            left = left_ref[step, r : r + 1, span]
            right = right_ref[step, r : r + 1, span]
            pre = (
                parts[1]
                + jnp.concatenate([left, parts[0][:-1]], axis=0)
                + jnp.concatenate([parts[2][1:], right], axis=0)
            )
            val, slope = gelu_slope(pre)
            mixed_ref[r, :, span] = val.astype(BF16)
            slope_ref[r, :, span] = slope.astype(BF16)
    branch = dot(mixed_ref[...].reshape(TOK, EXP), wp_ref[...])
    section = (x_ref[...].reshape(TOK, CHAN).astype(F32) + branch).astype(BF16)
    section = section.reshape(2, 2, 4, 16, CHAN)
    for pair in range(2):
        for quad in range(4):
            section_ref[4 * pair + quad] = section[pair, :, quad].reshape(32, CHAN)


def mix(hidden, halo, we, dk, wp, x):
    wide = jax.ShapeDtypeStruct((ROWS, COLS, EXP), BF16)
    return pl.pallas_call(
        mix_body,
        grid=(STEPS,),
        in_specs=[
            band((BLK, COLS, EXP)), ROW_BEFORE, ROW_AFTER, whole((HALO, CHAN)), whole((CHAN, EXP)),
            whole((9, EXP)), whole((EXP, CHAN)), band((BLK, COLS, CHAN)),
        ],
        out_specs=[band((8, 32, CHAN)), band((BLK, COLS, EXP)), band((BLK, COLS, EXP))],
        out_shape=[jax.ShapeDtypeStruct((64, 32, CHAN), BF16), wide, wide],
        scratch_shapes=[pltpu.VMEM((COLS, EXP), F32)] * 2 + [pltpu.VMEM((STEPS, 8, EXP), F32)] * 2,
        compiler_params=params(48),
        cost_estimate=pl.CostEstimate(
            flops=2 * ROWS * COLS * CHAN * EXP, bytes_accessed=16 * MIB, transcendentals=ROWS * COLS * EXP
        ),
        name="mix",
    )(hidden, hidden, hidden, halo, we, dk, wp, x)


SWAP = np.zeros((256, 256), np.float32)
for _s in range(16):
    for _g in range(16):
        SWAP[_g * 16 + _s, _s * 16 + _g] = 1.0


def diagonal(full, low):
    halves = []
    for half in range(2):
        lanes = slice(half * 128, half * 128 + 128)
        at = half * 128
        halves.append(jnp.where(low, full[at : at + 64, lanes], full[at + 64 : at + 128, lanes]))
    return jnp.concatenate(halves, axis=1)


def attention_body(
    x_ref, cot_ref, wqkv_ref, wout_ref, bias_ref, swap_ref,
    out_ref, qkv_sum_ref, out_sum_ref, bias_sum_ref, xs_ref, cs_ref, ds_ref,
):
    step = pl.program_id(0)
    n_groups = x_ref.shape[1]

    @pl.when(step == 0)
    def _():
        qkv_sum_ref[...] = jnp.zeros_like(qkv_sum_ref)
        out_sum_ref[...] = jnp.zeros_like(out_sum_ref)
        bias_sum_ref[...] = jnp.zeros_like(bias_sum_ref)
        for src, dst in ((x_ref, xs_ref), (cot_ref, cs_ref)):
            for s in range(0, 64, 16):
                for g in range(0, n_groups, 16):
                    tile = src[s : s + 16, g : g + 16].reshape(256, CHAN)
                    moved = dot(swap_ref[...], tile).astype(BF16)
                    dst[g : g + 16, s : s + 16] = moved.reshape(16, 16, CHAN)

    groups = pl.ds(step * 4, 4)
    tokens = xs_ref[groups].reshape(256, CHAN)
    grads = cs_ref[groups].reshape(256, CHAN)
    normed, inv_std = layer_norm(tokens.astype(F32))
    normed_b = normed.astype(BF16)
    projected = dot(normed_b, wqkv_ref[...]).astype(BF16)
    d_att = dot_nt(grads, wout_ref[...]).astype(BF16)
    low = lax.broadcasted_iota(jnp.int32, (64, 128), 1) < 64
    head_of = lax.broadcasted_iota(jnp.int32, (64, CHAN), 1) // 64
    masks = [(head_of == h).astype(F32).astype(BF16) for h in range(4)]
    attended, d_proj = [], []
    for g in range(4):
        part = slice(g * 64, g * 64 + 64)
        query = projected[part, :CHAN] * 0.125
        key = projected[part, CHAN : 2 * CHAN]
        value = projected[part, 2 * CHAN :]
        da = d_att[part]
        query_h = jnp.concatenate([query * m for m in masks], axis=0)
        da_h = jnp.concatenate([da * m for m in masks], axis=0)
        scores = dot_nt(key, query_h) + bias_ref[...]
        scores = jnp.exp(scores - jnp.max(scores, axis=0, keepdims=True))
        probs = scores * (1.0 / jnp.sum(scores, axis=0, keepdims=True))
        probs_b = probs.astype(BF16)
        d_probs = dot_nt(value, da_h)
        d_scores = probs * (d_probs - jnp.sum(probs * d_probs, axis=0, keepdims=True))
        bias_sum_ref[...] += d_scores
        d_scores_b = d_scores.astype(BF16)
        attended.append(diagonal(dot_tn(probs_b, value), low).astype(BF16))
        d_query = (diagonal(dot_tn(d_scores_b, key), low) * 0.125).astype(BF16)
        d_key = dot(d_scores_b, query_h).astype(BF16)
        d_value = dot(probs_b, da_h).astype(BF16)
        d_proj.append(jnp.concatenate([d_query, d_key, d_value], axis=1))
    attended = jnp.concatenate(attended, axis=0)
    d_proj = jnp.concatenate(d_proj, axis=0)
    out_sum_ref[...] += dot_tn(attended, grads)
    qkv_sum_ref[...] += dot_tn(normed_b, d_proj)
    d_normed = dot_nt(d_proj, wqkv_ref[...])
    d_tokens = layer_norm_back(normed, inv_std, d_normed).astype(BF16)
    ds_ref[groups] = d_tokens.reshape(4, 64, CHAN)

    @pl.when(step == n_groups // 4 - 1)
    def _():
        for s in range(0, 64, 16):
            for g in range(0, n_groups, 16):
                tile = ds_ref[g : g + 16, s : s + 16].reshape(256, CHAN)
                moved = dot(swap_ref[...], tile).astype(BF16)
                out_ref[s : s + 16, g : g + 16] = moved.reshape(16, 16, CHAN)


def attention(tokens, cot, wqkv, wout, bias):
    n_groups = tokens.shape[1]
    shape = (64, n_groups, CHAN)
    return pl.pallas_call(
        attention_body,
        grid=(n_groups // 4,),
        in_specs=[
            whole(shape), whole(shape), whole((CHAN, 3 * CHAN)), whole((CHAN, CHAN)),
            whole((64, CHAN)), whole((256, 256)),
        ],
        out_specs=[whole(shape), whole((CHAN, 3 * CHAN)), whole((CHAN, CHAN)), whole((64, CHAN))],
        out_shape=[
            jax.ShapeDtypeStruct(shape, BF16),
            jax.ShapeDtypeStruct((CHAN, 3 * CHAN), F32),
            jax.ShapeDtypeStruct((CHAN, CHAN), F32),
            jax.ShapeDtypeStruct((64, CHAN), F32),
        ],
        scratch_shapes=[pltpu.VMEM((n_groups, 64, CHAN), BF16)] * 3,
        compiler_params=params(48),
        cost_estimate=pl.CostEstimate(
            flops=n_groups * 64 * 4 * CHAN * CHAN * 5, bytes_accessed=6 * MIB, transcendentals=n_groups * 64 * 256
        ),
        name="attention",
    )(tokens, cot, wqkv, wout, bias, jnp.asarray(SWAP, BF16))


def project_body(cot_ref, db_ref, mixed_ref, slope_ref, wp_ref, ds_ref, dm_ref, sum_ref):
    @pl.when(pl.program_id(0) == 0)
    def _():
        sum_ref[...] = jnp.zeros_like(sum_ref)

    pieces = db_ref[...].reshape(2, 4, 2, 16, CHAN)
    branch = jnp.concatenate(
        [pieces[pair, quad, r] for pair in range(2) for r in range(2) for quad in range(4)], axis=0
    )
    d_section = cot_ref[...].reshape(TOK, CHAN).astype(F32) + branch.astype(F32)
    ds_ref[...] = d_section.reshape(BLK, COLS, CHAN)
    d_section_b = d_section.astype(BF16)
    sum_ref[...] += dot_tn(d_section_b, mixed_ref[...].reshape(TOK, EXP))
    for at in range(0, EXP, 256):
        grads = dot_nt(d_section_b, wp_ref[at : at + 256, :])
        slope = slope_ref[:, :, at : at + 256].reshape(TOK, 256).astype(F32)
        dm_ref[:, :, at : at + 256] = (grads * slope).astype(BF16).reshape(BLK, COLS, 256)


def project_back(cot, db, mixed, slope, wp):
    return pl.pallas_call(
        project_body,
        grid=(STEPS,),
        in_specs=[
            band((BLK, COLS, CHAN)), band((8, 32, CHAN)), band((BLK, COLS, EXP)),
            band((BLK, COLS, EXP)), whole((EXP, CHAN)),
        ],
        out_specs=[band((BLK, COLS, CHAN)), band((BLK, COLS, EXP)), whole((CHAN, EXP))],
        out_shape=[
            jax.ShapeDtypeStruct((ROWS, COLS, CHAN), F32),
            jax.ShapeDtypeStruct((ROWS, COLS, EXP), BF16),
            jax.ShapeDtypeStruct((CHAN, EXP), F32),
        ],
        compiler_params=params(48),
        cost_estimate=pl.CostEstimate(
            flops=4 * ROWS * COLS * CHAN * EXP, bytes_accessed=16 * MIB, transcendentals=0
        ),
        name="project_back",
    )(cot, db, mixed, slope, wp)


def expand_back_body(
    cur_ref, before_ref, after_ref, halo_ref, halo_slope_ref, wp_ref, hid_ref, slope_ref, x_ref,
    ds_ref, dk_ref, we_ref,
    grad_ref, sum_ref, depth_ref, top_ref, bottom_ref, left_ref, right_ref, acc_ref, dpre_ref,
):
    step = pl.program_id(0)

    @pl.when(step == 0)
    def _():
        sum_ref[...] = jnp.zeros_like(sum_ref)
        acc_ref[...] = jnp.zeros_like(acc_ref)
        for at in range(0, EXP, 256):
            span = slice(at, at + 256)
            grads = dot_nt(halo_ref[...], wp_ref[at : at + 256, :])
            grads = (grads * halo_slope_ref[:, span].astype(F32)).astype(BF16).astype(F32)
            top_ref[:, span] = grads[:COLS]
            bottom_ref[:, span] = grads[COLS : 2 * COLS]
            for ref, base in ((left_ref, 2 * COLS), (right_ref, 2 * COLS + EDGE)):
                for s in range(STEPS):
                    ref[s, : BLK + 2, span] = grads[base + BLK * s : base + BLK * s + BLK + 2]

    first, last = step == 0, step == STEPS - 1
    for at in range(0, EXP, LANES):
        span = slice(at, at + LANES)
        rows = [jnp.where(first, top_ref[:, span], before_ref[0, :, span].astype(F32))]
        rows += [cur_ref[r, :, span].astype(F32) for r in range(BLK)]
        rows += [jnp.where(last, bottom_ref[:, span], after_ref[0, :, span].astype(F32))]
        shifted = []
        for r in range(BLK + 2):
            left = left_ref[step, r : r + 1, span]
            right = right_ref[step, r : r + 1, span]
            shifted.append(
                (
                    jnp.concatenate([rows[r][1:], right], axis=0),
                    rows[r],
                    jnp.concatenate([left, rows[r][:-1]], axis=0),
                )
            )
        sums = [acc_ref[n, :, span] for n in range(9)]
        for r in range(BLK):
            hid = hid_ref[r, :, span].astype(F32)
            total = 0.0
            for a in range(3):
                for b in range(3):
                    piece = shifted[r + 2 - a][b]
                    n = 3 * a + b
                    total = total + dk_ref[n, span][None] * piece
                    sums[n] = sums[n] + jnp.sum((hid * piece).reshape(8, 8, LANES), axis=0)
            d_pre = total * slope_ref[r, :, span].astype(F32)
            dpre_ref[r * COLS : (r + 1) * COLS, span] = d_pre.astype(BF16)
        for n in range(9):
            acc_ref[n, :, span] = sums[n]

    normed, inv_std = layer_norm(x_ref[...].reshape(TOK, CHAN).astype(F32))
    sum_ref[...] += dot_tn(normed.astype(BF16), dpre_ref[...])
    d_normed = dot_nt(dpre_ref[...], we_ref[...])
    d_input = layer_norm_back(normed, inv_std, d_normed)
    grad_ref[...] = (ds_ref[...].reshape(TOK, CHAN) + d_input).astype(BF16).reshape(BLK, COLS, CHAN)

    @pl.when(last)
    def _():
        depth_ref[...] = jnp.sum(acc_ref[...], axis=1)


def expand_back(d_mixed, halo, halo_slope, wp, hidden, slope, x, ds, dk, we):
    return pl.pallas_call(
        expand_back_body,
        grid=(STEPS,),
        in_specs=[
            band((BLK, COLS, EXP)), ROW_BEFORE, ROW_AFTER, whole((HALO, CHAN)), whole((HALO, EXP)),
            whole((EXP, CHAN)), band((BLK, COLS, EXP)), band((BLK, COLS, EXP)),
            band((BLK, COLS, CHAN)), band((BLK, COLS, CHAN)), whole((9, EXP)), whole((CHAN, EXP)),
        ],
        out_specs=[band((BLK, COLS, CHAN)), whole((CHAN, EXP)), whole((9, EXP))],
        out_shape=[
            jax.ShapeDtypeStruct((ROWS, COLS, CHAN), BF16),
            jax.ShapeDtypeStruct((CHAN, EXP), F32),
            jax.ShapeDtypeStruct((9, EXP), F32),
        ],
        scratch_shapes=[pltpu.VMEM((COLS, EXP), F32)] * 2
        + [pltpu.VMEM((STEPS, 8, EXP), F32)] * 2
        + [pltpu.VMEM((9, 8, EXP), F32), pltpu.VMEM((TOK, EXP), BF16)],
        compiler_params=params(56),
        cost_estimate=pl.CostEstimate(
            flops=4 * ROWS * COLS * CHAN * EXP, bytes_accessed=20 * MIB, transcendentals=0
        ),
        name="expand_back",
    )(d_mixed, d_mixed, d_mixed, halo, halo_slope, wp, hidden, slope, x, ds, dk, we)


def halo_of(top, bottom, left, right):
    n_lat, n_lon = lax.axis_size("lat"), lax.axis_size("lon")
    south = [(i, i + 1) for i in range(n_lat - 1)]
    north = [(i + 1, i) for i in range(n_lat - 1)]
    east = [(i, (i + 1) % n_lon) for i in range(n_lon)]
    west = [((i + 1) % n_lon, i) for i in range(n_lon)]
    above = lax.ppermute(bottom, "lat", south)
    below = lax.ppermute(top, "lat", north)
    pad = jnp.zeros((EDGE - ROWS - 2, top.shape[1]), top.dtype)
    from_west = lax.ppermute(
        jnp.concatenate([above[-1:], right, below[-1:], pad], axis=0), "lon", east
    )
    from_east = lax.ppermute(
        jnp.concatenate([above[:1], left, below[:1], pad], axis=0), "lon", west
    )
    return jnp.concatenate([above, below, from_west, from_east], axis=0)


def halo_of_field(field):
    return halo_of(field[0], field[-1], field[:, 0], field[:, -1])


def exchange(pieces):
    n_lat, n_lon = lax.axis_size("lat"), lax.axis_size("lon")
    order = np.arange(n_lat * n_lon).reshape(n_lat, n_lon // 2, 2)
    members = order.transpose(2, 0, 1).reshape(2, -1).tolist()
    return lax.all_to_all(
        pieces, ("lat", "lon"), split_axis=0, concat_axis=0, axis_index_groups=members, tiled=True
    )


def to_pieces(field):
    shaped = field.reshape(16, 2, 4, 16, CHAN).transpose(0, 2, 1, 3, 4)
    return shaped.reshape(64, 32, CHAN)


def edge_cells(pieces):
    shaped = pieces.reshape(16, 4, 2, 16, CHAN)
    top = shaped[0, :, 0].reshape(COLS, CHAN)
    bottom = shaped[-1, :, -1].reshape(COLS, CHAN)
    left = shaped[:, 0, :, 0].reshape(ROWS, CHAN)
    right = shaped[:, -1, :, -1].reshape(ROWS, CHAN)
    return (top, bottom, left, right)


def rel_table():
    position = np.arange(64)
    pos_row, pos_col = position // 8, position % 8
    rel_index = (pos_row[:, None] - pos_row[None, :] + 7) * 15 + (
        pos_col[:, None] - pos_col[None, :] + 7
    )
    return jnp.asarray(rel_index)[:, :, None] == jnp.arange(225)[None, None, :]


def on_device(
    field_in, cotangent, expand_weight, depth_kernel, project_weight, qkv_weight, out_weight, rel_bias
):
    onehot = rel_table().astype(F32)
    bias = jnp.einsum(
        "tsr,hr->sht", onehot, rel_bias.reshape(4, 225), precision=lax.Precision.HIGHEST
    ).reshape(64, 256)
    dk = depth_kernel.reshape(9, EXP)

    field_halo = halo_of_field(field_in)
    cot_groups = exchange(to_pieces(cotangent))
    hidden, act_slope = expand(field_in, expand_weight)
    section, mixed, mixed_slope = mix(
        hidden, field_halo, expand_weight, dk, project_weight, field_in
    )
    slope_halo = halo_of_field(mixed_slope)
    groups = exchange(section)
    d_groups, qkv_sum, out_sum, bias_acc = attention(groups, cot_groups, qkv_weight, out_weight, bias)
    bias_sum = jnp.einsum(
        "sht,tsr->hr", bias_acc.reshape(64, 4, 64), onehot, precision=lax.Precision.HIGHEST
    )
    d_branch = exchange(d_groups)
    cot_edges = (cotangent[0], cotangent[-1], cotangent[:, 0], cotangent[:, -1])
    d_edges = [
        (c.astype(F32) + d.astype(F32)).astype(BF16)
        for c, d in zip(cot_edges, edge_cells(d_branch))
    ]
    d_halo = halo_of(*d_edges)
    d_section, d_mixed, project_sum = project_back(
        cotangent, d_branch, mixed, mixed_slope, project_weight
    )
    grad_in, expand_sum, depth_sum = expand_back(
        d_mixed, d_halo, slope_halo, project_weight, hidden, act_slope, field_in, d_section, dk,
        expand_weight,
    )
    sums = lax.psum((expand_sum, depth_sum, project_sum, qkv_sum, out_sum, bias_sum), ("lat", "lon"))
    factor = float(ROWS * COLS * lax.axis_size("lat") * lax.axis_size("lon")) ** (-0.5)
    return (
        grad_in,
        sums[0] * factor,
        sums[1].reshape(3, 3, EXP) * factor,
        sums[2].T * factor,
        sums[3] * factor,
        sums[4] * factor,
        sums[5].reshape(4, 15, 15) * factor,
    )


def solution(mesh):
    placed = (P("lat", "lon", None), P("lat", "lon", None), P(), P(), P(), P(), P(), P())
    return jax.shard_map(
        on_device,
        mesh=mesh,
        in_specs=placed,
        out_specs=(P("lat", "lon", None), P(), P(), P(), P(), P(), P()),
        check_vma=False,
    )
```

```python
import math

import jax
import jax.numpy as jnp
import numpy as np
from jax import lax
from jax.experimental import pallas as pl
from jax.experimental.pallas import tpu as pltpu
from jax.sharding import PartitionSpec as P

EPSILON = 1e-05
GELU_C = math.sqrt(2.0 / math.pi)
F32 = jnp.float32
BF16 = jnp.bfloat16
MIB = 1 << 20

ROWS, COLS, CHAN, EXP = 32, 64, 256, 1024
BLK = 4
STEPS = ROWS // BLK
TOK = BLK * COLS
LANES = 128
EDGE = 40
HALO = 2 * COLS + 2 * EDGE
LONG = 72


def layer_norm(values):
    average = jnp.mean(values, axis=-1, keepdims=True)
    centred = values - average
    variance = jnp.mean(centred * centred, axis=-1, keepdims=True)
    inv_std = lax.rsqrt(variance + EPSILON)
    return (centred * inv_std, inv_std)


def layer_norm_back(normed, inv_std, grads):
    mean_grad = jnp.mean(grads, axis=-1, keepdims=True)
    mean_cross = jnp.mean(grads * normed, axis=-1, keepdims=True)
    return (grads - mean_grad - normed * mean_cross) * inv_std


def gelu_slope(values):
    squared = values * values
    tanh_val = jnp.tanh(values * (GELU_C + (GELU_C * 0.044715) * squared))
    gate = 0.5 + 0.5 * tanh_val
    result = values * gate
    slopes = gate + result * (1.0 - gate) * (2.0 * GELU_C + (6.0 * GELU_C * 0.044715) * squared)
    return (result, slopes)


def dot(left, right):
    return lax.dot_general(left, right, (((1,), (0,)), ((), ())), preferred_element_type=F32)


def dot_nt(left, right):
    return lax.dot_general(left, right, (((1,), (1,)), ((), ())), preferred_element_type=F32)


def dot_tn(left, right):
    return lax.dot_general(left, right, (((0,), (0,)), ((), ())), preferred_element_type=F32)


def params(mib):
    return pltpu.CompilerParams(vmem_limit_bytes=mib * MIB)


def whole(shape):
    return pl.BlockSpec(shape, lambda i: (0,) * len(shape))


def band(shape):
    return pl.BlockSpec(shape, lambda i: (i,) + (0,) * (len(shape) - 1))


ROW_BEFORE = pl.BlockSpec((1, COLS, EXP), lambda i: (jnp.maximum(BLK * i - 1, 0), 0, 0))
ROW_AFTER = pl.BlockSpec((1, COLS, EXP), lambda i: (jnp.minimum(BLK * i + BLK, ROWS - 1), 0, 0))


TILED = (128, 16, 128)


def to_tiles(ref, out_ref, at):
    wide = ref.shape[1] // 128
    for r in range(ref.shape[0] // 16):
        for c in range(wide):
            tile = ref[16 * r : 16 * r + 16, 128 * c : 128 * c + 128]
            out_ref[at + wide * r + c, :16] = tile.astype(BF16)


def from_tiles(tiles, wide):
    shaped = tiles.reshape(-1, wide, 16, 128).transpose(0, 2, 1, 3)
    return shaped.reshape(-1, wide * 128).astype(F32)


def expand_body(x_ref, we_ref, hid_ref, slope_ref):
    normed, _ = layer_norm(x_ref[...].reshape(TOK, CHAN).astype(F32))
    normed_b = normed.astype(BF16)
    for at in range(0, EXP, 256):
        val, slope = gelu_slope(dot(normed_b, we_ref[:, at : at + 256]))
        hid_ref[:, :, at : at + 256] = val.astype(BF16).reshape(BLK, COLS, 256)
        slope_ref[:, :, at : at + 256] = slope.astype(BF16).reshape(BLK, COLS, 256)


def expand(x, we):
    wide = jax.ShapeDtypeStruct((ROWS, COLS, EXP), BF16)
    return pl.pallas_call(
        expand_body,
        grid=(STEPS,),
        in_specs=[band((BLK, COLS, CHAN)), whole((CHAN, EXP))],
        out_specs=[band((BLK, COLS, EXP))] * 2,
        out_shape=[wide, wide],
        compiler_params=params(58),
        cost_estimate=pl.CostEstimate(
            flops=2 * ROWS * COLS * CHAN * EXP, bytes_accessed=10 * MIB, transcendentals=ROWS * COLS * EXP
        ),
        name="expand",
    )(x, we)


def mix_body(
    cur_ref, before_ref, after_ref, top_ref, bottom_ref, left_ref, right_ref, dk_ref, wp_ref, x_ref,
    section_ref, mixed_ref, slope_ref,
):
    step = pl.program_id(0)
    first, last = step == 0, step == STEPS - 1
    for at in range(0, EXP, LANES):
        span = slice(at, at + LANES)
        rows = [jnp.where(first, top_ref[:, span], before_ref[0, :, span]).astype(F32)]
        rows += [cur_ref[r, :, span].astype(F32) for r in range(BLK)]
        rows += [jnp.where(last, bottom_ref[:, span], after_ref[0, :, span]).astype(F32)]
        kern = [dk_ref[n, span][None] for n in range(9)]
        for r in range(BLK):
            parts = [
                kern[b] * rows[r] + kern[3 + b] * rows[r + 1] + kern[6 + b] * rows[r + 2]
                for b in range(3)
            ]
            left = left_ref[step, r : r + 1, span]
            right = right_ref[step, r : r + 1, span]
            pre = (
                parts[1]
                + jnp.concatenate([left, parts[0][:-1]], axis=0)
                + jnp.concatenate([parts[2][1:], right], axis=0)
            )
            val, slope = gelu_slope(pre)
            mixed_ref[r, :, span] = val.astype(BF16)
            slope_ref[r, :, span] = slope.astype(BF16)
    branch = dot(mixed_ref[...].reshape(TOK, EXP), wp_ref[...])
    section = (x_ref[...].reshape(TOK, CHAN).astype(F32) + branch).astype(BF16)
    section = section.reshape(2, 2, 4, 16, CHAN)
    for pair in range(2):
        for quad in range(4):
            section_ref[4 * pair + quad] = section[pair, :, quad].reshape(32, CHAN)


def mix(hidden, ring_out, dk, wp, x):
    wide = jax.ShapeDtypeStruct((ROWS, COLS, EXP), BF16)
    return pl.pallas_call(
        mix_body,
        grid=(STEPS,),
        in_specs=[
            band((BLK, COLS, EXP)), ROW_BEFORE, ROW_AFTER, whole((COLS, EXP)), whole((COLS, EXP)),
            whole((STEPS, 8, EXP)), whole((STEPS, 8, EXP)),
            whole((9, EXP)), whole((EXP, CHAN)), band((BLK, COLS, CHAN)),
        ],
        out_specs=[band((8, 32, CHAN)), band((BLK, COLS, EXP)), band((BLK, COLS, EXP))],
        out_shape=[jax.ShapeDtypeStruct((64, 32, CHAN), BF16), wide, wide],
        compiler_params=params(58),
        cost_estimate=pl.CostEstimate(
            flops=2 * ROWS * COLS * CHAN * EXP, bytes_accessed=16 * MIB, transcendentals=ROWS * COLS * EXP
        ),
        name="mix",
    )(hidden, hidden, hidden, *ring_out, dk, wp, x)


def ring_body(
    above_ref, below_ref, first_ref, last_ref, west_ref, east_ref, own_west_ref, own_east_ref,
    we_ref, dk_ref,
    top_ref, bottom_ref, left_ref, right_ref, slope_ref,
):
    west, east = west_ref[...].astype(F32), east_ref[...].astype(F32)
    pad = jnp.zeros((LONG - COLS - 4, CHAN), F32)

    def along(row, at):
        return [
            west[0, at : at + 1], west[1, at : at + 1], row.astype(F32),
            east[0, at : at + 1], east[1, at : at + 1], pad,
        ]

    strips = along(above_ref[0], 0) + along(above_ref[1], 1) + along(first_ref[0], 2)
    strips += along(last_ref[0], 33) + along(below_ref[0], 34) + along(below_ref[1], 35)
    strips += [west[0], west[1], own_west_ref[0].astype(F32)]
    strips += [own_east_ref[1].astype(F32), east[0], east[1]]
    normed, _ = layer_norm(jnp.concatenate(strips, axis=0))
    normed_b = normed.astype(BF16)
    south, lefts, rights = 3 * LONG, 6 * LONG, 6 * LONG + 3 * EDGE
    for at in range(0, EXP, 256):
        span = slice(at, at + 256)
        val, _ = gelu_slope(dot(normed_b, we_ref[:, span]))
        val = val.astype(BF16).astype(F32)
        kern = [dk_ref[n, span][None] for n in range(9)]
        top_ref[:, span] = val[LONG + 2 : LONG + 2 + COLS].astype(BF16)
        bottom_ref[:, span] = val[south + LONG + 2 : south + LONG + 2 + COLS].astype(BF16)
        for ref, base, col in ((left_ref, lefts, 0), (right_ref, rights, 2)):
            total = 0.0
            for a in range(3):
                start = base + EDGE + a + 1
                total = total + kern[3 * a + col] * val[start : start + ROWS]
            for s in range(STEPS):
                ref[s, :BLK, span] = total[BLK * s : BLK * s + BLK]
        for base, out in ((0, 0), (south, COLS)):
            total = 0.0
            for a in range(3):
                for b in range(3):
                    start = base + LONG * a + b + 1
                    total = total + kern[3 * a + b] * val[start : start + COLS]
            slope_ref[out : out + COLS, span] = gelu_slope(total)[1]
        for base, out in ((lefts, 2 * COLS), (rights, 2 * COLS + EDGE)):
            total = 0.0
            for a in range(3):
                for b in range(3):
                    start = base + EDGE * b + a
                    total = total + kern[3 * a + b] * val[start : start + ROWS + 2]
            slope_ref[out : out + ROWS + 2, span] = gelu_slope(total)[1]
            slope_ref[out + ROWS + 2 : out + EDGE, span] = jnp.zeros((EDGE - ROWS - 2, 256), F32)


def ring(halo, field, we, dk):
    above, below, west, east, own_west, own_east = halo
    return pl.pallas_call(
        ring_body,
        grid=(1,),
        in_specs=[
            whole((2, COLS, CHAN)), whole((2, COLS, CHAN)),
            pl.BlockSpec((1, COLS, CHAN), lambda i: (0, 0, 0)),
            pl.BlockSpec((1, COLS, CHAN), lambda i: (ROWS - 1, 0, 0)),
            whole((2, EDGE, CHAN)), whole((2, EDGE, CHAN)), whole((2, EDGE, CHAN)), whole((2, EDGE, CHAN)),
            whole((CHAN, EXP)), whole((9, EXP)),
        ],
        out_specs=[
            whole((COLS, EXP)), whole((COLS, EXP)), whole((STEPS, 8, EXP)), whole((STEPS, 8, EXP)),
            whole((HALO, EXP)),
        ],
        out_shape=[
            jax.ShapeDtypeStruct((COLS, EXP), BF16),
            jax.ShapeDtypeStruct((COLS, EXP), BF16),
            jax.ShapeDtypeStruct((STEPS, 8, EXP), F32),
            jax.ShapeDtypeStruct((STEPS, 8, EXP), F32),
            jax.ShapeDtypeStruct((HALO, EXP), F32),
        ],
        compiler_params=params(58),
        cost_estimate=pl.CostEstimate(
            flops=2 * 672 * CHAN * EXP, bytes_accessed=3 * MIB, transcendentals=900 * EXP
        ),
        name="ring",
    )(above, below, field, field, west, east, own_west, own_east, we, dk)


SWAP = np.zeros((256, 256), np.float32)
for _s in range(16):
    for _g in range(16):
        SWAP[_g * 16 + _s, _s * 16 + _g] = 1.0


def diagonal(full, low):
    halves = []
    for half in range(2):
        lanes = slice(half * 128, half * 128 + 128)
        at = half * 128
        halves.append(jnp.where(low, full[at : at + 64, lanes], full[at + 64 : at + 128, lanes]))
    return jnp.concatenate(halves, axis=1)


def swap(src, dst, swap_ref, n_groups):
    for s in range(0, 64, 16):
        for g in range(0, n_groups, 16):
            moved = dot(swap_ref[...], src[s : s + 16, g : g + 16].reshape(256, CHAN)).astype(BF16)
            dst[g : g + 16, s : s + 16] = moved.reshape(16, 16, CHAN)


def prepare_body(cot_ref, wout_ref, swap_ref, cs_ref, da_ref):
    n_groups = cot_ref.shape[1]
    swap(cot_ref, cs_ref, swap_ref, n_groups)
    for g in range(0, n_groups, 4):
        grads = dot_nt(cs_ref[g : g + 4].reshape(256, CHAN), wout_ref[...])
        da_ref[g : g + 4] = grads.astype(BF16).reshape(4, 64, CHAN)


def prepare(cot, wout, n_groups):
    shape = (64, n_groups, CHAN)
    grouped = (n_groups, 64, CHAN)
    return pl.pallas_call(
        prepare_body,
        grid=(1,),
        in_specs=[whole(shape), whole((CHAN, CHAN)), whole((256, 256))],
        out_specs=[whole(grouped), whole(grouped)],
        out_shape=[jax.ShapeDtypeStruct(grouped, BF16)] * 2,
        compiler_params=params(58),
        cost_estimate=pl.CostEstimate(
            flops=n_groups * 64 * 4 * CHAN * CHAN, bytes_accessed=3 * MIB, transcendentals=0
        ),
        name="prepare",
    )(cot, wout, jnp.asarray(SWAP, BF16))


def attention_body(
    x_ref, da_ref, wqkv_ref, bias_ref, swap_ref,
    out_ref, att_ref, norm_ref, proj_ref, bias_sum_ref, xs_ref, ds_ref,
):
    step = pl.program_id(0)
    n_groups = x_ref.shape[1]

    @pl.when(step == 0)
    def _():
        bias_sum_ref[...] = jnp.zeros_like(bias_sum_ref)
        swap(x_ref, xs_ref, swap_ref, n_groups)

    groups = pl.ds(step * 4, 4)
    tokens = xs_ref[groups].reshape(256, CHAN)
    normed, inv_std = layer_norm(tokens.astype(F32))
    normed_b = normed.astype(BF16)
    norm_ref[...] = normed_b
    projected = dot(normed_b, wqkv_ref[...]).astype(BF16)
    low = lax.broadcasted_iota(jnp.int32, (64, 128), 1) < 64
    head_of = lax.broadcasted_iota(jnp.int32, (64, CHAN), 1) // 64
    masks = [(head_of == h).astype(F32).astype(BF16) for h in range(4)]
    for g in range(4):
        part = slice(g * 64, g * 64 + 64)
        query = projected[part, :CHAN] * 0.125
        key = projected[part, CHAN : 2 * CHAN]
        value = projected[part, 2 * CHAN :]
        da = da_ref[g]
        query_h = jnp.concatenate([query * m for m in masks], axis=0)
        da_h = jnp.concatenate([da * m for m in masks], axis=0)
        scores = dot_nt(key, query_h) + bias_ref[...]
        scores = jnp.exp(scores - jnp.max(scores, axis=0, keepdims=True))
        probs = scores * (1.0 / jnp.sum(scores, axis=0, keepdims=True))
        probs_b = probs.astype(BF16)
        d_probs = dot_nt(value, da_h)
        d_scores = probs * (d_probs - jnp.sum(probs * d_probs, axis=0, keepdims=True))
        bias_sum_ref[...] += d_scores
        d_scores_b = d_scores.astype(BF16)
        att_ref[part] = diagonal(dot_tn(probs_b, value), low).astype(BF16)
        proj_ref[part, :CHAN] = (diagonal(dot_tn(d_scores_b, key), low) * 0.125).astype(BF16)
        proj_ref[part, CHAN : 2 * CHAN] = dot(d_scores_b, query_h).astype(BF16)
        proj_ref[part, 2 * CHAN :] = dot(probs_b, da_h).astype(BF16)
    d_normed = dot_nt(proj_ref[...], wqkv_ref[...])
    d_tokens = layer_norm_back(normed, inv_std, d_normed).astype(BF16)
    ds_ref[groups] = d_tokens.reshape(4, 64, CHAN)

    @pl.when(step == n_groups // 4 - 1)
    def _():
        for s in range(0, 64, 16):
            for g in range(0, n_groups, 16):
                tile = ds_ref[g : g + 16, s : s + 16].reshape(256, CHAN)
                moved = dot(swap_ref[...], tile).astype(BF16)
                out_ref[s : s + 16, g : g + 16] = moved.reshape(16, 16, CHAN)


def attention(tokens, d_att, wqkv, bias):
    n_groups = tokens.shape[1]
    shape = (64, n_groups, CHAN)
    flat = n_groups * 64
    return pl.pallas_call(
        attention_body,
        grid=(n_groups // 4,),
        in_specs=[
            whole(shape), band((4, 64, CHAN)), whole((CHAN, 3 * CHAN)), whole((64, CHAN)),
            whole((256, 256)),
        ],
        out_specs=[
            whole(shape), band((256, CHAN)), band((256, CHAN)), band((256, 3 * CHAN)), whole((64, CHAN)),
        ],
        out_shape=[
            jax.ShapeDtypeStruct(shape, BF16),
            jax.ShapeDtypeStruct((flat, CHAN), BF16),
            jax.ShapeDtypeStruct((flat, CHAN), BF16),
            jax.ShapeDtypeStruct((flat, 3 * CHAN), BF16),
            jax.ShapeDtypeStruct((64, CHAN), F32),
        ],
        scratch_shapes=[pltpu.VMEM((n_groups, 64, CHAN), BF16)] * 2,
        compiler_params=params(58),
        cost_estimate=pl.CostEstimate(
            flops=flat * 4 * CHAN * CHAN * 5, bytes_accessed=8 * MIB, transcendentals=flat * 256
        ),
        name="attention",
    )(tokens, d_att, wqkv, bias, jnp.asarray(SWAP, BF16))


def attention_sums_body(att_ref, cot_ref, norm_ref, proj_ref, out_ref, qkv_acc, out_acc):
    step = pl.program_id(0)

    @pl.when(step == 0)
    def _():
        qkv_acc[...] = jnp.zeros_like(qkv_acc)
        out_acc[...] = jnp.zeros_like(out_acc)

    out_acc[...] += dot_tn(att_ref[...], cot_ref[...])
    qkv_acc[...] += dot_tn(norm_ref[...], proj_ref[...])

    @pl.when(step == pl.num_programs(0) - 1)
    def _():
        to_tiles(qkv_acc, out_ref, 0)
        to_tiles(out_acc, out_ref, 96)


def attention_sums(att, cot, normed, proj):
    flat = att.shape[0]
    return pl.pallas_call(
        attention_sums_body,
        grid=(flat // 512,),
        in_specs=[band((512, CHAN)), band((512, CHAN)), band((512, CHAN)), band((512, 3 * CHAN))],
        out_specs=whole(TILED),
        out_shape=jax.ShapeDtypeStruct(TILED, BF16),
        scratch_shapes=[pltpu.VMEM((CHAN, 3 * CHAN), F32), pltpu.VMEM((CHAN, CHAN), F32)],
        compiler_params=params(58),
        cost_estimate=pl.CostEstimate(
            flops=flat * 8 * CHAN * CHAN, bytes_accessed=6 * MIB, transcendentals=0
        ),
        name="attention_sums",
    )(att, cot, normed, proj)


def project_body(
    cot_ref, db_ref, mixed_ref, slope_ref, wp_ref, ds_ref, dm_ref, tiles_ref, sum_ref, turned_ref
):
    @pl.when(pl.program_id(0) == 0)
    def _():
        sum_ref[...] = jnp.zeros_like(sum_ref)

    pieces = db_ref[...].reshape(2, 4, 2, 16, CHAN)
    branch = jnp.concatenate(
        [pieces[pair, quad, r] for pair in range(2) for r in range(2) for quad in range(4)], axis=0
    )
    d_section = cot_ref[...].reshape(TOK, CHAN).astype(F32) + branch.astype(F32)
    ds_ref[...] = d_section.reshape(BLK, COLS, CHAN)
    d_section_b = d_section.astype(BF16)
    sum_ref[...] += dot_tn(d_section_b, mixed_ref[...].reshape(TOK, EXP))
    for at in range(0, EXP, 256):
        grads = dot_nt(d_section_b, wp_ref[at : at + 256, :])
        slope = slope_ref[:, :, at : at + 256].reshape(TOK, 256).astype(F32)
        dm_ref[:, :, at : at + 256] = (grads * slope).astype(BF16).reshape(BLK, COLS, 256)

    @pl.when(pl.program_id(0) == STEPS - 1)
    def _():
        turned_ref[...] = sum_ref[...].T
        to_tiles(turned_ref, tiles_ref, 0)


def project_back(cot, db, mixed, slope, wp):
    return pl.pallas_call(
        project_body,
        grid=(STEPS,),
        in_specs=[
            band((BLK, COLS, CHAN)), band((8, 32, CHAN)), band((BLK, COLS, EXP)),
            band((BLK, COLS, EXP)), whole((EXP, CHAN)),
        ],
        out_specs=[band((BLK, COLS, CHAN)), band((BLK, COLS, EXP)), whole(TILED)],
        out_shape=[
            jax.ShapeDtypeStruct((ROWS, COLS, CHAN), F32),
            jax.ShapeDtypeStruct((ROWS, COLS, EXP), BF16),
            jax.ShapeDtypeStruct(TILED, BF16),
        ],
        scratch_shapes=[pltpu.VMEM((CHAN, EXP), F32), pltpu.VMEM((EXP, CHAN), F32)],
        compiler_params=params(58),
        cost_estimate=pl.CostEstimate(
            flops=4 * ROWS * COLS * CHAN * EXP, bytes_accessed=16 * MIB, transcendentals=0
        ),
        name="project_back",
    )(cot, db, mixed, slope, wp)


def expand_back_body(
    cur_ref, before_ref, after_ref, halo_ref, halo_slope_ref, wp_ref, hid_ref, slope_ref, x_ref, dk_ref,
    dpre_ref, tiles_ref, depth_ref, top_ref, bottom_ref, left_ref, right_ref, acc_ref, sum_ref,
):
    step = pl.program_id(0)

    @pl.when(step == 0)
    def _():
        sum_ref[...] = jnp.zeros_like(sum_ref)
        acc_ref[...] = jnp.zeros_like(acc_ref)
        for at in range(0, EXP, 256):
            span = slice(at, at + 256)
            grads = dot_nt(halo_ref[...], wp_ref[at : at + 256, :])
            grads = (grads * halo_slope_ref[:, span]).astype(BF16).astype(F32)
            top_ref[:, span] = grads[:COLS]
            bottom_ref[:, span] = grads[COLS : 2 * COLS]
            for ref, base in ((left_ref, 2 * COLS), (right_ref, 2 * COLS + EDGE)):
                for s in range(STEPS):
                    ref[s, : BLK + 2, span] = grads[base + BLK * s : base + BLK * s + BLK + 2]

    first, last = step == 0, step == STEPS - 1
    for at in range(0, EXP, LANES):
        span = slice(at, at + LANES)
        rows = [jnp.where(first, top_ref[:, span], before_ref[0, :, span].astype(F32))]
        rows += [cur_ref[r, :, span].astype(F32) for r in range(BLK)]
        rows += [jnp.where(last, bottom_ref[:, span], after_ref[0, :, span].astype(F32))]
        shifted = []
        for r in range(BLK + 2):
            left = left_ref[step, r : r + 1, span]
            right = right_ref[step, r : r + 1, span]
            shifted.append(
                (
                    jnp.concatenate([rows[r][1:], right], axis=0),
                    rows[r],
                    jnp.concatenate([left, rows[r][:-1]], axis=0),
                )
            )
        sums = [acc_ref[n, :, span] for n in range(9)]
        for r in range(BLK):
            hid = hid_ref[r, :, span].astype(F32)
            total = 0.0
            for a in range(3):
                for b in range(3):
                    piece = shifted[r + 2 - a][b]
                    n = 3 * a + b
                    total = total + dk_ref[n, span][None] * piece
                    sums[n] = sums[n] + jnp.sum((hid * piece).reshape(8, 8, LANES), axis=0)
            d_pre = total * slope_ref[r, :, span].astype(F32)
            dpre_ref[r * COLS : (r + 1) * COLS, span] = d_pre.astype(BF16)
        for n in range(9):
            acc_ref[n, :, span] = sums[n]

    normed, _ = layer_norm(x_ref[...].reshape(TOK, CHAN).astype(F32))
    sum_ref[...] += dot_tn(normed.astype(BF16), dpre_ref[...])

    @pl.when(last)
    def _():
        depth_ref[...] = jnp.sum(acc_ref[...], axis=1)
        to_tiles(sum_ref, tiles_ref, 0)


def expand_back(d_mixed, halo, halo_slope, wp, hidden, slope, x, dk):
    return pl.pallas_call(
        expand_back_body,
        grid=(STEPS,),
        in_specs=[
            band((BLK, COLS, EXP)), ROW_BEFORE, ROW_AFTER, whole((HALO, CHAN)), whole((HALO, EXP)),
            whole((EXP, CHAN)), band((BLK, COLS, EXP)), band((BLK, COLS, EXP)),
            band((BLK, COLS, CHAN)), whole((9, EXP)),
        ],
        out_specs=[band((TOK, EXP)), whole(TILED), whole((9, EXP))],
        out_shape=[
            jax.ShapeDtypeStruct((ROWS * COLS, EXP), BF16),
            jax.ShapeDtypeStruct(TILED, BF16),
            jax.ShapeDtypeStruct((9, EXP), F32),
        ],
        scratch_shapes=[pltpu.VMEM((COLS, EXP), F32)] * 2
        + [pltpu.VMEM((STEPS, 8, EXP), F32)] * 2
        + [pltpu.VMEM((9, 8, EXP), F32), pltpu.VMEM((CHAN, EXP), F32)],
        compiler_params=params(58),
        cost_estimate=pl.CostEstimate(
            flops=2 * ROWS * COLS * CHAN * EXP, bytes_accessed=20 * MIB, transcendentals=0
        ),
        name="expand_back",
    )(d_mixed, d_mixed, d_mixed, halo, halo_slope, wp, hidden, slope, x, dk)


def finish_body(dpre_ref, x_ref, ds_ref, we_ref, grad_ref):
    normed, inv_std = layer_norm(x_ref[...].reshape(TOK, CHAN).astype(F32))
    d_normed = dot_nt(dpre_ref[...], we_ref[...])
    d_input = layer_norm_back(normed, inv_std, d_normed)
    grad_ref[...] = (ds_ref[...].reshape(TOK, CHAN) + d_input).astype(BF16).reshape(BLK, COLS, CHAN)


def finish(d_pre, x, d_section, we):
    return pl.pallas_call(
        finish_body,
        grid=(STEPS,),
        in_specs=[
            band((TOK, EXP)), band((BLK, COLS, CHAN)), band((BLK, COLS, CHAN)), whole((CHAN, EXP)),
        ],
        out_specs=band((BLK, COLS, CHAN)),
        out_shape=jax.ShapeDtypeStruct((ROWS, COLS, CHAN), BF16),
        compiler_params=params(58),
        cost_estimate=pl.CostEstimate(
            flops=2 * ROWS * COLS * CHAN * EXP, bytes_accessed=9 * MIB, transcendentals=0
        ),
        name="finish",
    )(d_pre, x, d_section, we)


FIRST_CELL = np.zeros((32, 512), np.float32)
LAST_CELL = np.zeros((32, 512), np.float32)
for _row in range(32):
    FIRST_CELL[_row, _row * 16] = 1.0
    LAST_CELL[_row, _row * 16 + 15] = 1.0


def edges_body(
    dt_ref, ct_ref, db_ref, cb_ref, dl_ref, cl_ref, dr_ref, cr_ref, first_ref, last_ref,
    top_ref, bottom_ref, left_ref, right_ref,
):
    def total(d_ref, c_ref):
        return (d_ref[...].astype(F32) + c_ref[...].astype(F32)).astype(BF16)

    top = total(dt_ref, ct_ref)
    bottom = total(db_ref, cb_ref)
    for quad in range(4):
        top_ref[16 * quad : 16 * quad + 16] = top[0, quad, :16]
        bottom_ref[16 * quad : 16 * quad + 16] = bottom[0, quad, 16:]
    left_ref[...] = dot(first_ref[...], total(dl_ref, cl_ref).reshape(512, CHAN)).astype(BF16)
    right_ref[...] = dot(last_ref[...], total(dr_ref, cr_ref).reshape(512, CHAN)).astype(BF16)


def edges(d_branch, cot):
    d_branch, cot = d_branch.reshape(16, 4, 32, CHAN), cot.reshape(16, 4, 32, CHAN)
    specs = []
    for row in (0, 15):
        specs += [pl.BlockSpec((1, 4, 32, CHAN), lambda i, row=row: (row, 0, 0, 0))] * 2
    for col in (0, 3):
        specs += [pl.BlockSpec((16, 1, 32, CHAN), lambda i, col=col: (0, col, 0, 0))] * 2
    return pl.pallas_call(
        edges_body,
        grid=(1,),
        in_specs=specs + [whole((32, 512))] * 2,
        out_specs=[whole((COLS, CHAN))] * 2 + [whole((ROWS, CHAN))] * 2,
        out_shape=[jax.ShapeDtypeStruct((COLS, CHAN), BF16)] * 2
        + [jax.ShapeDtypeStruct((ROWS, CHAN), BF16)] * 2,
        compiler_params=params(58),
        cost_estimate=pl.CostEstimate(flops=MIB, bytes_accessed=2 * MIB, transcendentals=0),
        name="edges",
    )(*([d_branch, cot] * 4), jnp.asarray(FIRST_CELL, BF16), jnp.asarray(LAST_CELL, BF16))


def shifts():
    n_lat, n_lon = lax.axis_size("lat"), lax.axis_size("lon")
    south = [(i, i + 1) for i in range(n_lat - 1)]
    north = [(i + 1, i) for i in range(n_lat - 1)]
    east = [(i, (i + 1) % n_lon) for i in range(n_lon)]
    west = [((i + 1) % n_lon, i) for i in range(n_lon)]
    return (south, north, east, west)


def halo_of(top, bottom, left, right):
    south, north, east, west = shifts()
    above = lax.ppermute(bottom, "lat", south)
    below = lax.ppermute(top, "lat", north)
    pad = jnp.zeros((EDGE - ROWS - 2, top.shape[1]), top.dtype)
    from_west = lax.ppermute(
        jnp.concatenate([above[-1:], right, below[-1:], pad], axis=0), "lon", east
    )
    from_east = lax.ppermute(
        jnp.concatenate([above[:1], left, below[:1], pad], axis=0), "lon", west
    )
    return jnp.concatenate([above, below, from_west, from_east], axis=0)


def wide_halo(field):
    south, north, east, west = shifts()
    above = lax.ppermute(field[-2:], "lat", south)
    below = lax.ppermute(field[:2], "lat", north)
    pad = jnp.zeros((2, EDGE - ROWS - 4, field.shape[2]), field.dtype)

    def columns(at):
        parts = [part[:, at : at + 2].transpose(1, 0, 2) for part in (above, field, below)]
        return jnp.concatenate(parts + [pad], axis=1)

    own_west, own_east = columns(0), columns(COLS - 2)
    from_west = lax.ppermute(own_east, "lon", east)
    from_east = lax.ppermute(own_west, "lon", west)
    return (above, below, from_west, from_east, own_west, own_east)


def exchange(pieces):
    n_lat, n_lon = lax.axis_size("lat"), lax.axis_size("lon")
    order = np.arange(n_lat * n_lon).reshape(n_lat, n_lon // 2, 2)
    members = order.transpose(2, 0, 1).reshape(2, -1).tolist()
    return lax.all_to_all(
        pieces, ("lat", "lon"), split_axis=0, concat_axis=0, axis_index_groups=members, tiled=True
    )


def to_pieces(field):
    shaped = field.reshape(16, 2, 4, 16, CHAN).transpose(0, 2, 1, 3, 4)
    return shaped.reshape(64, 32, CHAN)


def scatter_sum(tiles):
    terms = lax.all_to_all(tiles, ("lat", "lon"), split_axis=0, concat_axis=0, tiled=True)
    factor = float(ROWS * COLS * lax.axis_size("lat") * lax.axis_size("lon")) ** (-0.5)
    return (jnp.sum(terms.astype(F32), axis=0) * factor).astype(BF16)


def spread(tile):
    copies = jnp.broadcast_to(tile[None], (128,) + tile.shape)
    return lax.all_to_all(copies, ("lat", "lon"), split_axis=0, concat_axis=0, tiled=True)


def rel_table():
    position = np.arange(64)
    pos_row, pos_col = position // 8, position % 8
    rel_index = (pos_row[:, None] - pos_row[None, :] + 7) * 15 + (
        pos_col[:, None] - pos_col[None, :] + 7
    )
    return jnp.asarray(rel_index)[:, :, None] == jnp.arange(225)[None, None, :]


def on_device(
    field_in, cotangent, expand_weight, depth_kernel, project_weight, qkv_weight, out_weight, rel_bias
):
    onehot = rel_table().astype(F32)
    bias = jnp.einsum(
        "tsr,hr->sht", onehot, rel_bias.reshape(4, 225), precision=lax.Precision.HIGHEST
    ).reshape(64, 256)
    dk = depth_kernel.reshape(9, EXP)

    field_halo = wide_halo(field_in)
    cot_pieces = to_pieces(cotangent)
    cot_groups = exchange(cot_pieces)
    hidden, act_slope = expand(field_in, expand_weight)
    ring_out = ring(field_halo, field_in, expand_weight, dk)
    section, mixed, mixed_slope = mix(hidden, ring_out[:4], dk, project_weight, field_in)
    groups = exchange(section)
    cot_swapped, d_att = prepare(cot_groups, out_weight, 32)
    d_groups, attended, normed2, d_proj, bias_acc = attention(groups, d_att, qkv_weight, bias)
    d_branch = exchange(d_groups)
    attention_tiles = attention_sums(
        attended, cot_swapped.reshape(-1, CHAN), normed2, d_proj
    )
    bias_sum = jnp.einsum(
        "sht,tsr->hr", bias_acc.reshape(64, 4, 64), onehot, precision=lax.Precision.HIGHEST
    )
    d_halo = halo_of(*edges(d_branch, cot_pieces))
    d_section, d_mixed, project_tiles = project_back(
        cotangent, d_branch, mixed, mixed_slope, project_weight
    )
    early = scatter_sum(jnp.concatenate([attention_tiles, project_tiles], axis=1))
    d_pre, expand_tiles, depth_sum = expand_back(
        d_mixed, d_halo, ring_out[4], project_weight, hidden, act_slope, field_in, dk
    )
    small = jnp.concatenate(
        [depth_sum.reshape(-1), bias_sum.reshape(-1), jnp.zeros((128 * 128 - 9 * EXP - 900,), F32)]
    )
    small = jnp.pad(small.reshape(128, 1, 128), ((0, 0), (0, 7), (0, 0))).astype(BF16)
    late = scatter_sum(jnp.concatenate([expand_tiles, small], axis=1))
    grad_in = finish(d_pre, field_in, d_section, expand_weight)
    sums = spread(jnp.concatenate([early, late], axis=0))
    early, late = sums[:, :32], sums[:, 32:]
    small = late[:, 16].reshape(-1).astype(F32)
    return (
        grad_in,
        from_tiles(late[:, :16], 8),
        small[: 9 * EXP].reshape(3, 3, EXP),
        from_tiles(early[:, 16:], 2),
        from_tiles(early[:96, :16], 6),
        from_tiles(early[96:, :16], 2),
        small[9 * EXP : 9 * EXP + 900].reshape(4, 15, 15),
    )


def solution(mesh):
    placed = (P("lat", "lon", None), P("lat", "lon", None), P(), P(), P(), P(), P(), P())
    return jax.shard_map(
        on_device,
        mesh=mesh,
        in_specs=placed,
        out_specs=(P("lat", "lon", None), P(), P(), P(), P(), P(), P()),
        check_vma=False,
    )
```

```python
import math

import jax
import jax.numpy as jnp
import numpy as np
from jax import lax
from jax.experimental import pallas as pl
from jax.experimental.pallas import tpu as pltpu
from jax.sharding import PartitionSpec as P

EPSILON = 1e-05
GELU_C = math.sqrt(2.0 / math.pi)
F32 = jnp.float32
BF16 = jnp.bfloat16
MIB = 1 << 20

ROWS, COLS, CHAN, EXP = 32, 64, 256, 1024
BLK = 4
STEPS = ROWS // BLK
TOK = BLK * COLS
LANES = 128
EDGE = 40
HALO = 2 * COLS + 2 * EDGE
LONG = 72
PACKED = (4, 16, LANES)
JOINED = (64, 56, 128)


def layer_norm(values):
    average = jnp.mean(values, axis=-1, keepdims=True)
    centred = values - average
    variance = jnp.mean(centred * centred, axis=-1, keepdims=True)
    inv_std = lax.rsqrt(variance + EPSILON)
    return (centred * inv_std, inv_std)


def layer_norm_back(normed, inv_std, grads):
    mean_grad = jnp.mean(grads, axis=-1, keepdims=True)
    mean_cross = jnp.mean(grads * normed, axis=-1, keepdims=True)
    return (grads - mean_grad - normed * mean_cross) * inv_std


def gelu_slope(values):
    squared = values * values
    tanh_val = jnp.tanh(values * (GELU_C + (GELU_C * 0.044715) * squared))
    gate = 0.5 + 0.5 * tanh_val
    result = values * gate
    slopes = gate + result * (1.0 - gate) * (2.0 * GELU_C + (6.0 * GELU_C * 0.044715) * squared)
    return (result, slopes)


def dot(left, right):
    return lax.dot_general(left, right, (((1,), (0,)), ((), ())), preferred_element_type=F32)


def dot_nt(left, right):
    return lax.dot_general(left, right, (((1,), (1,)), ((), ())), preferred_element_type=F32)


def dot_tn(left, right):
    return lax.dot_general(left, right, (((0,), (0,)), ((), ())), preferred_element_type=F32)


def params(mib):
    return pltpu.CompilerParams(vmem_limit_bytes=mib * MIB)


def whole(shape):
    return pl.BlockSpec(shape, lambda i: (0,) * len(shape))


def band(shape):
    return pl.BlockSpec(shape, lambda i: (i,) + (0,) * (len(shape) - 1))


ROW_BEFORE = pl.BlockSpec(
    (1, COLS, EXP), lambda i: (jnp.maximum(BLK * i - 1, 0), 0, 0)
)
ROW_AFTER = pl.BlockSpec(
    (1, COLS, EXP), lambda i: (jnp.minimum(BLK * i + BLK, ROWS - 1), 0, 0)
)


TILED = (128, 16, 128)


def to_tiles(ref, out_ref, at):
    wide = ref.shape[1] // 128
    for r in range(ref.shape[0] // 16):
        for c in range(wide):
            tile = ref[16 * r : 16 * r + 16, 128 * c : 128 * c + 128]
            out_ref[at + wide * r + c, :16] = tile.astype(BF16)


def expand_body(x_ref, we_ref, hid_ref, slope_ref):
    normed, _ = layer_norm(x_ref[...].reshape(TOK, CHAN).astype(F32))
    normed_b = normed.astype(BF16)
    for at in range(0, EXP, 256):
        val, slope = gelu_slope(dot(normed_b, we_ref[:, at : at + 256]))
        hid_ref[:, :, at : at + 256] = val.astype(BF16).reshape(BLK, COLS, 256)
        slope_ref[:, :, at : at + 256] = slope.astype(BF16).reshape(BLK, COLS, 256)


def expand(x, we):
    wide = jax.ShapeDtypeStruct((ROWS, COLS, EXP), BF16)
    return pl.pallas_call(
        expand_body,
        grid=(STEPS,),
        in_specs=[band((BLK, COLS, CHAN)), whole((CHAN, EXP))],
        out_specs=[band((BLK, COLS, EXP))] * 2,
        out_shape=[wide, wide],
        compiler_params=params(58),
        cost_estimate=pl.CostEstimate(
            flops=2 * ROWS * COLS * CHAN * EXP, bytes_accessed=10 * MIB, transcendentals=ROWS * COLS * EXP
        ),
        name="expand",
    )(x, we)


def mix_body(
    cur_ref, before_ref, after_ref,
    above_ref, below_ref, first_ref, last_ref, west_ref, east_ref, own_west_ref, own_east_ref,
    we_ref, dk_ref, dkb_ref, wp_ref, x_ref,
    section_ref, mixed_ref, slope_ref, ring_slope_ref,
    top_ref, bottom_ref, left_ref, right_ref,
):
    step = pl.program_id(0)

    @pl.when(step == 0)
    def _():
        ring_body(
            above_ref, below_ref, first_ref, last_ref, west_ref, east_ref, own_west_ref, own_east_ref,
            we_ref, dk_ref,
            top_ref, bottom_ref, left_ref, right_ref, ring_slope_ref,
        )

    first, last = step == 0, step == STEPS - 1
    for at in range(0, EXP, LANES):
        span = slice(at, at + LANES)
        rows = [jnp.where(first, top_ref[:, span], before_ref[0, :, span])]
        rows += [cur_ref[r, :, span] for r in range(BLK)]
        rows += [jnp.where(last, bottom_ref[:, span], after_ref[0, :, span])]
        rows = [row.reshape(PACKED) for row in rows]
        kern = [dkb_ref[n, :, span][None] for n in range(9)]
        for r in range(BLK):
            parts = [
                kern[b] * rows[r] + kern[3 + b] * rows[r + 1] + kern[6 + b] * rows[r + 2]
                for b in range(3)
            ]
            parts = [part.reshape(COLS, LANES).astype(F32) for part in parts]
            left = left_ref[step, r : r + 1, span]
            right = right_ref[step, r : r + 1, span]
            pre = (
                parts[1]
                + jnp.concatenate([left, parts[0][:-1]], axis=0)
                + jnp.concatenate([parts[2][1:], right], axis=0)
            )
            val, slope = gelu_slope(pre)
            mixed_ref[r, :, span] = val.astype(BF16)
            slope_ref[r, :, span] = slope.astype(BF16)
    branch = dot(mixed_ref[...].reshape(TOK, EXP), wp_ref[...])
    section = (x_ref[...].reshape(TOK, CHAN).astype(F32) + branch).astype(BF16)
    section = section.reshape(2, 2, 4, 16, CHAN)
    for pair in range(2):
        for quad in range(4):
            section_ref[4 * pair + quad] = section[pair, :, quad].reshape(32, CHAN)


def ring_body(
    above_ref, below_ref, first_ref, last_ref, west_ref, east_ref, own_west_ref, own_east_ref,
    we_ref, dk_ref,
    top_ref, bottom_ref, left_ref, right_ref, slope_ref,
):
    west, east = west_ref[...].astype(F32), east_ref[...].astype(F32)
    pad = jnp.zeros((LONG - COLS - 4, CHAN), F32)

    def along(row, at):
        return [
            west[0, at : at + 1], west[1, at : at + 1], row.astype(F32),
            east[0, at : at + 1], east[1, at : at + 1], pad,
        ]

    strips = along(above_ref[0], 0) + along(above_ref[1], 1) + along(first_ref[0], 2)
    strips += along(last_ref[0], 33) + along(below_ref[0], 34) + along(below_ref[1], 35)
    strips += [west[0], west[1], own_west_ref[0].astype(F32)]
    strips += [own_east_ref[1].astype(F32), east[0], east[1]]
    normed, _ = layer_norm(jnp.concatenate(strips, axis=0))
    normed_b = normed.astype(BF16)
    south, lefts, rights = 3 * LONG, 6 * LONG, 6 * LONG + 3 * EDGE
    for at in range(0, EXP, 256):
        span = slice(at, at + 256)
        val, _ = gelu_slope(dot(normed_b, we_ref[:, span]))
        val = val.astype(BF16).astype(F32)
        kern = [dk_ref[n, span][None] for n in range(9)]
        top_ref[:, span] = val[LONG + 2 : LONG + 2 + COLS].astype(BF16)
        bottom_ref[:, span] = val[south + LONG + 2 : south + LONG + 2 + COLS].astype(BF16)
        for ref, base, col in ((left_ref, lefts, 0), (right_ref, rights, 2)):
            total = 0.0
            for a in range(3):
                start = base + EDGE + a + 1
                total = total + kern[3 * a + col] * val[start : start + ROWS]
            for s in range(STEPS):
                ref[s, :BLK, span] = total[BLK * s : BLK * s + BLK]
        for base, out in ((0, 0), (south, COLS)):
            total = 0.0
            for a in range(3):
                for b in range(3):
                    start = base + LONG * a + b + 1
                    total = total + kern[3 * a + b] * val[start : start + COLS]
            slope_ref[out : out + COLS, span] = gelu_slope(total)[1]
        for base, out in ((lefts, 2 * COLS), (rights, 2 * COLS + EDGE)):
            total = 0.0
            for a in range(3):
                for b in range(3):
                    start = base + EDGE * b + a
                    total = total + kern[3 * a + b] * val[start : start + ROWS + 2]
            slope_ref[out : out + ROWS + 2, span] = gelu_slope(total)[1]
            slope_ref[out + ROWS + 2 : out + EDGE, span] = jnp.zeros((EDGE - ROWS - 2, 256), F32)


def mix(hidden, halo, we, dk, dkb, wp, x):
    above, below, west, east, own_west, own_east = halo
    wide = jax.ShapeDtypeStruct((ROWS, COLS, EXP), BF16)
    return pl.pallas_call(
        mix_body,
        grid=(STEPS,),
        in_specs=[
            band((BLK, COLS, EXP)), ROW_BEFORE, ROW_AFTER,
            whole((2, COLS, CHAN)), whole((2, COLS, CHAN)),
            pl.BlockSpec((1, COLS, CHAN), lambda i: (0, 0, 0)),
            pl.BlockSpec((1, COLS, CHAN), lambda i: (ROWS - 1, 0, 0)),
            whole((2, EDGE, CHAN)), whole((2, EDGE, CHAN)), whole((2, EDGE, CHAN)), whole((2, EDGE, CHAN)),
            whole((CHAN, EXP)), whole((9, EXP)), whole((9, 16, EXP)), whole((EXP, CHAN)),
            band((BLK, COLS, CHAN)),
        ],
        out_specs=[
            band((8, 32, CHAN)), band((BLK, COLS, EXP)), band((BLK, COLS, EXP)), whole((HALO, EXP)),
        ],
        out_shape=[
            jax.ShapeDtypeStruct((64, 32, CHAN), BF16), wide, wide, jax.ShapeDtypeStruct((HALO, EXP), F32),
        ],
        scratch_shapes=[pltpu.VMEM((COLS, EXP), BF16)] * 2 + [pltpu.VMEM((STEPS, 8, EXP), F32)] * 2,
        compiler_params=params(58),
        cost_estimate=pl.CostEstimate(
            flops=3 * ROWS * COLS * CHAN * EXP, bytes_accessed=18 * MIB, transcendentals=2 * ROWS * COLS * EXP
        ),
        name="mix",
    )(
        hidden, hidden, hidden, above, below, x, x, west, east, own_west, own_east,
        we, dk, dkb, wp, x,
    )


SWAP = np.zeros((256, 256), np.float32)
for _s in range(16):
    for _g in range(16):
        SWAP[_g * 16 + _s, _s * 16 + _g] = 1.0


def diagonal(full, low):
    halves = []
    for half in range(2):
        lanes = slice(half * 128, half * 128 + 128)
        at = half * 128
        halves.append(jnp.where(low, full[at : at + 64, lanes], full[at + 64 : at + 128, lanes]))
    return jnp.concatenate(halves, axis=1)


def swap(src, dst, swap_ref, n_groups):
    for s in range(0, 64, 16):
        for g in range(0, n_groups, 16):
            moved = dot(swap_ref[...], src[s : s + 16, g : g + 16].reshape(256, CHAN)).astype(BF16)
            dst[g : g + 16, s : s + 16] = moved.reshape(16, 16, CHAN)


def prepare_body(cot_ref, wout_ref, swap_ref, cs_ref, da_ref):
    n_groups = cot_ref.shape[1]
    swap(cot_ref, cs_ref, swap_ref, n_groups)
    for g in range(0, n_groups, 4):
        grads = dot_nt(cs_ref[g : g + 4].reshape(256, CHAN), wout_ref[...])
        da_ref[g : g + 4] = grads.astype(BF16).reshape(4, 64, CHAN)


def prepare(cot, wout, n_groups):
    shape = (64, n_groups, CHAN)
    grouped = (n_groups, 64, CHAN)
    return pl.pallas_call(
        prepare_body,
        grid=(1,),
        in_specs=[whole(shape), whole((CHAN, CHAN)), whole((256, 256))],
        out_specs=[whole(grouped), whole(grouped)],
        out_shape=[jax.ShapeDtypeStruct(grouped, BF16)] * 2,
        compiler_params=params(58),
        cost_estimate=pl.CostEstimate(
            flops=n_groups * 64 * 4 * CHAN * CHAN, bytes_accessed=3 * MIB, transcendentals=0
        ),
        name="prepare",
    )(cot, wout, jnp.asarray(SWAP, BF16))


def attention_body(
    x_ref, da_ref, wqkv_ref, bias_ref, swap_ref,
    out_ref, att_ref, norm_ref, proj_ref, bias_sum_ref, xs_ref, ds_ref,
):
    step = pl.program_id(0)
    n_groups = x_ref.shape[1]

    @pl.when(step == 0)
    def _():
        bias_sum_ref[...] = jnp.zeros_like(bias_sum_ref)
        swap(x_ref, xs_ref, swap_ref, n_groups)

    groups = pl.ds(step * 4, 4)
    tokens = xs_ref[groups].reshape(256, CHAN)
    normed, inv_std = layer_norm(tokens.astype(F32))
    normed_b = normed.astype(BF16)
    norm_ref[...] = normed_b
    projected = dot(normed_b, wqkv_ref[...]).astype(BF16)
    low = lax.broadcasted_iota(jnp.int32, (64, 128), 1) < 64
    head_of = lax.broadcasted_iota(jnp.int32, (64, CHAN), 1) // 64
    masks = [(head_of == h).astype(F32).astype(BF16) for h in range(4)]
    for g in range(4):
        part = slice(g * 64, g * 64 + 64)
        query = projected[part, :CHAN] * 0.125
        key = projected[part, CHAN : 2 * CHAN]
        value = projected[part, 2 * CHAN :]
        da = da_ref[g]
        query_h = jnp.concatenate([query * m for m in masks], axis=0)
        da_h = jnp.concatenate([da * m for m in masks], axis=0)
        scores = dot_nt(key, query_h) + bias_ref[...]
        scores = jnp.exp(scores - jnp.max(scores, axis=0, keepdims=True))
        probs = scores * (1.0 / jnp.sum(scores, axis=0, keepdims=True))
        probs_b = probs.astype(BF16)
        d_probs = dot_nt(value, da_h)
        d_scores = probs * (d_probs - jnp.sum(probs * d_probs, axis=0, keepdims=True))
        bias_sum_ref[...] += d_scores
        d_scores_b = d_scores.astype(BF16)
        att_ref[part] = diagonal(dot_tn(probs_b, value), low).astype(BF16)
        proj_ref[part, :CHAN] = (diagonal(dot_tn(d_scores_b, key), low) * 0.125).astype(BF16)
        proj_ref[part, CHAN : 2 * CHAN] = dot(d_scores_b, query_h).astype(BF16)
        proj_ref[part, 2 * CHAN :] = dot(probs_b, da_h).astype(BF16)
    d_normed = dot_nt(proj_ref[...], wqkv_ref[...])
    d_tokens = layer_norm_back(normed, inv_std, d_normed).astype(BF16)
    ds_ref[groups] = d_tokens.reshape(4, 64, CHAN)

    @pl.when(step == n_groups // 4 - 1)
    def _():
        for s in range(0, 64, 16):
            for g in range(0, n_groups, 16):
                tile = ds_ref[g : g + 16, s : s + 16].reshape(256, CHAN)
                moved = dot(swap_ref[...], tile).astype(BF16)
                out_ref[s : s + 16, g : g + 16] = moved.reshape(16, 16, CHAN)


def attention(tokens, d_att, wqkv, bias):
    n_groups = tokens.shape[1]
    shape = (64, n_groups, CHAN)
    flat = n_groups * 64
    return pl.pallas_call(
        attention_body,
        grid=(n_groups // 4,),
        in_specs=[
            whole(shape), band((4, 64, CHAN)), whole((CHAN, 3 * CHAN)), whole((64, CHAN)),
            whole((256, 256)),
        ],
        out_specs=[
            whole(shape), band((256, CHAN)), band((256, CHAN)), band((256, 3 * CHAN)), whole((64, CHAN)),
        ],
        out_shape=[
            jax.ShapeDtypeStruct(shape, BF16),
            jax.ShapeDtypeStruct((flat, CHAN), BF16),
            jax.ShapeDtypeStruct((flat, CHAN), BF16),
            jax.ShapeDtypeStruct((flat, 3 * CHAN), BF16),
            jax.ShapeDtypeStruct((64, CHAN), F32),
        ],
        scratch_shapes=[pltpu.VMEM((n_groups, 64, CHAN), BF16)] * 2,
        compiler_params=params(58),
        cost_estimate=pl.CostEstimate(
            flops=flat * 4 * CHAN * CHAN * 5, bytes_accessed=8 * MIB, transcendentals=flat * 256
        ),
        name="attention",
    )(tokens, d_att, wqkv, bias, jnp.asarray(SWAP, BF16))


def attention_sums_body(att_ref, cot_ref, norm_ref, proj_ref, out_ref, qkv_acc, out_acc):
    step = pl.program_id(0)

    @pl.when(step == 0)
    def _():
        qkv_acc[...] = jnp.zeros_like(qkv_acc)
        out_acc[...] = jnp.zeros_like(out_acc)

    out_acc[...] += dot_tn(att_ref[...], cot_ref[...])
    qkv_acc[...] += dot_tn(norm_ref[...], proj_ref[...])

    @pl.when(step == pl.num_programs(0) - 1)
    def _():
        to_tiles(qkv_acc, out_ref, 0)
        to_tiles(out_acc, out_ref, 96)


def attention_sums(att, cot, normed, proj):
    flat = att.shape[0]
    return pl.pallas_call(
        attention_sums_body,
        grid=(flat // 512,),
        in_specs=[band((512, CHAN)), band((512, CHAN)), band((512, CHAN)), band((512, 3 * CHAN))],
        out_specs=whole(TILED),
        out_shape=jax.ShapeDtypeStruct(TILED, BF16),
        scratch_shapes=[pltpu.VMEM((CHAN, 3 * CHAN), F32), pltpu.VMEM((CHAN, CHAN), F32)],
        compiler_params=params(58),
        cost_estimate=pl.CostEstimate(
            flops=flat * 8 * CHAN * CHAN, bytes_accessed=6 * MIB, transcendentals=0
        ),
        name="attention_sums",
    )(att, cot, normed, proj)


def section_grad(cot_ref, db_ref):
    pieces = db_ref[...].reshape(2, 4, 2, 16, CHAN)
    branch = jnp.concatenate(
        [pieces[pair, quad, r] for pair in range(2) for r in range(2) for quad in range(4)], axis=0
    )
    return cot_ref[...].reshape(TOK, CHAN).astype(F32) + branch.astype(F32)


def project_body(cot_ref, db_ref, slope_ref, wp_ref, dm_ref):
    d_section_b = section_grad(cot_ref, db_ref).astype(BF16)
    for at in range(0, EXP, 256):
        grads = dot_nt(d_section_b, wp_ref[at : at + 256, :])
        slope = slope_ref[:, :, at : at + 256].reshape(TOK, 256).astype(F32)
        dm_ref[:, :, at : at + 256] = (grads * slope).astype(BF16).reshape(BLK, COLS, 256)


def project_back(cot, db, slope, wp):
    return pl.pallas_call(
        project_body,
        grid=(STEPS,),
        in_specs=[
            band((BLK, COLS, CHAN)), band((8, 32, CHAN)), band((BLK, COLS, EXP)), whole((EXP, CHAN)),
        ],
        out_specs=band((BLK, COLS, EXP)),
        out_shape=jax.ShapeDtypeStruct((ROWS, COLS, EXP), BF16),
        compiler_params=params(58),
        cost_estimate=pl.CostEstimate(
            flops=2 * ROWS * COLS * CHAN * EXP, bytes_accessed=10 * MIB, transcendentals=0
        ),
        name="project_back",
    )(cot, db, slope, wp)


def project_sum_body(cot_ref, db_ref, mixed_ref, tiles_ref, sum_ref, turned_ref):
    @pl.when(pl.program_id(0) == 0)
    def _():
        sum_ref[...] = jnp.zeros_like(sum_ref)

    d_section_b = section_grad(cot_ref, db_ref).astype(BF16)
    sum_ref[...] += dot_tn(d_section_b, mixed_ref[...].reshape(TOK, EXP))

    @pl.when(pl.program_id(0) == STEPS - 1)
    def _():
        turned_ref[...] = sum_ref[...].T
        to_tiles(turned_ref, tiles_ref, 0)


def project_sum(cot, db, mixed):
    return pl.pallas_call(
        project_sum_body,
        grid=(STEPS,),
        in_specs=[band((BLK, COLS, CHAN)), band((8, 32, CHAN)), band((BLK, COLS, EXP))],
        out_specs=whole(TILED),
        out_shape=jax.ShapeDtypeStruct(TILED, BF16),
        scratch_shapes=[pltpu.VMEM((CHAN, EXP), F32), pltpu.VMEM((EXP, CHAN), F32)],
        compiler_params=params(58),
        cost_estimate=pl.CostEstimate(
            flops=2 * ROWS * COLS * CHAN * EXP, bytes_accessed=8 * MIB, transcendentals=0
        ),
        name="project_sum",
    )(cot, db, mixed)


def expand_back_body(
    cur_ref, before_ref, after_ref, halo_ref, halo_slope_ref, wp_ref, hid_ref, slope_ref, x_ref, dkb_ref,
    extra_ref,
    dpre_ref, tiles_ref, top_ref, bottom_ref, left_ref, right_ref, acc_ref, sum_ref, depth_ref,
):
    step = pl.program_id(0)

    @pl.when(step == 0)
    def _():
        sum_ref[...] = jnp.zeros_like(sum_ref)
        acc_ref[...] = jnp.zeros_like(acc_ref)
        for at in range(0, EXP, 256):
            span = slice(at, at + 256)
            grads = dot_nt(halo_ref[...], wp_ref[at : at + 256, :])
            grads = (grads * halo_slope_ref[:, span]).astype(BF16).astype(F32)
            top_ref[:, span] = grads[:COLS]
            bottom_ref[:, span] = grads[COLS : 2 * COLS]
            for ref, base in ((left_ref, 2 * COLS), (right_ref, 2 * COLS + EDGE)):
                for s in range(STEPS):
                    ref[s, : BLK + 2, span] = grads[base + BLK * s : base + BLK * s + BLK + 2]

    first, last = step == 0, step == STEPS - 1
    for at in range(0, EXP, LANES):
        span = slice(at, at + LANES)
        rows = [jnp.where(first, top_ref[:, span], before_ref[0, :, span].astype(F32))]
        rows += [cur_ref[r, :, span].astype(F32) for r in range(BLK)]
        rows += [jnp.where(last, bottom_ref[:, span], after_ref[0, :, span].astype(F32))]
        shifted = []
        for r in range(BLK + 2):
            left = left_ref[step, r : r + 1, span]
            right = right_ref[step, r : r + 1, span]
            moved = (
                jnp.concatenate([rows[r][1:], right], axis=0),
                rows[r],
                jnp.concatenate([left, rows[r][:-1]], axis=0),
            )
            shifted.append([piece.astype(BF16).reshape(PACKED) for piece in moved])
        hid = [hid_ref[r, :, span].reshape(PACKED) for r in range(BLK)]
        totals = [None] * BLK
        for a in range(3):
            for b in range(3):
                n = 3 * a + b
                kern = dkb_ref[n, :, span][None]
                terms = []
                for r in range(BLK):
                    piece = shifted[r + 2 - a][b]
                    tap = kern * piece
                    totals[r] = tap if n == 0 else totals[r] + tap
                    terms.append(hid[r] * piece)
                part = (terms[0] + terms[1]) + (terms[2] + terms[3])
                part = ((part[0] + part[1]) + (part[2] + part[3])).astype(F32)
                acc_ref[n, :, span] += part[:8] + part[8:]
        for r in range(BLK):
            d_pre = totals[r].reshape(COLS, LANES) * slope_ref[r, :, span]
            dpre_ref[r * COLS : (r + 1) * COLS, span] = d_pre
    normed, _ = layer_norm(x_ref[...].reshape(TOK, CHAN).astype(F32))
    sum_ref[...] += dot_tn(normed.astype(BF16), dpre_ref[...])

    @pl.when(last)
    def _():
        depth_ref[...] = jnp.sum(acc_ref[...], axis=1)
        to_tiles(sum_ref, tiles_ref, 0)
        first_row = lax.broadcasted_iota(jnp.int32, (8, 128), 0) == 0
        for n in range(128):
            extra = extra_ref[n]
            if n < 72:
                row = depth_ref[n // 8 : n // 8 + 1, 128 * (n % 8) : 128 * (n % 8) + 128]
                extra = jnp.where(first_row, row, extra)
            tiles_ref[n, 16:] = extra.astype(BF16)


def expand_back(d_mixed, halo, halo_slope, wp, hidden, slope, x, dkb, extra):
    tiles = (128, 24, 128)
    cells = band((BLK, COLS, EXP))
    return pl.pallas_call(
        expand_back_body,
        grid=(STEPS,),
        in_specs=[
            cells, ROW_BEFORE, ROW_AFTER, whole((HALO, CHAN)), whole((HALO, EXP)),
            whole((EXP, CHAN)), cells, cells, band((BLK, COLS, CHAN)), whole((9, 16, EXP)),
            whole((128, 8, 128)),
        ],
        out_specs=[band((TOK, EXP)), whole(tiles)],
        out_shape=[
            jax.ShapeDtypeStruct((ROWS * COLS, EXP), BF16),
            jax.ShapeDtypeStruct(tiles, BF16),
        ],
        scratch_shapes=[pltpu.VMEM((COLS, EXP), F32)] * 2
        + [pltpu.VMEM((STEPS, 8, EXP), F32)] * 2
        + [pltpu.VMEM((9, 8, EXP), F32), pltpu.VMEM((CHAN, EXP), F32), pltpu.VMEM((9, EXP), F32)],
        compiler_params=params(58),
        cost_estimate=pl.CostEstimate(
            flops=2 * ROWS * COLS * CHAN * EXP, bytes_accessed=20 * MIB, transcendentals=0
        ),
        name="expand_back",
    )(d_mixed, d_mixed, d_mixed, halo, halo_slope, wp, hidden, slope, x, dkb, extra)


def finish_body(dpre_ref, x_ref, cot_ref, db_ref, we_ref, grad_ref):
    normed, inv_std = layer_norm(x_ref[...].reshape(TOK, CHAN).astype(F32))
    d_input = layer_norm_back(normed, inv_std, dot_nt(dpre_ref[...], we_ref[...]))
    grad_ref[...] = (section_grad(cot_ref, db_ref) + d_input).astype(BF16).reshape(BLK, COLS, CHAN)


def finish(d_pre, x, cot, db, we):
    return pl.pallas_call(
        finish_body,
        grid=(STEPS,),
        in_specs=[
            band((TOK, EXP)), band((BLK, COLS, CHAN)), band((BLK, COLS, CHAN)), band((8, 32, CHAN)),
            whole((CHAN, EXP)),
        ],
        out_specs=band((BLK, COLS, CHAN)),
        out_shape=jax.ShapeDtypeStruct((ROWS, COLS, CHAN), BF16),
        compiler_params=params(58),
        cost_estimate=pl.CostEstimate(
            flops=2 * ROWS * COLS * CHAN * EXP, bytes_accessed=9 * MIB, transcendentals=0
        ),
        name="finish",
    )(d_pre, x, cot, db, we)


def join_body(core_ref, *refs):
    half = pl.ds(core_ref[0] * 64, 64)
    out_ref = refs[-1]
    at = 0
    for own_ref, other_ref in zip(refs[0:-1:2], refs[1:-1:2]):
        total = own_ref[half].astype(F32) + other_ref[half].astype(F32)
        out_ref[:, at : at + own_ref.shape[1]] = total.astype(BF16)
        at += own_ref.shape[1]


def join(core, *tiles):
    vmem = pl.BlockSpec(memory_space=pltpu.VMEM)
    return pl.pallas_call(
        join_body,
        in_specs=[pl.BlockSpec(memory_space=pltpu.SMEM)] + [vmem] * len(tiles),
        out_shape=jax.ShapeDtypeStruct(JOINED, BF16),
        compiler_params=params(58),
        cost_estimate=pl.CostEstimate(flops=MIB, bytes_accessed=4 * MIB, transcendentals=0),
        name="join",
    )(core, *tiles)


def fold_body(terms_ref, out_ref):
    factor = float(128 * ROWS * COLS) ** (-0.5)
    total = jnp.sum(terms_ref[...].astype(F32), axis=0) * factor
    out_ref[...] = jnp.broadcast_to(total.astype(BF16)[None], out_ref.shape)


def fold(terms):
    return pl.pallas_call(
        fold_body,
        out_shape=jax.ShapeDtypeStruct(terms.shape, BF16),
        compiler_params=params(58),
        cost_estimate=pl.CostEstimate(flops=terms.size, bytes_accessed=4 * terms.size, transcendentals=0),
        name="fold",
    )(terms)


def unfold_body(core_ref, own_ref, other_ref, expand_ref, depth_ref, project_ref, qkv_ref, out_ref, bias_ref):
    first = core_ref[0] == 0

    def tile(n, rows):
        own, other = own_ref[n % 64, rows].astype(F32), other_ref[n % 64, rows].astype(F32)
        return jnp.where(first, own, other) if n < 64 else jnp.where(first, other, own)

    parts = ((qkv_ref, 0, 0), (out_ref, 96, 0), (project_ref, 0, 16), (expand_ref, 0, 32))
    for ref, at, low in parts:
        wide = ref.shape[1] // 128
        for r in range(ref.shape[0] // 16):
            for c in range(wide):
                piece = tile(at + wide * r + c, slice(low, low + 16))
                ref[16 * r : 16 * r + 16, 128 * c : 128 * c + 128] = piece
    for n in range(72):
        extra = tile(n, slice(48, 56))
        at = 128 * (n % 8)
        depth_ref[n // 24, n // 8 % 3 : n // 8 % 3 + 1, at : at + 128] = extra[:1]
        if n < 60:
            bias_ref[n % 15, n // 15 : n // 15 + 1, :] = extra[1:2, :15]


def unfold(core, own, other):
    vmem = pl.BlockSpec(memory_space=pltpu.VMEM)
    return pl.pallas_call(
        unfold_body,
        in_specs=[pl.BlockSpec(memory_space=pltpu.SMEM), vmem, vmem],
        out_shape=[
            jax.ShapeDtypeStruct((CHAN, EXP), F32),
            jax.ShapeDtypeStruct((3, 3, EXP), F32),
            jax.ShapeDtypeStruct((EXP, CHAN), F32),
            jax.ShapeDtypeStruct((CHAN, 3 * CHAN), F32),
            jax.ShapeDtypeStruct((CHAN, CHAN), F32),
            jax.ShapeDtypeStruct((15, 4, 15), F32),
        ],
        compiler_params=params(58),
        cost_estimate=pl.CostEstimate(flops=0, bytes_accessed=5 * MIB, transcendentals=0),
        name="unfold",
    )(core, own, other)


FIRST_CELL = np.zeros((32, 512), np.float32)
LAST_CELL = np.zeros((32, 512), np.float32)
for _row in range(32):
    FIRST_CELL[_row, _row * 16] = 1.0
    LAST_CELL[_row, _row * 16 + 15] = 1.0


def edges_body(
    dt_ref, ct_ref, db_ref, cb_ref, dl_ref, cl_ref, dr_ref, cr_ref, first_ref, last_ref,
    top_ref, bottom_ref, left_ref, right_ref,
):
    def total(d_ref, c_ref):
        return (d_ref[...].astype(F32) + c_ref[...].astype(F32)).astype(BF16)

    top = total(dt_ref, ct_ref)
    bottom = total(db_ref, cb_ref)
    for quad in range(4):
        top_ref[16 * quad : 16 * quad + 16] = top[0, quad, :16]
        bottom_ref[16 * quad : 16 * quad + 16] = bottom[0, quad, 16:]
    left_ref[...] = dot(first_ref[...], total(dl_ref, cl_ref).reshape(512, CHAN)).astype(BF16)
    right_ref[...] = dot(last_ref[...], total(dr_ref, cr_ref).reshape(512, CHAN)).astype(BF16)


def edges(d_branch, cot):
    d_branch, cot = d_branch.reshape(16, 4, 32, CHAN), cot.reshape(16, 4, 32, CHAN)
    specs = []
    for row in (0, 15):
        specs += [pl.BlockSpec((1, 4, 32, CHAN), lambda i, row=row: (row, 0, 0, 0))] * 2
    for col in (0, 3):
        specs += [pl.BlockSpec((16, 1, 32, CHAN), lambda i, col=col: (0, col, 0, 0))] * 2
    return pl.pallas_call(
        edges_body,
        grid=(1,),
        in_specs=specs + [whole((32, 512))] * 2,
        out_specs=[whole((COLS, CHAN))] * 2 + [whole((ROWS, CHAN))] * 2,
        out_shape=[jax.ShapeDtypeStruct((COLS, CHAN), BF16)] * 2
        + [jax.ShapeDtypeStruct((ROWS, CHAN), BF16)] * 2,
        compiler_params=params(58),
        cost_estimate=pl.CostEstimate(flops=MIB, bytes_accessed=2 * MIB, transcendentals=0),
        name="edges",
    )(*([d_branch, cot] * 4), jnp.asarray(FIRST_CELL, BF16), jnp.asarray(LAST_CELL, BF16))


def shifts():
    n_lat, n_lon = lax.axis_size("lat"), lax.axis_size("lon")
    south = [(i, i + 1) for i in range(n_lat - 1)]
    north = [(i + 1, i) for i in range(n_lat - 1)]
    east = [(i, (i + 1) % n_lon) for i in range(n_lon)]
    west = [((i + 1) % n_lon, i) for i in range(n_lon)]
    return (south, north, east, west)


def rows_of(top, bottom):
    south, north, _, _ = shifts()
    return (lax.ppermute(bottom, "lat", south), lax.ppermute(top, "lat", north))


def halo_of(above, below, left, right):
    _, _, east, west = shifts()
    pad = jnp.zeros((EDGE - ROWS - 2, left.shape[1]), left.dtype)
    from_west = lax.ppermute(
        jnp.concatenate([above[-1:], right, below[-1:], pad], axis=0), "lon", east
    )
    from_east = lax.ppermute(
        jnp.concatenate([above[:1], left, below[:1], pad], axis=0), "lon", west
    )
    return jnp.concatenate([above, below, from_west, from_east], axis=0)


def wide_halo(field):
    south, north, east, west = shifts()
    flat = (2 * COLS, CHAN)
    above = lax.ppermute(field[-2:].reshape(flat), "lat", south).reshape(2, COLS, CHAN)
    below = lax.ppermute(field[:2].reshape(flat), "lat", north).reshape(2, COLS, CHAN)
    pad = jnp.zeros((2, EDGE - ROWS - 4, field.shape[2]), field.dtype)

    def columns(at):
        parts = [part[:, at : at + 2].transpose(1, 0, 2) for part in (above, field, below)]
        return jnp.concatenate(parts + [pad], axis=1)

    own_west, own_east = columns(0), columns(COLS - 2)
    from_west = lax.ppermute(own_east, "lon", east)
    from_east = lax.ppermute(own_west, "lon", west)
    return (above, below, from_west, from_east, own_west, own_east)


def exchange(pieces):
    n_lat, n_lon = lax.axis_size("lat"), lax.axis_size("lon")
    order = np.arange(n_lat * n_lon).reshape(n_lat, n_lon // 2, 2)
    members = order.transpose(2, 0, 1).reshape(2, -1).tolist()
    return lax.all_to_all(
        pieces, ("lat", "lon"), split_axis=0, concat_axis=0, axis_index_groups=members, tiled=True
    )


def to_pieces(field):
    shaped = field.reshape(16, 2, 4, 16, CHAN).transpose(0, 2, 1, 3, 4)
    return shaped.reshape(64, 32, CHAN)


def pairs():
    return np.arange(lax.axis_size("lon")).reshape(-1, 2).tolist()


def other_core(tiles):
    swaps = [move for a, b in pairs() for move in ((a, b), (b, a))]
    return lax.ppermute(tiles, "lon", swaps)


def rel_table():
    position = np.arange(64)
    pos_row, pos_col = position // 8, position % 8
    rel_index = (pos_row[:, None] - pos_row[None, :] + 7) * 15 + (
        pos_col[:, None] - pos_col[None, :] + 7
    )
    return jnp.asarray(rel_index)[:, :, None] == jnp.arange(225)[None, None, :]


def on_device(
    field_in, cotangent, expand_weight, depth_kernel, project_weight, qkv_weight, out_weight, rel_bias
):
    onehot = rel_table().astype(F32)
    bias = jnp.einsum(
        "tsr,hr->sht", onehot, rel_bias.reshape(4, 225), precision=lax.Precision.HIGHEST
    ).reshape(64, 256)
    dk = depth_kernel.reshape(9, EXP)

    dkb = jnp.broadcast_to(dk[:, None], (9, 16, EXP)).astype(BF16)
    core = lax.axis_index("lon").astype(jnp.int32).reshape(1) & 1
    barrier = lax.optimization_barrier

    field_halo = wide_halo(field_in)
    hidden, act_slope = expand(field_in, expand_weight)
    field_halo, late_cot = barrier((field_halo, cotangent))
    hidden, cot_pieces = barrier((hidden, to_pieces(late_cot)))
    cot_groups = exchange(cot_pieces)
    section, mixed, mixed_slope, ring_slope = mix(
        hidden, field_halo, expand_weight, dk, dkb, project_weight, field_in
    )
    groups = exchange(section)
    cot_swapped, d_att = prepare(cot_groups, out_weight, 32)
    groups, bias, d_att = barrier((groups, bias, d_att))
    d_groups, attended, normed2, d_proj, bias_acc = attention(groups, d_att, qkv_weight, bias)

    d_branch = exchange(d_groups)
    attention_tiles = attention_sums(attended, cot_swapped.reshape(-1, CHAN), normed2, d_proj)
    bias_sum = jnp.einsum(
        "sht,tsr->hr", bias_acc.reshape(64, 4, 64), onehot, precision=lax.Precision.HIGHEST
    )
    extra = jnp.pad(bias_sum.reshape(60, 1, 15), ((0, 68), (1, 6), (0, 113)))
    d_branch, attention_tiles, extra = barrier((d_branch, attention_tiles, extra))

    top, bottom, left, right = edges(d_branch, cot_pieces)
    above, below = rows_of(top, bottom)
    d_mixed = project_back(cotangent, d_branch, mixed_slope, project_weight)
    above, below, d_mixed, attention_tiles = barrier((above, below, d_mixed, attention_tiles))
    d_halo = halo_of(above, below, left, right)
    project_tiles = project_sum(cotangent, d_branch, mixed)
    d_halo, project_tiles, d_mixed = barrier((d_halo, project_tiles, d_mixed))
    attention_pair = (attention_tiles, other_core(attention_tiles))
    project_pair = (project_tiles, other_core(project_tiles))
    d_pre, expand_tiles = expand_back(
        d_mixed, d_halo, ring_slope, project_weight, hidden, act_slope, field_in, dkb, extra
    )

    joined = join(core, *attention_pair, *project_pair, expand_tiles, other_core(expand_tiles))
    joined, d_pre = barrier((joined, d_pre))
    terms = exchange(joined)
    grad_in = finish(d_pre, field_in, cotangent, d_branch, expand_weight)
    terms, grad_in = barrier((terms, grad_in))
    sums = exchange(fold(terms))
    *grads, bias_grad = unfold(core, sums, other_core(sums))
    return (grad_in, *grads, bias_grad.transpose(1, 0, 2))


def solution(mesh):
    placed = (P("lat", "lon", None), P("lat", "lon", None), P(), P(), P(), P(), P(), P())
    return jax.shard_map(
        on_device,
        mesh=mesh,
        in_specs=placed,
        out_specs=(P("lat", "lon", None), P(), P(), P(), P(), P(), P()),
        check_vma=False,
    )
```

```python
import math

import jax
import jax.numpy as jnp
import numpy as np
from jax import lax
from jax.experimental import pallas as pl
from jax.experimental.pallas import tpu as pltpu
from jax.sharding import PartitionSpec as P

EPSILON = 1e-05
GELU_C = math.sqrt(2.0 / math.pi)
F32 = jnp.float32
BF16 = jnp.bfloat16
MIB = 1 << 20

ROWS, COLS, CHAN, EXP = 32, 64, 256, 1024
BLK = 4
STEPS = ROWS // BLK
TOK = BLK * COLS
LANES = 128
EDGE = 40
HALO = 2 * COLS + 2 * EDGE
LONG = 72
PACKED = (4, 16, LANES)
JOINED = (64, 56, 128)


def layer_norm(values):
    average = jnp.mean(values, axis=-1, keepdims=True)
    centred = values - average
    variance = jnp.mean(centred * centred, axis=-1, keepdims=True)
    inv_std = lax.rsqrt(variance + EPSILON)
    return (centred * inv_std, inv_std)


def layer_norm_back(normed, inv_std, grads):
    mean_grad = jnp.mean(grads, axis=-1, keepdims=True)
    mean_cross = jnp.mean(grads * normed, axis=-1, keepdims=True)
    return (grads - mean_grad - normed * mean_cross) * inv_std


def gelu_slope(values):
    squared = values * values
    tanh_val = jnp.tanh(values * (GELU_C + (GELU_C * 0.044715) * squared))
    gate = 0.5 + 0.5 * tanh_val
    result = values * gate
    slopes = gate + result * (1.0 - gate) * (2.0 * GELU_C + (6.0 * GELU_C * 0.044715) * squared)
    return (result, slopes)


def dot(left, right):
    return lax.dot_general(left, right, (((1,), (0,)), ((), ())), preferred_element_type=F32)


def dot_nt(left, right):
    return lax.dot_general(left, right, (((1,), (1,)), ((), ())), preferred_element_type=F32)


def dot_tn(left, right):
    return lax.dot_general(left, right, (((0,), (0,)), ((), ())), preferred_element_type=F32)


def params(mib):
    return pltpu.CompilerParams(vmem_limit_bytes=mib * MIB)


def whole(shape):
    return pl.BlockSpec(shape, lambda i: (0,) * len(shape))


def band(shape):
    return pl.BlockSpec(shape, lambda i: (i,) + (0,) * (len(shape) - 1))


ROW_BEFORE = pl.BlockSpec(
    (1, COLS, EXP), lambda i: (jnp.maximum(BLK * i - 1, 0), 0, 0)
)
ROW_AFTER = pl.BlockSpec(
    (1, COLS, EXP), lambda i: (jnp.minimum(BLK * i + BLK, ROWS - 1), 0, 0)
)


TILED = (128, 16, 128)


def to_tiles(ref, out_ref, at):
    wide = ref.shape[1] // 128
    for r in range(ref.shape[0] // 16):
        for c in range(wide):
            tile = ref[16 * r : 16 * r + 16, 128 * c : 128 * c + 128]
            out_ref[at + wide * r + c, :16] = tile.astype(BF16)


def expand_body(x_ref, we_ref, hid_ref, slope_ref):
    normed, _ = layer_norm(x_ref[...].reshape(TOK, CHAN).astype(F32))
    normed_b = normed.astype(BF16)
    for at in range(0, EXP, 256):
        val, slope = gelu_slope(dot(normed_b, we_ref[:, at : at + 256]))
        hid_ref[:, :, at : at + 256] = val.astype(BF16).reshape(BLK, COLS, 256)
        slope_ref[:, :, at : at + 256] = slope.astype(BF16).reshape(BLK, COLS, 256)


def expand(x, we):
    wide = jax.ShapeDtypeStruct((ROWS, COLS, EXP), BF16)
    return pl.pallas_call(
        expand_body,
        grid=(STEPS,),
        in_specs=[band((BLK, COLS, CHAN)), whole((CHAN, EXP))],
        out_specs=[band((BLK, COLS, EXP))] * 2,
        out_shape=[wide, wide],
        compiler_params=params(58),
        cost_estimate=pl.CostEstimate(
            flops=2 * ROWS * COLS * CHAN * EXP, bytes_accessed=10 * MIB, transcendentals=ROWS * COLS * EXP
        ),
        name="expand",
    )(x, we)


def mix_body(
    cur_ref, before_ref, after_ref,
    above_ref, below_ref, first_ref, last_ref, west_ref, east_ref, own_west_ref, own_east_ref,
    we_ref, dk_ref, dkb_ref, wp_ref, x_ref,
    section_ref, mixed_ref, slope_ref, ring_slope_ref,
    top_ref, bottom_ref, left_ref, right_ref,
):
    step = pl.program_id(0)

    @pl.when(step == 0)
    def _():
        ring_body(
            above_ref, below_ref, first_ref, last_ref, west_ref, east_ref, own_west_ref, own_east_ref,
            we_ref, dk_ref,
            top_ref, bottom_ref, left_ref, right_ref, ring_slope_ref,
        )

    first, last = step == 0, step == STEPS - 1
    for at in range(0, EXP, LANES):
        span = slice(at, at + LANES)
        rows = [jnp.where(first, top_ref[:, span], before_ref[0, :, span])]
        rows += [cur_ref[r, :, span] for r in range(BLK)]
        rows += [jnp.where(last, bottom_ref[:, span], after_ref[0, :, span])]
        rows = [row.reshape(PACKED) for row in rows]
        kern = [dkb_ref[n, :, span][None] for n in range(9)]
        for r in range(BLK):
            parts = [
                kern[b] * rows[r] + kern[3 + b] * rows[r + 1] + kern[6 + b] * rows[r + 2]
                for b in range(3)
            ]
            parts = [part.reshape(COLS, LANES).astype(F32) for part in parts]
            left = left_ref[step, r : r + 1, span]
            right = right_ref[step, r : r + 1, span]
            pre = (
                parts[1]
                + jnp.concatenate([left, parts[0][:-1]], axis=0)
                + jnp.concatenate([parts[2][1:], right], axis=0)
            )
            val, slope = gelu_slope(pre)
            mixed_ref[r, :, span] = val.astype(BF16)
            slope_ref[r, :, span] = slope.astype(BF16)
    branch = dot(mixed_ref[...].reshape(TOK, EXP), wp_ref[...])
    section = (x_ref[...].reshape(TOK, CHAN).astype(F32) + branch).astype(BF16)
    section = section.reshape(2, 2, 4, 16, CHAN)
    for pair in range(2):
        for quad in range(4):
            section_ref[4 * pair + quad] = section[pair, :, quad].reshape(32, CHAN)


def ring_body(
    above_ref, below_ref, first_ref, last_ref, west_ref, east_ref, own_west_ref, own_east_ref,
    we_ref, dk_ref,
    top_ref, bottom_ref, left_ref, right_ref, slope_ref,
):
    west, east = west_ref[...].astype(F32), east_ref[...].astype(F32)
    pad = jnp.zeros((LONG - COLS - 4, CHAN), F32)

    def along(row, at):
        return [
            west[0, at : at + 1], west[1, at : at + 1], row.astype(F32),
            east[0, at : at + 1], east[1, at : at + 1], pad,
        ]

    strips = along(above_ref[0], 0) + along(above_ref[1], 1) + along(first_ref[0], 2)
    strips += along(last_ref[0], 33) + along(below_ref[0], 34) + along(below_ref[1], 35)
    strips += [west[0], west[1], own_west_ref[0].astype(F32)]
    strips += [own_east_ref[1].astype(F32), east[0], east[1]]
    normed, _ = layer_norm(jnp.concatenate(strips, axis=0))
    normed_b = normed.astype(BF16)
    south, lefts, rights = 3 * LONG, 6 * LONG, 6 * LONG + 3 * EDGE
    for at in range(0, EXP, 256):
        span = slice(at, at + 256)
        val, _ = gelu_slope(dot(normed_b, we_ref[:, span]))
        val = val.astype(BF16).astype(F32)
        kern = [dk_ref[n, span][None] for n in range(9)]
        top_ref[:, span] = val[LONG + 2 : LONG + 2 + COLS].astype(BF16)
        bottom_ref[:, span] = val[south + LONG + 2 : south + LONG + 2 + COLS].astype(BF16)
        for ref, base, col in ((left_ref, lefts, 0), (right_ref, rights, 2)):
            total = 0.0
            for a in range(3):
                start = base + EDGE + a + 1
                total = total + kern[3 * a + col] * val[start : start + ROWS]
            for s in range(STEPS):
                ref[s, :BLK, span] = total[BLK * s : BLK * s + BLK]
        for base, out in ((0, 0), (south, COLS)):
            total = 0.0
            for a in range(3):
                for b in range(3):
                    start = base + LONG * a + b + 1
                    total = total + kern[3 * a + b] * val[start : start + COLS]
            slope_ref[out : out + COLS, span] = gelu_slope(total)[1]
        for base, out in ((lefts, 2 * COLS), (rights, 2 * COLS + EDGE)):
            total = 0.0
            for a in range(3):
                for b in range(3):
                    start = base + EDGE * b + a
                    total = total + kern[3 * a + b] * val[start : start + ROWS + 2]
            slope_ref[out : out + ROWS + 2, span] = gelu_slope(total)[1]
            slope_ref[out + ROWS + 2 : out + EDGE, span] = jnp.zeros((EDGE - ROWS - 2, 256), F32)


def mix(hidden, halo, we, dk, dkb, wp, x):
    above, below, west, east, own_west, own_east = halo
    wide = jax.ShapeDtypeStruct((ROWS, COLS, EXP), BF16)
    return pl.pallas_call(
        mix_body,
        grid=(STEPS,),
        in_specs=[
            band((BLK, COLS, EXP)), ROW_BEFORE, ROW_AFTER,
            whole((2, COLS, CHAN)), whole((2, COLS, CHAN)),
            pl.BlockSpec((1, COLS, CHAN), lambda i: (0, 0, 0)),
            pl.BlockSpec((1, COLS, CHAN), lambda i: (ROWS - 1, 0, 0)),
            whole((2, EDGE, CHAN)), whole((2, EDGE, CHAN)), whole((2, EDGE, CHAN)), whole((2, EDGE, CHAN)),
            whole((CHAN, EXP)), whole((9, EXP)), whole((9, 16, EXP)), whole((EXP, CHAN)),
            band((BLK, COLS, CHAN)),
        ],
        out_specs=[
            band((8, 32, CHAN)), band((BLK, COLS, EXP)), band((BLK, COLS, EXP)), whole((HALO, EXP)),
        ],
        out_shape=[
            jax.ShapeDtypeStruct((64, 32, CHAN), BF16), wide, wide, jax.ShapeDtypeStruct((HALO, EXP), F32),
        ],
        scratch_shapes=[pltpu.VMEM((COLS, EXP), BF16)] * 2 + [pltpu.VMEM((STEPS, 8, EXP), F32)] * 2,
        compiler_params=params(58),
        cost_estimate=pl.CostEstimate(
            flops=3 * ROWS * COLS * CHAN * EXP, bytes_accessed=18 * MIB, transcendentals=2 * ROWS * COLS * EXP
        ),
        name="mix",
    )(
        hidden, hidden, hidden, above, below, x, x, west, east, own_west, own_east,
        we, dk, dkb, wp, x,
    )


SWAP = np.zeros((256, 256), np.float32)
for _s in range(16):
    for _g in range(16):
        SWAP[_g * 16 + _s, _s * 16 + _g] = 1.0


def diagonal(full, low):
    halves = []
    for half in range(2):
        lanes = slice(half * 128, half * 128 + 128)
        at = half * 128
        halves.append(jnp.where(low, full[at : at + 64, lanes], full[at + 64 : at + 128, lanes]))
    return jnp.concatenate(halves, axis=1)


def swap(src, dst, swap_ref, n_groups):
    for s in range(0, 64, 16):
        for g in range(0, n_groups, 16):
            moved = dot(swap_ref[...], src[s : s + 16, g : g + 16].reshape(256, CHAN)).astype(BF16)
            dst[g : g + 16, s : s + 16] = moved.reshape(16, 16, CHAN)


def prepare_body(cot_ref, wout_ref, swap_ref, cs_ref, da_ref):
    n_groups = cot_ref.shape[1]
    swap(cot_ref, cs_ref, swap_ref, n_groups)
    for g in range(0, n_groups, 4):
        grads = dot_nt(cs_ref[g : g + 4].reshape(256, CHAN), wout_ref[...])
        da_ref[g : g + 4] = grads.astype(BF16).reshape(4, 64, CHAN)


def prepare(cot, wout, n_groups):
    shape = (64, n_groups, CHAN)
    grouped = (n_groups, 64, CHAN)
    return pl.pallas_call(
        prepare_body,
        grid=(1,),
        in_specs=[whole(shape), whole((CHAN, CHAN)), whole((256, 256))],
        out_specs=[whole(grouped), whole(grouped)],
        out_shape=[jax.ShapeDtypeStruct(grouped, BF16)] * 2,
        compiler_params=params(24),
        cost_estimate=pl.CostEstimate(
            flops=n_groups * 64 * 4 * CHAN * CHAN, bytes_accessed=3 * MIB, transcendentals=0
        ),
        name="prepare",
    )(cot, wout, jnp.asarray(SWAP, BF16))


def attention_body(
    x_ref, da_ref, wqkv_ref, bias_ref, swap_ref,
    out_ref, att_ref, norm_ref, proj_ref, bias_sum_ref, xs_ref, ds_ref,
):
    step = pl.program_id(0)
    n_groups = x_ref.shape[1]

    @pl.when(step == 0)
    def _():
        bias_sum_ref[...] = jnp.zeros_like(bias_sum_ref)
        swap(x_ref, xs_ref, swap_ref, n_groups)

    groups = pl.ds(step * 4, 4)
    tokens = xs_ref[groups].reshape(256, CHAN)
    normed, inv_std = layer_norm(tokens.astype(F32))
    normed_b = normed.astype(BF16)
    norm_ref[...] = normed_b
    projected = dot(normed_b, wqkv_ref[...]).astype(BF16)
    low = lax.broadcasted_iota(jnp.int32, (64, 128), 1) < 64
    head_of = lax.broadcasted_iota(jnp.int32, (64, CHAN), 1) // 64
    masks = [(head_of == h).astype(F32).astype(BF16) for h in range(4)]
    for g in range(4):
        part = slice(g * 64, g * 64 + 64)
        query = projected[part, :CHAN] * 0.125
        key = projected[part, CHAN : 2 * CHAN]
        value = projected[part, 2 * CHAN :]
        da = da_ref[g]
        query_h = jnp.concatenate([query * m for m in masks], axis=0)
        da_h = jnp.concatenate([da * m for m in masks], axis=0)
        scores = dot_nt(key, query_h) + bias_ref[...]
        scores = jnp.exp(scores - jnp.max(scores, axis=0, keepdims=True))
        probs = scores * (1.0 / jnp.sum(scores, axis=0, keepdims=True))
        probs_b = probs.astype(BF16)
        d_probs = dot_nt(value, da_h)
        d_scores = probs * (d_probs - jnp.sum(probs * d_probs, axis=0, keepdims=True))
        bias_sum_ref[...] += d_scores
        d_scores_b = d_scores.astype(BF16)
        att_ref[part] = diagonal(dot_tn(probs_b, value), low).astype(BF16)
        proj_ref[part, :CHAN] = (diagonal(dot_tn(d_scores_b, key), low) * 0.125).astype(BF16)
        proj_ref[part, CHAN : 2 * CHAN] = dot(d_scores_b, query_h).astype(BF16)
        proj_ref[part, 2 * CHAN :] = dot(probs_b, da_h).astype(BF16)
    d_normed = dot_nt(proj_ref[...], wqkv_ref[...])
    d_tokens = layer_norm_back(normed, inv_std, d_normed).astype(BF16)
    ds_ref[groups] = d_tokens.reshape(4, 64, CHAN)

    @pl.when(step == n_groups // 4 - 1)
    def _():
        for s in range(0, 64, 16):
            for g in range(0, n_groups, 16):
                tile = ds_ref[g : g + 16, s : s + 16].reshape(256, CHAN)
                moved = dot(swap_ref[...], tile).astype(BF16)
                out_ref[s : s + 16, g : g + 16] = moved.reshape(16, 16, CHAN)


def attention(tokens, d_att, wqkv, bias):
    n_groups = tokens.shape[1]
    shape = (64, n_groups, CHAN)
    flat = n_groups * 64
    return pl.pallas_call(
        attention_body,
        grid=(n_groups // 4,),
        in_specs=[
            whole(shape), band((4, 64, CHAN)), whole((CHAN, 3 * CHAN)), whole((64, CHAN)),
            whole((256, 256)),
        ],
        out_specs=[
            whole(shape), band((256, CHAN)), band((256, CHAN)), band((256, 3 * CHAN)), whole((64, CHAN)),
        ],
        out_shape=[
            jax.ShapeDtypeStruct(shape, BF16),
            jax.ShapeDtypeStruct((flat, CHAN), BF16),
            jax.ShapeDtypeStruct((flat, CHAN), BF16),
            jax.ShapeDtypeStruct((flat, 3 * CHAN), BF16),
            jax.ShapeDtypeStruct((64, CHAN), F32),
        ],
        scratch_shapes=[pltpu.VMEM((n_groups, 64, CHAN), BF16)] * 2,
        compiler_params=params(58),
        cost_estimate=pl.CostEstimate(
            flops=flat * 4 * CHAN * CHAN * 5, bytes_accessed=8 * MIB, transcendentals=flat * 256
        ),
        name="attention",
    )(tokens, d_att, wqkv, bias, jnp.asarray(SWAP, BF16))


def attention_sums_body(att_ref, cot_ref, norm_ref, proj_ref, out_ref, qkv_acc, out_acc):
    step = pl.program_id(0)

    @pl.when(step == 0)
    def _():
        qkv_acc[...] = jnp.zeros_like(qkv_acc)
        out_acc[...] = jnp.zeros_like(out_acc)

    out_acc[...] += dot_tn(att_ref[...], cot_ref[...])
    qkv_acc[...] += dot_tn(norm_ref[...], proj_ref[...])

    @pl.when(step == pl.num_programs(0) - 1)
    def _():
        to_tiles(qkv_acc, out_ref, 0)
        to_tiles(out_acc, out_ref, 96)


def attention_sums(att, cot, normed, proj):
    flat = att.shape[0]
    return pl.pallas_call(
        attention_sums_body,
        grid=(flat // 512,),
        in_specs=[band((512, CHAN)), band((512, CHAN)), band((512, CHAN)), band((512, 3 * CHAN))],
        out_specs=whole(TILED),
        out_shape=jax.ShapeDtypeStruct(TILED, BF16),
        scratch_shapes=[pltpu.VMEM((CHAN, 3 * CHAN), F32), pltpu.VMEM((CHAN, CHAN), F32)],
        compiler_params=params(58),
        cost_estimate=pl.CostEstimate(
            flops=flat * 8 * CHAN * CHAN, bytes_accessed=6 * MIB, transcendentals=0
        ),
        name="attention_sums",
    )(att, cot, normed, proj)


def section_grad(cot_ref, db_ref):
    pieces = db_ref[...].reshape(2, 4, 2, 16, CHAN)
    branch = jnp.concatenate(
        [pieces[pair, quad, r] for pair in range(2) for r in range(2) for quad in range(4)], axis=0
    )
    return cot_ref[...].reshape(TOK, CHAN).astype(F32) + branch.astype(F32)


def project_body(cot_ref, db_ref, slope_ref, wp_ref, dm_ref):
    d_section_b = section_grad(cot_ref, db_ref).astype(BF16)
    for at in range(0, EXP, 256):
        grads = dot_nt(d_section_b, wp_ref[at : at + 256, :])
        slope = slope_ref[:, :, at : at + 256].reshape(TOK, 256).astype(F32)
        dm_ref[:, :, at : at + 256] = (grads * slope).astype(BF16).reshape(BLK, COLS, 256)


def project_back(cot, db, slope, wp):
    return pl.pallas_call(
        project_body,
        grid=(STEPS,),
        in_specs=[
            band((BLK, COLS, CHAN)), band((8, 32, CHAN)), band((BLK, COLS, EXP)), whole((EXP, CHAN)),
        ],
        out_specs=band((BLK, COLS, EXP)),
        out_shape=jax.ShapeDtypeStruct((ROWS, COLS, EXP), BF16),
        compiler_params=params(58),
        cost_estimate=pl.CostEstimate(
            flops=2 * ROWS * COLS * CHAN * EXP, bytes_accessed=10 * MIB, transcendentals=0
        ),
        name="project_back",
    )(cot, db, slope, wp)


def project_sum_body(cot_ref, db_ref, mixed_ref, tiles_ref, sum_ref, turned_ref):
    @pl.when(pl.program_id(0) == 0)
    def _():
        sum_ref[...] = jnp.zeros_like(sum_ref)

    d_section_b = section_grad(cot_ref, db_ref).astype(BF16)
    sum_ref[...] += dot_tn(d_section_b, mixed_ref[...].reshape(TOK, EXP))

    @pl.when(pl.program_id(0) == STEPS - 1)
    def _():
        turned_ref[...] = sum_ref[...].T
        to_tiles(turned_ref, tiles_ref, 0)


def project_sum(cot, db, mixed):
    return pl.pallas_call(
        project_sum_body,
        grid=(STEPS,),
        in_specs=[band((BLK, COLS, CHAN)), band((8, 32, CHAN)), band((BLK, COLS, EXP))],
        out_specs=whole(TILED),
        out_shape=jax.ShapeDtypeStruct(TILED, BF16),
        scratch_shapes=[pltpu.VMEM((CHAN, EXP), F32), pltpu.VMEM((EXP, CHAN), F32)],
        compiler_params=params(58),
        cost_estimate=pl.CostEstimate(
            flops=2 * ROWS * COLS * CHAN * EXP, bytes_accessed=8 * MIB, transcendentals=0
        ),
        name="project_sum",
    )(cot, db, mixed)


def expand_back_body(
    cur_ref, before_ref, after_ref, halo_ref, halo_slope_ref, wp_ref, hid_ref, slope_ref, x_ref, dkb_ref,
    extra_ref,
    dpre_ref, tiles_ref, top_ref, bottom_ref, left_ref, right_ref, acc_ref, sum_ref, depth_ref, shift_ref,
):
    step = pl.program_id(0)

    @pl.when(step == 0)
    def _():
        sum_ref[...] = jnp.zeros_like(sum_ref)
        acc_ref[...] = jnp.zeros_like(acc_ref)
        for at in range(0, EXP, 256):
            span = slice(at, at + 256)
            grads = dot_nt(halo_ref[...], wp_ref[at : at + 256, :])
            grads = (grads * halo_slope_ref[:, span]).astype(BF16).astype(F32)
            top_ref[:, span] = grads[:COLS]
            bottom_ref[:, span] = grads[COLS : 2 * COLS]
            for ref, base in ((left_ref, 2 * COLS), (right_ref, 2 * COLS + EDGE)):
                for s in range(STEPS):
                    ref[s, : BLK + 2, span] = grads[base + BLK * s : base + BLK * s + BLK + 2]

    first, last = step == 0, step == STEPS - 1
    for at in range(0, EXP, LANES):
        span = slice(at, at + LANES)
        rows = [jnp.where(first, top_ref[:, span], before_ref[0, :, span].astype(F32))]
        rows += [cur_ref[r, :, span].astype(F32) for r in range(BLK)]
        rows += [jnp.where(last, bottom_ref[:, span], after_ref[0, :, span].astype(F32))]
        for r in range(BLK + 2):
            left = left_ref[step, r : r + 1, span]
            right = right_ref[step, r : r + 1, span]
            shift_ref[0, r, :, span] = jnp.concatenate([rows[r][1:], right], axis=0).astype(BF16)
            shift_ref[1, r, :, span] = rows[r].astype(BF16)
            shift_ref[2, r, :, span] = jnp.concatenate([left, rows[r][:-1]], axis=0).astype(BF16)
        kern = [dkb_ref[n, :, span] for n in range(9)]
        sums = [acc_ref[n, :, span] for n in range(9)]
        held = None
        for j in range(0, COLS, 16):
            cells = slice(j, j + 16)
            pieces = [[shift_ref[b, r, cells, span] for b in range(3)] for r in range(BLK + 2)]
            hid = [hid_ref[r, cells, span] for r in range(BLK)]
            totals = [None] * BLK
            parts = []
            for a in range(3):
                for b in range(3):
                    n = 3 * a + b
                    terms = []
                    for r in range(BLK):
                        piece = pieces[r + 2 - a][b]
                        tap = kern[n] * piece
                        totals[r] = tap if n == 0 else totals[r] + tap
                        terms.append(hid[r] * piece)
                    parts.append((terms[0] + terms[1]) + (terms[2] + terms[3]))
            if held is None:
                held = parts
            else:
                for n in range(9):
                    part = (held[n] + parts[n]).astype(F32)
                    sums[n] = sums[n] + (part[:8] + part[8:])
                held = None
            for r in range(BLK):
                dpre_ref[r * COLS + j : r * COLS + j + 16, span] = totals[r] * slope_ref[r, cells, span]
        for n in range(9):
            acc_ref[n, :, span] = sums[n]
    normed, _ = layer_norm(x_ref[...].reshape(TOK, CHAN).astype(F32))
    sum_ref[...] += dot_tn(normed.astype(BF16), dpre_ref[...])

    @pl.when(last)
    def _():
        depth_ref[...] = jnp.sum(acc_ref[...], axis=1)
        to_tiles(sum_ref, tiles_ref, 0)
        first_row = lax.broadcasted_iota(jnp.int32, (8, 128), 0) == 0
        for n in range(128):
            extra = extra_ref[n]
            if n < 72:
                row = depth_ref[n // 8 : n // 8 + 1, 128 * (n % 8) : 128 * (n % 8) + 128]
                extra = jnp.where(first_row, row, extra)
            tiles_ref[n, 16:] = extra.astype(BF16)


def expand_back(d_mixed, halo, halo_slope, wp, hidden, slope, x, dkb, extra):
    tiles = (128, 24, 128)
    cells = band((BLK, COLS, EXP))
    return pl.pallas_call(
        expand_back_body,
        grid=(STEPS,),
        in_specs=[
            cells, ROW_BEFORE, ROW_AFTER, whole((HALO, CHAN)), whole((HALO, EXP)),
            whole((EXP, CHAN)), cells, cells, band((BLK, COLS, CHAN)), whole((9, 16, EXP)),
            whole((128, 8, 128)),
        ],
        out_specs=[band((TOK, EXP)), whole(tiles)],
        out_shape=[
            jax.ShapeDtypeStruct((ROWS * COLS, EXP), BF16),
            jax.ShapeDtypeStruct(tiles, BF16),
        ],
        scratch_shapes=[pltpu.VMEM((COLS, EXP), F32)] * 2
        + [pltpu.VMEM((STEPS, 8, EXP), F32)] * 2
        + [pltpu.VMEM((9, 8, EXP), F32), pltpu.VMEM((CHAN, EXP), F32), pltpu.VMEM((9, EXP), F32)]
        + [pltpu.VMEM((3, BLK + 2, COLS, EXP), BF16)],
        compiler_params=params(58),
        cost_estimate=pl.CostEstimate(
            flops=2 * ROWS * COLS * CHAN * EXP, bytes_accessed=20 * MIB, transcendentals=0
        ),
        name="expand_back",
    )(d_mixed, d_mixed, d_mixed, halo, halo_slope, wp, hidden, slope, x, dkb, extra)


def finish_body(dpre_ref, x_ref, cot_ref, db_ref, we_ref, grad_ref):
    normed, inv_std = layer_norm(x_ref[...].reshape(TOK, CHAN).astype(F32))
    d_input = layer_norm_back(normed, inv_std, dot_nt(dpre_ref[...], we_ref[...]))
    grad_ref[...] = (section_grad(cot_ref, db_ref) + d_input).astype(BF16).reshape(BLK, COLS, CHAN)


def finish(d_pre, x, cot, db, we):
    return pl.pallas_call(
        finish_body,
        grid=(STEPS,),
        in_specs=[
            band((TOK, EXP)), band((BLK, COLS, CHAN)), band((BLK, COLS, CHAN)), band((8, 32, CHAN)),
            whole((CHAN, EXP)),
        ],
        out_specs=band((BLK, COLS, CHAN)),
        out_shape=jax.ShapeDtypeStruct((ROWS, COLS, CHAN), BF16),
        compiler_params=params(58),
        cost_estimate=pl.CostEstimate(
            flops=2 * ROWS * COLS * CHAN * EXP, bytes_accessed=9 * MIB, transcendentals=0
        ),
        name="finish",
    )(d_pre, x, cot, db, we)


def join_body(core_ref, *refs):
    half = pl.ds(core_ref[0] * 64, 64)
    out_ref = refs[-1]
    at = 0
    for own_ref, other_ref in zip(refs[0:-1:2], refs[1:-1:2]):
        total = own_ref[half].astype(F32) + other_ref[half].astype(F32)
        out_ref[:, at : at + own_ref.shape[1]] = total.astype(BF16)
        at += own_ref.shape[1]


def join(core, *tiles):
    vmem = pl.BlockSpec(memory_space=pltpu.VMEM)
    return pl.pallas_call(
        join_body,
        in_specs=[pl.BlockSpec(memory_space=pltpu.SMEM)] + [vmem] * len(tiles),
        out_shape=jax.ShapeDtypeStruct(JOINED, BF16),
        compiler_params=params(24),
        cost_estimate=pl.CostEstimate(flops=MIB, bytes_accessed=4 * MIB, transcendentals=0),
        name="join",
    )(core, *tiles)


def fold_body(terms_ref, out_ref):
    factor = float(128 * ROWS * COLS) ** (-0.5)
    total = jnp.sum(terms_ref[...].astype(F32), axis=0) * factor
    out_ref[...] = jnp.broadcast_to(total.astype(BF16)[None], out_ref.shape)


def fold(terms):
    return pl.pallas_call(
        fold_body,
        out_shape=jax.ShapeDtypeStruct(terms.shape, BF16),
        compiler_params=params(24),
        cost_estimate=pl.CostEstimate(flops=terms.size, bytes_accessed=4 * terms.size, transcendentals=0),
        name="fold",
    )(terms)


def unfold_body(core_ref, own_ref, other_ref, expand_ref, depth_ref, project_ref, qkv_ref, out_ref, bias_ref):
    first = core_ref[0] == 0

    def tile(n, rows):
        own, other = own_ref[n % 64, rows].astype(F32), other_ref[n % 64, rows].astype(F32)
        return jnp.where(first, own, other) if n < 64 else jnp.where(first, other, own)

    parts = ((qkv_ref, 0, 0), (out_ref, 96, 0), (project_ref, 0, 16), (expand_ref, 0, 32))
    for ref, at, low in parts:
        wide = ref.shape[1] // 128
        for r in range(ref.shape[0] // 16):
            for c in range(wide):
                piece = tile(at + wide * r + c, slice(low, low + 16))
                ref[16 * r : 16 * r + 16, 128 * c : 128 * c + 128] = piece
    for n in range(72):
        extra = tile(n, slice(48, 56))
        at = 128 * (n % 8)
        depth_ref[n // 24, n // 8 % 3 : n // 8 % 3 + 1, at : at + 128] = extra[:1]
        if n < 60:
            bias_ref[n % 15, n // 15 : n // 15 + 1, :] = extra[1:2, :15]


def unfold(core, own, other):
    vmem = pl.BlockSpec(memory_space=pltpu.VMEM)
    return pl.pallas_call(
        unfold_body,
        in_specs=[pl.BlockSpec(memory_space=pltpu.SMEM), vmem, vmem],
        out_shape=[
            jax.ShapeDtypeStruct((CHAN, EXP), F32),
            jax.ShapeDtypeStruct((3, 3, EXP), F32),
            jax.ShapeDtypeStruct((EXP, CHAN), F32),
            jax.ShapeDtypeStruct((CHAN, 3 * CHAN), F32),
            jax.ShapeDtypeStruct((CHAN, CHAN), F32),
            jax.ShapeDtypeStruct((15, 4, 15), F32),
        ],
        compiler_params=params(24),
        cost_estimate=pl.CostEstimate(flops=0, bytes_accessed=5 * MIB, transcendentals=0),
        name="unfold",
    )(core, own, other)


FIRST_CELL = np.zeros((32, 512), np.float32)
LAST_CELL = np.zeros((32, 512), np.float32)
for _row in range(32):
    FIRST_CELL[_row, _row * 16] = 1.0
    LAST_CELL[_row, _row * 16 + 15] = 1.0


def edges_body(
    dt_ref, ct_ref, db_ref, cb_ref, dl_ref, cl_ref, dr_ref, cr_ref, first_ref, last_ref,
    top_ref, bottom_ref, left_ref, right_ref,
):
    def total(d_ref, c_ref):
        return (d_ref[...].astype(F32) + c_ref[...].astype(F32)).astype(BF16)

    top = total(dt_ref, ct_ref)
    bottom = total(db_ref, cb_ref)
    for quad in range(4):
        top_ref[16 * quad : 16 * quad + 16] = top[0, quad, :16]
        bottom_ref[16 * quad : 16 * quad + 16] = bottom[0, quad, 16:]
    left_ref[...] = dot(first_ref[...], total(dl_ref, cl_ref).reshape(512, CHAN)).astype(BF16)
    right_ref[...] = dot(last_ref[...], total(dr_ref, cr_ref).reshape(512, CHAN)).astype(BF16)


def edges(d_branch, cot):
    d_branch, cot = d_branch.reshape(16, 4, 32, CHAN), cot.reshape(16, 4, 32, CHAN)
    specs = []
    for row in (0, 15):
        specs += [pl.BlockSpec((1, 4, 32, CHAN), lambda i, row=row: (row, 0, 0, 0))] * 2
    for col in (0, 3):
        specs += [pl.BlockSpec((16, 1, 32, CHAN), lambda i, col=col: (0, col, 0, 0))] * 2
    return pl.pallas_call(
        edges_body,
        grid=(1,),
        in_specs=specs + [whole((32, 512))] * 2,
        out_specs=[whole((COLS, CHAN))] * 2 + [whole((ROWS, CHAN))] * 2,
        out_shape=[jax.ShapeDtypeStruct((COLS, CHAN), BF16)] * 2
        + [jax.ShapeDtypeStruct((ROWS, CHAN), BF16)] * 2,
        compiler_params=params(24),
        cost_estimate=pl.CostEstimate(flops=MIB, bytes_accessed=2 * MIB, transcendentals=0),
        name="edges",
    )(*([d_branch, cot] * 4), jnp.asarray(FIRST_CELL, BF16), jnp.asarray(LAST_CELL, BF16))


def shifts():
    n_lat, n_lon = lax.axis_size("lat"), lax.axis_size("lon")
    south = [(i, i + 1) for i in range(n_lat - 1)]
    north = [(i + 1, i) for i in range(n_lat - 1)]
    east = [(i, (i + 1) % n_lon) for i in range(n_lon)]
    west = [((i + 1) % n_lon, i) for i in range(n_lon)]
    return (south, north, east, west)


def rows_of(top, bottom):
    south, north, _, _ = shifts()
    return (lax.ppermute(bottom, "lat", south), lax.ppermute(top, "lat", north))


def halo_of(above, below, left, right):
    _, _, east, west = shifts()
    pad = jnp.zeros((EDGE - ROWS - 2, left.shape[1]), left.dtype)
    from_west = lax.ppermute(
        jnp.concatenate([above[-1:], right, below[-1:], pad], axis=0), "lon", east
    )
    from_east = lax.ppermute(
        jnp.concatenate([above[:1], left, below[:1], pad], axis=0), "lon", west
    )
    return jnp.concatenate([above, below, from_west, from_east], axis=0)


def wide_rows(field):
    flat = (2 * COLS, CHAN)
    above, below = rows_of(field[:2].reshape(flat), field[-2:].reshape(flat))
    return (above.reshape(2, COLS, CHAN), below.reshape(2, COLS, CHAN))


def wide_columns(field, above, below):
    _, _, east, west = shifts()
    pad = jnp.zeros((2, EDGE - ROWS - 4, field.shape[2]), field.dtype)

    def columns(at):
        parts = [part[:, at : at + 2].transpose(1, 0, 2) for part in (above, field, below)]
        return jnp.concatenate(parts + [pad], axis=1)

    own_west, own_east = columns(0), columns(COLS - 2)
    from_west = lax.ppermute(own_east, "lon", east)
    from_east = lax.ppermute(own_west, "lon", west)
    return (from_west, from_east, own_west, own_east)


def exchange(pieces):
    n_lat, n_lon = lax.axis_size("lat"), lax.axis_size("lon")
    order = np.arange(n_lat * n_lon).reshape(n_lat, n_lon // 2, 2)
    members = order.transpose(2, 0, 1).reshape(2, -1).tolist()
    return lax.all_to_all(
        pieces, ("lat", "lon"), split_axis=0, concat_axis=0, axis_index_groups=members, tiled=True
    )


def to_pieces(field):
    shaped = field.reshape(16, 2, 4, 16, CHAN).transpose(0, 2, 1, 3, 4)
    return shaped.reshape(64, 32, CHAN)


def pairs():
    return np.arange(lax.axis_size("lon")).reshape(-1, 2).tolist()


def other_core(tiles):
    swaps = [move for a, b in pairs() for move in ((a, b), (b, a))]
    return lax.ppermute(tiles, "lon", swaps)


def rel_table():
    position = np.arange(64)
    pos_row, pos_col = position // 8, position % 8
    rel_index = (pos_row[:, None] - pos_row[None, :] + 7) * 15 + (
        pos_col[:, None] - pos_col[None, :] + 7
    )
    return jnp.asarray(rel_index)[:, :, None] == jnp.arange(225)[None, None, :]


def on_device(
    field_in, cotangent, expand_weight, depth_kernel, project_weight, qkv_weight, out_weight, rel_bias
):
    onehot = rel_table().astype(F32)
    bias = jnp.einsum(
        "tsr,hr->sht", onehot, rel_bias.reshape(4, 225), precision=lax.Precision.HIGHEST
    ).reshape(64, 256)
    dk = depth_kernel.reshape(9, EXP)

    dkb = jnp.broadcast_to(dk[:, None], (9, 16, EXP)).astype(BF16)
    core = lax.axis_index("lon").astype(jnp.int32).reshape(1) & 1
    barrier = lax.optimization_barrier

    above, below = wide_rows(field_in)
    hidden, act_slope = expand(field_in, expand_weight)
    above, below, hidden, late_cot = barrier((above, below, hidden, cotangent))
    field_halo = (above, below, *wide_columns(field_in, above, below))
    hidden, cot_pieces = barrier((hidden, to_pieces(late_cot)))
    cot_groups = exchange(cot_pieces)
    section, mixed, mixed_slope, ring_slope = mix(
        hidden, field_halo, expand_weight, dk, dkb, project_weight, field_in
    )
    groups = exchange(section)
    cot_swapped, d_att = prepare(cot_groups, out_weight, 32)
    groups, bias, d_att = barrier((groups, bias, d_att))
    d_groups, attended, normed2, d_proj, bias_acc = attention(groups, d_att, qkv_weight, bias)

    d_branch = exchange(d_groups)
    attention_tiles = attention_sums(attended, cot_swapped.reshape(-1, CHAN), normed2, d_proj)
    bias_sum = jnp.einsum(
        "sht,tsr->hr", bias_acc.reshape(64, 4, 64), onehot, precision=lax.Precision.HIGHEST
    )
    extra = jnp.pad(bias_sum.reshape(60, 1, 15), ((0, 68), (1, 6), (0, 113)))
    d_branch, attention_tiles, extra = barrier((d_branch, attention_tiles, extra))

    top, bottom, left, right = edges(d_branch, cot_pieces)
    above, below = rows_of(top, bottom)
    d_mixed = project_back(cotangent, d_branch, mixed_slope, project_weight)
    above, below, d_mixed, attention_tiles = barrier((above, below, d_mixed, attention_tiles))
    d_halo = halo_of(above, below, left, right)
    project_tiles = project_sum(cotangent, d_branch, mixed)
    d_halo, project_tiles, d_mixed = barrier((d_halo, project_tiles, d_mixed))
    attention_pair = (attention_tiles, other_core(attention_tiles))
    project_pair = (project_tiles, other_core(project_tiles))
    d_pre, expand_tiles = expand_back(
        d_mixed, d_halo, ring_slope, project_weight, hidden, act_slope, field_in, dkb, extra
    )

    joined = join(core, *attention_pair, *project_pair, expand_tiles, other_core(expand_tiles))
    joined, d_pre = barrier((joined, d_pre))
    terms = exchange(joined)
    grad_in = finish(d_pre, field_in, cotangent, d_branch, expand_weight)
    terms, grad_in = barrier((terms, grad_in))
    sums = exchange(fold(terms))
    *grads, bias_grad = unfold(core, sums, other_core(sums))
    return (grad_in, *grads, bias_grad.transpose(1, 0, 2))


def solution(mesh):
    placed = (P("lat", "lon", None), P("lat", "lon", None), P(), P(), P(), P(), P(), P())
    return jax.shard_map(
        on_device,
        mesh=mesh,
        in_specs=placed,
        out_specs=(P("lat", "lon", None), P(), P(), P(), P(), P(), P()),
        check_vma=False,
    )
```

```python
import math

import jax
import jax.numpy as jnp
import numpy as np
from jax import lax
from jax.experimental import pallas as pl
from jax.experimental.pallas import tpu as pltpu
from jax.sharding import PartitionSpec as P

EPSILON = 1e-05
GELU_C = math.sqrt(2.0 / math.pi)
F32 = jnp.float32
BF16 = jnp.bfloat16
MIB = 1 << 20

ROWS, COLS, CHAN, EXP = 32, 64, 256, 1024
BLK = 4
STEPS = ROWS // BLK
TOK = BLK * COLS
LANES = 128
EDGE = 40
HALO = 2 * COLS + 2 * EDGE
LONG = 72
JOINED = (64, 56, 128)


def layer_norm(values):
    average = jnp.mean(values, axis=-1, keepdims=True)
    centred = values - average
    variance = jnp.mean(centred * centred, axis=-1, keepdims=True)
    inv_std = lax.rsqrt(variance + EPSILON)
    return (centred * inv_std, inv_std)


def layer_norm_back(normed, inv_std, grads):
    mean_grad = jnp.mean(grads, axis=-1, keepdims=True)
    mean_cross = jnp.mean(grads * normed, axis=-1, keepdims=True)
    return (grads - mean_grad - normed * mean_cross) * inv_std


def gelu_slope(values):
    squared = values * values
    tanh_val = jnp.tanh(values * (GELU_C + (GELU_C * 0.044715) * squared))
    gate = 0.5 + 0.5 * tanh_val
    result = values * gate
    slopes = gate + result * (1.0 - gate) * (2.0 * GELU_C + (6.0 * GELU_C * 0.044715) * squared)
    return (result, slopes)


def dot(left, right):
    return lax.dot_general(left, right, (((1,), (0,)), ((), ())), preferred_element_type=F32)


def dot_nt(left, right):
    return lax.dot_general(left, right, (((1,), (1,)), ((), ())), preferred_element_type=F32)


def dot_tn(left, right):
    return lax.dot_general(left, right, (((0,), (0,)), ((), ())), preferred_element_type=F32)


def params(mib):
    return pltpu.CompilerParams(vmem_limit_bytes=mib * MIB)


def whole(shape):
    return pl.BlockSpec(shape, lambda i: (0,) * len(shape))


def band(shape):
    return pl.BlockSpec(shape, lambda i: (i,) + (0,) * (len(shape) - 1))


ROW_BEFORE = pl.BlockSpec(
    (1, COLS, EXP), lambda i: (jnp.maximum(BLK * i - 1, 0), 0, 0)
)
ROW_AFTER = pl.BlockSpec(
    (1, COLS, EXP), lambda i: (jnp.minimum(BLK * i + BLK, ROWS - 1), 0, 0)
)


TILED = (128, 16, 128)


def to_tiles(ref, out_ref, at):
    wide = ref.shape[1] // 128
    for r in range(ref.shape[0] // 16):
        for c in range(wide):
            tile = ref[16 * r : 16 * r + 16, 128 * c : 128 * c + 128]
            out_ref[at + wide * r + c, :16] = tile.astype(BF16)


def expand_body(x_ref, we_ref, hid_ref, slope_ref):
    normed, _ = layer_norm(x_ref[...].reshape(TOK, CHAN).astype(F32))
    normed_b = normed.astype(BF16)
    for at in range(0, EXP, 256):
        val, slope = gelu_slope(dot(normed_b, we_ref[:, at : at + 256]))
        hid_ref[:, :, at : at + 256] = val.astype(BF16).reshape(BLK, COLS, 256)
        slope_ref[:, :, at : at + 256] = slope.astype(BF16).reshape(BLK, COLS, 256)


def expand(x, we):
    wide = jax.ShapeDtypeStruct((ROWS, COLS, EXP), BF16)
    return pl.pallas_call(
        expand_body,
        grid=(STEPS,),
        in_specs=[band((BLK, COLS, CHAN)), whole((CHAN, EXP))],
        out_specs=[band((BLK, COLS, EXP))] * 2,
        out_shape=[wide, wide],
        compiler_params=params(58),
        cost_estimate=pl.CostEstimate(
            flops=2 * ROWS * COLS * CHAN * EXP, bytes_accessed=10 * MIB, transcendentals=ROWS * COLS * EXP
        ),
        name="expand",
    )(x, we)


def mix_body(
    cur_ref, before_ref, after_ref,
    above_ref, below_ref, first_ref, last_ref, west_ref, east_ref, own_west_ref, own_east_ref,
    we_ref, dk_ref, wp_ref, x_ref,
    section_ref, mixed_ref, slope_ref, ring_slope_ref,
    top_ref, bottom_ref, left_ref, right_ref,
):
    step = pl.program_id(0)

    @pl.when(step == 0)
    def _():
        ring_body(
            above_ref, below_ref, first_ref, last_ref, west_ref, east_ref, own_west_ref, own_east_ref,
            we_ref, dk_ref,
            top_ref, bottom_ref, left_ref, right_ref, ring_slope_ref,
        )

    first, last = step == 0, step == STEPS - 1
    for at in range(0, EXP, LANES):
        span = slice(at, at + LANES)
        rows = [jnp.where(first, top_ref[:, span], before_ref[0, :, span])]
        rows += [cur_ref[r, :, span] for r in range(BLK)]
        rows += [jnp.where(last, bottom_ref[:, span], after_ref[0, :, span])]
        rows = [row.astype(F32) for row in rows]
        kern = [dk_ref[n, span][None] for n in range(9)]
        for r in range(BLK):
            parts = [
                kern[b] * rows[r] + kern[3 + b] * rows[r + 1] + kern[6 + b] * rows[r + 2]
                for b in range(3)
            ]
            left = left_ref[step, r : r + 1, span]
            right = right_ref[step, r : r + 1, span]
            pre = (
                parts[1]
                + jnp.concatenate([left, parts[0][:-1]], axis=0)
                + jnp.concatenate([parts[2][1:], right], axis=0)
            )
            val, slope = gelu_slope(pre)
            mixed_ref[r, :, span] = val.astype(BF16)
            slope_ref[r, :, span] = slope.astype(BF16)
    branch = dot(mixed_ref[...].reshape(TOK, EXP), wp_ref[...])
    section = (x_ref[...].reshape(TOK, CHAN).astype(F32) + branch).astype(BF16)
    section = section.reshape(2, 2, 4, 16, CHAN)
    for pair in range(2):
        for quad in range(4):
            section_ref[4 * pair + quad] = section[pair, :, quad].reshape(32, CHAN)


def ring_body(
    above_ref, below_ref, first_ref, last_ref, west_ref, east_ref, own_west_ref, own_east_ref,
    we_ref, dk_ref,
    top_ref, bottom_ref, left_ref, right_ref, slope_ref,
):
    west, east = west_ref[...].astype(F32), east_ref[...].astype(F32)
    pad = jnp.zeros((LONG - COLS - 4, CHAN), F32)

    def along(row, at):
        return [
            west[0, at : at + 1], west[1, at : at + 1], row.astype(F32),
            east[0, at : at + 1], east[1, at : at + 1], pad,
        ]

    strips = along(above_ref[0], 0) + along(above_ref[1], 1) + along(first_ref[0], 2)
    strips += along(last_ref[0], 33) + along(below_ref[0], 34) + along(below_ref[1], 35)
    strips += [west[0], west[1], own_west_ref[0].astype(F32)]
    strips += [own_east_ref[1].astype(F32), east[0], east[1]]
    normed, _ = layer_norm(jnp.concatenate(strips, axis=0))
    normed_b = normed.astype(BF16)
    south, lefts, rights = 3 * LONG, 6 * LONG, 6 * LONG + 3 * EDGE
    for at in range(0, EXP, 256):
        span = slice(at, at + 256)
        val, _ = gelu_slope(dot(normed_b, we_ref[:, span]))
        val = val.astype(BF16).astype(F32)
        kern = [dk_ref[n, span][None] for n in range(9)]
        top_ref[:, span] = val[LONG + 2 : LONG + 2 + COLS].astype(BF16)
        bottom_ref[:, span] = val[south + LONG + 2 : south + LONG + 2 + COLS].astype(BF16)
        for ref, base, col in ((left_ref, lefts, 0), (right_ref, rights, 2)):
            total = 0.0
            for a in range(3):
                start = base + EDGE + a + 1
                total = total + kern[3 * a + col] * val[start : start + ROWS]
            for s in range(STEPS):
                ref[s, :BLK, span] = total[BLK * s : BLK * s + BLK]
        for base, out in ((0, 0), (south, COLS)):
            total = 0.0
            for a in range(3):
                for b in range(3):
                    start = base + LONG * a + b + 1
                    total = total + kern[3 * a + b] * val[start : start + COLS]
            slope_ref[out : out + COLS, span] = gelu_slope(total)[1]
        for base, out in ((lefts, 2 * COLS), (rights, 2 * COLS + EDGE)):
            total = 0.0
            for a in range(3):
                for b in range(3):
                    start = base + EDGE * b + a
                    total = total + kern[3 * a + b] * val[start : start + ROWS + 2]
            slope_ref[out : out + ROWS + 2, span] = gelu_slope(total)[1]
            slope_ref[out + ROWS + 2 : out + EDGE, span] = jnp.zeros((EDGE - ROWS - 2, 256), F32)


def mix(hidden, halo, we, dk, wp, x):
    above, below, west, east, own_west, own_east = halo
    wide = jax.ShapeDtypeStruct((ROWS, COLS, EXP), BF16)
    return pl.pallas_call(
        mix_body,
        grid=(STEPS,),
        in_specs=[
            band((BLK, COLS, EXP)), ROW_BEFORE, ROW_AFTER,
            whole((2, COLS, CHAN)), whole((2, COLS, CHAN)),
            pl.BlockSpec((1, COLS, CHAN), lambda i: (0, 0, 0)),
            pl.BlockSpec((1, COLS, CHAN), lambda i: (ROWS - 1, 0, 0)),
            whole((2, EDGE, CHAN)), whole((2, EDGE, CHAN)), whole((2, EDGE, CHAN)), whole((2, EDGE, CHAN)),
            whole((CHAN, EXP)), whole((9, EXP)), whole((EXP, CHAN)), band((BLK, COLS, CHAN)),
        ],
        out_specs=[
            band((8, 32, CHAN)), band((BLK, COLS, EXP)), band((BLK, COLS, EXP)), whole((HALO, EXP)),
        ],
        out_shape=[
            jax.ShapeDtypeStruct((64, 32, CHAN), BF16), wide, wide, jax.ShapeDtypeStruct((HALO, EXP), F32),
        ],
        scratch_shapes=[pltpu.VMEM((COLS, EXP), BF16)] * 2 + [pltpu.VMEM((STEPS, 8, EXP), F32)] * 2,
        compiler_params=params(58),
        cost_estimate=pl.CostEstimate(
            flops=3 * ROWS * COLS * CHAN * EXP, bytes_accessed=18 * MIB, transcendentals=2 * ROWS * COLS * EXP
        ),
        name="mix",
    )(
        hidden, hidden, hidden, above, below, x, x, west, east, own_west, own_east,
        we, dk, wp, x,
    )


SWAP = np.zeros((256, 256), np.float32)
for _s in range(16):
    for _g in range(16):
        SWAP[_g * 16 + _s, _s * 16 + _g] = 1.0


def diagonal(full, low):
    halves = []
    for half in range(2):
        lanes = slice(half * 128, half * 128 + 128)
        at = half * 128
        halves.append(jnp.where(low, full[at : at + 64, lanes], full[at + 64 : at + 128, lanes]))
    return jnp.concatenate(halves, axis=1)


def swap(src, dst, swap_ref, n_groups):
    for s in range(0, 64, 16):
        for g in range(0, n_groups, 16):
            moved = dot(swap_ref[...], src[s : s + 16, g : g + 16].reshape(256, CHAN)).astype(BF16)
            dst[g : g + 16, s : s + 16] = moved.reshape(16, 16, CHAN)


def prepare_body(cot_ref, wout_ref, swap_ref, cs_ref, da_ref):
    n_groups = cot_ref.shape[1]
    swap(cot_ref, cs_ref, swap_ref, n_groups)
    for g in range(0, n_groups, 4):
        grads = dot_nt(cs_ref[g : g + 4].reshape(256, CHAN), wout_ref[...])
        da_ref[g : g + 4] = grads.astype(BF16).reshape(4, 64, CHAN)


def prepare(cot, wout, n_groups):
    shape = (64, n_groups, CHAN)
    grouped = (n_groups, 64, CHAN)
    return pl.pallas_call(
        prepare_body,
        grid=(1,),
        in_specs=[whole(shape), whole((CHAN, CHAN)), whole((256, 256))],
        out_specs=[whole(grouped), whole(grouped)],
        out_shape=[jax.ShapeDtypeStruct(grouped, BF16)] * 2,
        compiler_params=params(24),
        cost_estimate=pl.CostEstimate(
            flops=n_groups * 64 * 4 * CHAN * CHAN, bytes_accessed=3 * MIB, transcendentals=0
        ),
        name="prepare",
    )(cot, wout, jnp.asarray(SWAP, BF16))


def attention_body(
    x_ref, da_ref, wqkv_ref, bias_ref, swap_ref,
    out_ref, att_ref, norm_ref, proj_ref, bias_sum_ref, xs_ref, ds_ref,
):
    step = pl.program_id(0)
    n_groups = x_ref.shape[1]

    @pl.when(step == 0)
    def _():
        bias_sum_ref[...] = jnp.zeros_like(bias_sum_ref)
        swap(x_ref, xs_ref, swap_ref, n_groups)

    groups = pl.ds(step * 4, 4)
    tokens = xs_ref[groups].reshape(256, CHAN)
    normed, inv_std = layer_norm(tokens.astype(F32))
    normed_b = normed.astype(BF16)
    norm_ref[...] = normed_b
    projected = dot(normed_b, wqkv_ref[...]).astype(BF16)
    low = lax.broadcasted_iota(jnp.int32, (64, 128), 1) < 64
    keep = [low.astype(F32).astype(BF16), (1.0 - low.astype(F32)).astype(BF16)]
    none = jnp.zeros((128, 128), BF16)

    def by_head(rows):
        blocks = []
        for half in range(2):
            lanes = rows[:, half * 128 : half * 128 + 128]
            pair = jnp.concatenate([lanes * keep[0], lanes * keep[1]], axis=0)
            blocks.append(jnp.concatenate([pair, none] if half == 0 else [none, pair], axis=1))
        return jnp.concatenate(blocks, axis=0)

    four = range(4)
    part = [slice(g * 64, g * 64 + 64) for g in four]
    query = (projected[:, :CHAN].astype(F32) * 0.125).astype(BF16)
    key = [projected[part[g], CHAN : 2 * CHAN] for g in four]
    value = [projected[part[g], 2 * CHAN :] for g in four]
    query_h = [by_head(query[part[g]]) for g in four]
    da_h = [by_head(da_ref[g]) for g in four]
    scores = [dot_nt(key[g], query_h[g]) + bias_ref[...] for g in four]
    d_probs = [dot_nt(value[g], da_h[g]) for g in four]
    tops = [jnp.max(scores[g], axis=0, keepdims=True) for g in four]
    scores = [jnp.exp(scores[g] - tops[g]) for g in four]
    scales = [1.0 / jnp.sum(scores[g], axis=0, keepdims=True) for g in four]
    probs = [scores[g] * scales[g] for g in four]
    probs_b = [probs[g].astype(BF16) for g in four]
    crosses = [jnp.sum(probs[g] * d_probs[g], axis=0, keepdims=True) for g in four]
    d_scores = [probs[g] * (d_probs[g] - crosses[g]) for g in four]
    bias_sum_ref[...] += (d_scores[0] + d_scores[1]) + (d_scores[2] + d_scores[3])
    d_scores_b = [d_scores[g].astype(BF16) for g in four]
    attended = [dot_tn(probs_b[g], value[g]) for g in four]
    d_query = [dot_tn(d_scores_b[g], key[g]) for g in four]
    d_key = [dot(d_scores_b[g], query_h[g]) for g in four]
    d_value = [dot(probs_b[g], da_h[g]) for g in four]
    for g in four:
        att_ref[part[g]] = diagonal(attended[g], low).astype(BF16)
        proj_ref[part[g], :CHAN] = (diagonal(d_query[g], low) * 0.125).astype(BF16)
        proj_ref[part[g], CHAN : 2 * CHAN] = d_key[g].astype(BF16)
        proj_ref[part[g], 2 * CHAN :] = d_value[g].astype(BF16)
    d_normed = dot_nt(proj_ref[...], wqkv_ref[...])
    d_tokens = layer_norm_back(normed, inv_std, d_normed).astype(BF16)
    ds_ref[groups] = d_tokens.reshape(4, 64, CHAN)

    @pl.when(step == n_groups // 4 - 1)
    def _():
        for s in range(0, 64, 16):
            for g in range(0, n_groups, 16):
                tile = ds_ref[g : g + 16, s : s + 16].reshape(256, CHAN)
                moved = dot(swap_ref[...], tile).astype(BF16)
                out_ref[s : s + 16, g : g + 16] = moved.reshape(16, 16, CHAN)


def attention(tokens, d_att, wqkv, bias):
    n_groups = tokens.shape[1]
    shape = (64, n_groups, CHAN)
    flat = n_groups * 64
    return pl.pallas_call(
        attention_body,
        grid=(n_groups // 4,),
        in_specs=[
            whole(shape), band((4, 64, CHAN)), whole((CHAN, 3 * CHAN)), whole((64, CHAN)),
            whole((256, 256)),
        ],
        out_specs=[
            whole(shape), band((256, CHAN)), band((256, CHAN)), band((256, 3 * CHAN)), whole((64, CHAN)),
        ],
        out_shape=[
            jax.ShapeDtypeStruct(shape, BF16),
            jax.ShapeDtypeStruct((flat, CHAN), BF16),
            jax.ShapeDtypeStruct((flat, CHAN), BF16),
            jax.ShapeDtypeStruct((flat, 3 * CHAN), BF16),
            jax.ShapeDtypeStruct((64, CHAN), F32),
        ],
        scratch_shapes=[pltpu.VMEM((n_groups, 64, CHAN), BF16)] * 2,
        compiler_params=params(58),
        cost_estimate=pl.CostEstimate(
            flops=flat * 4 * CHAN * CHAN * 5, bytes_accessed=8 * MIB, transcendentals=flat * 256
        ),
        name="attention",
    )(tokens, d_att, wqkv, bias, jnp.asarray(SWAP, BF16))


def attention_sums_body(att_ref, cot_ref, norm_ref, proj_ref, out_ref, qkv_acc, out_acc):
    step = pl.program_id(0)

    @pl.when(step == 0)
    def _():
        qkv_acc[...] = jnp.zeros_like(qkv_acc)
        out_acc[...] = jnp.zeros_like(out_acc)

    out_acc[...] += dot_tn(att_ref[...], cot_ref[...])
    qkv_acc[...] += dot_tn(norm_ref[...], proj_ref[...])

    @pl.when(step == pl.num_programs(0) - 1)
    def _():
        to_tiles(qkv_acc, out_ref, 0)
        to_tiles(out_acc, out_ref, 96)


def attention_sums(att, cot, normed, proj):
    flat = att.shape[0]
    return pl.pallas_call(
        attention_sums_body,
        grid=(flat // 512,),
        in_specs=[band((512, CHAN)), band((512, CHAN)), band((512, CHAN)), band((512, 3 * CHAN))],
        out_specs=whole(TILED),
        out_shape=jax.ShapeDtypeStruct(TILED, BF16),
        scratch_shapes=[pltpu.VMEM((CHAN, 3 * CHAN), F32), pltpu.VMEM((CHAN, CHAN), F32)],
        compiler_params=params(58),
        cost_estimate=pl.CostEstimate(
            flops=flat * 8 * CHAN * CHAN, bytes_accessed=6 * MIB, transcendentals=0
        ),
        name="attention_sums",
    )(att, cot, normed, proj)


def section_grad(cot_ref, db_ref):
    pieces = db_ref[...].reshape(2, 4, 2, 16, CHAN)
    branch = jnp.concatenate(
        [pieces[pair, quad, r] for pair in range(2) for r in range(2) for quad in range(4)], axis=0
    )
    return cot_ref[...].reshape(TOK, CHAN).astype(F32) + branch.astype(F32)


def project_body(cot_ref, db_ref, slope_ref, wp_ref, dm_ref):
    d_section_b = section_grad(cot_ref, db_ref).astype(BF16)
    for at in range(0, EXP, 256):
        grads = dot_nt(d_section_b, wp_ref[at : at + 256, :])
        slope = slope_ref[:, :, at : at + 256].reshape(TOK, 256).astype(F32)
        dm_ref[:, :, at : at + 256] = (grads * slope).astype(BF16).reshape(BLK, COLS, 256)


def project_back(cot, db, slope, wp):
    return pl.pallas_call(
        project_body,
        grid=(STEPS,),
        in_specs=[
            band((BLK, COLS, CHAN)), band((8, 32, CHAN)), band((BLK, COLS, EXP)), whole((EXP, CHAN)),
        ],
        out_specs=band((BLK, COLS, EXP)),
        out_shape=jax.ShapeDtypeStruct((ROWS, COLS, EXP), BF16),
        compiler_params=params(58),
        cost_estimate=pl.CostEstimate(
            flops=2 * ROWS * COLS * CHAN * EXP, bytes_accessed=10 * MIB, transcendentals=0
        ),
        name="project_back",
    )(cot, db, slope, wp)


def project_sum_body(cot_ref, db_ref, mixed_ref, tiles_ref, sum_ref, turned_ref):
    @pl.when(pl.program_id(0) == 0)
    def _():
        sum_ref[...] = jnp.zeros_like(sum_ref)

    d_section_b = section_grad(cot_ref, db_ref).astype(BF16)
    sum_ref[...] += dot_tn(d_section_b, mixed_ref[...].reshape(TOK, EXP))

    @pl.when(pl.program_id(0) == STEPS - 1)
    def _():
        turned_ref[...] = sum_ref[...].T
        to_tiles(turned_ref, tiles_ref, 0)


def project_sum(cot, db, mixed):
    return pl.pallas_call(
        project_sum_body,
        grid=(STEPS,),
        in_specs=[band((BLK, COLS, CHAN)), band((8, 32, CHAN)), band((BLK, COLS, EXP))],
        out_specs=whole(TILED),
        out_shape=jax.ShapeDtypeStruct(TILED, BF16),
        scratch_shapes=[pltpu.VMEM((CHAN, EXP), F32), pltpu.VMEM((EXP, CHAN), F32)],
        compiler_params=params(58),
        cost_estimate=pl.CostEstimate(
            flops=2 * ROWS * COLS * CHAN * EXP, bytes_accessed=8 * MIB, transcendentals=0
        ),
        name="project_sum",
    )(cot, db, mixed)


def expand_back_body(
    cur_ref, before_ref, after_ref, halo_ref, halo_slope_ref, wp_ref, hid_ref, slope_ref, x_ref, dkb_ref,
    extra_ref,
    dpre_ref, tiles_ref, top_ref, bottom_ref, left_ref, right_ref, acc_ref, sum_ref, depth_ref, shift_ref,
):
    step = pl.program_id(0)

    @pl.when(step == 0)
    def _():
        sum_ref[...] = jnp.zeros_like(sum_ref)
        acc_ref[...] = jnp.zeros_like(acc_ref)
        for at in range(0, EXP, 256):
            span = slice(at, at + 256)
            grads = dot_nt(halo_ref[...], wp_ref[at : at + 256, :])
            grads = (grads * halo_slope_ref[:, span]).astype(BF16).astype(F32)
            top_ref[:, span] = grads[:COLS]
            bottom_ref[:, span] = grads[COLS : 2 * COLS]
            for ref, base in ((left_ref, 2 * COLS), (right_ref, 2 * COLS + EDGE)):
                for s in range(STEPS):
                    ref[s, : BLK + 2, span] = grads[base + BLK * s : base + BLK * s + BLK + 2]

    first, last = step == 0, step == STEPS - 1
    for at in range(0, EXP, LANES):
        span = slice(at, at + LANES)
        rows = [jnp.where(first, top_ref[:, span], before_ref[0, :, span].astype(F32))]
        rows += [cur_ref[r, :, span].astype(F32) for r in range(BLK)]
        rows += [jnp.where(last, bottom_ref[:, span], after_ref[0, :, span].astype(F32))]
        for r in range(BLK + 2):
            left = left_ref[step, r : r + 1, span]
            right = right_ref[step, r : r + 1, span]
            shift_ref[0, r, :, span] = jnp.concatenate([rows[r][1:], right], axis=0)
            shift_ref[1, r, :, span] = rows[r]
            shift_ref[2, r, :, span] = jnp.concatenate([left, rows[r][:-1]], axis=0)
        kern = [dkb_ref[n, :, span] for n in range(9)]
        sums = [acc_ref[n, :, span] for n in range(9)]
        for j in range(0, COLS, 16):
            hid = [hid_ref[r, j : j + 16, span].astype(F32) for r in range(BLK)]
            halves = []
            for low in (0, 8):
                cells = slice(j + low, j + low + 8)
                pieces = [[shift_ref[b, r, cells, span] for b in range(3)] for r in range(BLK + 2)]
                totals = [None] * BLK
                for r in range(BLK):
                    cell = hid[r][low : low + 8]
                    for a in range(3):
                        for b in range(3):
                            n = 3 * a + b
                            piece = pieces[r + 2 - a][b]
                            tap = kern[n] * piece
                            totals[r] = tap if n == 0 else totals[r] + tap
                            sums[n] = sums[n] + cell * piece
                halves.append(totals)
            for r in range(BLK):
                total = jnp.concatenate([halves[0][r], halves[1][r]], axis=0)
                d_pre = total * slope_ref[r, j : j + 16, span].astype(F32)
                dpre_ref[r * COLS + j : r * COLS + j + 16, span] = d_pre.astype(BF16)
        for n in range(9):
            acc_ref[n, :, span] = sums[n]
    normed, _ = layer_norm(x_ref[...].reshape(TOK, CHAN).astype(F32))
    sum_ref[...] += dot_tn(normed.astype(BF16), dpre_ref[...])

    @pl.when(last)
    def _():
        depth_ref[...] = jnp.sum(acc_ref[...], axis=1)
        to_tiles(sum_ref, tiles_ref, 0)
        first_row = lax.broadcasted_iota(jnp.int32, (8, 128), 0) == 0
        for n in range(128):
            extra = extra_ref[n]
            if n < 72:
                row = depth_ref[n // 8 : n // 8 + 1, 128 * (n % 8) : 128 * (n % 8) + 128]
                extra = jnp.where(first_row, row, extra)
            tiles_ref[n, 16:] = extra.astype(BF16)


def expand_back(d_mixed, halo, halo_slope, wp, hidden, slope, x, dkb, extra):
    tiles = (128, 24, 128)
    cells = band((BLK, COLS, EXP))
    return pl.pallas_call(
        expand_back_body,
        grid=(STEPS,),
        in_specs=[
            cells, ROW_BEFORE, ROW_AFTER, whole((HALO, CHAN)), whole((HALO, EXP)),
            whole((EXP, CHAN)), cells, cells, band((BLK, COLS, CHAN)), whole((9, 8, EXP)),
            whole((128, 8, 128)),
        ],
        out_specs=[band((TOK, EXP)), whole(tiles)],
        out_shape=[
            jax.ShapeDtypeStruct((ROWS * COLS, EXP), BF16),
            jax.ShapeDtypeStruct(tiles, BF16),
        ],
        scratch_shapes=[pltpu.VMEM((COLS, EXP), F32)] * 2
        + [pltpu.VMEM((STEPS, 8, EXP), F32)] * 2
        + [pltpu.VMEM((9, 8, EXP), F32), pltpu.VMEM((CHAN, EXP), F32), pltpu.VMEM((9, EXP), F32)]
        + [pltpu.VMEM((3, BLK + 2, COLS, EXP), F32)],
        compiler_params=params(58),
        cost_estimate=pl.CostEstimate(
            flops=2 * ROWS * COLS * CHAN * EXP, bytes_accessed=20 * MIB, transcendentals=0
        ),
        name="expand_back",
    )(d_mixed, d_mixed, d_mixed, halo, halo_slope, wp, hidden, slope, x, dkb, extra)


def finish_body(dpre_ref, x_ref, cot_ref, db_ref, we_ref, grad_ref):
    normed, inv_std = layer_norm(x_ref[...].reshape(TOK, CHAN).astype(F32))
    d_input = layer_norm_back(normed, inv_std, dot_nt(dpre_ref[...], we_ref[...]))
    grad_ref[...] = (section_grad(cot_ref, db_ref) + d_input).astype(BF16).reshape(BLK, COLS, CHAN)


def finish(d_pre, x, cot, db, we):
    return pl.pallas_call(
        finish_body,
        grid=(STEPS,),
        in_specs=[
            band((TOK, EXP)), band((BLK, COLS, CHAN)), band((BLK, COLS, CHAN)), band((8, 32, CHAN)),
            whole((CHAN, EXP)),
        ],
        out_specs=band((BLK, COLS, CHAN)),
        out_shape=jax.ShapeDtypeStruct((ROWS, COLS, CHAN), BF16),
        compiler_params=params(58),
        cost_estimate=pl.CostEstimate(
            flops=2 * ROWS * COLS * CHAN * EXP, bytes_accessed=9 * MIB, transcendentals=0
        ),
        name="finish",
    )(d_pre, x, cot, db, we)


def join_body(core_ref, *refs):
    half = pl.ds(core_ref[0] * 64, 64)
    out_ref = refs[-1]
    at = 0
    for own_ref, other_ref in zip(refs[0:-1:2], refs[1:-1:2]):
        total = own_ref[half].astype(F32) + other_ref[half].astype(F32)
        out_ref[:, at : at + own_ref.shape[1]] = total.astype(BF16)
        at += own_ref.shape[1]


def join(core, *tiles):
    vmem = pl.BlockSpec(memory_space=pltpu.VMEM)
    return pl.pallas_call(
        join_body,
        in_specs=[pl.BlockSpec(memory_space=pltpu.SMEM)] + [vmem] * len(tiles),
        out_shape=jax.ShapeDtypeStruct(JOINED, BF16),
        compiler_params=params(24),
        cost_estimate=pl.CostEstimate(flops=MIB, bytes_accessed=4 * MIB, transcendentals=0),
        name="join",
    )(core, *tiles)


def fold_body(terms_ref, out_ref):
    factor = float(128 * ROWS * COLS) ** (-0.5)
    total = jnp.sum(terms_ref[...].astype(F32), axis=0) * factor
    out_ref[...] = jnp.broadcast_to(total.astype(BF16)[None], out_ref.shape)


def fold(terms):
    return pl.pallas_call(
        fold_body,
        out_shape=jax.ShapeDtypeStruct(terms.shape, BF16),
        compiler_params=params(24),
        cost_estimate=pl.CostEstimate(flops=terms.size, bytes_accessed=4 * terms.size, transcendentals=0),
        name="fold",
    )(terms)


def unfold_body(core_ref, own_ref, other_ref, expand_ref, depth_ref, project_ref, qkv_ref, out_ref, bias_ref):
    first = core_ref[0] == 0

    def tile(n, rows):
        own, other = own_ref[n % 64, rows].astype(F32), other_ref[n % 64, rows].astype(F32)
        return jnp.where(first, own, other) if n < 64 else jnp.where(first, other, own)

    parts = ((qkv_ref, 0, 0), (out_ref, 96, 0), (project_ref, 0, 16), (expand_ref, 0, 32))
    for ref, at, low in parts:
        wide = ref.shape[1] // 128
        for r in range(ref.shape[0] // 16):
            for c in range(wide):
                piece = tile(at + wide * r + c, slice(low, low + 16))
                ref[16 * r : 16 * r + 16, 128 * c : 128 * c + 128] = piece
    for n in range(72):
        extra = tile(n, slice(48, 56))
        at = 128 * (n % 8)
        depth_ref[n // 24, n // 8 % 3 : n // 8 % 3 + 1, at : at + 128] = extra[:1]
        if n < 60:
            bias_ref[n % 15, n // 15 : n // 15 + 1, :] = extra[1:2, :15]


def unfold(core, own, other):
    vmem = pl.BlockSpec(memory_space=pltpu.VMEM)
    return pl.pallas_call(
        unfold_body,
        in_specs=[pl.BlockSpec(memory_space=pltpu.SMEM), vmem, vmem],
        out_shape=[
            jax.ShapeDtypeStruct((CHAN, EXP), F32),
            jax.ShapeDtypeStruct((3, 3, EXP), F32),
            jax.ShapeDtypeStruct((EXP, CHAN), F32),
            jax.ShapeDtypeStruct((CHAN, 3 * CHAN), F32),
            jax.ShapeDtypeStruct((CHAN, CHAN), F32),
            jax.ShapeDtypeStruct((15, 4, 15), F32),
        ],
        compiler_params=params(24),
        cost_estimate=pl.CostEstimate(flops=0, bytes_accessed=5 * MIB, transcendentals=0),
        name="unfold",
    )(core, own, other)


FIRST_CELL = np.zeros((32, 512), np.float32)
LAST_CELL = np.zeros((32, 512), np.float32)
for _row in range(32):
    FIRST_CELL[_row, _row * 16] = 1.0
    LAST_CELL[_row, _row * 16 + 15] = 1.0


def edges_body(
    dt_ref, ct_ref, db_ref, cb_ref, dl_ref, cl_ref, dr_ref, cr_ref, first_ref, last_ref,
    top_ref, bottom_ref, left_ref, right_ref,
):
    def total(d_ref, c_ref):
        return (d_ref[...].astype(F32) + c_ref[...].astype(F32)).astype(BF16)

    top = total(dt_ref, ct_ref)
    bottom = total(db_ref, cb_ref)
    for quad in range(4):
        top_ref[16 * quad : 16 * quad + 16] = top[0, quad, :16]
        bottom_ref[16 * quad : 16 * quad + 16] = bottom[0, quad, 16:]
    left_ref[...] = dot(first_ref[...], total(dl_ref, cl_ref).reshape(512, CHAN)).astype(BF16)
    right_ref[...] = dot(last_ref[...], total(dr_ref, cr_ref).reshape(512, CHAN)).astype(BF16)


def edges(d_branch, cot):
    d_branch, cot = d_branch.reshape(16, 4, 32, CHAN), cot.reshape(16, 4, 32, CHAN)
    specs = []
    for row in (0, 15):
        specs += [pl.BlockSpec((1, 4, 32, CHAN), lambda i, row=row: (row, 0, 0, 0))] * 2
    for col in (0, 3):
        specs += [pl.BlockSpec((16, 1, 32, CHAN), lambda i, col=col: (0, col, 0, 0))] * 2
    return pl.pallas_call(
        edges_body,
        grid=(1,),
        in_specs=specs + [whole((32, 512))] * 2,
        out_specs=[whole((COLS, CHAN))] * 2 + [whole((ROWS, CHAN))] * 2,
        out_shape=[jax.ShapeDtypeStruct((COLS, CHAN), BF16)] * 2
        + [jax.ShapeDtypeStruct((ROWS, CHAN), BF16)] * 2,
        compiler_params=params(24),
        cost_estimate=pl.CostEstimate(flops=MIB, bytes_accessed=2 * MIB, transcendentals=0),
        name="edges",
    )(*([d_branch, cot] * 4), jnp.asarray(FIRST_CELL, BF16), jnp.asarray(LAST_CELL, BF16))


def shifts():
    n_lat, n_lon = lax.axis_size("lat"), lax.axis_size("lon")
    south = [(i, i + 1) for i in range(n_lat - 1)]
    north = [(i + 1, i) for i in range(n_lat - 1)]
    east = [(i, (i + 1) % n_lon) for i in range(n_lon)]
    west = [((i + 1) % n_lon, i) for i in range(n_lon)]
    return (south, north, east, west)


def rows_of(top, bottom):
    south, north, _, _ = shifts()
    return (lax.ppermute(bottom, "lat", south), lax.ppermute(top, "lat", north))


def halo_of(above, below, left, right):
    _, _, east, west = shifts()
    pad = jnp.zeros((EDGE - ROWS - 2, left.shape[1]), left.dtype)
    from_west = lax.ppermute(
        jnp.concatenate([above[-1:], right, below[-1:], pad], axis=0), "lon", east
    )
    from_east = lax.ppermute(
        jnp.concatenate([above[:1], left, below[:1], pad], axis=0), "lon", west
    )
    return jnp.concatenate([above, below, from_west, from_east], axis=0)


def wide_rows(field):
    flat = (2 * COLS, CHAN)
    above, below = rows_of(field[:2].reshape(flat), field[-2:].reshape(flat))
    return (above.reshape(2, COLS, CHAN), below.reshape(2, COLS, CHAN))


def wide_columns(field, above, below):
    _, _, east, west = shifts()
    pad = jnp.zeros((2, EDGE - ROWS - 4, field.shape[2]), field.dtype)

    def columns(at):
        parts = [part[:, at : at + 2].transpose(1, 0, 2) for part in (above, field, below)]
        return jnp.concatenate(parts + [pad], axis=1)

    own_west, own_east = columns(0), columns(COLS - 2)
    from_west = lax.ppermute(own_east, "lon", east)
    from_east = lax.ppermute(own_west, "lon", west)
    return (from_west, from_east, own_west, own_east)


def exchange(pieces):
    n_lat, n_lon = lax.axis_size("lat"), lax.axis_size("lon")
    order = np.arange(n_lat * n_lon).reshape(n_lat, n_lon // 2, 2)
    members = order.transpose(2, 0, 1).reshape(2, -1).tolist()
    return lax.all_to_all(
        pieces, ("lat", "lon"), split_axis=0, concat_axis=0, axis_index_groups=members, tiled=True
    )


def to_pieces(field):
    shaped = field.reshape(16, 2, 4, 16, CHAN).transpose(0, 2, 1, 3, 4)
    return shaped.reshape(64, 32, CHAN)


def pairs():
    return np.arange(lax.axis_size("lon")).reshape(-1, 2).tolist()


def other_core(tiles):
    swaps = [move for a, b in pairs() for move in ((a, b), (b, a))]
    return lax.ppermute(tiles, "lon", swaps)


def rel_table():
    position = np.arange(64)
    pos_row, pos_col = position // 8, position % 8
    rel_index = (pos_row[:, None] - pos_row[None, :] + 7) * 15 + (
        pos_col[:, None] - pos_col[None, :] + 7
    )
    return jnp.asarray(rel_index)[:, :, None] == jnp.arange(225)[None, None, :]


def on_device(
    field_in, cotangent, expand_weight, depth_kernel, project_weight, qkv_weight, out_weight, rel_bias
):
    onehot = rel_table().astype(F32)
    bias = jnp.einsum(
        "tsr,hr->sht", onehot, rel_bias.reshape(4, 225), precision=lax.Precision.HIGHEST
    ).reshape(64, 256)
    dk = depth_kernel.reshape(9, EXP)

    dkb = jnp.broadcast_to(dk[:, None], (9, 8, EXP))
    core = lax.axis_index("lon").astype(jnp.int32).reshape(1) & 1
    barrier = lax.optimization_barrier

    above, below = wide_rows(field_in)
    hidden, act_slope = expand(field_in, expand_weight)
    field_halo = (above, below, *wide_columns(field_in, above, below))
    field_halo, late_cot = barrier((field_halo, cotangent))
    hidden, cot_pieces = barrier((hidden, to_pieces(late_cot)))
    cot_groups = exchange(cot_pieces)
    section, mixed, mixed_slope, ring_slope = mix(
        hidden, field_halo, expand_weight, dk, project_weight, field_in
    )
    groups = exchange(section)
    cot_swapped, d_att = prepare(cot_groups, out_weight, 32)
    groups, bias, d_att = barrier((groups, bias, d_att))
    d_groups, attended, normed2, d_proj, bias_acc = attention(groups, d_att, qkv_weight, bias)

    d_branch = exchange(d_groups)
    attention_tiles = attention_sums(attended, cot_swapped.reshape(-1, CHAN), normed2, d_proj)
    bias_sum = jnp.einsum(
        "sht,tsr->hr", bias_acc.reshape(64, 4, 64), onehot, precision=lax.Precision.HIGHEST
    )
    extra = jnp.pad(bias_sum.reshape(60, 1, 15), ((0, 68), (1, 6), (0, 113)))
    d_branch, attention_tiles, extra = barrier((d_branch, attention_tiles, extra))

    top, bottom, left, right = edges(d_branch, cot_pieces)
    above, below = rows_of(top, bottom)
    d_mixed = project_back(cotangent, d_branch, mixed_slope, project_weight)
    above, below, d_mixed, attention_tiles = barrier((above, below, d_mixed, attention_tiles))
    d_halo = halo_of(above, below, left, right)
    project_tiles = project_sum(cotangent, d_branch, mixed)
    d_halo, project_tiles, d_mixed = barrier((d_halo, project_tiles, d_mixed))
    attention_pair = (attention_tiles, other_core(attention_tiles))
    project_pair = (project_tiles, other_core(project_tiles))
    d_pre, expand_tiles = expand_back(
        d_mixed, d_halo, ring_slope, project_weight, hidden, act_slope, field_in, dkb, extra
    )

    joined = join(core, *attention_pair, *project_pair, expand_tiles, other_core(expand_tiles))
    joined, d_pre = barrier((joined, d_pre))
    terms = exchange(joined)
    grad_in = finish(d_pre, field_in, cotangent, d_branch, expand_weight)
    terms, grad_in = barrier((terms, grad_in))
    sums = exchange(fold(terms))
    *grads, bias_grad = unfold(core, sums, other_core(sums))
    return (grad_in, *grads, bias_grad.transpose(1, 0, 2))


def solution(mesh):
    placed = (P("lat", "lon", None), P("lat", "lon", None), P(), P(), P(), P(), P(), P())
    return jax.shard_map(
        on_device,
        mesh=mesh,
        in_specs=placed,
        out_specs=(P("lat", "lon", None), P(), P(), P(), P(), P(), P()),
        check_vma=False,
    )
```

```python
import functools
import math

import jax
import jax.numpy as jnp
import numpy as np
from jax import lax
from jax.experimental import pallas as pl
from jax.experimental.pallas import tpu as pltpu
from jax.sharding import PartitionSpec as P

EPSILON = 1e-05
GELU_C = math.sqrt(2.0 / math.pi)
F32 = jnp.float32
BF16 = jnp.bfloat16
MIB = 1 << 20

ROWS, COLS, CHAN, EXP = 32, 64, 256, 1024
BLK = 8
STEPS = ROWS // BLK
TOK = BLK * COLS
LANES = 128
EDGE = 40
HALO = 2 * COLS + 2 * EDGE
LONG = 72
JOINED = (64, 56, 128)


def layer_norm(values):
    average = jnp.mean(values, axis=-1, keepdims=True)
    centred = values - average
    variance = jnp.mean(centred * centred, axis=-1, keepdims=True)
    inv_std = lax.rsqrt(variance + EPSILON)
    return (centred * inv_std, inv_std)


def layer_norm_back(normed, inv_std, grads):
    mean_grad = jnp.mean(grads, axis=-1, keepdims=True)
    mean_cross = jnp.mean(grads * normed, axis=-1, keepdims=True)
    return (grads - mean_grad - normed * mean_cross) * inv_std


def gelu(values):
    return values * (0.5 + 0.5 * jnp.tanh(values * (GELU_C + (GELU_C * 0.044715) * (values * values))))


def gelu_slope(values):
    squared = values * values
    tanh_val = jnp.tanh(values * (GELU_C + (GELU_C * 0.044715) * squared))
    gate = 0.5 + 0.5 * tanh_val
    result = values * gate
    slopes = gate + result * (1.0 - gate) * (2.0 * GELU_C + (6.0 * GELU_C * 0.044715) * squared)
    return (result, slopes)


def dot(left, right):
    return lax.dot_general(left, right, (((1,), (0,)), ((), ())), preferred_element_type=F32)


def dot_nt(left, right):
    return lax.dot_general(left, right, (((1,), (1,)), ((), ())), preferred_element_type=F32)


def dot_tn(left, right):
    return lax.dot_general(left, right, (((0,), (0,)), ((), ())), preferred_element_type=F32)


def params(mib):
    return pltpu.CompilerParams(vmem_limit_bytes=mib * MIB)


def whole(shape):
    return pl.BlockSpec(shape, lambda i: (0,) * len(shape))


def band(shape):
    return pl.BlockSpec(shape, lambda i: (i,) + (0,) * (len(shape) - 1))


ROW_BEFORE = pl.BlockSpec(
    (1, COLS, EXP), lambda i: (jnp.maximum(BLK * i - 1, 0), 0, 0)
)
ROW_AFTER = pl.BlockSpec(
    (1, COLS, EXP), lambda i: (jnp.minimum(BLK * i + BLK, ROWS - 1), 0, 0)
)


TILED = (128, 16, 128)


def to_tiles(ref, out_ref, at):
    wide = ref.shape[1] // 128
    for r in range(ref.shape[0] // 16):
        for c in range(wide):
            tile = ref[16 * r : 16 * r + 16, 128 * c : 128 * c + 128]
            out_ref[at + wide * r + c, :16] = tile.astype(BF16)


def expand_body(x_ref, we_ref, out_ref, slopes):
    normed, _ = layer_norm(x_ref[...].reshape(TOK, CHAN).astype(F32))
    normed_b = normed.astype(BF16)
    for at in range(0, EXP, 256):
        pre = dot(normed_b, we_ref[:, at : at + 256])
        result = gelu_slope(pre)[1] if slopes else gelu(pre)
        out_ref[:, :, at : at + 256] = result.astype(BF16).reshape(BLK, COLS, 256)


def expand(x, we, slopes):
    return pl.pallas_call(
        functools.partial(expand_body, slopes=slopes),
        grid=(STEPS,),
        in_specs=[band((BLK, COLS, CHAN)), whole((CHAN, EXP))],
        out_specs=band((BLK, COLS, EXP)),
        out_shape=jax.ShapeDtypeStruct((ROWS, COLS, EXP), BF16),
        compiler_params=params(58),
        cost_estimate=pl.CostEstimate(
            flops=2 * ROWS * COLS * CHAN * EXP, bytes_accessed=6 * MIB, transcendentals=ROWS * COLS * EXP
        ),
        name="expand_slopes" if slopes else "expand",
    )(x, we)


def mixed_slopes_body(pre_ref, slope_ref):
    for at in range(0, EXP, 256):
        span = slice(at, at + 256)
        slope_ref[:, :, span] = gelu_slope(pre_ref[:, :, span].astype(F32))[1].astype(BF16)


def mixed_slopes(pre):
    return pl.pallas_call(
        mixed_slopes_body,
        grid=(STEPS,),
        in_specs=[band((BLK, COLS, EXP))],
        out_specs=band((BLK, COLS, EXP)),
        out_shape=jax.ShapeDtypeStruct((ROWS, COLS, EXP), BF16),
        compiler_params=params(58),
        cost_estimate=pl.CostEstimate(
            flops=20 * ROWS * COLS * EXP, bytes_accessed=8 * MIB, transcendentals=ROWS * COLS * EXP
        ),
        name="mixed_slopes",
    )(pre)


def mix_body(
    cur_ref, before_ref, after_ref,
    above_ref, below_ref, first_ref, last_ref, west_ref, east_ref, own_west_ref, own_east_ref,
    we_ref, dk_ref, wp_ref, x_ref,
    section_ref, mixed_ref, pre_ref, ring_slope_ref,
    top_ref, bottom_ref, left_ref, right_ref,
):
    step = pl.program_id(0)

    @pl.when(step == 0)
    def _():
        ring_body(
            above_ref, below_ref, first_ref, last_ref, west_ref, east_ref, own_west_ref, own_east_ref,
            we_ref, dk_ref,
            top_ref, bottom_ref, left_ref, right_ref, ring_slope_ref,
        )

    first, last = step == 0, step == STEPS - 1
    branch = None
    for at in range(0, EXP, LANES):
        span = slice(at, at + LANES)
        rows = [jnp.where(first, top_ref[:, span], before_ref[0, :, span])]
        rows += [cur_ref[r, :, span] for r in range(BLK)]
        rows += [jnp.where(last, bottom_ref[:, span], after_ref[0, :, span])]
        rows = [row.astype(F32) for row in rows]
        kern = [dk_ref[n, span][None] for n in range(9)]
        for r in range(BLK):
            parts = [
                kern[b] * rows[r] + kern[3 + b] * rows[r + 1] + kern[6 + b] * rows[r + 2]
                for b in range(3)
            ]
            left = left_ref[step, r : r + 1, span]
            right = right_ref[step, r : r + 1, span]
            pre = (
                parts[1]
                + jnp.concatenate([left, parts[0][:-1]], axis=0)
                + jnp.concatenate([parts[2][1:], right], axis=0)
            )
            mixed_ref[r, :, span] = gelu(pre).astype(BF16)
            pre_ref[r, :, span] = pre.astype(BF16)
        if at % 256:
            pair = slice(at - LANES, at + LANES)
            part = dot(mixed_ref[:, :, pair].reshape(TOK, 256), wp_ref[pair, :])
            branch = part if branch is None else branch + part
    section = (x_ref[...].reshape(TOK, CHAN).astype(F32) + branch).astype(BF16)
    section = section.reshape(BLK // 2, 2, 4, 16, CHAN)
    for pair in range(BLK // 2):
        for quad in range(4):
            section_ref[4 * pair + quad] = section[pair, :, quad].reshape(32, CHAN)


def ring_body(
    above_ref, below_ref, first_ref, last_ref, west_ref, east_ref, own_west_ref, own_east_ref,
    we_ref, dk_ref,
    top_ref, bottom_ref, left_ref, right_ref, slope_ref,
):
    west, east = west_ref[...].astype(F32), east_ref[...].astype(F32)
    pad = jnp.zeros((LONG - COLS - 4, CHAN), F32)

    def along(row, at):
        return [
            west[0, at : at + 1], west[1, at : at + 1], row.astype(F32),
            east[0, at : at + 1], east[1, at : at + 1], pad,
        ]

    strips = along(above_ref[0], 0) + along(above_ref[1], 1) + along(first_ref[0], 2)
    strips += along(last_ref[0], 33) + along(below_ref[0], 34) + along(below_ref[1], 35)
    strips += [west[0], west[1], own_west_ref[0].astype(F32)]
    strips += [own_east_ref[1].astype(F32), east[0], east[1]]
    normed, _ = layer_norm(jnp.concatenate(strips, axis=0))
    normed_b = normed.astype(BF16)
    south, lefts, rights = 3 * LONG, 6 * LONG, 6 * LONG + 3 * EDGE
    for at in range(0, EXP, 256):
        span = slice(at, at + 256)
        val = gelu(dot(normed_b, we_ref[:, span])).astype(BF16).astype(F32)
        kern = [dk_ref[n, span][None] for n in range(9)]
        top_ref[:, span] = val[LONG + 2 : LONG + 2 + COLS].astype(BF16)
        bottom_ref[:, span] = val[south + LONG + 2 : south + LONG + 2 + COLS].astype(BF16)
        for ref, base, col in ((left_ref, lefts, 0), (right_ref, rights, 2)):
            total = 0.0
            for a in range(3):
                start = base + EDGE + a + 1
                total = total + kern[3 * a + col] * val[start : start + ROWS]
            for s in range(STEPS):
                ref[s, :BLK, span] = total[BLK * s : BLK * s + BLK]
        for base, out in ((0, 0), (south, COLS)):
            total = 0.0
            for a in range(3):
                for b in range(3):
                    start = base + LONG * a + b + 1
                    total = total + kern[3 * a + b] * val[start : start + COLS]
            slope_ref[out : out + COLS, span] = gelu_slope(total)[1]
        for base, out in ((lefts, 2 * COLS), (rights, 2 * COLS + EDGE)):
            total = 0.0
            for a in range(3):
                for b in range(3):
                    start = base + EDGE * b + a
                    total = total + kern[3 * a + b] * val[start : start + ROWS + 2]
            slope_ref[out : out + ROWS + 2, span] = gelu_slope(total)[1]
            slope_ref[out + ROWS + 2 : out + EDGE, span] = jnp.zeros((EDGE - ROWS - 2, 256), F32)


def mix(hidden, halo, we, dk, wp, x):
    above, below, west, east, own_west, own_east = halo
    wide = jax.ShapeDtypeStruct((ROWS, COLS, EXP), BF16)
    return pl.pallas_call(
        mix_body,
        grid=(STEPS,),
        in_specs=[
            band((BLK, COLS, EXP)), ROW_BEFORE, ROW_AFTER,
            whole((2, COLS, CHAN)), whole((2, COLS, CHAN)),
            pl.BlockSpec((1, COLS, CHAN), lambda i: (0, 0, 0)),
            pl.BlockSpec((1, COLS, CHAN), lambda i: (ROWS - 1, 0, 0)),
            whole((2, EDGE, CHAN)), whole((2, EDGE, CHAN)), whole((2, EDGE, CHAN)), whole((2, EDGE, CHAN)),
            whole((CHAN, EXP)), whole((9, EXP)), whole((EXP, CHAN)), band((BLK, COLS, CHAN)),
        ],
        out_specs=[
            band((2 * BLK, 32, CHAN)), band((BLK, COLS, EXP)), band((BLK, COLS, EXP)), whole((HALO, EXP)),
        ],
        out_shape=[
            jax.ShapeDtypeStruct((64, 32, CHAN), BF16), wide, wide, jax.ShapeDtypeStruct((HALO, EXP), F32),
        ],
        scratch_shapes=[pltpu.VMEM((COLS, EXP), BF16)] * 2 + [pltpu.VMEM((STEPS, 16, EXP), F32)] * 2,
        compiler_params=params(58),
        cost_estimate=pl.CostEstimate(
            flops=3 * ROWS * COLS * CHAN * EXP, bytes_accessed=18 * MIB, transcendentals=2 * ROWS * COLS * EXP
        ),
        name="mix",
    )(
        hidden, hidden, hidden, above, below, x, x, west, east, own_west, own_east,
        we, dk, wp, x,
    )


SWAP = np.zeros((256, 256), np.float32)
for _s in range(16):
    for _g in range(16):
        SWAP[_g * 16 + _s, _s * 16 + _g] = 1.0


def diagonal(full, low):
    halves = []
    for half in range(2):
        lanes = slice(half * 128, half * 128 + 128)
        at = half * 128
        halves.append(jnp.where(low, full[at : at + 64, lanes], full[at + 64 : at + 128, lanes]))
    return jnp.concatenate(halves, axis=1)


def swap(src, dst, swap_ref, n_groups):
    for s in range(0, 64, 16):
        for g in range(0, n_groups, 16):
            moved = dot(swap_ref[...], src[s : s + 16, g : g + 16].reshape(256, CHAN)).astype(BF16)
            dst[g : g + 16, s : s + 16] = moved.reshape(16, 16, CHAN)


def prepare_body(cot_ref, wout_ref, swap_ref, cs_ref, da_ref):
    n_groups = cot_ref.shape[1]
    swap(cot_ref, cs_ref, swap_ref, n_groups)
    for g in range(0, n_groups, 4):
        grads = dot_nt(cs_ref[g : g + 4].reshape(256, CHAN), wout_ref[...])
        da_ref[g : g + 4] = grads.astype(BF16).reshape(4, 64, CHAN)


def prepare(cot, wout, n_groups):
    shape = (64, n_groups, CHAN)
    grouped = (n_groups, 64, CHAN)
    return pl.pallas_call(
        prepare_body,
        grid=(1,),
        in_specs=[whole(shape), whole((CHAN, CHAN)), whole((256, 256))],
        out_specs=[whole(grouped), whole(grouped)],
        out_shape=[jax.ShapeDtypeStruct(grouped, BF16)] * 2,
        compiler_params=params(24),
        cost_estimate=pl.CostEstimate(
            flops=n_groups * 64 * 4 * CHAN * CHAN, bytes_accessed=3 * MIB, transcendentals=0
        ),
        name="prepare",
    )(cot, wout, jnp.asarray(SWAP, BF16))


def attention_body(
    x_ref, da_ref, wqkv_ref, bias_ref, swap_ref,
    out_ref, att_ref, norm_ref, proj_ref, bias_sum_ref, xs_ref, ds_ref,
):
    step = pl.program_id(0)
    n_groups = x_ref.shape[1]

    @pl.when(step == 0)
    def _():
        bias_sum_ref[...] = jnp.zeros_like(bias_sum_ref)
        swap(x_ref, xs_ref, swap_ref, n_groups)

    groups = pl.ds(step * 4, 4)
    tokens = xs_ref[groups].reshape(256, CHAN)
    normed, inv_std = layer_norm(tokens.astype(F32))
    normed_b = normed.astype(BF16)
    norm_ref[...] = normed_b
    projected = dot(normed_b, wqkv_ref[...]).astype(BF16)
    low = lax.broadcasted_iota(jnp.int32, (64, 128), 1) < 64
    keep = [low.astype(F32).astype(BF16), (1.0 - low.astype(F32)).astype(BF16)]
    none = jnp.zeros((128, 128), BF16)

    def by_head(rows):
        blocks = []
        for half in range(2):
            lanes = rows[:, half * 128 : half * 128 + 128]
            pair = jnp.concatenate([lanes * keep[0], lanes * keep[1]], axis=0)
            blocks.append(jnp.concatenate([pair, none] if half == 0 else [none, pair], axis=1))
        return jnp.concatenate(blocks, axis=0)

    four = range(4)
    part = [slice(g * 64, g * 64 + 64) for g in four]
    query = (projected[:, :CHAN].astype(F32) * 0.125).astype(BF16)
    key = [projected[part[g], CHAN : 2 * CHAN] for g in four]
    value = [projected[part[g], 2 * CHAN :] for g in four]
    query_h = [by_head(query[part[g]]) for g in four]
    da_h = [by_head(da_ref[g]) for g in four]
    scores = [dot_nt(key[g], query_h[g]) + bias_ref[...] for g in four]
    d_probs = [dot_nt(value[g], da_h[g]) for g in four]
    tops = [jnp.max(scores[g], axis=0, keepdims=True) for g in four]
    scores = [jnp.exp(scores[g] - tops[g]) for g in four]
    scales = [1.0 / jnp.sum(scores[g], axis=0, keepdims=True) for g in four]
    probs = [scores[g] * scales[g] for g in four]
    probs_b = [probs[g].astype(BF16) for g in four]
    crosses = [jnp.sum(probs[g] * d_probs[g], axis=0, keepdims=True) for g in four]
    d_scores = [probs[g] * (d_probs[g] - crosses[g]) for g in four]
    bias_sum_ref[...] += (d_scores[0] + d_scores[1]) + (d_scores[2] + d_scores[3])
    d_scores_b = [d_scores[g].astype(BF16) for g in four]
    attended = [dot_tn(probs_b[g], value[g]) for g in four]
    d_query = [dot_tn(d_scores_b[g], key[g]) for g in four]
    d_key = [dot(d_scores_b[g], query_h[g]) for g in four]
    d_value = [dot(probs_b[g], da_h[g]) for g in four]
    for g in four:
        att_ref[part[g]] = diagonal(attended[g], low).astype(BF16)
        proj_ref[part[g], :CHAN] = (diagonal(d_query[g], low) * 0.125).astype(BF16)
        proj_ref[part[g], CHAN : 2 * CHAN] = d_key[g].astype(BF16)
        proj_ref[part[g], 2 * CHAN :] = d_value[g].astype(BF16)
    d_normed = dot_nt(proj_ref[...], wqkv_ref[...])
    d_tokens = layer_norm_back(normed, inv_std, d_normed).astype(BF16)
    ds_ref[groups] = d_tokens.reshape(4, 64, CHAN)

    @pl.when(step == n_groups // 4 - 1)
    def _():
        for s in range(0, 64, 16):
            for g in range(0, n_groups, 16):
                tile = ds_ref[g : g + 16, s : s + 16].reshape(256, CHAN)
                moved = dot(swap_ref[...], tile).astype(BF16)
                out_ref[s : s + 16, g : g + 16] = moved.reshape(16, 16, CHAN)


def attention(tokens, d_att, wqkv, bias):
    n_groups = tokens.shape[1]
    shape = (64, n_groups, CHAN)
    flat = n_groups * 64
    return pl.pallas_call(
        attention_body,
        grid=(n_groups // 4,),
        in_specs=[
            whole(shape), band((4, 64, CHAN)), whole((CHAN, 3 * CHAN)), whole((64, CHAN)),
            whole((256, 256)),
        ],
        out_specs=[
            whole(shape), band((256, CHAN)), band((256, CHAN)), band((256, 3 * CHAN)), whole((64, CHAN)),
        ],
        out_shape=[
            jax.ShapeDtypeStruct(shape, BF16),
            jax.ShapeDtypeStruct((flat, CHAN), BF16),
            jax.ShapeDtypeStruct((flat, CHAN), BF16),
            jax.ShapeDtypeStruct((flat, 3 * CHAN), BF16),
            jax.ShapeDtypeStruct((64, CHAN), F32),
        ],
        scratch_shapes=[pltpu.VMEM((n_groups, 64, CHAN), BF16)] * 2,
        compiler_params=params(26),
        cost_estimate=pl.CostEstimate(
            flops=flat * 4 * CHAN * CHAN * 5, bytes_accessed=8 * MIB, transcendentals=flat * 256
        ),
        name="attention",
    )(tokens, d_att, wqkv, bias, jnp.asarray(SWAP, BF16))


def attention_sums_body(att_ref, cot_ref, norm_ref, proj_ref, out_ref, qkv_acc, out_acc):
    step = pl.program_id(0)

    @pl.when(step == 0)
    def _():
        qkv_acc[...] = jnp.zeros_like(qkv_acc)
        out_acc[...] = jnp.zeros_like(out_acc)

    out_acc[...] += dot_tn(att_ref[...], cot_ref[...])
    qkv_acc[...] += dot_tn(norm_ref[...], proj_ref[...])

    @pl.when(step == pl.num_programs(0) - 1)
    def _():
        to_tiles(qkv_acc, out_ref, 0)
        to_tiles(out_acc, out_ref, 96)


def attention_sums(att, cot, normed, proj):
    flat = att.shape[0]
    return pl.pallas_call(
        attention_sums_body,
        grid=(flat // 512,),
        in_specs=[band((512, CHAN)), band((512, CHAN)), band((512, CHAN)), band((512, 3 * CHAN))],
        out_specs=whole(TILED),
        out_shape=jax.ShapeDtypeStruct(TILED, BF16),
        scratch_shapes=[pltpu.VMEM((CHAN, 3 * CHAN), F32), pltpu.VMEM((CHAN, CHAN), F32)],
        compiler_params=params(26),
        cost_estimate=pl.CostEstimate(
            flops=flat * 8 * CHAN * CHAN, bytes_accessed=6 * MIB, transcendentals=0
        ),
        name="attention_sums",
    )(att, cot, normed, proj)


def section_grad(cot_ref, db_ref):
    n_pairs = cot_ref.shape[0] // 2
    pieces = db_ref[...].reshape(n_pairs, 4, 2, 16, CHAN)
    branch = jnp.concatenate(
        [pieces[pair, quad, r] for pair in range(n_pairs) for r in range(2) for quad in range(4)], axis=0
    )
    return cot_ref[...].reshape(-1, CHAN).astype(F32) + branch.astype(F32)


def project_body(cot_ref, db_ref, slope_ref, wp_ref, dm_ref):
    d_section_b = section_grad(cot_ref, db_ref).astype(BF16)
    for at in range(0, EXP, 256):
        grads = dot_nt(d_section_b, wp_ref[at : at + 256, :])
        slope = slope_ref[:, :, at : at + 256].reshape(-1, 256).astype(F32)
        dm_ref[:, :, at : at + 256] = (grads * slope).astype(BF16).reshape(BLK, COLS, 256)


def project_back(cot, db, slope, wp):
    return pl.pallas_call(
        project_body,
        grid=(STEPS,),
        in_specs=[
            band((BLK, COLS, CHAN)), band((2 * BLK, 32, CHAN)), band((BLK, COLS, EXP)), whole((EXP, CHAN)),
        ],
        out_specs=band((BLK, COLS, EXP)),
        out_shape=jax.ShapeDtypeStruct((ROWS, COLS, EXP), BF16),
        compiler_params=params(58),
        cost_estimate=pl.CostEstimate(
            flops=2 * ROWS * COLS * CHAN * EXP, bytes_accessed=10 * MIB, transcendentals=0
        ),
        name="project_back",
    )(cot, db, slope, wp)


def project_sum_body(cot_ref, db_ref, mixed_ref, tiles_ref, sum_ref, turned_ref):
    @pl.when(pl.program_id(0) == 0)
    def _():
        sum_ref[...] = jnp.zeros_like(sum_ref)

    d_section_b = section_grad(cot_ref, db_ref).astype(BF16)
    sum_ref[...] += dot_tn(d_section_b, mixed_ref[...].reshape(-1, EXP))

    @pl.when(pl.program_id(0) == STEPS - 1)
    def _():
        turned_ref[...] = sum_ref[...].T
        to_tiles(turned_ref, tiles_ref, 0)


def project_sum(cot, db, mixed):
    return pl.pallas_call(
        project_sum_body,
        grid=(STEPS,),
        in_specs=[band((BLK, COLS, CHAN)), band((2 * BLK, 32, CHAN)), band((BLK, COLS, EXP))],
        out_specs=whole(TILED),
        out_shape=jax.ShapeDtypeStruct(TILED, BF16),
        scratch_shapes=[pltpu.VMEM((CHAN, EXP), F32), pltpu.VMEM((EXP, CHAN), F32)],
        compiler_params=params(58),
        cost_estimate=pl.CostEstimate(
            flops=2 * ROWS * COLS * CHAN * EXP, bytes_accessed=8 * MIB, transcendentals=0
        ),
        name="project_sum",
    )(cot, db, mixed)


def expand_back_body(
    cur_ref, before_ref, after_ref, halo_ref, halo_slope_ref, wp_ref, hid_ref, slope_ref, x_ref, dkb_ref,
    extra_ref,
    dpre_ref, tiles_ref, top_ref, bottom_ref, left_ref, right_ref, acc_ref, sum_ref, depth_ref, shift_ref,
):
    step = pl.program_id(0)

    @pl.when(step == 0)
    def _():
        sum_ref[...] = jnp.zeros_like(sum_ref)
        acc_ref[...] = jnp.zeros_like(acc_ref)
        for at in range(0, EXP, 256):
            span = slice(at, at + 256)
            grads = dot_nt(halo_ref[...], wp_ref[at : at + 256, :])
            grads = (grads * halo_slope_ref[:, span]).astype(BF16).astype(F32)
            top_ref[:, span] = grads[:COLS]
            bottom_ref[:, span] = grads[COLS : 2 * COLS]
            for ref, base in ((left_ref, 2 * COLS), (right_ref, 2 * COLS + EDGE)):
                for s in range(STEPS):
                    ref[s, : BLK + 2, span] = grads[base + BLK * s : base + BLK * s + BLK + 2]

    normed, _ = layer_norm(x_ref[...].reshape(TOK, CHAN).astype(F32))
    normed_t = normed.T.astype(BF16)
    first, last = step == 0, step == STEPS - 1
    for at in range(0, EXP, LANES):
        span = slice(at, at + LANES)
        rows = [jnp.where(first, top_ref[:, span], before_ref[0, :, span].astype(F32))]
        rows += [cur_ref[r, :, span].astype(F32) for r in range(BLK)]
        rows += [jnp.where(last, bottom_ref[:, span], after_ref[0, :, span].astype(F32))]
        for r in range(BLK + 2):
            left = left_ref[step, r : r + 1, span]
            right = right_ref[step, r : r + 1, span]
            shift_ref[0, r, :, span] = jnp.concatenate([rows[r][1:], right], axis=0)
            shift_ref[1, r, :, span] = rows[r]
            shift_ref[2, r, :, span] = jnp.concatenate([left, rows[r][:-1]], axis=0)
        kern = [dkb_ref[n, :, span] for n in range(9)]
        sums = [acc_ref[n, :, span] for n in range(9)]
        for j in range(0, COLS, 16):
            hid = [hid_ref[r, j : j + 16, span].astype(F32) for r in range(BLK)]
            halves = []
            for low in (0, 8):
                cells = slice(j + low, j + low + 8)
                pieces = [[shift_ref[b, r, cells, span] for b in range(3)] for r in range(BLK + 2)]
                totals = [None] * BLK
                for r in range(BLK):
                    cell = hid[r][low : low + 8]
                    for a in range(3):
                        for b in range(3):
                            n = 3 * a + b
                            piece = pieces[r + 2 - a][b]
                            tap = kern[n] * piece
                            totals[r] = tap if n == 0 else totals[r] + tap
                            sums[n] = sums[n] + cell * piece
                halves.append(totals)
            for r in range(BLK):
                total = jnp.concatenate([halves[0][r], halves[1][r]], axis=0)
                d_pre = total * slope_ref[r, j : j + 16, span].astype(F32)
                dpre_ref[r * COLS + j : r * COLS + j + 16, span] = d_pre.astype(BF16)
        for n in range(9):
            acc_ref[n, :, span] = sums[n]
        if at % 256:
            pair = slice(at - LANES, at + LANES)
            sum_ref[:, pair] += dot(normed_t, dpre_ref[:, pair])

    @pl.when(last)
    def _():
        depth_ref[...] = jnp.sum(acc_ref[...], axis=1)
        to_tiles(sum_ref, tiles_ref, 0)
        first_row = lax.broadcasted_iota(jnp.int32, (8, 128), 0) == 0
        for n in range(128):
            extra = extra_ref[n]
            if n < 72:
                row = depth_ref[n // 8 : n // 8 + 1, 128 * (n % 8) : 128 * (n % 8) + 128]
                extra = jnp.where(first_row, row, extra)
            tiles_ref[n, 16:] = extra.astype(BF16)


def expand_back(d_mixed, halo, halo_slope, wp, hidden, slope, x, dkb, extra):
    tiles = (128, 24, 128)
    cells = band((BLK, COLS, EXP))
    return pl.pallas_call(
        expand_back_body,
        grid=(STEPS,),
        in_specs=[
            cells, ROW_BEFORE, ROW_AFTER, whole((HALO, CHAN)), whole((HALO, EXP)),
            whole((EXP, CHAN)), cells, cells, band((BLK, COLS, CHAN)), whole((9, 8, EXP)),
            whole((128, 8, 128)),
        ],
        out_specs=[band((TOK, EXP)), whole(tiles)],
        out_shape=[
            jax.ShapeDtypeStruct((ROWS * COLS, EXP), BF16),
            jax.ShapeDtypeStruct(tiles, BF16),
        ],
        scratch_shapes=[pltpu.VMEM((COLS, EXP), F32)] * 2
        + [pltpu.VMEM((STEPS, 16, EXP), F32)] * 2
        + [pltpu.VMEM((9, 8, EXP), F32), pltpu.VMEM((CHAN, EXP), F32), pltpu.VMEM((9, EXP), F32)]
        + [pltpu.VMEM((3, BLK + 2, COLS, EXP), F32)],
        compiler_params=params(58),
        cost_estimate=pl.CostEstimate(
            flops=2 * ROWS * COLS * CHAN * EXP, bytes_accessed=20 * MIB, transcendentals=0
        ),
        name="expand_back",
    )(d_mixed, d_mixed, d_mixed, halo, halo_slope, wp, hidden, slope, x, dkb, extra)


def finish_body(dpre_ref, x_ref, cot_ref, db_ref, we_ref, grad_ref):
    normed, inv_std = layer_norm(x_ref[...].reshape(-1, CHAN).astype(F32))
    d_input = layer_norm_back(normed, inv_std, dot_nt(dpre_ref[...], we_ref[...]))
    grad_ref[...] = (section_grad(cot_ref, db_ref) + d_input).astype(BF16).reshape(BLK, COLS, CHAN)


def finish(d_pre, x, cot, db, we):
    return pl.pallas_call(
        finish_body,
        grid=(STEPS,),
        in_specs=[
            band((BLK * COLS, EXP)), band((BLK, COLS, CHAN)), band((BLK, COLS, CHAN)), band((2 * BLK, 32, CHAN)),
            whole((CHAN, EXP)),
        ],
        out_specs=band((BLK, COLS, CHAN)),
        out_shape=jax.ShapeDtypeStruct((ROWS, COLS, CHAN), BF16),
        compiler_params=params(58),
        cost_estimate=pl.CostEstimate(
            flops=2 * ROWS * COLS * CHAN * EXP, bytes_accessed=9 * MIB, transcendentals=0
        ),
        name="finish",
    )(d_pre, x, cot, db, we)


def join_body(core_ref, *refs):
    half = pl.ds(core_ref[0] * 64, 64)
    out_ref = refs[-1]
    at = 0
    for own_ref, other_ref in zip(refs[0:-1:2], refs[1:-1:2]):
        total = own_ref[half].astype(F32) + other_ref[half].astype(F32)
        out_ref[:, at : at + own_ref.shape[1]] = total.astype(BF16)
        at += own_ref.shape[1]


def join(core, *tiles):
    vmem = pl.BlockSpec(memory_space=pltpu.VMEM)
    return pl.pallas_call(
        join_body,
        in_specs=[pl.BlockSpec(memory_space=pltpu.SMEM)] + [vmem] * len(tiles),
        out_shape=jax.ShapeDtypeStruct(JOINED, BF16),
        compiler_params=params(24),
        cost_estimate=pl.CostEstimate(flops=MIB, bytes_accessed=4 * MIB, transcendentals=0),
        name="join",
    )(core, *tiles)


def fold_body(terms_ref, out_ref):
    factor = float(128 * ROWS * COLS) ** (-0.5)
    total = jnp.sum(terms_ref[...].astype(F32), axis=0) * factor
    out_ref[...] = jnp.broadcast_to(total.astype(BF16)[None], out_ref.shape)


def fold(terms):
    return pl.pallas_call(
        fold_body,
        out_shape=jax.ShapeDtypeStruct(terms.shape, BF16),
        compiler_params=params(24),
        cost_estimate=pl.CostEstimate(flops=terms.size, bytes_accessed=2 * terms.size, transcendentals=0),
        name="fold",
    )(terms)


def unfold_body(core_ref, own_ref, other_ref, expand_ref, depth_ref, project_ref, qkv_ref, out_ref, bias_ref):
    first = core_ref[0] == 0

    def tile(n, rows):
        own, other = own_ref[n % 64, rows].astype(F32), other_ref[n % 64, rows].astype(F32)
        return jnp.where(first, own, other) if n < 64 else jnp.where(first, other, own)

    parts = ((qkv_ref, 0, 0), (out_ref, 96, 0), (project_ref, 0, 16), (expand_ref, 0, 32))
    for ref, at, low in parts:
        wide = ref.shape[1] // 128
        for r in range(ref.shape[0] // 16):
            for c in range(wide):
                piece = tile(at + wide * r + c, slice(low, low + 16))
                ref[16 * r : 16 * r + 16, 128 * c : 128 * c + 128] = piece
    for n in range(72):
        extra = tile(n, slice(48, 56))
        at = 128 * (n % 8)
        depth_ref[n // 24, n // 8 % 3 : n // 8 % 3 + 1, at : at + 128] = extra[:1]
        if n < 60:
            bias_ref[n % 15, n // 15 : n // 15 + 1, :] = extra[1:2, :15]


def unfold(core, own, other):
    vmem = pl.BlockSpec(memory_space=pltpu.VMEM)
    return pl.pallas_call(
        unfold_body,
        in_specs=[pl.BlockSpec(memory_space=pltpu.SMEM), vmem, vmem],
        out_shape=[
            jax.ShapeDtypeStruct((CHAN, EXP), F32),
            jax.ShapeDtypeStruct((3, 3, EXP), F32),
            jax.ShapeDtypeStruct((EXP, CHAN), F32),
            jax.ShapeDtypeStruct((CHAN, 3 * CHAN), F32),
            jax.ShapeDtypeStruct((CHAN, CHAN), F32),
            jax.ShapeDtypeStruct((15, 4, 15), F32),
        ],
        compiler_params=params(24),
        cost_estimate=pl.CostEstimate(flops=0, bytes_accessed=5 * MIB, transcendentals=0),
        name="unfold",
    )(core, own, other)


FIRST_CELL = np.zeros((32, 512), np.float32)
LAST_CELL = np.zeros((32, 512), np.float32)
for _row in range(32):
    FIRST_CELL[_row, _row * 16] = 1.0
    LAST_CELL[_row, _row * 16 + 15] = 1.0


def edges_body(
    dt_ref, ct_ref, db_ref, cb_ref, dl_ref, cl_ref, dr_ref, cr_ref, first_ref, last_ref,
    top_ref, bottom_ref, left_ref, right_ref,
):
    def total(d_ref, c_ref):
        return (d_ref[...].astype(F32) + c_ref[...].astype(F32)).astype(BF16)

    top = total(dt_ref, ct_ref)
    bottom = total(db_ref, cb_ref)
    for quad in range(4):
        top_ref[16 * quad : 16 * quad + 16] = top[0, quad, :16]
        bottom_ref[16 * quad : 16 * quad + 16] = bottom[0, quad, 16:]
    left_ref[...] = dot(first_ref[...], total(dl_ref, cl_ref).reshape(512, CHAN)).astype(BF16)
    right_ref[...] = dot(last_ref[...], total(dr_ref, cr_ref).reshape(512, CHAN)).astype(BF16)


def edges(d_branch, cot):
    d_branch, cot = d_branch.reshape(16, 4, 32, CHAN), cot.reshape(16, 4, 32, CHAN)
    specs = []
    for row in (0, 15):
        specs += [pl.BlockSpec((1, 4, 32, CHAN), lambda i, row=row: (row, 0, 0, 0))] * 2
    for col in (0, 3):
        specs += [pl.BlockSpec((16, 1, 32, CHAN), lambda i, col=col: (0, col, 0, 0))] * 2
    return pl.pallas_call(
        edges_body,
        grid=(1,),
        in_specs=specs + [whole((32, 512))] * 2,
        out_specs=[whole((COLS, CHAN))] * 2 + [whole((ROWS, CHAN))] * 2,
        out_shape=[jax.ShapeDtypeStruct((COLS, CHAN), BF16)] * 2
        + [jax.ShapeDtypeStruct((ROWS, CHAN), BF16)] * 2,
        compiler_params=params(24),
        cost_estimate=pl.CostEstimate(flops=MIB, bytes_accessed=2 * MIB, transcendentals=0),
        name="edges",
    )(*([d_branch, cot] * 4), jnp.asarray(FIRST_CELL, BF16), jnp.asarray(LAST_CELL, BF16))


def shifts():
    n_lat, n_lon = lax.axis_size("lat"), lax.axis_size("lon")
    south = [(i, i + 1) for i in range(n_lat - 1)]
    north = [(i + 1, i) for i in range(n_lat - 1)]
    east = [(i, (i + 1) % n_lon) for i in range(n_lon)]
    west = [((i + 1) % n_lon, i) for i in range(n_lon)]
    return (south, north, east, west)


def rows_of(top, bottom):
    south, north, _, _ = shifts()
    return (lax.ppermute(bottom, "lat", south), lax.ppermute(top, "lat", north))


def halo_of(above, below, left, right):
    _, _, east, west = shifts()
    pad = jnp.zeros((EDGE - ROWS - 2, left.shape[1]), left.dtype)
    from_west = lax.ppermute(
        jnp.concatenate([above[-1:], right, below[-1:], pad], axis=0), "lon", east
    )
    from_east = lax.ppermute(
        jnp.concatenate([above[:1], left, below[:1], pad], axis=0), "lon", west
    )
    return jnp.concatenate([above, below, from_west, from_east], axis=0)


def wide_rows(field):
    flat = (2 * COLS, CHAN)
    above, below = rows_of(field[:2].reshape(flat), field[-2:].reshape(flat))
    return (above.reshape(2, COLS, CHAN), below.reshape(2, COLS, CHAN))


def wide_columns(field, above, below):
    _, _, east, west = shifts()
    pad = jnp.zeros((2, EDGE - ROWS - 4, field.shape[2]), field.dtype)

    def columns(at):
        parts = [part[:, at : at + 2].transpose(1, 0, 2) for part in (above, field, below)]
        return jnp.concatenate(parts + [pad], axis=1)

    own_west, own_east = columns(0), columns(COLS - 2)
    from_west = lax.ppermute(own_east, "lon", east)
    from_east = lax.ppermute(own_west, "lon", west)
    return (from_west, from_east, own_west, own_east)


def members():
    n_lat, n_lon = lax.axis_size("lat"), lax.axis_size("lon")
    order = np.arange(n_lat * n_lon).reshape(n_lat, n_lon // 2, 2)
    return order.transpose(2, 0, 1).reshape(2, -1).tolist()


def exchange(pieces):
    return lax.all_to_all(
        pieces, ("lat", "lon"), split_axis=0, concat_axis=0, axis_index_groups=members(), tiled=True
    )


def to_pieces(field):
    shaped = field.reshape(16, 2, 4, 16, CHAN).transpose(0, 2, 1, 3, 4)
    return shaped.reshape(64, 32, CHAN)


def pairs():
    return np.arange(lax.axis_size("lon")).reshape(-1, 2).tolist()


def other_core(tiles):
    swaps = [move for a, b in pairs() for move in ((a, b), (b, a))]
    return lax.ppermute(tiles, "lon", swaps)


def rel_table():
    position = np.arange(64)
    pos_row, pos_col = position // 8, position % 8
    rel_index = (pos_row[:, None] - pos_row[None, :] + 7) * 15 + (
        pos_col[:, None] - pos_col[None, :] + 7
    )
    return jnp.asarray(rel_index)[:, :, None] == jnp.arange(225)[None, None, :]


def on_device(
    field_in, cotangent, expand_weight, depth_kernel, project_weight, qkv_weight, out_weight, rel_bias
):
    onehot = rel_table().astype(F32)
    bias = jnp.einsum(
        "tsr,hr->sht", onehot, rel_bias.reshape(4, 225), precision=lax.Precision.HIGHEST
    ).reshape(64, 256)
    dk = depth_kernel.reshape(9, EXP)

    dkb = jnp.broadcast_to(dk[:, None], (9, 8, EXP))
    core = lax.axis_index("lon").astype(jnp.int32).reshape(1) & 1
    barrier = lax.optimization_barrier

    above, below = wide_rows(field_in)
    hidden = expand(field_in, expand_weight, False)
    above, below, hidden = barrier((above, below, hidden))
    field_halo = (above, below, *wide_columns(field_in, above, below))
    field_halo, late_cot = barrier((field_halo, cotangent))
    hidden, cot_pieces = barrier((hidden, to_pieces(late_cot)))
    cot_groups = exchange(cot_pieces)
    section, mixed, mixed_pre, ring_slope = mix(
        hidden, field_halo, expand_weight, dk, project_weight, field_in
    )
    groups = exchange(section)
    cot_swapped, d_att = prepare(cot_groups, out_weight, 32)
    section_field, _ = barrier((field_in, section))
    act_slope = expand(section_field, expand_weight, True)
    groups, bias, d_att, act_slope = barrier((groups, bias, d_att, act_slope))
    d_groups, attended, normed2, d_proj, bias_acc = attention(groups, d_att, qkv_weight, bias)

    d_branch = exchange(d_groups)
    attention_tiles = attention_sums(attended, cot_swapped.reshape(-1, CHAN), normed2, d_proj)
    bias_sum = jnp.einsum(
        "sht,tsr->hr", bias_acc.reshape(64, 4, 64), onehot, precision=lax.Precision.HIGHEST
    )
    extra = jnp.pad(bias_sum.reshape(60, 1, 15), ((0, 68), (1, 6), (0, 113)))
    mixed_pre, _ = barrier((mixed_pre, d_groups))
    mixed_slope = mixed_slopes(mixed_pre)
    d_branch, attention_tiles, extra, mixed_slope = barrier((d_branch, attention_tiles, extra, mixed_slope))

    top, bottom, left, right = edges(d_branch, cot_pieces)
    above, below = rows_of(top, bottom)
    d_mixed = project_back(cotangent, d_branch, mixed_slope, project_weight)
    above, below, d_mixed, attention_tiles = barrier((above, below, d_mixed, attention_tiles))
    d_halo = halo_of(above, below, left, right)
    project_tiles = project_sum(cotangent, d_branch, mixed)
    d_halo, project_tiles, d_mixed = barrier((d_halo, project_tiles, d_mixed))
    attention_pair = (attention_tiles, other_core(attention_tiles))
    project_pair = (project_tiles, other_core(project_tiles))
    d_pre, expand_tiles = expand_back(
        d_mixed, d_halo, ring_slope, project_weight, hidden, act_slope, field_in, dkb, extra
    )

    joined = join(core, *attention_pair, *project_pair, expand_tiles, other_core(expand_tiles))
    joined, d_pre = barrier((joined, d_pre))
    terms = exchange(joined)
    grad_in = finish(d_pre, field_in, cotangent, d_branch, expand_weight)
    terms, grad_in = barrier((terms, grad_in))
    sums = exchange(fold(terms))
    *grads, bias_grad = unfold(core, sums, other_core(sums))
    return (grad_in, *grads, bias_grad.transpose(1, 0, 2))


def solution(mesh):
    placed = (P("lat", "lon", None), P("lat", "lon", None), P(), P(), P(), P(), P(), P())
    return jax.shard_map(
        on_device,
        mesh=mesh,
        in_specs=placed,
        out_specs=(P("lat", "lon", None), P(), P(), P(), P(), P(), P()),
        check_vma=False,
    )
```

```python
import functools
import math

import jax
import jax.numpy as jnp
import numpy as np
from jax import lax
from jax.experimental import pallas as pl
from jax.experimental.pallas import tpu as pltpu
from jax.sharding import PartitionSpec as P

EPSILON = 1e-05
GELU_C = math.sqrt(2.0 / math.pi)
F32 = jnp.float32
BF16 = jnp.bfloat16
MIB = 1 << 20

ROWS, COLS, CHAN, EXP = 32, 64, 256, 1024
BLK = 8
STEPS = ROWS // BLK
TOK = BLK * COLS
LANES = 128
EDGE = 40
HALO = 2 * COLS + 2 * EDGE
LONG = 72
JOINED = (64, 56, 128)


def layer_norm(values):
    average = jnp.mean(values, axis=-1, keepdims=True)
    centred = values - average
    variance = jnp.mean(centred * centred, axis=-1, keepdims=True)
    inv_std = lax.rsqrt(variance + EPSILON)
    return (centred * inv_std, inv_std)


def layer_norm_back(normed, inv_std, grads):
    mean_grad = jnp.mean(grads, axis=-1, keepdims=True)
    mean_cross = jnp.mean(grads * normed, axis=-1, keepdims=True)
    return (grads - mean_grad - normed * mean_cross) * inv_std


def gelu(values):
    return values * (0.5 + 0.5 * jnp.tanh(values * (GELU_C + (GELU_C * 0.044715) * (values * values))))


def gelu_slope(values):
    squared = values * values
    tanh_val = jnp.tanh(values * (GELU_C + (GELU_C * 0.044715) * squared))
    gate = 0.5 + 0.5 * tanh_val
    result = values * gate
    slopes = gate + result * (1.0 - gate) * (2.0 * GELU_C + (6.0 * GELU_C * 0.044715) * squared)
    return (result, slopes)


def dot(left, right):
    return lax.dot_general(left, right, (((1,), (0,)), ((), ())), preferred_element_type=F32)


def dot_nt(left, right):
    return lax.dot_general(left, right, (((1,), (1,)), ((), ())), preferred_element_type=F32)


def dot_tn(left, right):
    return lax.dot_general(left, right, (((0,), (0,)), ((), ())), preferred_element_type=F32)


def params(mib):
    return pltpu.CompilerParams(vmem_limit_bytes=mib * MIB)


def whole(shape):
    return pl.BlockSpec(shape, lambda i: (0,) * len(shape))


def band(shape):
    return pl.BlockSpec(shape, lambda i: (i,) + (0,) * (len(shape) - 1))


ROW_BEFORE = pl.BlockSpec(
    (1, COLS, EXP), lambda i: (jnp.maximum(BLK * i - 1, 0), 0, 0)
)
ROW_AFTER = pl.BlockSpec(
    (1, COLS, EXP), lambda i: (jnp.minimum(BLK * i + BLK, ROWS - 1), 0, 0)
)


TILED = (128, 16, 128)


def to_tiles(ref, out_ref, at):
    wide = ref.shape[1] // 128
    for r in range(ref.shape[0] // 16):
        for c in range(wide):
            tile = ref[16 * r : 16 * r + 16, 128 * c : 128 * c + 128]
            out_ref[at + wide * r + c, :16] = tile.astype(BF16)


def expand_body(x_ref, we_ref, out_ref, slopes):
    normed, _ = layer_norm(x_ref[...].reshape(TOK, CHAN).astype(F32))
    normed_b = normed.astype(BF16)
    for at in range(0, EXP, 256):
        pre = dot(normed_b, we_ref[:, at : at + 256])
        result = gelu_slope(pre)[1] if slopes else gelu(pre)
        out_ref[:, :, at : at + 256] = result.astype(BF16).reshape(BLK, COLS, 256)


def expand(x, we, slopes):
    return pl.pallas_call(
        functools.partial(expand_body, slopes=slopes),
        grid=(STEPS,),
        in_specs=[band((BLK, COLS, CHAN)), whole((CHAN, EXP))],
        out_specs=band((BLK, COLS, EXP)),
        out_shape=jax.ShapeDtypeStruct((ROWS, COLS, EXP), BF16),
        compiler_params=params(58),
        cost_estimate=pl.CostEstimate(
            flops=2 * ROWS * COLS * CHAN * EXP, bytes_accessed=6 * MIB, transcendentals=ROWS * COLS * EXP
        ),
        name="expand_slopes" if slopes else "expand",
    )(x, we)


def mixed_slopes_body(pre_ref, slope_ref):
    for at in range(0, EXP, 256):
        span = slice(at, at + 256)
        slope_ref[:, :, span] = gelu_slope(pre_ref[:, :, span].astype(F32))[1].astype(BF16)


def mixed_slopes(pre):
    return pl.pallas_call(
        mixed_slopes_body,
        grid=(STEPS,),
        in_specs=[band((BLK, COLS, EXP))],
        out_specs=band((BLK, COLS, EXP)),
        out_shape=jax.ShapeDtypeStruct((ROWS, COLS, EXP), BF16),
        compiler_params=params(58),
        cost_estimate=pl.CostEstimate(
            flops=20 * ROWS * COLS * EXP, bytes_accessed=8 * MIB, transcendentals=ROWS * COLS * EXP
        ),
        name="mixed_slopes",
    )(pre)


def mix_body(
    cur_ref, before_ref, after_ref,
    above_ref, below_ref, first_ref, last_ref, west_ref, east_ref, own_west_ref, own_east_ref,
    we_ref, dk_ref, wp_ref, x_ref,
    section_ref, mixed_ref, pre_ref, ring_slope_ref,
    top_ref, bottom_ref, left_ref, right_ref,
):
    step = pl.program_id(0)

    @pl.when(step == 0)
    def _():
        ring_body(
            above_ref, below_ref, first_ref, last_ref, west_ref, east_ref, own_west_ref, own_east_ref,
            we_ref, dk_ref,
            top_ref, bottom_ref, left_ref, right_ref, ring_slope_ref,
        )

    first, last = step == 0, step == STEPS - 1
    branch = None
    for at in range(0, EXP, LANES):
        span = slice(at, at + LANES)
        rows = [jnp.where(first, top_ref[:, span], before_ref[0, :, span])]
        rows += [cur_ref[r, :, span] for r in range(BLK)]
        rows += [jnp.where(last, bottom_ref[:, span], after_ref[0, :, span])]
        rows = [row.astype(F32) for row in rows]
        kern = [dk_ref[n, span][None] for n in range(9)]
        for r in range(BLK):
            parts = [
                kern[b] * rows[r] + kern[3 + b] * rows[r + 1] + kern[6 + b] * rows[r + 2]
                for b in range(3)
            ]
            left = left_ref[step, r : r + 1, span]
            right = right_ref[step, r : r + 1, span]
            pre = (
                parts[1]
                + jnp.concatenate([left, parts[0][:-1]], axis=0)
                + jnp.concatenate([parts[2][1:], right], axis=0)
            )
            mixed_ref[r, :, span] = gelu(pre).astype(BF16)
            pre_ref[r, :, span] = pre.astype(BF16)
        if at % 256:
            pair = slice(at - LANES, at + LANES)
            part = dot(mixed_ref[:, :, pair].reshape(TOK, 256), wp_ref[pair, :])
            branch = part if branch is None else branch + part
    section = (x_ref[...].reshape(TOK, CHAN).astype(F32) + branch).astype(BF16)
    section = section.reshape(BLK // 2, 2, 4, 16, CHAN)
    for pair in range(BLK // 2):
        for quad in range(4):
            section_ref[4 * pair + quad] = section[pair, :, quad].reshape(32, CHAN)


def ring_body(
    above_ref, below_ref, first_ref, last_ref, west_ref, east_ref, own_west_ref, own_east_ref,
    we_ref, dk_ref,
    top_ref, bottom_ref, left_ref, right_ref, slope_ref,
):
    west, east = west_ref[...].astype(F32), east_ref[...].astype(F32)
    pad = jnp.zeros((LONG - COLS - 4, CHAN), F32)

    def along(row, at):
        return [
            west[0, at : at + 1], west[1, at : at + 1], row.astype(F32),
            east[0, at : at + 1], east[1, at : at + 1], pad,
        ]

    strips = along(above_ref[0], 0) + along(above_ref[1], 1) + along(first_ref[0], 2)
    strips += along(last_ref[0], 33) + along(below_ref[0], 34) + along(below_ref[1], 35)
    strips += [west[0], west[1], own_west_ref[0].astype(F32)]
    strips += [own_east_ref[1].astype(F32), east[0], east[1]]
    normed, _ = layer_norm(jnp.concatenate(strips, axis=0))
    normed_b = normed.astype(BF16)
    south, lefts, rights = 3 * LONG, 6 * LONG, 6 * LONG + 3 * EDGE
    for at in range(0, EXP, 256):
        span = slice(at, at + 256)
        val = gelu(dot(normed_b, we_ref[:, span])).astype(BF16).astype(F32)
        kern = [dk_ref[n, span][None] for n in range(9)]
        top_ref[:, span] = val[LONG + 2 : LONG + 2 + COLS].astype(BF16)
        bottom_ref[:, span] = val[south + LONG + 2 : south + LONG + 2 + COLS].astype(BF16)
        for ref, base, col in ((left_ref, lefts, 0), (right_ref, rights, 2)):
            total = 0.0
            for a in range(3):
                start = base + EDGE + a + 1
                total = total + kern[3 * a + col] * val[start : start + ROWS]
            for s in range(STEPS):
                ref[s, :BLK, span] = total[BLK * s : BLK * s + BLK]
        for base, out in ((0, 0), (south, COLS)):
            total = 0.0
            for a in range(3):
                for b in range(3):
                    start = base + LONG * a + b + 1
                    total = total + kern[3 * a + b] * val[start : start + COLS]
            slope_ref[out : out + COLS, span] = gelu_slope(total)[1]
        for base, out in ((lefts, 2 * COLS), (rights, 2 * COLS + EDGE)):
            total = 0.0
            for a in range(3):
                for b in range(3):
                    start = base + EDGE * b + a
                    total = total + kern[3 * a + b] * val[start : start + ROWS + 2]
            slope_ref[out : out + ROWS + 2, span] = gelu_slope(total)[1]
            slope_ref[out + ROWS + 2 : out + EDGE, span] = jnp.zeros((EDGE - ROWS - 2, 256), F32)


def mix(hidden, halo, we, dk, wp, x):
    above, below, west, east, own_west, own_east = halo
    wide = jax.ShapeDtypeStruct((ROWS, COLS, EXP), BF16)
    return pl.pallas_call(
        mix_body,
        grid=(STEPS,),
        in_specs=[
            band((BLK, COLS, EXP)), ROW_BEFORE, ROW_AFTER,
            whole((2, COLS, CHAN)), whole((2, COLS, CHAN)),
            pl.BlockSpec((1, COLS, CHAN), lambda i: (0, 0, 0)),
            pl.BlockSpec((1, COLS, CHAN), lambda i: (ROWS - 1, 0, 0)),
            whole((2, EDGE, CHAN)), whole((2, EDGE, CHAN)), whole((2, EDGE, CHAN)), whole((2, EDGE, CHAN)),
            whole((CHAN, EXP)), whole((9, EXP)), whole((EXP, CHAN)), band((BLK, COLS, CHAN)),
        ],
        out_specs=[
            band((2 * BLK, 32, CHAN)), band((BLK, COLS, EXP)), band((BLK, COLS, EXP)), whole((HALO, EXP)),
        ],
        out_shape=[
            jax.ShapeDtypeStruct((64, 32, CHAN), BF16), wide, wide, jax.ShapeDtypeStruct((HALO, EXP), F32),
        ],
        scratch_shapes=[pltpu.VMEM((COLS, EXP), BF16)] * 2 + [pltpu.VMEM((STEPS, 16, EXP), F32)] * 2,
        compiler_params=params(58),
        cost_estimate=pl.CostEstimate(
            flops=3 * ROWS * COLS * CHAN * EXP, bytes_accessed=18 * MIB, transcendentals=2 * ROWS * COLS * EXP
        ),
        name="mix",
    )(
        hidden, hidden, hidden, above, below, x, x, west, east, own_west, own_east,
        we, dk, wp, x,
    )


SWAP = np.zeros((256, 256), np.float32)
for _s in range(16):
    for _g in range(16):
        SWAP[_g * 16 + _s, _s * 16 + _g] = 1.0


def diagonal(full, low):
    halves = []
    for half in range(2):
        lanes = slice(half * 128, half * 128 + 128)
        at = half * 128
        halves.append(jnp.where(low, full[at : at + 64, lanes], full[at + 64 : at + 128, lanes]))
    return jnp.concatenate(halves, axis=1)


def swap(src, dst, swap_ref, n_groups):
    for s in range(0, 64, 16):
        for g in range(0, n_groups, 16):
            moved = dot(swap_ref[...], src[s : s + 16, g : g + 16].reshape(256, CHAN)).astype(BF16)
            dst[g : g + 16, s : s + 16] = moved.reshape(16, 16, CHAN)


def prepare_body(cot_ref, wout_ref, swap_ref, cs_ref, da_ref):
    n_groups = cot_ref.shape[1]
    swap(cot_ref, cs_ref, swap_ref, n_groups)
    for g in range(0, n_groups, 4):
        grads = dot_nt(cs_ref[g : g + 4].reshape(256, CHAN), wout_ref[...])
        da_ref[g : g + 4] = grads.astype(BF16).reshape(4, 64, CHAN)


def prepare(cot, wout, n_groups):
    shape = (64, n_groups, CHAN)
    grouped = (n_groups, 64, CHAN)
    return pl.pallas_call(
        prepare_body,
        grid=(1,),
        in_specs=[whole(shape), whole((CHAN, CHAN)), whole((256, 256))],
        out_specs=[whole(grouped), whole(grouped)],
        out_shape=[jax.ShapeDtypeStruct(grouped, BF16)] * 2,
        compiler_params=params(24),
        cost_estimate=pl.CostEstimate(
            flops=n_groups * 64 * 4 * CHAN * CHAN, bytes_accessed=3 * MIB, transcendentals=0
        ),
        name="prepare",
    )(cot, wout, jnp.asarray(SWAP, BF16))


def attention_body(
    x_ref, da_ref, wqkv_ref, bias_ref, swap_ref,
    out_ref, att_ref, norm_ref, proj_ref, bias_sum_ref, xs_ref, ds_ref,
):
    step = pl.program_id(0)
    n_groups = x_ref.shape[1]

    @pl.when(step == 0)
    def _():
        bias_sum_ref[...] = jnp.zeros_like(bias_sum_ref)
        swap(x_ref, xs_ref, swap_ref, n_groups)

    groups = pl.ds(step * 4, 4)
    tokens = xs_ref[groups].reshape(256, CHAN)
    normed, inv_std = layer_norm(tokens.astype(F32))
    normed_b = normed.astype(BF16)
    norm_ref[...] = normed_b
    projected = dot(normed_b, wqkv_ref[...]).astype(BF16)
    low = lax.broadcasted_iota(jnp.int32, (64, 128), 1) < 64
    keep = [low.astype(F32).astype(BF16), (1.0 - low.astype(F32)).astype(BF16)]
    none = jnp.zeros((128, 128), BF16)

    def by_head(rows):
        blocks = []
        for half in range(2):
            lanes = rows[:, half * 128 : half * 128 + 128]
            pair = jnp.concatenate([lanes * keep[0], lanes * keep[1]], axis=0)
            blocks.append(jnp.concatenate([pair, none] if half == 0 else [none, pair], axis=1))
        return jnp.concatenate(blocks, axis=0)

    four = range(4)
    part = [slice(g * 64, g * 64 + 64) for g in four]
    query = (projected[:, :CHAN].astype(F32) * 0.125).astype(BF16)
    key = [projected[part[g], CHAN : 2 * CHAN] for g in four]
    value = [projected[part[g], 2 * CHAN :] for g in four]
    query_h = [by_head(query[part[g]]) for g in four]
    da_h = [by_head(da_ref[g]) for g in four]
    scores = [dot_nt(key[g], query_h[g]) + bias_ref[...] for g in four]
    d_probs = [dot_nt(value[g], da_h[g]) for g in four]
    tops = [jnp.max(scores[g], axis=0, keepdims=True) for g in four]
    scores = [jnp.exp(scores[g] - tops[g]) for g in four]
    scales = [1.0 / jnp.sum(scores[g], axis=0, keepdims=True) for g in four]
    probs = [scores[g] * scales[g] for g in four]
    probs_b = [probs[g].astype(BF16) for g in four]
    crosses = [jnp.sum(probs[g] * d_probs[g], axis=0, keepdims=True) for g in four]
    d_scores = [probs[g] * (d_probs[g] - crosses[g]) for g in four]
    bias_sum_ref[...] += (d_scores[0] + d_scores[1]) + (d_scores[2] + d_scores[3])
    d_scores_b = [d_scores[g].astype(BF16) for g in four]
    attended = [dot_tn(probs_b[g], value[g]) for g in four]
    d_query = [dot_tn(d_scores_b[g], key[g]) for g in four]
    d_key = [dot(d_scores_b[g], query_h[g]) for g in four]
    d_value = [dot(probs_b[g], da_h[g]) for g in four]
    for g in four:
        att_ref[part[g]] = diagonal(attended[g], low).astype(BF16)
        proj_ref[part[g], :CHAN] = (diagonal(d_query[g], low) * 0.125).astype(BF16)
        proj_ref[part[g], CHAN : 2 * CHAN] = d_key[g].astype(BF16)
        proj_ref[part[g], 2 * CHAN :] = d_value[g].astype(BF16)
    d_normed = dot_nt(proj_ref[...], wqkv_ref[...])
    d_tokens = layer_norm_back(normed, inv_std, d_normed).astype(BF16)
    ds_ref[groups] = d_tokens.reshape(4, 64, CHAN)

    @pl.when(step == n_groups // 4 - 1)
    def _():
        for s in range(0, 64, 16):
            for g in range(0, n_groups, 16):
                tile = ds_ref[g : g + 16, s : s + 16].reshape(256, CHAN)
                moved = dot(swap_ref[...], tile).astype(BF16)
                out_ref[s : s + 16, g : g + 16] = moved.reshape(16, 16, CHAN)


def attention(tokens, d_att, wqkv, bias):
    n_groups = tokens.shape[1]
    shape = (64, n_groups, CHAN)
    flat = n_groups * 64
    return pl.pallas_call(
        attention_body,
        grid=(n_groups // 4,),
        in_specs=[
            whole(shape), band((4, 64, CHAN)), whole((CHAN, 3 * CHAN)), whole((64, CHAN)),
            whole((256, 256)),
        ],
        out_specs=[
            whole(shape), band((256, CHAN)), band((256, CHAN)), band((256, 3 * CHAN)), whole((64, CHAN)),
        ],
        out_shape=[
            jax.ShapeDtypeStruct(shape, BF16),
            jax.ShapeDtypeStruct((flat, CHAN), BF16),
            jax.ShapeDtypeStruct((flat, CHAN), BF16),
            jax.ShapeDtypeStruct((flat, 3 * CHAN), BF16),
            jax.ShapeDtypeStruct((64, CHAN), F32),
        ],
        scratch_shapes=[pltpu.VMEM((n_groups, 64, CHAN), BF16)] * 2,
        compiler_params=params(58),
        cost_estimate=pl.CostEstimate(
            flops=flat * 4 * CHAN * CHAN * 5, bytes_accessed=8 * MIB, transcendentals=flat * 256
        ),
        name="attention",
    )(tokens, d_att, wqkv, bias, jnp.asarray(SWAP, BF16))


def attention_sums_body(att_ref, cot_ref, norm_ref, proj_ref, out_ref, qkv_acc, out_acc):
    step = pl.program_id(0)

    @pl.when(step == 0)
    def _():
        qkv_acc[...] = jnp.zeros_like(qkv_acc)
        out_acc[...] = jnp.zeros_like(out_acc)

    out_acc[...] += dot_tn(att_ref[...], cot_ref[...])
    qkv_acc[...] += dot_tn(norm_ref[...], proj_ref[...])

    @pl.when(step == pl.num_programs(0) - 1)
    def _():
        to_tiles(qkv_acc, out_ref, 0)
        to_tiles(out_acc, out_ref, 96)


def attention_sums(att, cot, normed, proj):
    flat = att.shape[0]
    return pl.pallas_call(
        attention_sums_body,
        grid=(flat // 512,),
        in_specs=[band((512, CHAN)), band((512, CHAN)), band((512, CHAN)), band((512, 3 * CHAN))],
        out_specs=whole(TILED),
        out_shape=jax.ShapeDtypeStruct(TILED, BF16),
        scratch_shapes=[pltpu.VMEM((CHAN, 3 * CHAN), F32), pltpu.VMEM((CHAN, CHAN), F32)],
        compiler_params=params(58),
        cost_estimate=pl.CostEstimate(
            flops=flat * 8 * CHAN * CHAN, bytes_accessed=6 * MIB, transcendentals=0
        ),
        name="attention_sums",
    )(att, cot, normed, proj)


def section_grad(cot_ref, db_ref):
    n_pairs = cot_ref.shape[0] // 2
    pieces = db_ref[...].reshape(n_pairs, 4, 2, 16, CHAN)
    branch = jnp.concatenate(
        [pieces[pair, quad, r] for pair in range(n_pairs) for r in range(2) for quad in range(4)], axis=0
    )
    return cot_ref[...].reshape(-1, CHAN).astype(F32) + branch.astype(F32)


def project_body(cot_ref, db_ref, slope_ref, wp_ref, dm_ref):
    d_section_b = section_grad(cot_ref, db_ref).astype(BF16)
    for at in range(0, EXP, 256):
        grads = dot_nt(d_section_b, wp_ref[at : at + 256, :])
        slope = slope_ref[:, :, at : at + 256].reshape(-1, 256).astype(F32)
        dm_ref[:, :, at : at + 256] = (grads * slope).astype(BF16).reshape(BLK, COLS, 256)


def project_back(cot, db, slope, wp):
    return pl.pallas_call(
        project_body,
        grid=(STEPS,),
        in_specs=[
            band((BLK, COLS, CHAN)), band((2 * BLK, 32, CHAN)), band((BLK, COLS, EXP)), whole((EXP, CHAN)),
        ],
        out_specs=band((BLK, COLS, EXP)),
        out_shape=jax.ShapeDtypeStruct((ROWS, COLS, EXP), BF16),
        compiler_params=params(58),
        cost_estimate=pl.CostEstimate(
            flops=2 * ROWS * COLS * CHAN * EXP, bytes_accessed=10 * MIB, transcendentals=0
        ),
        name="project_back",
    )(cot, db, slope, wp)


def project_sum_body(cot_ref, db_ref, mixed_ref, tiles_ref, sum_ref, turned_ref):
    @pl.when(pl.program_id(0) == 0)
    def _():
        sum_ref[...] = jnp.zeros_like(sum_ref)

    d_section_b = section_grad(cot_ref, db_ref).astype(BF16)
    sum_ref[...] += dot_tn(d_section_b, mixed_ref[...].reshape(-1, EXP))

    @pl.when(pl.program_id(0) == STEPS - 1)
    def _():
        turned_ref[...] = sum_ref[...].T
        to_tiles(turned_ref, tiles_ref, 0)


def project_sum(cot, db, mixed):
    return pl.pallas_call(
        project_sum_body,
        grid=(STEPS,),
        in_specs=[band((BLK, COLS, CHAN)), band((2 * BLK, 32, CHAN)), band((BLK, COLS, EXP))],
        out_specs=whole(TILED),
        out_shape=jax.ShapeDtypeStruct(TILED, BF16),
        scratch_shapes=[pltpu.VMEM((CHAN, EXP), F32), pltpu.VMEM((EXP, CHAN), F32)],
        compiler_params=params(58),
        cost_estimate=pl.CostEstimate(
            flops=2 * ROWS * COLS * CHAN * EXP, bytes_accessed=8 * MIB, transcendentals=0
        ),
        name="project_sum",
    )(cot, db, mixed)


def expand_back_body(
    cur_ref, before_ref, after_ref, halo_ref, halo_slope_ref, wp_ref, hid_ref, slope_ref, x_ref, dkb_ref,
    extra_ref,
    dpre_ref, tiles_ref, top_ref, bottom_ref, left_ref, right_ref, acc_ref, sum_ref, depth_ref, shift_ref,
    narrow_ref,
):
    step = pl.program_id(0)

    @pl.when(step == 0)
    def _():
        sum_ref[...] = jnp.zeros_like(sum_ref)
        acc_ref[...] = jnp.zeros_like(acc_ref)
        for at in range(0, EXP, 256):
            span = slice(at, at + 256)
            grads = dot_nt(halo_ref[...], wp_ref[at : at + 256, :])
            grads = (grads * halo_slope_ref[:, span]).astype(BF16).astype(F32)
            top_ref[:, span] = grads[:COLS]
            bottom_ref[:, span] = grads[COLS : 2 * COLS]
            for ref, base in ((left_ref, 2 * COLS), (right_ref, 2 * COLS + EDGE)):
                for s in range(STEPS):
                    ref[s, : BLK + 2, span] = grads[base + BLK * s : base + BLK * s + BLK + 2]

    normed, _ = layer_norm(x_ref[...].reshape(TOK, CHAN).astype(F32))
    normed_t = normed.T.astype(BF16)
    diagonal_cells = lax.broadcasted_iota(jnp.int32, (LANES, LANES), 0) == lax.broadcasted_iota(
        jnp.int32, (LANES, LANES), 1
    )
    first, last = step == 0, step == STEPS - 1
    for at in range(0, EXP, LANES):
        span = slice(at, at + LANES)
        rows = [jnp.where(first, top_ref[:, span], before_ref[0, :, span].astype(F32))]
        rows += [cur_ref[r, :, span].astype(F32) for r in range(BLK)]
        rows += [jnp.where(last, bottom_ref[:, span], after_ref[0, :, span].astype(F32))]
        for r in range(BLK + 2):
            left = left_ref[step, r : r + 1, span]
            right = right_ref[step, r : r + 1, span]
            moved = (
                jnp.concatenate([rows[r][1:], right], axis=0),
                rows[r],
                jnp.concatenate([left, rows[r][:-1]], axis=0),
            )
            for b in range(3):
                shift_ref[b, r, :, span] = moved[b]
                narrow_ref[b, r, :, span] = moved[b].astype(BF16)
        hid_t = hid_ref[:, :, span].reshape(TOK, LANES).T
        for a in range(3):
            shifted = [
                narrow_ref[b, 2 - a : 2 - a + BLK, :, span].reshape(TOK, LANES) for b in range(3)
            ]
            product = dot(hid_t, jnp.concatenate(shifted, axis=1))
            for b in range(3):
                cross = jnp.where(diagonal_cells, product[:, b * LANES : b * LANES + LANES], 0.0)
                acc_ref[3 * a + b, :, span] += jnp.sum(cross.reshape(16, 8, LANES), axis=0)
        kern = [dkb_ref[n, :, span] for n in range(9)]
        for j in range(0, COLS, 16):
            halves = []
            for low in (0, 8):
                cells = slice(j + low, j + low + 8)
                pieces = [[shift_ref[b, r, cells, span] for b in range(3)] for r in range(BLK + 2)]
                totals = []
                for r in range(BLK):
                    taps = [kern[3 * a + b] * pieces[r + 2 - a][b] for a in range(3) for b in range(3)]
                    totals.append(sum(taps[1:], taps[0]))
                halves.append(totals)
            for r in range(BLK):
                total = jnp.concatenate([halves[0][r], halves[1][r]], axis=0)
                d_pre = total * slope_ref[r, j : j + 16, span].astype(F32)
                dpre_ref[r * COLS + j : r * COLS + j + 16, span] = d_pre.astype(BF16)
        if at % 256:
            pair = slice(at - LANES, at + LANES)
            sum_ref[:, pair] += dot(normed_t, dpre_ref[:, pair])

    @pl.when(last)
    def _():
        depth_ref[...] = jnp.sum(acc_ref[...], axis=1)
        to_tiles(sum_ref, tiles_ref, 0)
        first_row = lax.broadcasted_iota(jnp.int32, (8, 128), 0) == 0
        for n in range(128):
            extra = extra_ref[n]
            if n < 72:
                row = depth_ref[n // 8 : n // 8 + 1, 128 * (n % 8) : 128 * (n % 8) + 128]
                extra = jnp.where(first_row, row, extra)
            tiles_ref[n, 16:] = extra.astype(BF16)


def expand_back(d_mixed, halo, halo_slope, wp, hidden, slope, x, dkb, extra):
    tiles = (128, 24, 128)
    cells = band((BLK, COLS, EXP))
    return pl.pallas_call(
        expand_back_body,
        grid=(STEPS,),
        in_specs=[
            cells, ROW_BEFORE, ROW_AFTER, whole((HALO, CHAN)), whole((HALO, EXP)),
            whole((EXP, CHAN)), cells, cells, band((BLK, COLS, CHAN)), whole((9, 8, EXP)),
            whole((128, 8, 128)),
        ],
        out_specs=[band((TOK, EXP)), whole(tiles)],
        out_shape=[
            jax.ShapeDtypeStruct((ROWS * COLS, EXP), BF16),
            jax.ShapeDtypeStruct(tiles, BF16),
        ],
        scratch_shapes=[pltpu.VMEM((COLS, EXP), F32)] * 2
        + [pltpu.VMEM((STEPS, 16, EXP), F32)] * 2
        + [pltpu.VMEM((9, 8, EXP), F32), pltpu.VMEM((CHAN, EXP), F32), pltpu.VMEM((9, EXP), F32)]
        + [pltpu.VMEM((3, BLK + 2, COLS, EXP), F32), pltpu.VMEM((3, BLK + 2, COLS, EXP), BF16)],
        compiler_params=params(58),
        cost_estimate=pl.CostEstimate(
            flops=2 * ROWS * COLS * CHAN * EXP, bytes_accessed=20 * MIB, transcendentals=0
        ),
        name="expand_back",
    )(d_mixed, d_mixed, d_mixed, halo, halo_slope, wp, hidden, slope, x, dkb, extra)


def finish_body(dpre_ref, x_ref, cot_ref, db_ref, we_ref, grad_ref):
    normed, inv_std = layer_norm(x_ref[...].reshape(-1, CHAN).astype(F32))
    d_input = layer_norm_back(normed, inv_std, dot_nt(dpre_ref[...], we_ref[...]))
    grad_ref[...] = (section_grad(cot_ref, db_ref) + d_input).astype(BF16).reshape(BLK, COLS, CHAN)


def finish(d_pre, x, cot, db, we):
    return pl.pallas_call(
        finish_body,
        grid=(STEPS,),
        in_specs=[
            band((BLK * COLS, EXP)), band((BLK, COLS, CHAN)), band((BLK, COLS, CHAN)), band((2 * BLK, 32, CHAN)),
            whole((CHAN, EXP)),
        ],
        out_specs=band((BLK, COLS, CHAN)),
        out_shape=jax.ShapeDtypeStruct((ROWS, COLS, CHAN), BF16),
        compiler_params=params(58),
        cost_estimate=pl.CostEstimate(
            flops=2 * ROWS * COLS * CHAN * EXP, bytes_accessed=9 * MIB, transcendentals=0
        ),
        name="finish",
    )(d_pre, x, cot, db, we)


def join_body(core_ref, *refs):
    half = pl.ds(core_ref[0] * 64, 64)
    out_ref = refs[-1]
    at = 0
    for own_ref, other_ref in zip(refs[0:-1:2], refs[1:-1:2]):
        total = own_ref[half].astype(F32) + other_ref[half].astype(F32)
        out_ref[:, at : at + own_ref.shape[1]] = total.astype(BF16)
        at += own_ref.shape[1]


def join(core, *tiles):
    vmem = pl.BlockSpec(memory_space=pltpu.VMEM)
    return pl.pallas_call(
        join_body,
        in_specs=[pl.BlockSpec(memory_space=pltpu.SMEM)] + [vmem] * len(tiles),
        out_shape=jax.ShapeDtypeStruct(JOINED, BF16),
        compiler_params=params(24),
        cost_estimate=pl.CostEstimate(flops=MIB, bytes_accessed=4 * MIB, transcendentals=0),
        name="join",
    )(core, *tiles)


def fold_body(terms_ref, out_ref):
    factor = float(128 * ROWS * COLS) ** (-0.5)
    total = jnp.sum(terms_ref[...].astype(F32), axis=0) * factor
    out_ref[...] = jnp.broadcast_to(total.astype(BF16)[None], out_ref.shape)


def fold(terms):
    return pl.pallas_call(
        fold_body,
        out_shape=jax.ShapeDtypeStruct(terms.shape, BF16),
        compiler_params=params(24),
        cost_estimate=pl.CostEstimate(flops=terms.size, bytes_accessed=2 * terms.size, transcendentals=0),
        name="fold",
    )(terms)


def unfold_body(core_ref, own_ref, other_ref, expand_ref, depth_ref, project_ref, qkv_ref, out_ref, bias_ref):
    first = core_ref[0] == 0

    def tile(n, rows):
        own, other = own_ref[n % 64, rows].astype(F32), other_ref[n % 64, rows].astype(F32)
        return jnp.where(first, own, other) if n < 64 else jnp.where(first, other, own)

    parts = ((qkv_ref, 0, 0), (out_ref, 96, 0), (project_ref, 0, 16), (expand_ref, 0, 32))
    for ref, at, low in parts:
        wide = ref.shape[1] // 128
        for r in range(ref.shape[0] // 16):
            for c in range(wide):
                piece = tile(at + wide * r + c, slice(low, low + 16))
                ref[16 * r : 16 * r + 16, 128 * c : 128 * c + 128] = piece
    for n in range(72):
        extra = tile(n, slice(48, 56))
        at = 128 * (n % 8)
        depth_ref[n // 24, n // 8 % 3 : n // 8 % 3 + 1, at : at + 128] = extra[:1]
        if n < 60:
            bias_ref[n % 15, n // 15 : n // 15 + 1, :] = extra[1:2, :15]


def unfold(core, own, other):
    vmem = pl.BlockSpec(memory_space=pltpu.VMEM)
    return pl.pallas_call(
        unfold_body,
        in_specs=[pl.BlockSpec(memory_space=pltpu.SMEM), vmem, vmem],
        out_shape=[
            jax.ShapeDtypeStruct((CHAN, EXP), F32),
            jax.ShapeDtypeStruct((3, 3, EXP), F32),
            jax.ShapeDtypeStruct((EXP, CHAN), F32),
            jax.ShapeDtypeStruct((CHAN, 3 * CHAN), F32),
            jax.ShapeDtypeStruct((CHAN, CHAN), F32),
            jax.ShapeDtypeStruct((15, 4, 15), F32),
        ],
        compiler_params=params(24),
        cost_estimate=pl.CostEstimate(flops=0, bytes_accessed=5 * MIB, transcendentals=0),
        name="unfold",
    )(core, own, other)


FIRST_CELL = np.zeros((32, 512), np.float32)
LAST_CELL = np.zeros((32, 512), np.float32)
for _row in range(32):
    FIRST_CELL[_row, _row * 16] = 1.0
    LAST_CELL[_row, _row * 16 + 15] = 1.0


def edges_body(
    dt_ref, ct_ref, db_ref, cb_ref, dl_ref, cl_ref, dr_ref, cr_ref, first_ref, last_ref,
    top_ref, bottom_ref, left_ref, right_ref,
):
    def total(d_ref, c_ref):
        return (d_ref[...].astype(F32) + c_ref[...].astype(F32)).astype(BF16)

    top = total(dt_ref, ct_ref)
    bottom = total(db_ref, cb_ref)
    for quad in range(4):
        top_ref[16 * quad : 16 * quad + 16] = top[0, quad, :16]
        bottom_ref[16 * quad : 16 * quad + 16] = bottom[0, quad, 16:]
    left_ref[...] = dot(first_ref[...], total(dl_ref, cl_ref).reshape(512, CHAN)).astype(BF16)
    right_ref[...] = dot(last_ref[...], total(dr_ref, cr_ref).reshape(512, CHAN)).astype(BF16)


def edges(d_branch, cot):
    d_branch, cot = d_branch.reshape(16, 4, 32, CHAN), cot.reshape(16, 4, 32, CHAN)
    specs = []
    for row in (0, 15):
        specs += [pl.BlockSpec((1, 4, 32, CHAN), lambda i, row=row: (row, 0, 0, 0))] * 2
    for col in (0, 3):
        specs += [pl.BlockSpec((16, 1, 32, CHAN), lambda i, col=col: (0, col, 0, 0))] * 2
    return pl.pallas_call(
        edges_body,
        grid=(1,),
        in_specs=specs + [whole((32, 512))] * 2,
        out_specs=[whole((COLS, CHAN))] * 2 + [whole((ROWS, CHAN))] * 2,
        out_shape=[jax.ShapeDtypeStruct((COLS, CHAN), BF16)] * 2
        + [jax.ShapeDtypeStruct((ROWS, CHAN), BF16)] * 2,
        compiler_params=params(24),
        cost_estimate=pl.CostEstimate(flops=MIB, bytes_accessed=2 * MIB, transcendentals=0),
        name="edges",
    )(*([d_branch, cot] * 4), jnp.asarray(FIRST_CELL, BF16), jnp.asarray(LAST_CELL, BF16))


def shifts():
    n_lat, n_lon = lax.axis_size("lat"), lax.axis_size("lon")
    south = [(i, i + 1) for i in range(n_lat - 1)]
    north = [(i + 1, i) for i in range(n_lat - 1)]
    east = [(i, (i + 1) % n_lon) for i in range(n_lon)]
    west = [((i + 1) % n_lon, i) for i in range(n_lon)]
    return (south, north, east, west)


def rows_of(top, bottom):
    south, north, _, _ = shifts()
    return (lax.ppermute(bottom, "lat", south), lax.ppermute(top, "lat", north))


def halo_of(above, below, left, right):
    _, _, east, west = shifts()
    pad = jnp.zeros((EDGE - ROWS - 2, left.shape[1]), left.dtype)
    from_west = lax.ppermute(
        jnp.concatenate([above[-1:], right, below[-1:], pad], axis=0), "lon", east
    )
    from_east = lax.ppermute(
        jnp.concatenate([above[:1], left, below[:1], pad], axis=0), "lon", west
    )
    return jnp.concatenate([above, below, from_west, from_east], axis=0)


def wide_rows(field):
    flat = (2 * COLS, CHAN)
    above, below = rows_of(field[:2].reshape(flat), field[-2:].reshape(flat))
    return (above.reshape(2, COLS, CHAN), below.reshape(2, COLS, CHAN))


def wide_columns(field, above, below):
    _, _, east, west = shifts()
    pad = jnp.zeros((2, EDGE - ROWS - 4, field.shape[2]), field.dtype)

    def columns(at):
        parts = [part[:, at : at + 2].transpose(1, 0, 2) for part in (above, field, below)]
        return jnp.concatenate(parts + [pad], axis=1)

    own_west, own_east = columns(0), columns(COLS - 2)
    from_west = lax.ppermute(own_east, "lon", east)
    from_east = lax.ppermute(own_west, "lon", west)
    return (from_west, from_east, own_west, own_east)


def members():
    n_lat, n_lon = lax.axis_size("lat"), lax.axis_size("lon")
    order = np.arange(n_lat * n_lon).reshape(n_lat, n_lon // 2, 2)
    return order.transpose(2, 0, 1).reshape(2, -1).tolist()


def exchange(pieces):
    return lax.all_to_all(
        pieces, ("lat", "lon"), split_axis=0, concat_axis=0, axis_index_groups=members(), tiled=True
    )


def to_pieces(field):
    shaped = field.reshape(16, 2, 4, 16, CHAN).transpose(0, 2, 1, 3, 4)
    return shaped.reshape(64, 32, CHAN)


def pairs():
    return np.arange(lax.axis_size("lon")).reshape(-1, 2).tolist()


def other_core(tiles):
    swaps = [move for a, b in pairs() for move in ((a, b), (b, a))]
    return lax.ppermute(tiles, "lon", swaps)


def rel_table():
    position = np.arange(64)
    pos_row, pos_col = position // 8, position % 8
    rel_index = (pos_row[:, None] - pos_row[None, :] + 7) * 15 + (
        pos_col[:, None] - pos_col[None, :] + 7
    )
    return jnp.asarray(rel_index)[:, :, None] == jnp.arange(225)[None, None, :]


def on_device(
    field_in, cotangent, expand_weight, depth_kernel, project_weight, qkv_weight, out_weight, rel_bias
):
    onehot = rel_table().astype(F32)
    bias = jnp.einsum(
        "tsr,hr->sht", onehot, rel_bias.reshape(4, 225), precision=lax.Precision.HIGHEST
    ).reshape(64, 256)
    dk = depth_kernel.reshape(9, EXP)

    dkb = jnp.broadcast_to(dk[:, None], (9, 8, EXP))
    core = lax.axis_index("lon").astype(jnp.int32).reshape(1) & 1
    barrier = lax.optimization_barrier

    above, below = wide_rows(field_in)
    hidden = expand(field_in, expand_weight, False)
    above, below, hidden = barrier((above, below, hidden))
    field_halo = (above, below, *wide_columns(field_in, above, below))
    field_halo, late_cot = barrier((field_halo, cotangent))
    hidden, cot_pieces = barrier((hidden, to_pieces(late_cot)))
    cot_groups = exchange(cot_pieces)
    section, mixed, mixed_pre, ring_slope = mix(
        hidden, field_halo, expand_weight, dk, project_weight, field_in
    )
    groups = exchange(section)
    cot_swapped, d_att = prepare(cot_groups, out_weight, 32)
    section_field, _ = barrier((field_in, section))
    act_slope = expand(section_field, expand_weight, True)
    groups, bias, d_att, act_slope = barrier((groups, bias, d_att, act_slope))
    d_groups, attended, normed2, d_proj, bias_acc = attention(groups, d_att, qkv_weight, bias)

    d_branch = exchange(d_groups)
    attention_tiles = attention_sums(attended, cot_swapped.reshape(-1, CHAN), normed2, d_proj)
    bias_sum = jnp.einsum(
        "sht,tsr->hr", bias_acc.reshape(64, 4, 64), onehot, precision=lax.Precision.HIGHEST
    )
    extra = jnp.pad(bias_sum.reshape(60, 1, 15), ((0, 68), (1, 6), (0, 113)))
    mixed_pre, _ = barrier((mixed_pre, d_groups))
    mixed_slope = mixed_slopes(mixed_pre)
    d_branch, attention_tiles, extra, mixed_slope = barrier((d_branch, attention_tiles, extra, mixed_slope))

    top, bottom, left, right = edges(d_branch, cot_pieces)
    above, below = rows_of(top, bottom)
    d_mixed = project_back(cotangent, d_branch, mixed_slope, project_weight)
    above, below, d_mixed, attention_tiles = barrier((above, below, d_mixed, attention_tiles))
    d_halo = halo_of(above, below, left, right)
    project_tiles = project_sum(cotangent, d_branch, mixed)
    d_halo, project_tiles, d_mixed = barrier((d_halo, project_tiles, d_mixed))
    attention_pair = (attention_tiles, other_core(attention_tiles))
    project_pair = (project_tiles, other_core(project_tiles))
    d_pre, expand_tiles = expand_back(
        d_mixed, d_halo, ring_slope, project_weight, hidden, act_slope, field_in, dkb, extra
    )

    joined = join(core, *attention_pair, *project_pair, expand_tiles, other_core(expand_tiles))
    joined, d_pre = barrier((joined, d_pre))
    terms = exchange(joined)
    grad_in = finish(d_pre, field_in, cotangent, d_branch, expand_weight)
    terms, grad_in = barrier((terms, grad_in))
    sums = exchange(fold(terms))
    *grads, bias_grad = unfold(core, sums, other_core(sums))
    return (grad_in, *grads, bias_grad.transpose(1, 0, 2))


def solution(mesh):
    placed = (P("lat", "lon", None), P("lat", "lon", None), P(), P(), P(), P(), P(), P())
    return jax.shard_map(
        on_device,
        mesh=mesh,
        in_specs=placed,
        out_specs=(P("lat", "lon", None), P(), P(), P(), P(), P(), P()),
        check_vma=False,
    )
```

```python
import functools
import math

import jax
import jax.numpy as jnp
import numpy as np
from jax import lax
from jax.experimental import pallas as pl
from jax.experimental.pallas import tpu as pltpu
from jax.sharding import PartitionSpec as P

EPSILON = 1e-05
GELU_C = math.sqrt(2.0 / math.pi)
F32 = jnp.float32
BF16 = jnp.bfloat16
MIB = 1 << 20

ROWS, COLS, CHAN, EXP = 32, 64, 256, 1024
BLK = 8
STEPS = ROWS // BLK
TOK = BLK * COLS
LANES = 128
EDGE = 40
HALO = 2 * COLS + 2 * EDGE
LONG = 72
JOINED = (64, 56, 128)


def layer_norm(values):
    average = jnp.mean(values, axis=-1, keepdims=True)
    centred = values - average
    variance = jnp.mean(centred * centred, axis=-1, keepdims=True)
    inv_std = lax.rsqrt(variance + EPSILON)
    return (centred * inv_std, inv_std)


def layer_norm_back(normed, inv_std, grads):
    mean_grad = jnp.mean(grads, axis=-1, keepdims=True)
    mean_cross = jnp.mean(grads * normed, axis=-1, keepdims=True)
    return (grads - mean_grad - normed * mean_cross) * inv_std


def gelu(values):
    return values * (0.5 + 0.5 * jnp.tanh(values * (GELU_C + (GELU_C * 0.044715) * (values * values))))


def gelu_slope(values):
    squared = values * values
    tanh_val = jnp.tanh(values * (GELU_C + (GELU_C * 0.044715) * squared))
    gate = 0.5 + 0.5 * tanh_val
    result = values * gate
    slopes = gate + result * (1.0 - gate) * (2.0 * GELU_C + (6.0 * GELU_C * 0.044715) * squared)
    return (result, slopes)


def dot(left, right):
    return lax.dot_general(left, right, (((1,), (0,)), ((), ())), preferred_element_type=F32)


def dot_nt(left, right):
    return lax.dot_general(left, right, (((1,), (1,)), ((), ())), preferred_element_type=F32)


def dot_tn(left, right):
    return lax.dot_general(left, right, (((0,), (0,)), ((), ())), preferred_element_type=F32)


def params(mib):
    return pltpu.CompilerParams(vmem_limit_bytes=mib * MIB)


def whole(shape):
    return pl.BlockSpec(shape, lambda i: (0,) * len(shape))


def band(shape):
    return pl.BlockSpec(shape, lambda i: (i,) + (0,) * (len(shape) - 1))


ROW_BEFORE = pl.BlockSpec(
    (1, COLS, EXP), lambda i: (jnp.maximum(BLK * i - 1, 0), 0, 0)
)
ROW_AFTER = pl.BlockSpec(
    (1, COLS, EXP), lambda i: (jnp.minimum(BLK * i + BLK, ROWS - 1), 0, 0)
)


TILED = (128, 16, 128)


def to_tiles(ref, out_ref, at):
    wide = ref.shape[1] // 128
    for r in range(ref.shape[0] // 16):
        for c in range(wide):
            tile = ref[16 * r : 16 * r + 16, 128 * c : 128 * c + 128]
            out_ref[at + wide * r + c, :16] = tile.astype(BF16)


def expand_body(x_ref, we_ref, out_ref, slopes):
    normed, _ = layer_norm(x_ref[...].reshape(TOK, CHAN).astype(F32))
    normed_b = normed.astype(BF16)
    for at in range(0, EXP, 256):
        pre = dot(normed_b, we_ref[:, at : at + 256])
        result = gelu_slope(pre)[1] if slopes else gelu(pre)
        out_ref[:, :, at : at + 256] = result.astype(BF16).reshape(BLK, COLS, 256)


def expand(x, we, slopes):
    return pl.pallas_call(
        functools.partial(expand_body, slopes=slopes),
        grid=(STEPS,),
        in_specs=[band((BLK, COLS, CHAN)), whole((CHAN, EXP))],
        out_specs=band((BLK, COLS, EXP)),
        out_shape=jax.ShapeDtypeStruct((ROWS, COLS, EXP), BF16),
        compiler_params=params(58),
        cost_estimate=pl.CostEstimate(
            flops=2 * ROWS * COLS * CHAN * EXP, bytes_accessed=6 * MIB, transcendentals=ROWS * COLS * EXP
        ),
        name="expand_slopes" if slopes else "expand",
    )(x, we)


def mixed_slopes_body(pre_ref, slope_ref):
    for at in range(0, EXP, 256):
        span = slice(at, at + 256)
        slope_ref[:, :, span] = gelu_slope(pre_ref[:, :, span].astype(F32))[1].astype(BF16)


def mixed_slopes(pre):
    return pl.pallas_call(
        mixed_slopes_body,
        grid=(STEPS,),
        in_specs=[band((BLK, COLS, EXP))],
        out_specs=band((BLK, COLS, EXP)),
        out_shape=jax.ShapeDtypeStruct((ROWS, COLS, EXP), BF16),
        compiler_params=params(58),
        cost_estimate=pl.CostEstimate(
            flops=20 * ROWS * COLS * EXP, bytes_accessed=8 * MIB, transcendentals=ROWS * COLS * EXP
        ),
        name="mixed_slopes",
    )(pre)


def mix_body(
    cur_ref, before_ref, after_ref,
    above_ref, below_ref, first_ref, last_ref, west_ref, east_ref, own_west_ref, own_east_ref,
    we_ref, dk_ref, wp_ref, x_ref,
    section_ref, mixed_ref, pre_ref, ring_slope_ref,
    top_ref, bottom_ref, left_ref, right_ref,
):
    step = pl.program_id(0)

    @pl.when(step == 0)
    def _():
        ring_body(
            above_ref, below_ref, first_ref, last_ref, west_ref, east_ref, own_west_ref, own_east_ref,
            we_ref, dk_ref,
            top_ref, bottom_ref, left_ref, right_ref, ring_slope_ref,
        )

    first, last = step == 0, step == STEPS - 1
    branch = None
    for at in range(0, EXP, LANES):
        span = slice(at, at + LANES)
        rows = [jnp.where(first, top_ref[:, span], before_ref[0, :, span])]
        rows += [cur_ref[r, :, span] for r in range(BLK)]
        rows += [jnp.where(last, bottom_ref[:, span], after_ref[0, :, span])]
        rows = [row.astype(F32) for row in rows]
        kern = [dk_ref[n, span][None] for n in range(9)]
        for r in range(BLK):
            parts = [
                kern[b] * rows[r] + kern[3 + b] * rows[r + 1] + kern[6 + b] * rows[r + 2]
                for b in range(3)
            ]
            left = left_ref[step, r : r + 1, span]
            right = right_ref[step, r : r + 1, span]
            pre = (
                parts[1]
                + jnp.concatenate([left, parts[0][:-1]], axis=0)
                + jnp.concatenate([parts[2][1:], right], axis=0)
            )
            mixed_ref[r, :, span] = gelu(pre).astype(BF16)
            pre_ref[r, :, span] = pre.astype(BF16)
        if at % 256:
            pair = slice(at - LANES, at + LANES)
            part = dot(mixed_ref[:, :, pair].reshape(TOK, 256), wp_ref[pair, :])
            branch = part if branch is None else branch + part
    section = (x_ref[...].reshape(TOK, CHAN).astype(F32) + branch).astype(BF16)
    section = section.reshape(BLK // 2, 2, 4, 16, CHAN)
    for pair in range(BLK // 2):
        for quad in range(4):
            section_ref[4 * pair + quad] = section[pair, :, quad].reshape(32, CHAN)


def ring_body(
    above_ref, below_ref, first_ref, last_ref, west_ref, east_ref, own_west_ref, own_east_ref,
    we_ref, dk_ref,
    top_ref, bottom_ref, left_ref, right_ref, slope_ref,
):
    west, east = west_ref[...].astype(F32), east_ref[...].astype(F32)
    pad = jnp.zeros((LONG - COLS - 4, CHAN), F32)

    def along(row, at):
        return [
            west[0, at : at + 1], west[1, at : at + 1], row.astype(F32),
            east[0, at : at + 1], east[1, at : at + 1], pad,
        ]

    strips = along(above_ref[0], 0) + along(above_ref[1], 1) + along(first_ref[0], 2)
    strips += along(last_ref[0], 33) + along(below_ref[0], 34) + along(below_ref[1], 35)
    strips += [west[0], west[1], own_west_ref[0].astype(F32)]
    strips += [own_east_ref[1].astype(F32), east[0], east[1]]
    normed, _ = layer_norm(jnp.concatenate(strips, axis=0))
    normed_b = normed.astype(BF16)
    south, lefts, rights = 3 * LONG, 6 * LONG, 6 * LONG + 3 * EDGE
    for at in range(0, EXP, 256):
        span = slice(at, at + 256)
        val = gelu(dot(normed_b, we_ref[:, span])).astype(BF16).astype(F32)
        kern = [dk_ref[n, span][None] for n in range(9)]
        top_ref[:, span] = val[LONG + 2 : LONG + 2 + COLS].astype(BF16)
        bottom_ref[:, span] = val[south + LONG + 2 : south + LONG + 2 + COLS].astype(BF16)
        for ref, base, col in ((left_ref, lefts, 0), (right_ref, rights, 2)):
            total = 0.0
            for a in range(3):
                start = base + EDGE + a + 1
                total = total + kern[3 * a + col] * val[start : start + ROWS]
            for s in range(STEPS):
                ref[s, :BLK, span] = total[BLK * s : BLK * s + BLK]
        for base, out in ((0, 0), (south, COLS)):
            total = 0.0
            for a in range(3):
                for b in range(3):
                    start = base + LONG * a + b + 1
                    total = total + kern[3 * a + b] * val[start : start + COLS]
            slope_ref[out : out + COLS, span] = gelu_slope(total)[1]
        for base, out in ((lefts, 2 * COLS), (rights, 2 * COLS + EDGE)):
            total = 0.0
            for a in range(3):
                for b in range(3):
                    start = base + EDGE * b + a
                    total = total + kern[3 * a + b] * val[start : start + ROWS + 2]
            slope_ref[out : out + ROWS + 2, span] = gelu_slope(total)[1]
            slope_ref[out + ROWS + 2 : out + EDGE, span] = jnp.zeros((EDGE - ROWS - 2, 256), F32)


def mix(hidden, halo, we, dk, wp, x):
    above, below, west, east, own_west, own_east = halo
    wide = jax.ShapeDtypeStruct((ROWS, COLS, EXP), BF16)
    return pl.pallas_call(
        mix_body,
        grid=(STEPS,),
        in_specs=[
            band((BLK, COLS, EXP)), ROW_BEFORE, ROW_AFTER,
            whole((2, COLS, CHAN)), whole((2, COLS, CHAN)),
            pl.BlockSpec((1, COLS, CHAN), lambda i: (0, 0, 0)),
            pl.BlockSpec((1, COLS, CHAN), lambda i: (ROWS - 1, 0, 0)),
            whole((2, EDGE, CHAN)), whole((2, EDGE, CHAN)), whole((2, EDGE, CHAN)), whole((2, EDGE, CHAN)),
            whole((CHAN, EXP)), whole((9, EXP)), whole((EXP, CHAN)), band((BLK, COLS, CHAN)),
        ],
        out_specs=[
            band((2 * BLK, 32, CHAN)), band((BLK, COLS, EXP)), band((BLK, COLS, EXP)), whole((HALO, EXP)),
        ],
        out_shape=[
            jax.ShapeDtypeStruct((64, 32, CHAN), BF16), wide, wide, jax.ShapeDtypeStruct((HALO, EXP), F32),
        ],
        scratch_shapes=[pltpu.VMEM((COLS, EXP), BF16)] * 2 + [pltpu.VMEM((STEPS, 16, EXP), F32)] * 2,
        compiler_params=params(58),
        cost_estimate=pl.CostEstimate(
            flops=3 * ROWS * COLS * CHAN * EXP, bytes_accessed=18 * MIB, transcendentals=2 * ROWS * COLS * EXP
        ),
        name="mix",
    )(
        hidden, hidden, hidden, above, below, x, x, west, east, own_west, own_east,
        we, dk, wp, x,
    )


SWAP = np.zeros((256, 256), np.float32)
for _s in range(16):
    for _g in range(16):
        SWAP[_g * 16 + _s, _s * 16 + _g] = 1.0


def diagonal(full, low):
    halves = []
    for half in range(2):
        lanes = slice(half * 128, half * 128 + 128)
        at = half * 128
        halves.append(jnp.where(low, full[at : at + 64, lanes], full[at + 64 : at + 128, lanes]))
    return jnp.concatenate(halves, axis=1)


def swap(src, dst, swap_ref, n_groups):
    for s in range(0, 64, 16):
        for g in range(0, n_groups, 16):
            moved = dot(swap_ref[...], src[s : s + 16, g : g + 16].reshape(256, CHAN)).astype(BF16)
            dst[g : g + 16, s : s + 16] = moved.reshape(16, 16, CHAN)


def prepare_body(cot_ref, wout_ref, swap_ref, cs_ref, da_ref):
    n_groups = cot_ref.shape[1]
    swap(cot_ref, cs_ref, swap_ref, n_groups)
    for g in range(0, n_groups, 4):
        grads = dot_nt(cs_ref[g : g + 4].reshape(256, CHAN), wout_ref[...])
        da_ref[g : g + 4] = grads.astype(BF16).reshape(4, 64, CHAN)


def prepare(cot, wout, n_groups):
    shape = (64, n_groups, CHAN)
    grouped = (n_groups, 64, CHAN)
    return pl.pallas_call(
        prepare_body,
        grid=(1,),
        in_specs=[whole(shape), whole((CHAN, CHAN)), whole((256, 256))],
        out_specs=[whole(grouped), whole(grouped)],
        out_shape=[jax.ShapeDtypeStruct(grouped, BF16)] * 2,
        compiler_params=params(24),
        cost_estimate=pl.CostEstimate(
            flops=n_groups * 64 * 4 * CHAN * CHAN, bytes_accessed=3 * MIB, transcendentals=0
        ),
        name="prepare",
    )(cot, wout, jnp.asarray(SWAP, BF16))


def attention_body(
    x_ref, da_ref, wqkv_ref, bias_ref, swap_ref,
    out_ref, att_ref, norm_ref, proj_ref, bias_sum_ref, xs_ref, ds_ref,
):
    step = pl.program_id(0)
    n_groups = x_ref.shape[1]

    @pl.when(step == 0)
    def _():
        bias_sum_ref[...] = jnp.zeros_like(bias_sum_ref)
        swap(x_ref, xs_ref, swap_ref, n_groups)

    groups = pl.ds(step * 4, 4)
    tokens = xs_ref[groups].reshape(256, CHAN)
    normed, inv_std = layer_norm(tokens.astype(F32))
    normed_b = normed.astype(BF16)
    norm_ref[...] = normed_b
    projected = dot(normed_b, wqkv_ref[...]).astype(BF16)
    low = lax.broadcasted_iota(jnp.int32, (64, 128), 1) < 64
    keep = [low.astype(F32).astype(BF16), (1.0 - low.astype(F32)).astype(BF16)]
    none = jnp.zeros((128, 128), BF16)

    def by_head(rows):
        blocks = []
        for half in range(2):
            lanes = rows[:, half * 128 : half * 128 + 128]
            pair = jnp.concatenate([lanes * keep[0], lanes * keep[1]], axis=0)
            blocks.append(jnp.concatenate([pair, none] if half == 0 else [none, pair], axis=1))
        return jnp.concatenate(blocks, axis=0)

    four = range(4)
    part = [slice(g * 64, g * 64 + 64) for g in four]
    query = (projected[:, :CHAN].astype(F32) * 0.125).astype(BF16)
    key = [projected[part[g], CHAN : 2 * CHAN] for g in four]
    value = [projected[part[g], 2 * CHAN :] for g in four]
    query_h = [by_head(query[part[g]]) for g in four]
    da_h = [by_head(da_ref[g]) for g in four]
    scores = [dot_nt(key[g], query_h[g]) + bias_ref[...] for g in four]
    d_probs = [dot_nt(value[g], da_h[g]) for g in four]
    tops = [jnp.max(scores[g], axis=0, keepdims=True) for g in four]
    scores = [jnp.exp(scores[g] - tops[g]) for g in four]
    scales = [1.0 / jnp.sum(scores[g], axis=0, keepdims=True) for g in four]
    probs = [scores[g] * scales[g] for g in four]
    probs_b = [probs[g].astype(BF16) for g in four]
    crosses = [jnp.sum(probs[g] * d_probs[g], axis=0, keepdims=True) for g in four]
    d_scores = [probs[g] * (d_probs[g] - crosses[g]) for g in four]
    bias_sum_ref[...] += (d_scores[0] + d_scores[1]) + (d_scores[2] + d_scores[3])
    d_scores_b = [d_scores[g].astype(BF16) for g in four]
    attended = [dot_tn(probs_b[g], value[g]) for g in four]
    d_query = [dot_tn(d_scores_b[g], key[g]) for g in four]
    d_key = [dot(d_scores_b[g], query_h[g]) for g in four]
    d_value = [dot(probs_b[g], da_h[g]) for g in four]
    for g in four:
        att_ref[part[g]] = diagonal(attended[g], low).astype(BF16)
        proj_ref[part[g], :CHAN] = (diagonal(d_query[g], low) * 0.125).astype(BF16)
        proj_ref[part[g], CHAN : 2 * CHAN] = d_key[g].astype(BF16)
        proj_ref[part[g], 2 * CHAN :] = d_value[g].astype(BF16)
    d_normed = dot_nt(proj_ref[...], wqkv_ref[...])
    d_tokens = layer_norm_back(normed, inv_std, d_normed).astype(BF16)
    ds_ref[groups] = d_tokens.reshape(4, 64, CHAN)

    @pl.when(step == n_groups // 4 - 1)
    def _():
        for s in range(0, 64, 16):
            for g in range(0, n_groups, 16):
                tile = ds_ref[g : g + 16, s : s + 16].reshape(256, CHAN)
                moved = dot(swap_ref[...], tile).astype(BF16)
                out_ref[s : s + 16, g : g + 16] = moved.reshape(16, 16, CHAN)


def attention(tokens, d_att, wqkv, bias):
    n_groups = tokens.shape[1]
    shape = (64, n_groups, CHAN)
    flat = n_groups * 64
    return pl.pallas_call(
        attention_body,
        grid=(n_groups // 4,),
        in_specs=[
            whole(shape), band((4, 64, CHAN)), whole((CHAN, 3 * CHAN)), whole((64, CHAN)),
            whole((256, 256)),
        ],
        out_specs=[
            whole(shape), band((256, CHAN)), band((256, CHAN)), band((256, 3 * CHAN)), whole((64, CHAN)),
        ],
        out_shape=[
            jax.ShapeDtypeStruct(shape, BF16),
            jax.ShapeDtypeStruct((flat, CHAN), BF16),
            jax.ShapeDtypeStruct((flat, CHAN), BF16),
            jax.ShapeDtypeStruct((flat, 3 * CHAN), BF16),
            jax.ShapeDtypeStruct((64, CHAN), F32),
        ],
        scratch_shapes=[pltpu.VMEM((n_groups, 64, CHAN), BF16)] * 2,
        compiler_params=params(58),
        cost_estimate=pl.CostEstimate(
            flops=flat * 4 * CHAN * CHAN * 5, bytes_accessed=8 * MIB, transcendentals=flat * 256
        ),
        name="attention",
    )(tokens, d_att, wqkv, bias, jnp.asarray(SWAP, BF16))


def attention_sums_body(att_ref, cot_ref, norm_ref, proj_ref, out_ref, qkv_acc, out_acc):
    step = pl.program_id(0)

    @pl.when(step == 0)
    def _():
        qkv_acc[...] = jnp.zeros_like(qkv_acc)
        out_acc[...] = jnp.zeros_like(out_acc)

    out_acc[...] += dot_tn(att_ref[...], cot_ref[...])
    qkv_acc[...] += dot_tn(norm_ref[...], proj_ref[...])

    @pl.when(step == pl.num_programs(0) - 1)
    def _():
        to_tiles(qkv_acc, out_ref, 0)
        to_tiles(out_acc, out_ref, 96)


def attention_sums(att, cot, normed, proj):
    flat = att.shape[0]
    return pl.pallas_call(
        attention_sums_body,
        grid=(flat // 512,),
        in_specs=[band((512, CHAN)), band((512, CHAN)), band((512, CHAN)), band((512, 3 * CHAN))],
        out_specs=whole(TILED),
        out_shape=jax.ShapeDtypeStruct(TILED, BF16),
        scratch_shapes=[pltpu.VMEM((CHAN, 3 * CHAN), F32), pltpu.VMEM((CHAN, CHAN), F32)],
        compiler_params=params(58),
        cost_estimate=pl.CostEstimate(
            flops=flat * 8 * CHAN * CHAN, bytes_accessed=6 * MIB, transcendentals=0
        ),
        name="attention_sums",
    )(att, cot, normed, proj)


def section_grad(cot_ref, db_ref):
    n_pairs = cot_ref.shape[0] // 2
    pieces = db_ref[...].reshape(n_pairs, 4, 2, 16, CHAN)
    branch = jnp.concatenate(
        [pieces[pair, quad, r] for pair in range(n_pairs) for r in range(2) for quad in range(4)], axis=0
    )
    return cot_ref[...].reshape(-1, CHAN).astype(F32) + branch.astype(F32)


def project_body(cot_ref, db_ref, slope_ref, wp_ref, dm_ref):
    d_section_b = section_grad(cot_ref, db_ref).astype(BF16)
    for at in range(0, EXP, 256):
        grads = dot_nt(d_section_b, wp_ref[at : at + 256, :])
        slope = slope_ref[:, :, at : at + 256].reshape(-1, 256).astype(F32)
        dm_ref[:, :, at : at + 256] = (grads * slope).astype(BF16).reshape(BLK, COLS, 256)


def project_back(cot, db, slope, wp):
    return pl.pallas_call(
        project_body,
        grid=(STEPS,),
        in_specs=[
            band((BLK, COLS, CHAN)), band((2 * BLK, 32, CHAN)), band((BLK, COLS, EXP)), whole((EXP, CHAN)),
        ],
        out_specs=band((BLK, COLS, EXP)),
        out_shape=jax.ShapeDtypeStruct((ROWS, COLS, EXP), BF16),
        compiler_params=params(58),
        cost_estimate=pl.CostEstimate(
            flops=2 * ROWS * COLS * CHAN * EXP, bytes_accessed=10 * MIB, transcendentals=0
        ),
        name="project_back",
    )(cot, db, slope, wp)


def project_sum_body(cot_ref, db_ref, mixed_ref, tiles_ref, sum_ref, turned_ref):
    @pl.when(pl.program_id(0) == 0)
    def _():
        sum_ref[...] = jnp.zeros_like(sum_ref)

    d_section_b = section_grad(cot_ref, db_ref).astype(BF16)
    sum_ref[...] += dot_tn(d_section_b, mixed_ref[...].reshape(-1, EXP))

    @pl.when(pl.program_id(0) == STEPS - 1)
    def _():
        turned_ref[...] = sum_ref[...].T
        to_tiles(turned_ref, tiles_ref, 0)


def project_sum(cot, db, mixed):
    return pl.pallas_call(
        project_sum_body,
        grid=(STEPS,),
        in_specs=[band((BLK, COLS, CHAN)), band((2 * BLK, 32, CHAN)), band((BLK, COLS, EXP))],
        out_specs=whole(TILED),
        out_shape=jax.ShapeDtypeStruct(TILED, BF16),
        scratch_shapes=[pltpu.VMEM((CHAN, EXP), F32), pltpu.VMEM((EXP, CHAN), F32)],
        compiler_params=params(58),
        cost_estimate=pl.CostEstimate(
            flops=2 * ROWS * COLS * CHAN * EXP, bytes_accessed=8 * MIB, transcendentals=0
        ),
        name="project_sum",
    )(cot, db, mixed)


def expand_back_body(
    cur_ref, before_ref, after_ref, halo_ref, halo_slope_ref, wp_ref, hid_ref, slope_ref, x_ref, dkb_ref,
    extra_ref,
    dpre_ref, tiles_ref, top_ref, bottom_ref, left_ref, right_ref, acc_ref, sum_ref, depth_ref, shift_ref,
):
    step = pl.program_id(0)

    @pl.when(step == 0)
    def _():
        sum_ref[...] = jnp.zeros_like(sum_ref)
        acc_ref[...] = jnp.zeros_like(acc_ref)
        for at in range(0, EXP, 256):
            span = slice(at, at + 256)
            grads = dot_nt(halo_ref[...], wp_ref[at : at + 256, :])
            grads = (grads * halo_slope_ref[:, span]).astype(BF16).astype(F32)
            top_ref[:, span] = grads[:COLS]
            bottom_ref[:, span] = grads[COLS : 2 * COLS]
            for ref, base in ((left_ref, 2 * COLS), (right_ref, 2 * COLS + EDGE)):
                for s in range(STEPS):
                    ref[s, : BLK + 2, span] = grads[base + BLK * s : base + BLK * s + BLK + 2]

    normed, _ = layer_norm(x_ref[...].reshape(TOK, CHAN).astype(F32))
    normed_t = normed.T.astype(BF16)
    first, last = step == 0, step == STEPS - 1
    for at in range(0, EXP, LANES):
        span = slice(at, at + LANES)
        rows = [jnp.where(first, top_ref[:, span], before_ref[0, :, span].astype(F32))]
        rows += [cur_ref[r, :, span].astype(F32) for r in range(BLK)]
        rows += [jnp.where(last, bottom_ref[:, span], after_ref[0, :, span].astype(F32))]
        for r in range(BLK + 2):
            left = left_ref[step, r : r + 1, span]
            right = right_ref[step, r : r + 1, span]
            shift_ref[0, r, :, span] = jnp.concatenate([rows[r][1:], right], axis=0)
            shift_ref[1, r, :, span] = rows[r]
            shift_ref[2, r, :, span] = jnp.concatenate([left, rows[r][:-1]], axis=0)
        kern = [dkb_ref[n, :, span] for n in range(9)]
        sums = [acc_ref[n, :, span] for n in range(9)]
        for j in range(0, COLS, 16):
            hid = [hid_ref[r, j : j + 16, span].astype(F32) for r in range(BLK)]
            halves = []
            for low in (0, 8):
                cells = slice(j + low, j + low + 8)
                pieces = [[shift_ref[b, r, cells, span] for b in range(3)] for r in range(BLK + 2)]
                totals = [None] * BLK
                for r in range(BLK):
                    cell = hid[r][low : low + 8]
                    for a in range(3):
                        for b in range(3):
                            n = 3 * a + b
                            piece = pieces[r + 2 - a][b]
                            tap = kern[n] * piece
                            totals[r] = tap if n == 0 else totals[r] + tap
                            sums[n] = sums[n] + cell * piece
                halves.append(totals)
            for r in range(BLK):
                total = jnp.concatenate([halves[0][r], halves[1][r]], axis=0)
                d_pre = total * slope_ref[r, j : j + 16, span].astype(F32)
                dpre_ref[r * COLS + j : r * COLS + j + 16, span] = d_pre.astype(BF16)
        for n in range(9):
            acc_ref[n, :, span] = sums[n]
        if at % 256:
            pair = slice(at - LANES, at + LANES)
            sum_ref[:, pair] += dot(normed_t, dpre_ref[:, pair])

    @pl.when(last)
    def _():
        depth_ref[...] = jnp.sum(acc_ref[...], axis=1)
        to_tiles(sum_ref, tiles_ref, 0)
        first_row = lax.broadcasted_iota(jnp.int32, (8, 128), 0) == 0
        for n in range(128):
            extra = extra_ref[n]
            if n < 72:
                row = depth_ref[n // 8 : n // 8 + 1, 128 * (n % 8) : 128 * (n % 8) + 128]
                extra = jnp.where(first_row, row, extra)
            tiles_ref[n, 16:] = extra.astype(BF16)


def expand_back(d_mixed, halo, halo_slope, wp, hidden, slope, x, dkb, extra):
    tiles = (128, 24, 128)
    cells = band((BLK, COLS, EXP))
    return pl.pallas_call(
        expand_back_body,
        grid=(STEPS,),
        in_specs=[
            cells, ROW_BEFORE, ROW_AFTER, whole((HALO, CHAN)), whole((HALO, EXP)),
            whole((EXP, CHAN)), cells, cells, band((BLK, COLS, CHAN)), whole((9, 8, EXP)),
            whole((128, 8, 128)),
        ],
        out_specs=[band((TOK, EXP)), whole(tiles)],
        out_shape=[
            jax.ShapeDtypeStruct((ROWS * COLS, EXP), BF16),
            jax.ShapeDtypeStruct(tiles, BF16),
        ],
        scratch_shapes=[pltpu.VMEM((COLS, EXP), F32)] * 2
        + [pltpu.VMEM((STEPS, 16, EXP), F32)] * 2
        + [pltpu.VMEM((9, 8, EXP), F32), pltpu.VMEM((CHAN, EXP), F32), pltpu.VMEM((9, EXP), F32)]
        + [pltpu.VMEM((3, BLK + 2, COLS, EXP), F32)],
        compiler_params=params(58),
        cost_estimate=pl.CostEstimate(
            flops=2 * ROWS * COLS * CHAN * EXP, bytes_accessed=20 * MIB, transcendentals=0
        ),
        name="expand_back",
    )(d_mixed, d_mixed, d_mixed, halo, halo_slope, wp, hidden, slope, x, dkb, extra)


def finish_body(dpre_ref, x_ref, cot_ref, db_ref, we_ref, grad_ref):
    normed, inv_std = layer_norm(x_ref[...].reshape(-1, CHAN).astype(F32))
    d_input = layer_norm_back(normed, inv_std, dot_nt(dpre_ref[...], we_ref[...]))
    grad_ref[...] = (section_grad(cot_ref, db_ref) + d_input).astype(BF16).reshape(BLK, COLS, CHAN)


def finish(d_pre, x, cot, db, we):
    return pl.pallas_call(
        finish_body,
        grid=(STEPS,),
        in_specs=[
            band((BLK * COLS, EXP)), band((BLK, COLS, CHAN)), band((BLK, COLS, CHAN)), band((2 * BLK, 32, CHAN)),
            whole((CHAN, EXP)),
        ],
        out_specs=band((BLK, COLS, CHAN)),
        out_shape=jax.ShapeDtypeStruct((ROWS, COLS, CHAN), BF16),
        compiler_params=params(58),
        cost_estimate=pl.CostEstimate(
            flops=2 * ROWS * COLS * CHAN * EXP, bytes_accessed=9 * MIB, transcendentals=0
        ),
        name="finish",
    )(d_pre, x, cot, db, we)


def join_body(core_ref, *refs):
    half = pl.ds(core_ref[0] * 64, 64)
    out_ref = refs[-1]
    at = 0
    for own_ref, other_ref in zip(refs[0:-1:2], refs[1:-1:2]):
        total = own_ref[half].astype(F32) + other_ref[half].astype(F32)
        out_ref[:, at : at + own_ref.shape[1]] = total.astype(BF16)
        at += own_ref.shape[1]


def join(core, *tiles):
    vmem = pl.BlockSpec(memory_space=pltpu.VMEM)
    return pl.pallas_call(
        join_body,
        in_specs=[pl.BlockSpec(memory_space=pltpu.SMEM)] + [vmem] * len(tiles),
        out_shape=jax.ShapeDtypeStruct(JOINED, BF16),
        compiler_params=params(24),
        cost_estimate=pl.CostEstimate(flops=MIB, bytes_accessed=4 * MIB, transcendentals=0),
        name="join",
    )(core, *tiles)


def fold_body(terms_ref, out_ref):
    factor = float(128 * ROWS * COLS) ** (-0.5)
    total = jnp.sum(terms_ref[...].astype(F32), axis=0) * factor
    out_ref[...] = jnp.broadcast_to(total.astype(BF16)[None], out_ref.shape)


def fold(terms):
    return pl.pallas_call(
        fold_body,
        out_shape=jax.ShapeDtypeStruct(terms.shape, BF16),
        compiler_params=params(24),
        cost_estimate=pl.CostEstimate(flops=terms.size, bytes_accessed=2 * terms.size, transcendentals=0),
        name="fold",
    )(terms)


def unfold_body(core_ref, own_ref, other_ref, expand_ref, depth_ref, project_ref, qkv_ref, out_ref, bias_ref):
    first = core_ref[0] == 0

    def tile(n, rows):
        own, other = own_ref[n % 64, rows].astype(F32), other_ref[n % 64, rows].astype(F32)
        return jnp.where(first, own, other) if n < 64 else jnp.where(first, other, own)

    parts = ((qkv_ref, 0, 0), (out_ref, 96, 0), (project_ref, 0, 16), (expand_ref, 0, 32))
    for ref, at, low in parts:
        wide = ref.shape[1] // 128
        for r in range(ref.shape[0] // 16):
            for c in range(wide):
                piece = tile(at + wide * r + c, slice(low, low + 16))
                ref[16 * r : 16 * r + 16, 128 * c : 128 * c + 128] = piece
    for n in range(72):
        extra = tile(n, slice(48, 56))
        at = 128 * (n % 8)
        depth_ref[n // 24, n // 8 % 3 : n // 8 % 3 + 1, at : at + 128] = extra[:1]
        if n < 60:
            bias_ref[n % 15, n // 15 : n // 15 + 1, :] = extra[1:2, :15]


def unfold(core, own, other):
    vmem = pl.BlockSpec(memory_space=pltpu.VMEM)
    return pl.pallas_call(
        unfold_body,
        in_specs=[pl.BlockSpec(memory_space=pltpu.SMEM), vmem, vmem],
        out_shape=[
            jax.ShapeDtypeStruct((CHAN, EXP), F32),
            jax.ShapeDtypeStruct((3, 3, EXP), F32),
            jax.ShapeDtypeStruct((EXP, CHAN), F32),
            jax.ShapeDtypeStruct((CHAN, 3 * CHAN), F32),
            jax.ShapeDtypeStruct((CHAN, CHAN), F32),
            jax.ShapeDtypeStruct((15, 4, 15), F32),
        ],
        compiler_params=params(24),
        cost_estimate=pl.CostEstimate(flops=0, bytes_accessed=5 * MIB, transcendentals=0),
        name="unfold",
    )(core, own, other)


FIRST_CELL = np.zeros((32, 512), np.float32)
LAST_CELL = np.zeros((32, 512), np.float32)
for _row in range(32):
    FIRST_CELL[_row, _row * 16] = 1.0
    LAST_CELL[_row, _row * 16 + 15] = 1.0


def edges_body(
    dt_ref, ct_ref, db_ref, cb_ref, dl_ref, cl_ref, dr_ref, cr_ref, first_ref, last_ref,
    top_ref, bottom_ref, left_ref, right_ref,
):
    def total(d_ref, c_ref):
        return (d_ref[...].astype(F32) + c_ref[...].astype(F32)).astype(BF16)

    top = total(dt_ref, ct_ref)
    bottom = total(db_ref, cb_ref)
    for quad in range(4):
        top_ref[16 * quad : 16 * quad + 16] = top[0, quad, :16]
        bottom_ref[16 * quad : 16 * quad + 16] = bottom[0, quad, 16:]
    left_ref[...] = dot(first_ref[...], total(dl_ref, cl_ref).reshape(512, CHAN)).astype(BF16)
    right_ref[...] = dot(last_ref[...], total(dr_ref, cr_ref).reshape(512, CHAN)).astype(BF16)


def edges(d_branch, cot):
    d_branch, cot = d_branch.reshape(16, 4, 32, CHAN), cot.reshape(16, 4, 32, CHAN)
    specs = []
    for row in (0, 15):
        specs += [pl.BlockSpec((1, 4, 32, CHAN), lambda i, row=row: (row, 0, 0, 0))] * 2
    for col in (0, 3):
        specs += [pl.BlockSpec((16, 1, 32, CHAN), lambda i, col=col: (0, col, 0, 0))] * 2
    return pl.pallas_call(
        edges_body,
        grid=(1,),
        in_specs=specs + [whole((32, 512))] * 2,
        out_specs=[whole((COLS, CHAN))] * 2 + [whole((ROWS, CHAN))] * 2,
        out_shape=[jax.ShapeDtypeStruct((COLS, CHAN), BF16)] * 2
        + [jax.ShapeDtypeStruct((ROWS, CHAN), BF16)] * 2,
        compiler_params=params(24),
        cost_estimate=pl.CostEstimate(flops=MIB, bytes_accessed=2 * MIB, transcendentals=0),
        name="edges",
    )(*([d_branch, cot] * 4), jnp.asarray(FIRST_CELL, BF16), jnp.asarray(LAST_CELL, BF16))


def shifts():
    n_lat, n_lon = lax.axis_size("lat"), lax.axis_size("lon")
    south = [(i, i + 1) for i in range(n_lat - 1)]
    north = [(i + 1, i) for i in range(n_lat - 1)]
    east = [(i, (i + 1) % n_lon) for i in range(n_lon)]
    west = [((i + 1) % n_lon, i) for i in range(n_lon)]
    return (south, north, east, west)


def rows_of(top, bottom):
    south, north, _, _ = shifts()
    return (lax.ppermute(bottom, "lat", south), lax.ppermute(top, "lat", north))


def halo_of(above, below, left, right):
    _, _, east, west = shifts()
    pad = jnp.zeros((EDGE - ROWS - 2, left.shape[1]), left.dtype)
    from_west = lax.ppermute(
        jnp.concatenate([above[-1:], right, below[-1:], pad], axis=0), "lon", east
    )
    from_east = lax.ppermute(
        jnp.concatenate([above[:1], left, below[:1], pad], axis=0), "lon", west
    )
    return jnp.concatenate([above, below, from_west, from_east], axis=0)


def wide_rows(field):
    flat = (2 * COLS, CHAN)
    above, below = rows_of(field[:2].reshape(flat), field[-2:].reshape(flat))
    return (above.reshape(2, COLS, CHAN), below.reshape(2, COLS, CHAN))


def wide_columns(field, above, below):
    _, _, east, west = shifts()
    pad = jnp.zeros((2, EDGE - ROWS - 4, field.shape[2]), field.dtype)

    def columns(at):
        parts = [part[:, at : at + 2].transpose(1, 0, 2) for part in (above, field, below)]
        return jnp.concatenate(parts + [pad], axis=1)

    own_west, own_east = columns(0), columns(COLS - 2)
    from_west = lax.ppermute(own_east, "lon", east)
    from_east = lax.ppermute(own_west, "lon", west)
    return (from_west, from_east, own_west, own_east)


def members():
    n_lat, n_lon = lax.axis_size("lat"), lax.axis_size("lon")
    order = np.arange(n_lat * n_lon).reshape(n_lat, n_lon // 2, 2)
    return order.transpose(2, 0, 1).reshape(2, -1).tolist()


def exchange(pieces):
    return lax.all_to_all(
        pieces, ("lat", "lon"), split_axis=0, concat_axis=0, axis_index_groups=members(), tiled=True
    )


def to_pieces(field):
    shaped = field.reshape(16, 2, 4, 16, CHAN).transpose(0, 2, 1, 3, 4)
    return shaped.reshape(64, 32, CHAN)


def pairs():
    return np.arange(lax.axis_size("lon")).reshape(-1, 2).tolist()


def other_core(tiles):
    swaps = [move for a, b in pairs() for move in ((a, b), (b, a))]
    return lax.ppermute(tiles, "lon", swaps)


def rel_table():
    position = np.arange(64)
    pos_row, pos_col = position // 8, position % 8
    rel_index = (pos_row[:, None] - pos_row[None, :] + 7) * 15 + (
        pos_col[:, None] - pos_col[None, :] + 7
    )
    return jnp.asarray(rel_index)[:, :, None] == jnp.arange(225)[None, None, :]


def on_device(
    field_in, cotangent, expand_weight, depth_kernel, project_weight, qkv_weight, out_weight, rel_bias
):
    onehot = rel_table().astype(F32)
    bias = jnp.einsum(
        "tsr,hr->sht", onehot, rel_bias.reshape(4, 225), precision=lax.Precision.HIGHEST
    ).reshape(64, 256)
    dk = depth_kernel.reshape(9, EXP)

    dkb = jnp.broadcast_to(dk[:, None], (9, 8, EXP))
    core = lax.axis_index("lon").astype(jnp.int32).reshape(1) & 1
    barrier = lax.optimization_barrier

    above, below = wide_rows(field_in)
    hidden = expand(field_in, expand_weight, False)
    above, below, hidden, late_cot = barrier((above, below, hidden, cotangent))
    field_halo = (above, below, *wide_columns(field_in, above, below))
    field_halo, cot_pieces = barrier((field_halo, to_pieces(late_cot)))
    hidden, cot_pieces = barrier((hidden, cot_pieces))
    cot_groups = exchange(cot_pieces)
    section, mixed, mixed_pre, ring_slope = mix(
        hidden, field_halo, expand_weight, dk, project_weight, field_in
    )
    groups = exchange(section)
    cot_swapped, d_att = prepare(cot_groups, out_weight, 32)
    section_field, _ = barrier((field_in, section))
    act_slope = expand(section_field, expand_weight, True)
    groups, bias, d_att, act_slope = barrier((groups, bias, d_att, act_slope))
    d_groups, attended, normed2, d_proj, bias_acc = attention(groups, d_att, qkv_weight, bias)

    d_branch = exchange(d_groups)
    attention_tiles = attention_sums(attended, cot_swapped.reshape(-1, CHAN), normed2, d_proj)
    bias_sum = jnp.einsum(
        "sht,tsr->hr", bias_acc.reshape(64, 4, 64), onehot, precision=lax.Precision.HIGHEST
    )
    extra = jnp.pad(bias_sum.reshape(60, 1, 15), ((0, 68), (1, 6), (0, 113)))
    mixed_pre, _ = barrier((mixed_pre, d_groups))
    mixed_slope = mixed_slopes(mixed_pre)
    d_branch, attention_tiles, extra, mixed_slope = barrier((d_branch, attention_tiles, extra, mixed_slope))

    top, bottom, left, right = edges(d_branch, cot_pieces)
    above, below = rows_of(top, bottom)
    project_tiles = project_sum(cotangent, d_branch, mixed)
    above, below, project_tiles, attention_tiles, mixed_slope = barrier(
        (above, below, project_tiles, attention_tiles, mixed_slope)
    )
    d_halo = halo_of(above, below, left, right)
    attention_other, project_other = other_core(attention_tiles), other_core(project_tiles)
    d_mixed = project_back(cotangent, d_branch, mixed_slope, project_weight)
    d_halo, d_mixed, attention_other, project_other = barrier(
        (d_halo, d_mixed, attention_other, project_other)
    )
    attention_pair = (attention_tiles, attention_other)
    project_pair = (project_tiles, project_other)
    d_pre, expand_tiles = expand_back(
        d_mixed, d_halo, ring_slope, project_weight, hidden, act_slope, field_in, dkb, extra
    )

    joined = join(core, *attention_pair, *project_pair, expand_tiles, other_core(expand_tiles))
    joined, d_pre = barrier((joined, d_pre))
    terms = exchange(joined)
    grad_in = finish(d_pre, field_in, cotangent, d_branch, expand_weight)
    terms, grad_in = barrier((terms, grad_in))
    sums = exchange(fold(terms))
    *grads, bias_grad = unfold(core, sums, other_core(sums))
    return (grad_in, *grads, bias_grad.transpose(1, 0, 2))


def solution(mesh):
    placed = (P("lat", "lon", None), P("lat", "lon", None), P(), P(), P(), P(), P(), P())
    return jax.shard_map(
        on_device,
        mesh=mesh,
        in_specs=placed,
        out_specs=(P("lat", "lon", None), P(), P(), P(), P(), P(), P()),
        check_vma=False,
    )
```

```python
import functools
import math

import jax
import jax.numpy as jnp
import numpy as np
from jax import lax
from jax.experimental import pallas as pl
from jax.experimental.pallas import tpu as pltpu
from jax.sharding import PartitionSpec as P

EPSILON = 1e-05
GELU_C = math.sqrt(2.0 / math.pi)
F32 = jnp.float32
BF16 = jnp.bfloat16
MIB = 1 << 20

ROWS, COLS, CHAN, EXP = 32, 64, 256, 1024
BLK = 8
STEPS = ROWS // BLK
TOK = BLK * COLS
LANES = 128
EDGE = 40
HALO = 2 * COLS + 2 * EDGE
LONG = 72
AT_ONCE = 8
JOINED = (64, 56, 128)


def layer_norm(values):
    average = jnp.mean(values, axis=-1, keepdims=True)
    centred = values - average
    variance = jnp.mean(centred * centred, axis=-1, keepdims=True)
    inv_std = lax.rsqrt(variance + EPSILON)
    return (centred * inv_std, inv_std)


def layer_norm_back(normed, inv_std, grads):
    mean_grad = jnp.mean(grads, axis=-1, keepdims=True)
    mean_cross = jnp.mean(grads * normed, axis=-1, keepdims=True)
    return (grads - mean_grad - normed * mean_cross) * inv_std


def gelu(values):
    return values * (0.5 + 0.5 * jnp.tanh(values * (GELU_C + (GELU_C * 0.044715) * (values * values))))


def gelu_slope(values):
    squared = values * values
    tanh_val = jnp.tanh(values * (GELU_C + (GELU_C * 0.044715) * squared))
    gate = 0.5 + 0.5 * tanh_val
    result = values * gate
    slopes = gate + result * (1.0 - gate) * (2.0 * GELU_C + (6.0 * GELU_C * 0.044715) * squared)
    return (result, slopes)


def dot(left, right):
    return lax.dot_general(left, right, (((1,), (0,)), ((), ())), preferred_element_type=F32)


def dot_nt(left, right):
    return lax.dot_general(left, right, (((1,), (1,)), ((), ())), preferred_element_type=F32)


def dot_tn(left, right):
    return lax.dot_general(left, right, (((0,), (0,)), ((), ())), preferred_element_type=F32)


def params(mib):
    return pltpu.CompilerParams(vmem_limit_bytes=mib * MIB)


def whole(shape):
    return pl.BlockSpec(shape, lambda i: (0,) * len(shape))


def band(shape):
    return pl.BlockSpec(shape, lambda i: (i,) + (0,) * (len(shape) - 1))


ROW_BEFORE = pl.BlockSpec(
    (1, COLS, EXP), lambda i: (jnp.maximum(BLK * i - 1, 0), 0, 0)
)
ROW_AFTER = pl.BlockSpec(
    (1, COLS, EXP), lambda i: (jnp.minimum(BLK * i + BLK, ROWS - 1), 0, 0)
)


TILED = (128, 16, 128)


def to_tiles(ref, out_ref, at):
    wide = ref.shape[1] // 128
    for r in range(ref.shape[0] // 16):
        for c in range(wide):
            tile = ref[16 * r : 16 * r + 16, 128 * c : 128 * c + 128]
            out_ref[at + wide * r + c, :16] = tile.astype(BF16)


def expand_body(x_ref, we_ref, out_ref, slopes):
    normed, _ = layer_norm(x_ref[...].reshape(TOK, CHAN).astype(F32))
    normed_b = normed.astype(BF16)
    for at in range(0, EXP, 256):
        pre = dot(normed_b, we_ref[:, at : at + 256])
        result = gelu_slope(pre)[1] if slopes else gelu(pre)
        out_ref[:, :, at : at + 256] = result.astype(BF16).reshape(BLK, COLS, 256)


def expand(x, we, slopes):
    return pl.pallas_call(
        functools.partial(expand_body, slopes=slopes),
        grid=(STEPS,),
        in_specs=[band((BLK, COLS, CHAN)), whole((CHAN, EXP))],
        out_specs=band((BLK, COLS, EXP)),
        out_shape=jax.ShapeDtypeStruct((ROWS, COLS, EXP), BF16),
        compiler_params=params(58),
        cost_estimate=pl.CostEstimate(
            flops=2 * ROWS * COLS * CHAN * EXP, bytes_accessed=6 * MIB, transcendentals=ROWS * COLS * EXP
        ),
        name="expand_slopes" if slopes else "expand",
    )(x, we)


def mixed_slopes_body(pre_ref, slope_ref):
    for at in range(0, EXP, 256):
        span = slice(at, at + 256)
        slope_ref[:, :, span] = gelu_slope(pre_ref[:, :, span].astype(F32))[1].astype(BF16)


def mixed_slopes(pre):
    return pl.pallas_call(
        mixed_slopes_body,
        grid=(STEPS,),
        in_specs=[band((BLK, COLS, EXP))],
        out_specs=band((BLK, COLS, EXP)),
        out_shape=jax.ShapeDtypeStruct((ROWS, COLS, EXP), BF16),
        compiler_params=params(58),
        cost_estimate=pl.CostEstimate(
            flops=20 * ROWS * COLS * EXP, bytes_accessed=8 * MIB, transcendentals=ROWS * COLS * EXP
        ),
        name="mixed_slopes",
    )(pre)


def mix_body(
    cur_ref, before_ref, after_ref,
    above_ref, below_ref, first_ref, last_ref, west_ref, east_ref, own_west_ref, own_east_ref,
    we_ref, dk_ref, wp_ref, x_ref,
    section_ref, mixed_ref, pre_ref, ring_slope_ref,
    top_ref, bottom_ref, left_ref, right_ref,
):
    step = pl.program_id(0)

    @pl.when(step == 0)
    def _():
        ring_body(
            above_ref, below_ref, first_ref, last_ref, west_ref, east_ref, own_west_ref, own_east_ref,
            we_ref, dk_ref,
            top_ref, bottom_ref, left_ref, right_ref, ring_slope_ref,
        )

    first, last = step == 0, step == STEPS - 1
    branch = None
    for at in range(0, EXP, LANES):
        span = slice(at, at + LANES)
        rows = [jnp.where(first, top_ref[:, span], before_ref[0, :, span])]
        rows += [cur_ref[r, :, span] for r in range(BLK)]
        rows += [jnp.where(last, bottom_ref[:, span], after_ref[0, :, span])]
        rows = [row.astype(F32) for row in rows]
        kern = [dk_ref[n, span][None] for n in range(9)]
        for r in range(BLK):
            parts = [
                kern[b] * rows[r] + kern[3 + b] * rows[r + 1] + kern[6 + b] * rows[r + 2]
                for b in range(3)
            ]
            left = left_ref[step, r : r + 1, span]
            right = right_ref[step, r : r + 1, span]
            pre = (
                parts[1]
                + jnp.concatenate([left, parts[0][:-1]], axis=0)
                + jnp.concatenate([parts[2][1:], right], axis=0)
            )
            mixed_ref[r, :, span] = gelu(pre).astype(BF16)
            pre_ref[r, :, span] = pre.astype(BF16)
        if at % 256:
            pair = slice(at - LANES, at + LANES)
            part = dot(mixed_ref[:, :, pair].reshape(TOK, 256), wp_ref[pair, :])
            branch = part if branch is None else branch + part
    section = (x_ref[...].reshape(TOK, CHAN).astype(F32) + branch).astype(BF16)
    section = section.reshape(BLK // 2, 2, 4, 16, CHAN)
    for pair in range(BLK // 2):
        for quad in range(4):
            section_ref[4 * pair + quad] = section[pair, :, quad].reshape(32, CHAN)


def ring_body(
    above_ref, below_ref, first_ref, last_ref, west_ref, east_ref, own_west_ref, own_east_ref,
    we_ref, dk_ref,
    top_ref, bottom_ref, left_ref, right_ref, slope_ref,
):
    west, east = west_ref[...].astype(F32), east_ref[...].astype(F32)
    pad = jnp.zeros((LONG - COLS - 4, CHAN), F32)

    def along(row, at):
        return [
            west[0, at : at + 1], west[1, at : at + 1], row.astype(F32),
            east[0, at : at + 1], east[1, at : at + 1], pad,
        ]

    strips = along(above_ref[0], 0) + along(above_ref[1], 1) + along(first_ref[0], 2)
    strips += along(last_ref[0], 33) + along(below_ref[0], 34) + along(below_ref[1], 35)
    strips += [west[0], west[1], own_west_ref[0].astype(F32)]
    strips += [own_east_ref[1].astype(F32), east[0], east[1]]
    normed, _ = layer_norm(jnp.concatenate(strips, axis=0))
    normed_b = normed.astype(BF16)
    south, lefts, rights = 3 * LONG, 6 * LONG, 6 * LONG + 3 * EDGE
    for at in range(0, EXP, 256):
        span = slice(at, at + 256)
        val = gelu(dot(normed_b, we_ref[:, span])).astype(BF16).astype(F32)
        kern = [dk_ref[n, span][None] for n in range(9)]
        top_ref[:, span] = val[LONG + 2 : LONG + 2 + COLS].astype(BF16)
        bottom_ref[:, span] = val[south + LONG + 2 : south + LONG + 2 + COLS].astype(BF16)
        for ref, base, col in ((left_ref, lefts, 0), (right_ref, rights, 2)):
            total = 0.0
            for a in range(3):
                start = base + EDGE + a + 1
                total = total + kern[3 * a + col] * val[start : start + ROWS]
            for s in range(STEPS):
                ref[s, :BLK, span] = total[BLK * s : BLK * s + BLK]
        for base, out in ((0, 0), (south, COLS)):
            total = 0.0
            for a in range(3):
                for b in range(3):
                    start = base + LONG * a + b + 1
                    total = total + kern[3 * a + b] * val[start : start + COLS]
            slope_ref[out : out + COLS, span] = gelu_slope(total)[1]
        for base, out in ((lefts, 2 * COLS), (rights, 2 * COLS + EDGE)):
            total = 0.0
            for a in range(3):
                for b in range(3):
                    start = base + EDGE * b + a
                    total = total + kern[3 * a + b] * val[start : start + ROWS + 2]
            slope_ref[out : out + ROWS + 2, span] = gelu_slope(total)[1]
            slope_ref[out + ROWS + 2 : out + EDGE, span] = jnp.zeros((EDGE - ROWS - 2, 256), F32)


def mix(hidden, halo, we, dk, wp, x):
    above, below, west, east, own_west, own_east = halo
    wide = jax.ShapeDtypeStruct((ROWS, COLS, EXP), BF16)
    return pl.pallas_call(
        mix_body,
        grid=(STEPS,),
        in_specs=[
            band((BLK, COLS, EXP)), ROW_BEFORE, ROW_AFTER,
            whole((2, COLS, CHAN)), whole((2, COLS, CHAN)),
            pl.BlockSpec((1, COLS, CHAN), lambda i: (0, 0, 0)),
            pl.BlockSpec((1, COLS, CHAN), lambda i: (ROWS - 1, 0, 0)),
            whole((2, EDGE, CHAN)), whole((2, EDGE, CHAN)), whole((2, EDGE, CHAN)), whole((2, EDGE, CHAN)),
            whole((CHAN, EXP)), whole((9, EXP)), whole((EXP, CHAN)), band((BLK, COLS, CHAN)),
        ],
        out_specs=[
            band((2 * BLK, 32, CHAN)), band((BLK, COLS, EXP)), band((BLK, COLS, EXP)), whole((HALO, EXP)),
        ],
        out_shape=[
            jax.ShapeDtypeStruct((64, 32, CHAN), BF16), wide, wide, jax.ShapeDtypeStruct((HALO, EXP), F32),
        ],
        scratch_shapes=[pltpu.VMEM((COLS, EXP), BF16)] * 2 + [pltpu.VMEM((STEPS, 16, EXP), F32)] * 2,
        compiler_params=params(58),
        cost_estimate=pl.CostEstimate(
            flops=3 * ROWS * COLS * CHAN * EXP, bytes_accessed=18 * MIB, transcendentals=2 * ROWS * COLS * EXP
        ),
        name="mix",
    )(
        hidden, hidden, hidden, above, below, x, x, west, east, own_west, own_east,
        we, dk, wp, x,
    )


SWAP = np.zeros((256, 256), np.float32)
for _s in range(16):
    for _g in range(16):
        SWAP[_g * 16 + _s, _s * 16 + _g] = 1.0


def diagonal(full, low):
    halves = []
    for half in range(2):
        lanes = slice(half * 128, half * 128 + 128)
        at = half * 128
        halves.append(jnp.where(low, full[at : at + 64, lanes], full[at + 64 : at + 128, lanes]))
    return jnp.concatenate(halves, axis=1)


def swap(src, dst, swap_ref, n_groups):
    for s in range(0, 64, 16):
        for g in range(0, n_groups, 16):
            moved = dot(swap_ref[...], src[s : s + 16, g : g + 16].reshape(256, CHAN)).astype(BF16)
            dst[g : g + 16, s : s + 16] = moved.reshape(16, 16, CHAN)


def prepare_body(cot_ref, wout_ref, swap_ref, cs_ref, da_ref):
    n_groups = cot_ref.shape[1]
    swap(cot_ref, cs_ref, swap_ref, n_groups)
    for g in range(0, n_groups, 4):
        grads = dot_nt(cs_ref[g : g + 4].reshape(256, CHAN), wout_ref[...])
        da_ref[g : g + 4] = grads.astype(BF16).reshape(4, 64, CHAN)


def prepare(cot, wout, n_groups):
    shape = (64, n_groups, CHAN)
    grouped = (n_groups, 64, CHAN)
    return pl.pallas_call(
        prepare_body,
        grid=(1,),
        in_specs=[whole(shape), whole((CHAN, CHAN)), whole((256, 256))],
        out_specs=[whole(grouped), whole(grouped)],
        out_shape=[jax.ShapeDtypeStruct(grouped, BF16)] * 2,
        compiler_params=params(24),
        cost_estimate=pl.CostEstimate(
            flops=n_groups * 64 * 4 * CHAN * CHAN, bytes_accessed=3 * MIB, transcendentals=0
        ),
        name="prepare",
    )(cot, wout, jnp.asarray(SWAP, BF16))


def attention_body(
    x_ref, da_ref, wqkv_ref, bias_ref, swap_ref,
    out_ref, att_ref, norm_ref, proj_ref, bias_sum_ref, xs_ref, ds_ref,
):
    step = pl.program_id(0)
    n_groups = x_ref.shape[1]

    @pl.when(step == 0)
    def _():
        bias_sum_ref[...] = jnp.zeros_like(bias_sum_ref)
        swap(x_ref, xs_ref, swap_ref, n_groups)

    groups = pl.ds(step * AT_ONCE, AT_ONCE)
    tokens = xs_ref[groups].reshape(AT_ONCE * 64, CHAN)
    normed, inv_std = layer_norm(tokens.astype(F32))
    normed_b = normed.astype(BF16)
    norm_ref[...] = normed_b
    projected = dot(normed_b, wqkv_ref[...]).astype(BF16)
    low = lax.broadcasted_iota(jnp.int32, (64, 128), 1) < 64
    keep = [low.astype(F32).astype(BF16), (1.0 - low.astype(F32)).astype(BF16)]
    none = jnp.zeros((128, 128), BF16)

    def by_head(rows):
        blocks = []
        for half in range(2):
            lanes = rows[:, half * 128 : half * 128 + 128]
            pair = jnp.concatenate([lanes * keep[0], lanes * keep[1]], axis=0)
            blocks.append(jnp.concatenate([pair, none] if half == 0 else [none, pair], axis=1))
        return jnp.concatenate(blocks, axis=0)

    batch = range(AT_ONCE)
    part = [slice(g * 64, g * 64 + 64) for g in batch]
    query = (projected[:, :CHAN].astype(F32) * 0.125).astype(BF16)
    key = [projected[part[g], CHAN : 2 * CHAN] for g in batch]
    value = [projected[part[g], 2 * CHAN :] for g in batch]
    query_h = [by_head(query[part[g]]) for g in batch]
    da_h = [by_head(da_ref[g]) for g in batch]
    scores = [dot_nt(key[g], query_h[g]) + bias_ref[...] for g in batch]
    d_probs = [dot_nt(value[g], da_h[g]) for g in batch]
    tops = [jnp.max(scores[g], axis=0, keepdims=True) for g in batch]
    scores = [jnp.exp(scores[g] - tops[g]) for g in batch]
    scales = [1.0 / jnp.sum(scores[g], axis=0, keepdims=True) for g in batch]
    probs = [scores[g] * scales[g] for g in batch]
    probs_b = [probs[g].astype(BF16) for g in batch]
    crosses = [jnp.sum(probs[g] * d_probs[g], axis=0, keepdims=True) for g in batch]
    d_scores = [probs[g] * (d_probs[g] - crosses[g]) for g in batch]
    bias_sum_ref[...] += sum(d_scores[1:], d_scores[0])
    d_scores_b = [d_scores[g].astype(BF16) for g in batch]
    attended = [dot_tn(probs_b[g], value[g]) for g in batch]
    d_query = [dot_tn(d_scores_b[g], key[g]) for g in batch]
    d_key = [dot(d_scores_b[g], query_h[g]) for g in batch]
    d_value = [dot(probs_b[g], da_h[g]) for g in batch]
    for g in batch:
        att_ref[part[g]] = diagonal(attended[g], low).astype(BF16)
        proj_ref[part[g], :CHAN] = (diagonal(d_query[g], low) * 0.125).astype(BF16)
        proj_ref[part[g], CHAN : 2 * CHAN] = d_key[g].astype(BF16)
        proj_ref[part[g], 2 * CHAN :] = d_value[g].astype(BF16)
    d_normed = dot_nt(proj_ref[...], wqkv_ref[...])
    d_tokens = layer_norm_back(normed, inv_std, d_normed).astype(BF16)
    ds_ref[groups] = d_tokens.reshape(AT_ONCE, 64, CHAN)

    @pl.when(step == n_groups // AT_ONCE - 1)
    def _():
        for s in range(0, 64, 16):
            for g in range(0, n_groups, 16):
                tile = ds_ref[g : g + 16, s : s + 16].reshape(256, CHAN)
                moved = dot(swap_ref[...], tile).astype(BF16)
                out_ref[s : s + 16, g : g + 16] = moved.reshape(16, 16, CHAN)


def attention(tokens, d_att, wqkv, bias):
    n_groups = tokens.shape[1]
    shape = (64, n_groups, CHAN)
    flat = n_groups * 64
    return pl.pallas_call(
        attention_body,
        grid=(n_groups // AT_ONCE,),
        in_specs=[
            whole(shape), band((AT_ONCE, 64, CHAN)), whole((CHAN, 3 * CHAN)), whole((64, CHAN)),
            whole((256, 256)),
        ],
        out_specs=[
            whole(shape), band((AT_ONCE * 64, CHAN)), band((AT_ONCE * 64, CHAN)),
            band((AT_ONCE * 64, 3 * CHAN)), whole((64, CHAN)),
        ],
        out_shape=[
            jax.ShapeDtypeStruct(shape, BF16),
            jax.ShapeDtypeStruct((flat, CHAN), BF16),
            jax.ShapeDtypeStruct((flat, CHAN), BF16),
            jax.ShapeDtypeStruct((flat, 3 * CHAN), BF16),
            jax.ShapeDtypeStruct((64, CHAN), F32),
        ],
        scratch_shapes=[pltpu.VMEM((n_groups, 64, CHAN), BF16)] * 2,
        compiler_params=params(58),
        cost_estimate=pl.CostEstimate(
            flops=flat * 4 * CHAN * CHAN * 5, bytes_accessed=8 * MIB, transcendentals=flat * 256
        ),
        name="attention",
    )(tokens, d_att, wqkv, bias, jnp.asarray(SWAP, BF16))


def attention_sums_body(att_ref, cot_ref, norm_ref, proj_ref, out_ref, qkv_acc, out_acc):
    step = pl.program_id(0)

    @pl.when(step == 0)
    def _():
        qkv_acc[...] = jnp.zeros_like(qkv_acc)
        out_acc[...] = jnp.zeros_like(out_acc)

    out_acc[...] += dot_tn(att_ref[...], cot_ref[...])
    qkv_acc[...] += dot_tn(norm_ref[...], proj_ref[...])

    @pl.when(step == pl.num_programs(0) - 1)
    def _():
        to_tiles(qkv_acc, out_ref, 0)
        to_tiles(out_acc, out_ref, 96)


def attention_sums(att, cot, normed, proj):
    flat = att.shape[0]
    return pl.pallas_call(
        attention_sums_body,
        grid=(flat // 512,),
        in_specs=[band((512, CHAN)), band((512, CHAN)), band((512, CHAN)), band((512, 3 * CHAN))],
        out_specs=whole(TILED),
        out_shape=jax.ShapeDtypeStruct(TILED, BF16),
        scratch_shapes=[pltpu.VMEM((CHAN, 3 * CHAN), F32), pltpu.VMEM((CHAN, CHAN), F32)],
        compiler_params=params(58),
        cost_estimate=pl.CostEstimate(
            flops=flat * 8 * CHAN * CHAN, bytes_accessed=6 * MIB, transcendentals=0
        ),
        name="attention_sums",
    )(att, cot, normed, proj)


def section_grad(cot_ref, db_ref):
    n_pairs = cot_ref.shape[0] // 2
    pieces = db_ref[...].reshape(n_pairs, 4, 2, 16, CHAN)
    branch = jnp.concatenate(
        [pieces[pair, quad, r] for pair in range(n_pairs) for r in range(2) for quad in range(4)], axis=0
    )
    return cot_ref[...].reshape(-1, CHAN).astype(F32) + branch.astype(F32)


def project_body(cot_ref, db_ref, slope_ref, wp_ref, dm_ref):
    d_section_b = section_grad(cot_ref, db_ref).astype(BF16)
    for at in range(0, EXP, 256):
        grads = dot_nt(d_section_b, wp_ref[at : at + 256, :])
        slope = slope_ref[:, :, at : at + 256].reshape(-1, 256).astype(F32)
        dm_ref[:, :, at : at + 256] = (grads * slope).astype(BF16).reshape(BLK, COLS, 256)


def project_back(cot, db, slope, wp):
    return pl.pallas_call(
        project_body,
        grid=(STEPS,),
        in_specs=[
            band((BLK, COLS, CHAN)), band((2 * BLK, 32, CHAN)), band((BLK, COLS, EXP)), whole((EXP, CHAN)),
        ],
        out_specs=band((BLK, COLS, EXP)),
        out_shape=jax.ShapeDtypeStruct((ROWS, COLS, EXP), BF16),
        compiler_params=params(58),
        cost_estimate=pl.CostEstimate(
            flops=2 * ROWS * COLS * CHAN * EXP, bytes_accessed=10 * MIB, transcendentals=0
        ),
        name="project_back",
    )(cot, db, slope, wp)


def project_sum_body(cot_ref, db_ref, mixed_ref, tiles_ref, sum_ref, turned_ref):
    @pl.when(pl.program_id(0) == 0)
    def _():
        sum_ref[...] = jnp.zeros_like(sum_ref)

    d_section_b = section_grad(cot_ref, db_ref).astype(BF16)
    sum_ref[...] += dot_tn(d_section_b, mixed_ref[...].reshape(-1, EXP))

    @pl.when(pl.program_id(0) == STEPS - 1)
    def _():
        turned_ref[...] = sum_ref[...].T
        to_tiles(turned_ref, tiles_ref, 0)


def project_sum(cot, db, mixed):
    return pl.pallas_call(
        project_sum_body,
        grid=(STEPS,),
        in_specs=[band((BLK, COLS, CHAN)), band((2 * BLK, 32, CHAN)), band((BLK, COLS, EXP))],
        out_specs=whole(TILED),
        out_shape=jax.ShapeDtypeStruct(TILED, BF16),
        scratch_shapes=[pltpu.VMEM((CHAN, EXP), F32), pltpu.VMEM((EXP, CHAN), F32)],
        compiler_params=params(58),
        cost_estimate=pl.CostEstimate(
            flops=2 * ROWS * COLS * CHAN * EXP, bytes_accessed=8 * MIB, transcendentals=0
        ),
        name="project_sum",
    )(cot, db, mixed)


def expand_back_body(
    cur_ref, before_ref, after_ref, halo_ref, halo_slope_ref, wp_ref, hid_ref, slope_ref, x_ref, dkb_ref,
    extra_ref,
    dpre_ref, tiles_ref, top_ref, bottom_ref, left_ref, right_ref, acc_ref, sum_ref, depth_ref, shift_ref,
):
    step = pl.program_id(0)

    @pl.when(step == 0)
    def _():
        sum_ref[...] = jnp.zeros_like(sum_ref)
        acc_ref[...] = jnp.zeros_like(acc_ref)
        for at in range(0, EXP, 256):
            span = slice(at, at + 256)
            grads = dot_nt(halo_ref[...], wp_ref[at : at + 256, :])
            grads = (grads * halo_slope_ref[:, span]).astype(BF16).astype(F32)
            top_ref[:, span] = grads[:COLS]
            bottom_ref[:, span] = grads[COLS : 2 * COLS]
            for ref, base in ((left_ref, 2 * COLS), (right_ref, 2 * COLS + EDGE)):
                for s in range(STEPS):
                    ref[s, : BLK + 2, span] = grads[base + BLK * s : base + BLK * s + BLK + 2]

    normed, _ = layer_norm(x_ref[...].reshape(TOK, CHAN).astype(F32))
    normed_t = normed.T.astype(BF16)
    first, last = step == 0, step == STEPS - 1
    for at in range(0, EXP, LANES):
        span = slice(at, at + LANES)
        rows = [jnp.where(first, top_ref[:, span], before_ref[0, :, span].astype(F32))]
        rows += [cur_ref[r, :, span].astype(F32) for r in range(BLK)]
        rows += [jnp.where(last, bottom_ref[:, span], after_ref[0, :, span].astype(F32))]
        for r in range(BLK + 2):
            left = left_ref[step, r : r + 1, span]
            right = right_ref[step, r : r + 1, span]
            shift_ref[0, r, :, span] = jnp.concatenate([rows[r][1:], right], axis=0)
            shift_ref[1, r, :, span] = rows[r]
            shift_ref[2, r, :, span] = jnp.concatenate([left, rows[r][:-1]], axis=0)
        kern = [dkb_ref[n, :, span] for n in range(9)]
        sums = [acc_ref[n, :, span] for n in range(9)]
        for j in range(0, COLS, 16):
            hid = [hid_ref[r, j : j + 16, span].astype(F32) for r in range(BLK)]
            halves = []
            for low in (0, 8):
                cells = slice(j + low, j + low + 8)
                pieces = [[shift_ref[b, r, cells, span] for b in range(3)] for r in range(BLK + 2)]
                totals = [None] * BLK
                for r in range(BLK):
                    cell = hid[r][low : low + 8]
                    for a in range(3):
                        for b in range(3):
                            n = 3 * a + b
                            piece = pieces[r + 2 - a][b]
                            tap = kern[n] * piece
                            totals[r] = tap if n == 0 else totals[r] + tap
                            sums[n] = sums[n] + cell * piece
                halves.append(totals)
            for r in range(BLK):
                total = jnp.concatenate([halves[0][r], halves[1][r]], axis=0)
                d_pre = total * slope_ref[r, j : j + 16, span].astype(F32)
                dpre_ref[r * COLS + j : r * COLS + j + 16, span] = d_pre.astype(BF16)
        for n in range(9):
            acc_ref[n, :, span] = sums[n]
        if at % 256:
            pair = slice(at - LANES, at + LANES)
            sum_ref[:, pair] += dot(normed_t, dpre_ref[:, pair])

    @pl.when(last)
    def _():
        depth_ref[...] = jnp.sum(acc_ref[...], axis=1)
        to_tiles(sum_ref, tiles_ref, 0)
        first_row = lax.broadcasted_iota(jnp.int32, (8, 128), 0) == 0
        for n in range(128):
            extra = extra_ref[n]
            if n < 72:
                row = depth_ref[n // 8 : n // 8 + 1, 128 * (n % 8) : 128 * (n % 8) + 128]
                extra = jnp.where(first_row, row, extra)
            tiles_ref[n, 16:] = extra.astype(BF16)


def expand_back(d_mixed, halo, halo_slope, wp, hidden, slope, x, dkb, extra):
    tiles = (128, 24, 128)
    cells = band((BLK, COLS, EXP))
    return pl.pallas_call(
        expand_back_body,
        grid=(STEPS,),
        in_specs=[
            cells, ROW_BEFORE, ROW_AFTER, whole((HALO, CHAN)), whole((HALO, EXP)),
            whole((EXP, CHAN)), cells, cells, band((BLK, COLS, CHAN)), whole((9, 8, EXP)),
            whole((128, 8, 128)),
        ],
        out_specs=[band((TOK, EXP)), whole(tiles)],
        out_shape=[
            jax.ShapeDtypeStruct((ROWS * COLS, EXP), BF16),
            jax.ShapeDtypeStruct(tiles, BF16),
        ],
        scratch_shapes=[pltpu.VMEM((COLS, EXP), F32)] * 2
        + [pltpu.VMEM((STEPS, 16, EXP), F32)] * 2
        + [pltpu.VMEM((9, 8, EXP), F32), pltpu.VMEM((CHAN, EXP), F32), pltpu.VMEM((9, EXP), F32)]
        + [pltpu.VMEM((3, BLK + 2, COLS, EXP), F32)],
        compiler_params=params(58),
        cost_estimate=pl.CostEstimate(
            flops=2 * ROWS * COLS * CHAN * EXP, bytes_accessed=20 * MIB, transcendentals=0
        ),
        name="expand_back",
    )(d_mixed, d_mixed, d_mixed, halo, halo_slope, wp, hidden, slope, x, dkb, extra)


def finish_body(dpre_ref, x_ref, cot_ref, db_ref, we_ref, grad_ref):
    normed, inv_std = layer_norm(x_ref[...].reshape(-1, CHAN).astype(F32))
    d_input = layer_norm_back(normed, inv_std, dot_nt(dpre_ref[...], we_ref[...]))
    grad_ref[...] = (section_grad(cot_ref, db_ref) + d_input).astype(BF16).reshape(BLK, COLS, CHAN)


def finish(d_pre, x, cot, db, we):
    return pl.pallas_call(
        finish_body,
        grid=(STEPS,),
        in_specs=[
            band((BLK * COLS, EXP)), band((BLK, COLS, CHAN)), band((BLK, COLS, CHAN)), band((2 * BLK, 32, CHAN)),
            whole((CHAN, EXP)),
        ],
        out_specs=band((BLK, COLS, CHAN)),
        out_shape=jax.ShapeDtypeStruct((ROWS, COLS, CHAN), BF16),
        compiler_params=params(58),
        cost_estimate=pl.CostEstimate(
            flops=2 * ROWS * COLS * CHAN * EXP, bytes_accessed=9 * MIB, transcendentals=0
        ),
        name="finish",
    )(d_pre, x, cot, db, we)


def join_body(core_ref, *refs):
    half = pl.ds(core_ref[0] * 64, 64)
    out_ref = refs[-1]
    at = 0
    for own_ref, other_ref in zip(refs[0:-1:2], refs[1:-1:2]):
        total = own_ref[half].astype(F32) + other_ref[half].astype(F32)
        out_ref[:, at : at + own_ref.shape[1]] = total.astype(BF16)
        at += own_ref.shape[1]


def join(core, *tiles):
    vmem = pl.BlockSpec(memory_space=pltpu.VMEM)
    return pl.pallas_call(
        join_body,
        in_specs=[pl.BlockSpec(memory_space=pltpu.SMEM)] + [vmem] * len(tiles),
        out_shape=jax.ShapeDtypeStruct(JOINED, BF16),
        compiler_params=params(24),
        cost_estimate=pl.CostEstimate(flops=MIB, bytes_accessed=4 * MIB, transcendentals=0),
        name="join",
    )(core, *tiles)


def fold_body(terms_ref, out_ref):
    factor = float(128 * ROWS * COLS) ** (-0.5)
    total = jnp.sum(terms_ref[...].astype(F32), axis=0) * factor
    out_ref[...] = jnp.broadcast_to(total.astype(BF16)[None], out_ref.shape)


def fold(terms):
    return pl.pallas_call(
        fold_body,
        out_shape=jax.ShapeDtypeStruct(terms.shape, BF16),
        compiler_params=params(24),
        cost_estimate=pl.CostEstimate(flops=terms.size, bytes_accessed=2 * terms.size, transcendentals=0),
        name="fold",
    )(terms)


def unfold_body(core_ref, own_ref, other_ref, expand_ref, depth_ref, project_ref, qkv_ref, out_ref, bias_ref):
    first = core_ref[0] == 0

    def tile(n, rows):
        own, other = own_ref[n % 64, rows].astype(F32), other_ref[n % 64, rows].astype(F32)
        return jnp.where(first, own, other) if n < 64 else jnp.where(first, other, own)

    parts = ((qkv_ref, 0, 0), (out_ref, 96, 0), (project_ref, 0, 16), (expand_ref, 0, 32))
    for ref, at, low in parts:
        wide = ref.shape[1] // 128
        for r in range(ref.shape[0] // 16):
            for c in range(wide):
                piece = tile(at + wide * r + c, slice(low, low + 16))
                ref[16 * r : 16 * r + 16, 128 * c : 128 * c + 128] = piece
    for n in range(72):
        extra = tile(n, slice(48, 56))
        at = 128 * (n % 8)
        depth_ref[n // 24, n // 8 % 3 : n // 8 % 3 + 1, at : at + 128] = extra[:1]
        if n < 60:
            bias_ref[n % 15, n // 15 : n // 15 + 1, :] = extra[1:2, :15]


def unfold(core, own, other):
    vmem = pl.BlockSpec(memory_space=pltpu.VMEM)
    return pl.pallas_call(
        unfold_body,
        in_specs=[pl.BlockSpec(memory_space=pltpu.SMEM), vmem, vmem],
        out_shape=[
            jax.ShapeDtypeStruct((CHAN, EXP), F32),
            jax.ShapeDtypeStruct((3, 3, EXP), F32),
            jax.ShapeDtypeStruct((EXP, CHAN), F32),
            jax.ShapeDtypeStruct((CHAN, 3 * CHAN), F32),
            jax.ShapeDtypeStruct((CHAN, CHAN), F32),
            jax.ShapeDtypeStruct((15, 4, 15), F32),
        ],
        compiler_params=params(24),
        cost_estimate=pl.CostEstimate(flops=0, bytes_accessed=5 * MIB, transcendentals=0),
        name="unfold",
    )(core, own, other)


FIRST_CELL = np.zeros((32, 512), np.float32)
LAST_CELL = np.zeros((32, 512), np.float32)
for _row in range(32):
    FIRST_CELL[_row, _row * 16] = 1.0
    LAST_CELL[_row, _row * 16 + 15] = 1.0


def edges_body(
    dt_ref, ct_ref, db_ref, cb_ref, dl_ref, cl_ref, dr_ref, cr_ref, first_ref, last_ref,
    top_ref, bottom_ref, left_ref, right_ref,
):
    def total(d_ref, c_ref):
        return (d_ref[...].astype(F32) + c_ref[...].astype(F32)).astype(BF16)

    top = total(dt_ref, ct_ref)
    bottom = total(db_ref, cb_ref)
    for quad in range(4):
        top_ref[16 * quad : 16 * quad + 16] = top[0, quad, :16]
        bottom_ref[16 * quad : 16 * quad + 16] = bottom[0, quad, 16:]
    left_ref[...] = dot(first_ref[...], total(dl_ref, cl_ref).reshape(512, CHAN)).astype(BF16)
    right_ref[...] = dot(last_ref[...], total(dr_ref, cr_ref).reshape(512, CHAN)).astype(BF16)


def edges(d_branch, cot):
    d_branch, cot = d_branch.reshape(16, 4, 32, CHAN), cot.reshape(16, 4, 32, CHAN)
    specs = []
    for row in (0, 15):
        specs += [pl.BlockSpec((1, 4, 32, CHAN), lambda i, row=row: (row, 0, 0, 0))] * 2
    for col in (0, 3):
        specs += [pl.BlockSpec((16, 1, 32, CHAN), lambda i, col=col: (0, col, 0, 0))] * 2
    return pl.pallas_call(
        edges_body,
        grid=(1,),
        in_specs=specs + [whole((32, 512))] * 2,
        out_specs=[whole((COLS, CHAN))] * 2 + [whole((ROWS, CHAN))] * 2,
        out_shape=[jax.ShapeDtypeStruct((COLS, CHAN), BF16)] * 2
        + [jax.ShapeDtypeStruct((ROWS, CHAN), BF16)] * 2,
        compiler_params=params(24),
        cost_estimate=pl.CostEstimate(flops=MIB, bytes_accessed=2 * MIB, transcendentals=0),
        name="edges",
    )(*([d_branch, cot] * 4), jnp.asarray(FIRST_CELL, BF16), jnp.asarray(LAST_CELL, BF16))


def shifts():
    n_lat, n_lon = lax.axis_size("lat"), lax.axis_size("lon")
    south = [(i, i + 1) for i in range(n_lat - 1)]
    north = [(i + 1, i) for i in range(n_lat - 1)]
    east = [(i, (i + 1) % n_lon) for i in range(n_lon)]
    west = [((i + 1) % n_lon, i) for i in range(n_lon)]
    return (south, north, east, west)


def rows_of(top, bottom):
    south, north, _, _ = shifts()
    return (lax.ppermute(bottom, "lat", south), lax.ppermute(top, "lat", north))


def halo_of(above, below, left, right):
    _, _, east, west = shifts()
    pad = jnp.zeros((EDGE - ROWS - 2, left.shape[1]), left.dtype)
    from_west = lax.ppermute(
        jnp.concatenate([above[-1:], right, below[-1:], pad], axis=0), "lon", east
    )
    from_east = lax.ppermute(
        jnp.concatenate([above[:1], left, below[:1], pad], axis=0), "lon", west
    )
    return jnp.concatenate([above, below, from_west, from_east], axis=0)


def wide_rows(field):
    flat = (2 * COLS, CHAN)
    above, below = rows_of(field[:2].reshape(flat), field[-2:].reshape(flat))
    return (above.reshape(2, COLS, CHAN), below.reshape(2, COLS, CHAN))


def wide_columns(field, above, below):
    _, _, east, west = shifts()
    pad = jnp.zeros((2, EDGE - ROWS - 4, field.shape[2]), field.dtype)

    def columns(at):
        parts = [part[:, at : at + 2].transpose(1, 0, 2) for part in (above, field, below)]
        return jnp.concatenate(parts + [pad], axis=1)

    own_west, own_east = columns(0), columns(COLS - 2)
    from_west = lax.ppermute(own_east, "lon", east)
    from_east = lax.ppermute(own_west, "lon", west)
    return (from_west, from_east, own_west, own_east)


def members():
    n_lat, n_lon = lax.axis_size("lat"), lax.axis_size("lon")
    order = np.arange(n_lat * n_lon).reshape(n_lat, n_lon // 2, 2)
    return order.transpose(2, 0, 1).reshape(2, -1).tolist()


def exchange(pieces):
    return lax.all_to_all(
        pieces, ("lat", "lon"), split_axis=0, concat_axis=0, axis_index_groups=members(), tiled=True
    )


def to_pieces(field):
    shaped = field.reshape(16, 2, 4, 16, CHAN).transpose(0, 2, 1, 3, 4)
    return shaped.reshape(64, 32, CHAN)


def pairs():
    return np.arange(lax.axis_size("lon")).reshape(-1, 2).tolist()


def other_core(tiles):
    swaps = [move for a, b in pairs() for move in ((a, b), (b, a))]
    return lax.ppermute(tiles, "lon", swaps)


def rel_table():
    position = np.arange(64)
    pos_row, pos_col = position // 8, position % 8
    rel_index = (pos_row[:, None] - pos_row[None, :] + 7) * 15 + (
        pos_col[:, None] - pos_col[None, :] + 7
    )
    return jnp.asarray(rel_index)[:, :, None] == jnp.arange(225)[None, None, :]


def on_device(
    field_in, cotangent, expand_weight, depth_kernel, project_weight, qkv_weight, out_weight, rel_bias
):
    onehot = rel_table().astype(F32)
    bias = jnp.einsum(
        "tsr,hr->sht", onehot, rel_bias.reshape(4, 225), precision=lax.Precision.HIGHEST
    ).reshape(64, 256)
    dk = depth_kernel.reshape(9, EXP)

    dkb = jnp.broadcast_to(dk[:, None], (9, 8, EXP))
    core = lax.axis_index("lon").astype(jnp.int32).reshape(1) & 1
    barrier = lax.optimization_barrier

    above, below = wide_rows(field_in)
    hidden = expand(field_in, expand_weight, False)
    above, below, hidden, late_cot = barrier((above, below, hidden, cotangent))
    field_halo = (above, below, *wide_columns(field_in, above, below))
    field_halo, cot_pieces = barrier((field_halo, to_pieces(late_cot)))
    hidden, cot_pieces = barrier((hidden, cot_pieces))
    cot_groups = exchange(cot_pieces)
    section, mixed, mixed_pre, ring_slope = mix(
        hidden, field_halo, expand_weight, dk, project_weight, field_in
    )
    groups = exchange(section)
    cot_swapped, d_att = prepare(cot_groups, out_weight, 32)
    section_field, _ = barrier((field_in, section))
    act_slope = expand(section_field, expand_weight, True)
    groups, bias, d_att, act_slope = barrier((groups, bias, d_att, act_slope))
    d_groups, attended, normed2, d_proj, bias_acc = attention(groups, d_att, qkv_weight, bias)

    d_branch = exchange(d_groups)
    attention_tiles = attention_sums(attended, cot_swapped.reshape(-1, CHAN), normed2, d_proj)
    bias_sum = jnp.einsum(
        "sht,tsr->hr", bias_acc.reshape(64, 4, 64), onehot, precision=lax.Precision.HIGHEST
    )
    extra = jnp.pad(bias_sum.reshape(60, 1, 15), ((0, 68), (1, 6), (0, 113)))
    mixed_pre, _ = barrier((mixed_pre, d_groups))
    mixed_slope = mixed_slopes(mixed_pre)
    d_branch, attention_tiles, extra, mixed_slope = barrier((d_branch, attention_tiles, extra, mixed_slope))

    top, bottom, left, right = edges(d_branch, cot_pieces)
    above, below = rows_of(top, bottom)
    project_tiles = project_sum(cotangent, d_branch, mixed)
    above, below, project_tiles, attention_tiles, mixed_slope = barrier(
        (above, below, project_tiles, attention_tiles, mixed_slope)
    )
    d_halo = halo_of(above, below, left, right)
    attention_other, project_other = other_core(attention_tiles), other_core(project_tiles)
    d_mixed = project_back(cotangent, d_branch, mixed_slope, project_weight)
    d_halo, d_mixed, attention_other, project_other = barrier(
        (d_halo, d_mixed, attention_other, project_other)
    )
    attention_pair = (attention_tiles, attention_other)
    project_pair = (project_tiles, project_other)
    d_pre, expand_tiles = expand_back(
        d_mixed, d_halo, ring_slope, project_weight, hidden, act_slope, field_in, dkb, extra
    )

    joined = join(core, *attention_pair, *project_pair, expand_tiles, other_core(expand_tiles))
    joined, d_pre = barrier((joined, d_pre))
    terms = exchange(joined)
    grad_in = finish(d_pre, field_in, cotangent, d_branch, expand_weight)
    terms, grad_in = barrier((terms, grad_in))
    sums = exchange(fold(terms))
    *grads, bias_grad = unfold(core, sums, other_core(sums))
    return (grad_in, *grads, bias_grad.transpose(1, 0, 2))


def solution(mesh):
    placed = (P("lat", "lon", None), P("lat", "lon", None), P(), P(), P(), P(), P(), P())
    return jax.shard_map(
        on_device,
        mesh=mesh,
        in_specs=placed,
        out_specs=(P("lat", "lon", None), P(), P(), P(), P(), P(), P()),
        check_vma=False,
    )
```

```python
import functools
import math

import jax
import jax.numpy as jnp
import numpy as np
from jax import lax
from jax.experimental import pallas as pl
from jax.experimental.pallas import tpu as pltpu
from jax.sharding import PartitionSpec as P

EPSILON = 1e-05
GELU_C = math.sqrt(2.0 / math.pi)
F32 = jnp.float32
BF16 = jnp.bfloat16
MIB = 1 << 20

ROWS, COLS, CHAN, EXP = 32, 64, 256, 1024
BLK = 8
STEPS = ROWS // BLK
TOK = BLK * COLS
LANES = 128
EDGE = 40
HALO = 2 * COLS + 2 * EDGE
LONG = 72
AT_ONCE = 16
JOINED = (64, 56, 128)


def layer_norm(values):
    average = jnp.mean(values, axis=-1, keepdims=True)
    centred = values - average
    variance = jnp.mean(centred * centred, axis=-1, keepdims=True)
    inv_std = lax.rsqrt(variance + EPSILON)
    return (centred * inv_std, inv_std)


def layer_norm_back(normed, inv_std, grads):
    mean_grad = jnp.mean(grads, axis=-1, keepdims=True)
    mean_cross = jnp.mean(grads * normed, axis=-1, keepdims=True)
    return (grads - mean_grad - normed * mean_cross) * inv_std


def gelu(values):
    return values * (0.5 + 0.5 * jnp.tanh(values * (GELU_C + (GELU_C * 0.044715) * (values * values))))


def gelu_slope(values):
    squared = values * values
    tanh_val = jnp.tanh(values * (GELU_C + (GELU_C * 0.044715) * squared))
    gate = 0.5 + 0.5 * tanh_val
    result = values * gate
    slopes = gate + result * (1.0 - gate) * (2.0 * GELU_C + (6.0 * GELU_C * 0.044715) * squared)
    return (result, slopes)


def dot(left, right):
    return lax.dot_general(left, right, (((1,), (0,)), ((), ())), preferred_element_type=F32)


def dot_nt(left, right):
    return lax.dot_general(left, right, (((1,), (1,)), ((), ())), preferred_element_type=F32)


def dot_tn(left, right):
    return lax.dot_general(left, right, (((0,), (0,)), ((), ())), preferred_element_type=F32)


def params(mib):
    return pltpu.CompilerParams(vmem_limit_bytes=mib * MIB)


def whole(shape):
    return pl.BlockSpec(shape, lambda i: (0,) * len(shape))


def band(shape):
    return pl.BlockSpec(shape, lambda i: (i,) + (0,) * (len(shape) - 1))


ROW_BEFORE = pl.BlockSpec(
    (1, COLS, EXP), lambda i: (jnp.maximum(BLK * i - 1, 0), 0, 0)
)
ROW_AFTER = pl.BlockSpec(
    (1, COLS, EXP), lambda i: (jnp.minimum(BLK * i + BLK, ROWS - 1), 0, 0)
)


TILED = (128, 16, 128)


def to_tiles(ref, out_ref, at):
    wide = ref.shape[1] // 128
    for r in range(ref.shape[0] // 16):
        for c in range(wide):
            tile = ref[16 * r : 16 * r + 16, 128 * c : 128 * c + 128]
            out_ref[at + wide * r + c, :16] = tile.astype(BF16)


def expand_body(x_ref, we_ref, out_ref, slopes):
    normed, _ = layer_norm(x_ref[...].reshape(TOK, CHAN).astype(F32))
    normed_b = normed.astype(BF16)
    for at in range(0, EXP, 256):
        pre = dot(normed_b, we_ref[:, at : at + 256])
        result = gelu_slope(pre)[1] if slopes else gelu(pre)
        out_ref[:, :, at : at + 256] = result.astype(BF16).reshape(BLK, COLS, 256)


def expand(x, we, slopes):
    return pl.pallas_call(
        functools.partial(expand_body, slopes=slopes),
        grid=(STEPS,),
        in_specs=[band((BLK, COLS, CHAN)), whole((CHAN, EXP))],
        out_specs=band((BLK, COLS, EXP)),
        out_shape=jax.ShapeDtypeStruct((ROWS, COLS, EXP), BF16),
        compiler_params=params(58),
        cost_estimate=pl.CostEstimate(
            flops=2 * ROWS * COLS * CHAN * EXP, bytes_accessed=6 * MIB, transcendentals=ROWS * COLS * EXP
        ),
        name="expand_slopes" if slopes else "expand",
    )(x, we)


def mixed_slopes_body(pre_ref, slope_ref):
    for at in range(0, EXP, 256):
        span = slice(at, at + 256)
        slope_ref[:, :, span] = gelu_slope(pre_ref[:, :, span].astype(F32))[1].astype(BF16)


def mixed_slopes(pre):
    return pl.pallas_call(
        mixed_slopes_body,
        grid=(STEPS,),
        in_specs=[band((BLK, COLS, EXP))],
        out_specs=band((BLK, COLS, EXP)),
        out_shape=jax.ShapeDtypeStruct((ROWS, COLS, EXP), BF16),
        compiler_params=params(58),
        cost_estimate=pl.CostEstimate(
            flops=20 * ROWS * COLS * EXP, bytes_accessed=8 * MIB, transcendentals=ROWS * COLS * EXP
        ),
        name="mixed_slopes",
    )(pre)


def mix_body(
    cur_ref, before_ref, after_ref,
    above_ref, below_ref, first_ref, last_ref, west_ref, east_ref, own_west_ref, own_east_ref,
    we_ref, dk_ref, wp_ref, x_ref,
    section_ref, mixed_ref, pre_ref, ring_slope_ref,
    top_ref, bottom_ref, left_ref, right_ref,
):
    step = pl.program_id(0)

    @pl.when(step == 0)
    def _():
        ring_body(
            above_ref, below_ref, first_ref, last_ref, west_ref, east_ref, own_west_ref, own_east_ref,
            we_ref, dk_ref,
            top_ref, bottom_ref, left_ref, right_ref, ring_slope_ref,
        )

    first, last = step == 0, step == STEPS - 1
    branch = None
    for at in range(0, EXP, LANES):
        span = slice(at, at + LANES)
        rows = [jnp.where(first, top_ref[:, span], before_ref[0, :, span])]
        rows += [cur_ref[r, :, span] for r in range(BLK)]
        rows += [jnp.where(last, bottom_ref[:, span], after_ref[0, :, span])]
        rows = [row.astype(F32) for row in rows]
        kern = [dk_ref[n, span][None] for n in range(9)]
        for r in range(BLK):
            parts = [
                kern[b] * rows[r] + kern[3 + b] * rows[r + 1] + kern[6 + b] * rows[r + 2]
                for b in range(3)
            ]
            left = left_ref[step, r : r + 1, span]
            right = right_ref[step, r : r + 1, span]
            pre = (
                parts[1]
                + jnp.concatenate([left, parts[0][:-1]], axis=0)
                + jnp.concatenate([parts[2][1:], right], axis=0)
            )
            mixed_ref[r, :, span] = gelu(pre).astype(BF16)
            pre_ref[r, :, span] = pre.astype(BF16)
        if at % 256:
            pair = slice(at - LANES, at + LANES)
            part = dot(mixed_ref[:, :, pair].reshape(TOK, 256), wp_ref[pair, :])
            branch = part if branch is None else branch + part
    section = (x_ref[...].reshape(TOK, CHAN).astype(F32) + branch).astype(BF16)
    section = section.reshape(BLK // 2, 2, 4, 16, CHAN)
    for pair in range(BLK // 2):
        for quad in range(4):
            section_ref[4 * pair + quad] = section[pair, :, quad].reshape(32, CHAN)


def ring_body(
    above_ref, below_ref, first_ref, last_ref, west_ref, east_ref, own_west_ref, own_east_ref,
    we_ref, dk_ref,
    top_ref, bottom_ref, left_ref, right_ref, slope_ref,
):
    west, east = west_ref[...].astype(F32), east_ref[...].astype(F32)
    pad = jnp.zeros((LONG - COLS - 4, CHAN), F32)

    def along(row, at):
        return [
            west[0, at : at + 1], west[1, at : at + 1], row.astype(F32),
            east[0, at : at + 1], east[1, at : at + 1], pad,
        ]

    strips = along(above_ref[0], 0) + along(above_ref[1], 1) + along(first_ref[0], 2)
    strips += along(last_ref[0], 33) + along(below_ref[0], 34) + along(below_ref[1], 35)
    strips += [west[0], west[1], own_west_ref[0].astype(F32)]
    strips += [own_east_ref[1].astype(F32), east[0], east[1]]
    normed, _ = layer_norm(jnp.concatenate(strips, axis=0))
    normed_b = normed.astype(BF16)
    south, lefts, rights = 3 * LONG, 6 * LONG, 6 * LONG + 3 * EDGE
    for at in range(0, EXP, 256):
        span = slice(at, at + 256)
        val = gelu(dot(normed_b, we_ref[:, span])).astype(BF16).astype(F32)
        kern = [dk_ref[n, span][None] for n in range(9)]
        top_ref[:, span] = val[LONG + 2 : LONG + 2 + COLS].astype(BF16)
        bottom_ref[:, span] = val[south + LONG + 2 : south + LONG + 2 + COLS].astype(BF16)
        for ref, base, col in ((left_ref, lefts, 0), (right_ref, rights, 2)):
            total = 0.0
            for a in range(3):
                start = base + EDGE + a + 1
                total = total + kern[3 * a + col] * val[start : start + ROWS]
            for s in range(STEPS):
                ref[s, :BLK, span] = total[BLK * s : BLK * s + BLK]
        for base, out in ((0, 0), (south, COLS)):
            total = 0.0
            for a in range(3):
                for b in range(3):
                    start = base + LONG * a + b + 1
                    total = total + kern[3 * a + b] * val[start : start + COLS]
            slope_ref[out : out + COLS, span] = gelu_slope(total)[1]
        for base, out in ((lefts, 2 * COLS), (rights, 2 * COLS + EDGE)):
            total = 0.0
            for a in range(3):
                for b in range(3):
                    start = base + EDGE * b + a
                    total = total + kern[3 * a + b] * val[start : start + ROWS + 2]
            slope_ref[out : out + ROWS + 2, span] = gelu_slope(total)[1]
            slope_ref[out + ROWS + 2 : out + EDGE, span] = jnp.zeros((EDGE - ROWS - 2, 256), F32)


def mix(hidden, halo, we, dk, wp, x):
    above, below, west, east, own_west, own_east = halo
    wide = jax.ShapeDtypeStruct((ROWS, COLS, EXP), BF16)
    return pl.pallas_call(
        mix_body,
        grid=(STEPS,),
        in_specs=[
            band((BLK, COLS, EXP)), ROW_BEFORE, ROW_AFTER,
            whole((2, COLS, CHAN)), whole((2, COLS, CHAN)),
            pl.BlockSpec((1, COLS, CHAN), lambda i: (0, 0, 0)),
            pl.BlockSpec((1, COLS, CHAN), lambda i: (ROWS - 1, 0, 0)),
            whole((2, EDGE, CHAN)), whole((2, EDGE, CHAN)), whole((2, EDGE, CHAN)), whole((2, EDGE, CHAN)),
            whole((CHAN, EXP)), whole((9, EXP)), whole((EXP, CHAN)), band((BLK, COLS, CHAN)),
        ],
        out_specs=[
            band((2 * BLK, 32, CHAN)), band((BLK, COLS, EXP)), band((BLK, COLS, EXP)), whole((HALO, EXP)),
        ],
        out_shape=[
            jax.ShapeDtypeStruct((64, 32, CHAN), BF16), wide, wide, jax.ShapeDtypeStruct((HALO, EXP), F32),
        ],
        scratch_shapes=[pltpu.VMEM((COLS, EXP), BF16)] * 2 + [pltpu.VMEM((STEPS, 16, EXP), F32)] * 2,
        compiler_params=params(58),
        cost_estimate=pl.CostEstimate(
            flops=3 * ROWS * COLS * CHAN * EXP, bytes_accessed=18 * MIB, transcendentals=2 * ROWS * COLS * EXP
        ),
        name="mix",
    )(
        hidden, hidden, hidden, above, below, x, x, west, east, own_west, own_east,
        we, dk, wp, x,
    )


SWAP = np.zeros((256, 256), np.float32)
for _s in range(16):
    for _g in range(16):
        SWAP[_g * 16 + _s, _s * 16 + _g] = 1.0


def diagonal(full, low):
    halves = []
    for half in range(2):
        lanes = slice(half * 128, half * 128 + 128)
        at = half * 128
        halves.append(jnp.where(low, full[at : at + 64, lanes], full[at + 64 : at + 128, lanes]))
    return jnp.concatenate(halves, axis=1)


def swap(src, dst, swap_ref, n_groups):
    for s in range(0, 64, 16):
        for g in range(0, n_groups, 16):
            moved = dot(swap_ref[...], src[s : s + 16, g : g + 16].reshape(256, CHAN)).astype(BF16)
            dst[g : g + 16, s : s + 16] = moved.reshape(16, 16, CHAN)


def prepare_body(cot_ref, wout_ref, swap_ref, cs_ref, da_ref):
    n_groups = cot_ref.shape[1]
    swap(cot_ref, cs_ref, swap_ref, n_groups)
    for g in range(0, n_groups, 4):
        grads = dot_nt(cs_ref[g : g + 4].reshape(256, CHAN), wout_ref[...])
        da_ref[g : g + 4] = grads.astype(BF16).reshape(4, 64, CHAN)


def prepare(cot, wout, n_groups):
    shape = (64, n_groups, CHAN)
    grouped = (n_groups, 64, CHAN)
    return pl.pallas_call(
        prepare_body,
        grid=(1,),
        in_specs=[whole(shape), whole((CHAN, CHAN)), whole((256, 256))],
        out_specs=[whole(grouped), whole(grouped)],
        out_shape=[jax.ShapeDtypeStruct(grouped, BF16)] * 2,
        compiler_params=params(24),
        cost_estimate=pl.CostEstimate(
            flops=n_groups * 64 * 4 * CHAN * CHAN, bytes_accessed=3 * MIB, transcendentals=0
        ),
        name="prepare",
    )(cot, wout, jnp.asarray(SWAP, BF16))


def attention_body(
    x_ref, da_ref, wqkv_ref, bias_ref, swap_ref,
    out_ref, att_ref, norm_ref, proj_ref, bias_sum_ref, xs_ref, ds_ref,
):
    step = pl.program_id(0)
    n_groups = x_ref.shape[1]

    @pl.when(step == 0)
    def _():
        bias_sum_ref[...] = jnp.zeros_like(bias_sum_ref)
        swap(x_ref, xs_ref, swap_ref, n_groups)

    groups = pl.ds(step * AT_ONCE, AT_ONCE)
    tokens = xs_ref[groups].reshape(AT_ONCE * 64, CHAN)
    normed, inv_std = layer_norm(tokens.astype(F32))
    normed_b = normed.astype(BF16)
    norm_ref[...] = normed_b
    projected = dot(normed_b, wqkv_ref[...]).astype(BF16)
    low = lax.broadcasted_iota(jnp.int32, (64, 128), 1) < 64
    keep = [low.astype(F32).astype(BF16), (1.0 - low.astype(F32)).astype(BF16)]
    none = jnp.zeros((128, 128), BF16)

    def by_head(rows):
        blocks = []
        for half in range(2):
            lanes = rows[:, half * 128 : half * 128 + 128]
            pair = jnp.concatenate([lanes * keep[0], lanes * keep[1]], axis=0)
            blocks.append(jnp.concatenate([pair, none] if half == 0 else [none, pair], axis=1))
        return jnp.concatenate(blocks, axis=0)

    batch = range(AT_ONCE)
    part = [slice(g * 64, g * 64 + 64) for g in batch]
    query = (projected[:, :CHAN].astype(F32) * 0.125).astype(BF16)
    key = [projected[part[g], CHAN : 2 * CHAN] for g in batch]
    value = [projected[part[g], 2 * CHAN :] for g in batch]
    query_h = [by_head(query[part[g]]) for g in batch]
    da_h = [by_head(da_ref[g]) for g in batch]
    scores = [dot_nt(key[g], query_h[g]) + bias_ref[...] for g in batch]
    d_probs = [dot_nt(value[g], da_h[g]) for g in batch]
    tops = [jnp.max(scores[g], axis=0, keepdims=True) for g in batch]
    scores = [jnp.exp(scores[g] - tops[g]) for g in batch]
    scales = [1.0 / jnp.sum(scores[g], axis=0, keepdims=True) for g in batch]
    probs = [scores[g] * scales[g] for g in batch]
    probs_b = [probs[g].astype(BF16) for g in batch]
    crosses = [jnp.sum(probs[g] * d_probs[g], axis=0, keepdims=True) for g in batch]
    d_scores = [probs[g] * (d_probs[g] - crosses[g]) for g in batch]
    bias_sum_ref[...] += sum(d_scores[1:], d_scores[0])
    d_scores_b = [d_scores[g].astype(BF16) for g in batch]
    attended = [dot_tn(probs_b[g], value[g]) for g in batch]
    d_query = [dot_tn(d_scores_b[g], key[g]) for g in batch]
    d_key = [dot(d_scores_b[g], query_h[g]) for g in batch]
    d_value = [dot(probs_b[g], da_h[g]) for g in batch]
    for g in batch:
        att_ref[part[g]] = diagonal(attended[g], low).astype(BF16)
        proj_ref[part[g], :CHAN] = (diagonal(d_query[g], low) * 0.125).astype(BF16)
        proj_ref[part[g], CHAN : 2 * CHAN] = d_key[g].astype(BF16)
        proj_ref[part[g], 2 * CHAN :] = d_value[g].astype(BF16)
    d_normed = dot_nt(proj_ref[...], wqkv_ref[...])
    d_tokens = layer_norm_back(normed, inv_std, d_normed).astype(BF16)
    ds_ref[groups] = d_tokens.reshape(AT_ONCE, 64, CHAN)

    @pl.when(step == n_groups // AT_ONCE - 1)
    def _():
        for s in range(0, 64, 16):
            for g in range(0, n_groups, 16):
                tile = ds_ref[g : g + 16, s : s + 16].reshape(256, CHAN)
                moved = dot(swap_ref[...], tile).astype(BF16)
                out_ref[s : s + 16, g : g + 16] = moved.reshape(16, 16, CHAN)


def attention(tokens, d_att, wqkv, bias):
    n_groups = tokens.shape[1]
    shape = (64, n_groups, CHAN)
    flat = n_groups * 64
    return pl.pallas_call(
        attention_body,
        grid=(n_groups // AT_ONCE,),
        in_specs=[
            whole(shape), band((AT_ONCE, 64, CHAN)), whole((CHAN, 3 * CHAN)), whole((64, CHAN)),
            whole((256, 256)),
        ],
        out_specs=[
            whole(shape), band((AT_ONCE * 64, CHAN)), band((AT_ONCE * 64, CHAN)),
            band((AT_ONCE * 64, 3 * CHAN)), whole((64, CHAN)),
        ],
        out_shape=[
            jax.ShapeDtypeStruct(shape, BF16),
            jax.ShapeDtypeStruct((flat, CHAN), BF16),
            jax.ShapeDtypeStruct((flat, CHAN), BF16),
            jax.ShapeDtypeStruct((flat, 3 * CHAN), BF16),
            jax.ShapeDtypeStruct((64, CHAN), F32),
        ],
        scratch_shapes=[pltpu.VMEM((n_groups, 64, CHAN), BF16)] * 2,
        compiler_params=params(58),
        cost_estimate=pl.CostEstimate(
            flops=flat * 4 * CHAN * CHAN * 5, bytes_accessed=8 * MIB, transcendentals=flat * 256
        ),
        name="attention",
    )(tokens, d_att, wqkv, bias, jnp.asarray(SWAP, BF16))


def attention_sums_body(att_ref, cot_ref, norm_ref, proj_ref, out_ref, qkv_acc, out_acc):
    step = pl.program_id(0)

    @pl.when(step == 0)
    def _():
        qkv_acc[...] = jnp.zeros_like(qkv_acc)
        out_acc[...] = jnp.zeros_like(out_acc)

    out_acc[...] += dot_tn(att_ref[...], cot_ref[...])
    qkv_acc[...] += dot_tn(norm_ref[...], proj_ref[...])

    @pl.when(step == pl.num_programs(0) - 1)
    def _():
        to_tiles(qkv_acc, out_ref, 0)
        to_tiles(out_acc, out_ref, 96)


def attention_sums(att, cot, normed, proj):
    flat = att.shape[0]
    return pl.pallas_call(
        attention_sums_body,
        grid=(flat // 512,),
        in_specs=[band((512, CHAN)), band((512, CHAN)), band((512, CHAN)), band((512, 3 * CHAN))],
        out_specs=whole(TILED),
        out_shape=jax.ShapeDtypeStruct(TILED, BF16),
        scratch_shapes=[pltpu.VMEM((CHAN, 3 * CHAN), F32), pltpu.VMEM((CHAN, CHAN), F32)],
        compiler_params=params(58),
        cost_estimate=pl.CostEstimate(
            flops=flat * 8 * CHAN * CHAN, bytes_accessed=6 * MIB, transcendentals=0
        ),
        name="attention_sums",
    )(att, cot, normed, proj)


def section_grad(cot_ref, db_ref):
    n_pairs = cot_ref.shape[0] // 2
    pieces = db_ref[...].reshape(n_pairs, 4, 2, 16, CHAN)
    branch = jnp.concatenate(
        [pieces[pair, quad, r] for pair in range(n_pairs) for r in range(2) for quad in range(4)], axis=0
    )
    return cot_ref[...].reshape(-1, CHAN).astype(F32) + branch.astype(F32)


def project_body(cot_ref, db_ref, slope_ref, wp_ref, dm_ref):
    d_section_b = section_grad(cot_ref, db_ref).astype(BF16)
    for at in range(0, EXP, 256):
        grads = dot_nt(d_section_b, wp_ref[at : at + 256, :])
        slope = slope_ref[:, :, at : at + 256].reshape(-1, 256).astype(F32)
        dm_ref[:, :, at : at + 256] = (grads * slope).astype(BF16).reshape(BLK, COLS, 256)


def project_back(cot, db, slope, wp):
    return pl.pallas_call(
        project_body,
        grid=(STEPS,),
        in_specs=[
            band((BLK, COLS, CHAN)), band((2 * BLK, 32, CHAN)), band((BLK, COLS, EXP)), whole((EXP, CHAN)),
        ],
        out_specs=band((BLK, COLS, EXP)),
        out_shape=jax.ShapeDtypeStruct((ROWS, COLS, EXP), BF16),
        compiler_params=params(58),
        cost_estimate=pl.CostEstimate(
            flops=2 * ROWS * COLS * CHAN * EXP, bytes_accessed=10 * MIB, transcendentals=0
        ),
        name="project_back",
    )(cot, db, slope, wp)


def project_sum_body(cot_ref, db_ref, mixed_ref, tiles_ref, sum_ref, turned_ref):
    @pl.when(pl.program_id(0) == 0)
    def _():
        sum_ref[...] = jnp.zeros_like(sum_ref)

    d_section_b = section_grad(cot_ref, db_ref).astype(BF16)
    sum_ref[...] += dot_tn(d_section_b, mixed_ref[...].reshape(-1, EXP))

    @pl.when(pl.program_id(0) == STEPS - 1)
    def _():
        turned_ref[...] = sum_ref[...].T
        to_tiles(turned_ref, tiles_ref, 0)


def project_sum(cot, db, mixed):
    return pl.pallas_call(
        project_sum_body,
        grid=(STEPS,),
        in_specs=[band((BLK, COLS, CHAN)), band((2 * BLK, 32, CHAN)), band((BLK, COLS, EXP))],
        out_specs=whole(TILED),
        out_shape=jax.ShapeDtypeStruct(TILED, BF16),
        scratch_shapes=[pltpu.VMEM((CHAN, EXP), F32), pltpu.VMEM((EXP, CHAN), F32)],
        compiler_params=params(58),
        cost_estimate=pl.CostEstimate(
            flops=2 * ROWS * COLS * CHAN * EXP, bytes_accessed=8 * MIB, transcendentals=0
        ),
        name="project_sum",
    )(cot, db, mixed)


def expand_back_body(
    cur_ref, before_ref, after_ref, halo_ref, halo_slope_ref, wp_ref, hid_ref, slope_ref, x_ref, dkb_ref,
    extra_ref,
    dpre_ref, tiles_ref, top_ref, bottom_ref, left_ref, right_ref, acc_ref, sum_ref, depth_ref, shift_ref,
):
    step = pl.program_id(0)

    @pl.when(step == 0)
    def _():
        sum_ref[...] = jnp.zeros_like(sum_ref)
        acc_ref[...] = jnp.zeros_like(acc_ref)
        for at in range(0, EXP, 256):
            span = slice(at, at + 256)
            grads = dot_nt(halo_ref[...], wp_ref[at : at + 256, :])
            grads = (grads * halo_slope_ref[:, span]).astype(BF16).astype(F32)
            top_ref[:, span] = grads[:COLS]
            bottom_ref[:, span] = grads[COLS : 2 * COLS]
            for ref, base in ((left_ref, 2 * COLS), (right_ref, 2 * COLS + EDGE)):
                for s in range(STEPS):
                    ref[s, : BLK + 2, span] = grads[base + BLK * s : base + BLK * s + BLK + 2]

    normed, _ = layer_norm(x_ref[...].reshape(TOK, CHAN).astype(F32))
    normed_t = normed.T.astype(BF16)
    first, last = step == 0, step == STEPS - 1
    for at in range(0, EXP, LANES):
        span = slice(at, at + LANES)
        rows = [jnp.where(first, top_ref[:, span], before_ref[0, :, span].astype(F32))]
        rows += [cur_ref[r, :, span].astype(F32) for r in range(BLK)]
        rows += [jnp.where(last, bottom_ref[:, span], after_ref[0, :, span].astype(F32))]
        for r in range(BLK + 2):
            left = left_ref[step, r : r + 1, span]
            right = right_ref[step, r : r + 1, span]
            shift_ref[0, r, :, span] = jnp.concatenate([rows[r][1:], right], axis=0)
            shift_ref[1, r, :, span] = rows[r]
            shift_ref[2, r, :, span] = jnp.concatenate([left, rows[r][:-1]], axis=0)
        kern = [dkb_ref[n, :, span] for n in range(9)]
        sums = [acc_ref[n, :, span] for n in range(9)]
        for j in range(0, COLS, 16):
            hid = [hid_ref[r, j : j + 16, span].astype(F32) for r in range(BLK)]
            halves = []
            for low in (0, 8):
                cells = slice(j + low, j + low + 8)
                pieces = [[shift_ref[b, r, cells, span] for b in range(3)] for r in range(BLK + 2)]
                totals = [None] * BLK
                for r in range(BLK):
                    cell = hid[r][low : low + 8]
                    for a in range(3):
                        for b in range(3):
                            n = 3 * a + b
                            piece = pieces[r + 2 - a][b]
                            tap = kern[n] * piece
                            totals[r] = tap if n == 0 else totals[r] + tap
                            sums[n] = sums[n] + cell * piece
                halves.append(totals)
            for r in range(BLK):
                total = jnp.concatenate([halves[0][r], halves[1][r]], axis=0)
                d_pre = total * slope_ref[r, j : j + 16, span].astype(F32)
                dpre_ref[r * COLS + j : r * COLS + j + 16, span] = d_pre.astype(BF16)
        for n in range(9):
            acc_ref[n, :, span] = sums[n]
        if at % 256:
            pair = slice(at - LANES, at + LANES)
            sum_ref[:, pair] += dot(normed_t, dpre_ref[:, pair])

    @pl.when(last)
    def _():
        depth_ref[...] = jnp.sum(acc_ref[...], axis=1)
        to_tiles(sum_ref, tiles_ref, 0)
        first_row = lax.broadcasted_iota(jnp.int32, (8, 128), 0) == 0
        for n in range(128):
            extra = extra_ref[n]
            if n < 72:
                row = depth_ref[n // 8 : n // 8 + 1, 128 * (n % 8) : 128 * (n % 8) + 128]
                extra = jnp.where(first_row, row, extra)
            tiles_ref[n, 16:] = extra.astype(BF16)


def expand_back(d_mixed, halo, halo_slope, wp, hidden, slope, x, dkb, extra):
    tiles = (128, 24, 128)
    cells = band((BLK, COLS, EXP))
    return pl.pallas_call(
        expand_back_body,
        grid=(STEPS,),
        in_specs=[
            cells, ROW_BEFORE, ROW_AFTER, whole((HALO, CHAN)), whole((HALO, EXP)),
            whole((EXP, CHAN)), cells, cells, band((BLK, COLS, CHAN)), whole((9, 8, EXP)),
            whole((128, 8, 128)),
        ],
        out_specs=[band((TOK, EXP)), whole(tiles)],
        out_shape=[
            jax.ShapeDtypeStruct((ROWS * COLS, EXP), BF16),
            jax.ShapeDtypeStruct(tiles, BF16),
        ],
        scratch_shapes=[pltpu.VMEM((COLS, EXP), F32)] * 2
        + [pltpu.VMEM((STEPS, 16, EXP), F32)] * 2
        + [pltpu.VMEM((9, 8, EXP), F32), pltpu.VMEM((CHAN, EXP), F32), pltpu.VMEM((9, EXP), F32)]
        + [pltpu.VMEM((3, BLK + 2, COLS, EXP), F32)],
        compiler_params=params(58),
        cost_estimate=pl.CostEstimate(
            flops=2 * ROWS * COLS * CHAN * EXP, bytes_accessed=20 * MIB, transcendentals=0
        ),
        name="expand_back",
    )(d_mixed, d_mixed, d_mixed, halo, halo_slope, wp, hidden, slope, x, dkb, extra)


def finish_body(dpre_ref, x_ref, cot_ref, db_ref, we_ref, grad_ref):
    normed, inv_std = layer_norm(x_ref[...].reshape(-1, CHAN).astype(F32))
    d_input = layer_norm_back(normed, inv_std, dot_nt(dpre_ref[...], we_ref[...]))
    grad_ref[...] = (section_grad(cot_ref, db_ref) + d_input).astype(BF16).reshape(BLK, COLS, CHAN)


def finish(d_pre, x, cot, db, we):
    return pl.pallas_call(
        finish_body,
        grid=(STEPS,),
        in_specs=[
            band((BLK * COLS, EXP)), band((BLK, COLS, CHAN)), band((BLK, COLS, CHAN)), band((2 * BLK, 32, CHAN)),
            whole((CHAN, EXP)),
        ],
        out_specs=band((BLK, COLS, CHAN)),
        out_shape=jax.ShapeDtypeStruct((ROWS, COLS, CHAN), BF16),
        compiler_params=params(58),
        cost_estimate=pl.CostEstimate(
            flops=2 * ROWS * COLS * CHAN * EXP, bytes_accessed=9 * MIB, transcendentals=0
        ),
        name="finish",
    )(d_pre, x, cot, db, we)


def join_body(core_ref, *refs):
    half = pl.ds(core_ref[0] * 64, 64)
    out_ref = refs[-1]
    at = 0
    for own_ref, other_ref in zip(refs[0:-1:2], refs[1:-1:2]):
        total = own_ref[half].astype(F32) + other_ref[half].astype(F32)
        out_ref[:, at : at + own_ref.shape[1]] = total.astype(BF16)
        at += own_ref.shape[1]


def join(core, *tiles):
    vmem = pl.BlockSpec(memory_space=pltpu.VMEM)
    return pl.pallas_call(
        join_body,
        in_specs=[pl.BlockSpec(memory_space=pltpu.SMEM)] + [vmem] * len(tiles),
        out_shape=jax.ShapeDtypeStruct(JOINED, BF16),
        compiler_params=params(24),
        cost_estimate=pl.CostEstimate(flops=MIB, bytes_accessed=4 * MIB, transcendentals=0),
        name="join",
    )(core, *tiles)


def fold_body(terms_ref, out_ref):
    factor = float(128 * ROWS * COLS) ** (-0.5)
    total = jnp.sum(terms_ref[...].astype(F32), axis=0) * factor
    out_ref[...] = jnp.broadcast_to(total.astype(BF16)[None], out_ref.shape)


def fold(terms):
    return pl.pallas_call(
        fold_body,
        out_shape=jax.ShapeDtypeStruct(terms.shape, BF16),
        compiler_params=params(24),
        cost_estimate=pl.CostEstimate(flops=terms.size, bytes_accessed=2 * terms.size, transcendentals=0),
        name="fold",
    )(terms)


def unfold_body(core_ref, own_ref, other_ref, expand_ref, depth_ref, project_ref, qkv_ref, out_ref, bias_ref):
    first = core_ref[0] == 0

    def tile(n, rows):
        own, other = own_ref[n % 64, rows].astype(F32), other_ref[n % 64, rows].astype(F32)
        return jnp.where(first, own, other) if n < 64 else jnp.where(first, other, own)

    parts = ((qkv_ref, 0, 0), (out_ref, 96, 0), (project_ref, 0, 16), (expand_ref, 0, 32))
    for ref, at, low in parts:
        wide = ref.shape[1] // 128
        for r in range(ref.shape[0] // 16):
            for c in range(wide):
                piece = tile(at + wide * r + c, slice(low, low + 16))
                ref[16 * r : 16 * r + 16, 128 * c : 128 * c + 128] = piece
    for n in range(72):
        extra = tile(n, slice(48, 56))
        at = 128 * (n % 8)
        depth_ref[n // 24, n // 8 % 3 : n // 8 % 3 + 1, at : at + 128] = extra[:1]
        if n < 60:
            bias_ref[n % 15, n // 15 : n // 15 + 1, :] = extra[1:2, :15]


def unfold(core, own, other):
    vmem = pl.BlockSpec(memory_space=pltpu.VMEM)
    return pl.pallas_call(
        unfold_body,
        in_specs=[pl.BlockSpec(memory_space=pltpu.SMEM), vmem, vmem],
        out_shape=[
            jax.ShapeDtypeStruct((CHAN, EXP), F32),
            jax.ShapeDtypeStruct((3, 3, EXP), F32),
            jax.ShapeDtypeStruct((EXP, CHAN), F32),
            jax.ShapeDtypeStruct((CHAN, 3 * CHAN), F32),
            jax.ShapeDtypeStruct((CHAN, CHAN), F32),
            jax.ShapeDtypeStruct((15, 4, 15), F32),
        ],
        compiler_params=params(24),
        cost_estimate=pl.CostEstimate(flops=0, bytes_accessed=5 * MIB, transcendentals=0),
        name="unfold",
    )(core, own, other)


FIRST_CELL = np.zeros((32, 512), np.float32)
LAST_CELL = np.zeros((32, 512), np.float32)
for _row in range(32):
    FIRST_CELL[_row, _row * 16] = 1.0
    LAST_CELL[_row, _row * 16 + 15] = 1.0


def edges_body(
    dt_ref, ct_ref, db_ref, cb_ref, dl_ref, cl_ref, dr_ref, cr_ref, first_ref, last_ref,
    top_ref, bottom_ref, left_ref, right_ref,
):
    def total(d_ref, c_ref):
        return (d_ref[...].astype(F32) + c_ref[...].astype(F32)).astype(BF16)

    top = total(dt_ref, ct_ref)
    bottom = total(db_ref, cb_ref)
    for quad in range(4):
        top_ref[16 * quad : 16 * quad + 16] = top[0, quad, :16]
        bottom_ref[16 * quad : 16 * quad + 16] = bottom[0, quad, 16:]
    left_ref[...] = dot(first_ref[...], total(dl_ref, cl_ref).reshape(512, CHAN)).astype(BF16)
    right_ref[...] = dot(last_ref[...], total(dr_ref, cr_ref).reshape(512, CHAN)).astype(BF16)


def edges(d_branch, cot):
    d_branch, cot = d_branch.reshape(16, 4, 32, CHAN), cot.reshape(16, 4, 32, CHAN)
    specs = []
    for row in (0, 15):
        specs += [pl.BlockSpec((1, 4, 32, CHAN), lambda i, row=row: (row, 0, 0, 0))] * 2
    for col in (0, 3):
        specs += [pl.BlockSpec((16, 1, 32, CHAN), lambda i, col=col: (0, col, 0, 0))] * 2
    return pl.pallas_call(
        edges_body,
        grid=(1,),
        in_specs=specs + [whole((32, 512))] * 2,
        out_specs=[whole((COLS, CHAN))] * 2 + [whole((ROWS, CHAN))] * 2,
        out_shape=[jax.ShapeDtypeStruct((COLS, CHAN), BF16)] * 2
        + [jax.ShapeDtypeStruct((ROWS, CHAN), BF16)] * 2,
        compiler_params=params(24),
        cost_estimate=pl.CostEstimate(flops=MIB, bytes_accessed=2 * MIB, transcendentals=0),
        name="edges",
    )(*([d_branch, cot] * 4), jnp.asarray(FIRST_CELL, BF16), jnp.asarray(LAST_CELL, BF16))


def shifts():
    n_lat, n_lon = lax.axis_size("lat"), lax.axis_size("lon")
    south = [(i, i + 1) for i in range(n_lat - 1)]
    north = [(i + 1, i) for i in range(n_lat - 1)]
    east = [(i, (i + 1) % n_lon) for i in range(n_lon)]
    west = [((i + 1) % n_lon, i) for i in range(n_lon)]
    return (south, north, east, west)


def rows_of(top, bottom):
    south, north, _, _ = shifts()
    return (lax.ppermute(bottom, "lat", south), lax.ppermute(top, "lat", north))


def halo_of(above, below, left, right):
    _, _, east, west = shifts()
    pad = jnp.zeros((EDGE - ROWS - 2, left.shape[1]), left.dtype)
    from_west = lax.ppermute(
        jnp.concatenate([above[-1:], right, below[-1:], pad], axis=0), "lon", east
    )
    from_east = lax.ppermute(
        jnp.concatenate([above[:1], left, below[:1], pad], axis=0), "lon", west
    )
    return jnp.concatenate([above, below, from_west, from_east], axis=0)


def wide_rows(field):
    flat = (2 * COLS, CHAN)
    above, below = rows_of(field[:2].reshape(flat), field[-2:].reshape(flat))
    return (above.reshape(2, COLS, CHAN), below.reshape(2, COLS, CHAN))


def wide_columns(field, above, below):
    _, _, east, west = shifts()
    pad = jnp.zeros((2, EDGE - ROWS - 4, field.shape[2]), field.dtype)

    def columns(at):
        parts = [part[:, at : at + 2].transpose(1, 0, 2) for part in (above, field, below)]
        return jnp.concatenate(parts + [pad], axis=1)

    own_west, own_east = columns(0), columns(COLS - 2)
    from_west = lax.ppermute(own_east, "lon", east)
    from_east = lax.ppermute(own_west, "lon", west)
    return (from_west, from_east, own_west, own_east)


def members():
    n_lat, n_lon = lax.axis_size("lat"), lax.axis_size("lon")
    order = np.arange(n_lat * n_lon).reshape(n_lat, n_lon // 2, 2)
    return order.transpose(2, 0, 1).reshape(2, -1).tolist()


def exchange(pieces):
    return lax.all_to_all(
        pieces, ("lat", "lon"), split_axis=0, concat_axis=0, axis_index_groups=members(), tiled=True
    )


def to_pieces(field):
    shaped = field.reshape(16, 2, 4, 16, CHAN).transpose(0, 2, 1, 3, 4)
    return shaped.reshape(64, 32, CHAN)


def pairs():
    return np.arange(lax.axis_size("lon")).reshape(-1, 2).tolist()


def other_core(tiles):
    swaps = [move for a, b in pairs() for move in ((a, b), (b, a))]
    return lax.ppermute(tiles, "lon", swaps)


def rel_table():
    position = np.arange(64)
    pos_row, pos_col = position // 8, position % 8
    rel_index = (pos_row[:, None] - pos_row[None, :] + 7) * 15 + (
        pos_col[:, None] - pos_col[None, :] + 7
    )
    return jnp.asarray(rel_index)[:, :, None] == jnp.arange(225)[None, None, :]


def on_device(
    field_in, cotangent, expand_weight, depth_kernel, project_weight, qkv_weight, out_weight, rel_bias
):
    onehot = rel_table().astype(F32)
    bias = jnp.einsum(
        "tsr,hr->sht", onehot, rel_bias.reshape(4, 225), precision=lax.Precision.HIGHEST
    ).reshape(64, 256)
    dk = depth_kernel.reshape(9, EXP)

    dkb = jnp.broadcast_to(dk[:, None], (9, 8, EXP))
    core = lax.axis_index("lon").astype(jnp.int32).reshape(1) & 1
    barrier = lax.optimization_barrier

    above, below = wide_rows(field_in)
    hidden = expand(field_in, expand_weight, False)
    above, below, hidden, late_cot = barrier((above, below, hidden, cotangent))
    field_halo = (above, below, *wide_columns(field_in, above, below))
    field_halo, cot_pieces = barrier((field_halo, to_pieces(late_cot)))
    hidden, cot_pieces = barrier((hidden, cot_pieces))
    cot_groups = exchange(cot_pieces)
    section, mixed, mixed_pre, ring_slope = mix(
        hidden, field_halo, expand_weight, dk, project_weight, field_in
    )
    groups = exchange(section)
    cot_swapped, d_att = prepare(cot_groups, out_weight, 32)
    section_field, _ = barrier((field_in, section))
    act_slope = expand(section_field, expand_weight, True)
    groups, bias, d_att, act_slope = barrier((groups, bias, d_att, act_slope))
    d_groups, attended, normed2, d_proj, bias_acc = attention(groups, d_att, qkv_weight, bias)

    d_branch = exchange(d_groups)
    attention_tiles = attention_sums(attended, cot_swapped.reshape(-1, CHAN), normed2, d_proj)
    bias_sum = jnp.einsum(
        "sht,tsr->hr", bias_acc.reshape(64, 4, 64), onehot, precision=lax.Precision.HIGHEST
    )
    extra = jnp.pad(bias_sum.reshape(60, 1, 15), ((0, 68), (1, 6), (0, 113)))
    mixed_pre, _ = barrier((mixed_pre, d_groups))
    mixed_slope = mixed_slopes(mixed_pre)
    d_branch, attention_tiles, extra, mixed_slope = barrier((d_branch, attention_tiles, extra, mixed_slope))

    top, bottom, left, right = edges(d_branch, cot_pieces)
    above, below = rows_of(top, bottom)
    project_tiles = project_sum(cotangent, d_branch, mixed)
    above, below, project_tiles, attention_tiles, mixed_slope = barrier(
        (above, below, project_tiles, attention_tiles, mixed_slope)
    )
    d_halo = halo_of(above, below, left, right)
    attention_other, project_other = other_core(attention_tiles), other_core(project_tiles)
    d_mixed = project_back(cotangent, d_branch, mixed_slope, project_weight)
    d_halo, d_mixed, attention_other, project_other = barrier(
        (d_halo, d_mixed, attention_other, project_other)
    )
    attention_pair = (attention_tiles, attention_other)
    project_pair = (project_tiles, project_other)
    d_pre, expand_tiles = expand_back(
        d_mixed, d_halo, ring_slope, project_weight, hidden, act_slope, field_in, dkb, extra
    )

    joined = join(core, *attention_pair, *project_pair, expand_tiles, other_core(expand_tiles))
    joined, d_pre = barrier((joined, d_pre))
    terms = exchange(joined)
    grad_in = finish(d_pre, field_in, cotangent, d_branch, expand_weight)
    terms, grad_in = barrier((terms, grad_in))
    sums = exchange(fold(terms))
    *grads, bias_grad = unfold(core, sums, other_core(sums))
    return (grad_in, *grads, bias_grad.transpose(1, 0, 2))


def solution(mesh):
    placed = (P("lat", "lon", None), P("lat", "lon", None), P(), P(), P(), P(), P(), P())
    return jax.shard_map(
        on_device,
        mesh=mesh,
        in_specs=placed,
        out_specs=(P("lat", "lon", None), P(), P(), P(), P(), P(), P()),
        check_vma=False,
    )
```
